32 devices in a mesh: frames: 8 (over z, x), tokens: 4 (over y, core).
Axes of the slice: x: 2, y: 2, z: 4, core: 2. Of those that a mesh axis runs over, the one named last changes fastest.
Arguments:
- encoder_out: bfloat16 [8, 512, 512], P('tokens', 'frames'), may hold values from -6 to 6
- encoder_weight: bfloat16 [512, 512], replicated, may hold values from -0.1875 to 0.1875
- encoder_bias: float32 [512], replicated, may hold values from -2 to 2
- predictor_out: bfloat16 [8, 24, 512], P('frames', 'tokens'), may hold values from -6 to 6
- predictor_weight: bfloat16 [512, 512], replicated, may hold values from -0.1875 to 0.1875
- predictor_bias: float32 [512], replicated, may hold values from -2 to 2
- output_weight: bfloat16 [512, 1024], replicated, may hold values from -0.5 to 0.5
- output_bias: float32 [1024], replicated, may hold values from -3 to 3
- labels: int32 [8, 24], P(None, 'tokens'), may hold values from 1 to 1023
- frame_lens: int32 [8], replicated, may hold values from 85 to 512, as said below
- token_lens: int32 [8], replicated, may hold values from 1 to 23, as said below
- loss_scale: float32 [8], replicated, may hold values from 0.5 to 1.5
Outputs:
- losses: float32 [8], P('frames')
- encoder_gradient: float32 [8, 512, 512], P('tokens', 'frames')
- predictor_gradient: float32 [8, 24, 512], P('frames', 'tokens')
- encoder_weight_gradient: float32 [512, 512], replicated
- encoder_bias_gradient: float32 [512], replicated
- predictor_weight_gradient: float32 [512, 512], replicated
- predictor_bias_gradient: float32 [512], replicated
- output_weight_gradient: float32 [512, 1024], replicated
- output_bias_gradient: float32 [1024], replicated
The draws below stay inside these ranges and needn't reach their ends.
Inputs may be any that keep to these rules, and one draw needn't show every extreme that they name: `frame_lens`: some sequence, drawn from the seed, has all 512 frames. `token_lens`: the sequence with all 512 frames has 23 labels.
All inputs are finite; a program needn't handle non-finite values.
Results may differ from the reference program's by a relative error of at most 0.0087.
Values may be sent and summed in bfloat16 or wider, within the bound.
No kernel may reach another device: no remote copies, remote signals or barrier semaphores. Data moves between devices by JAX's collectives and lax.ppermute only.
A program may use at most 256 MiB of HBM per device.

```python
from functools import partial
import jax
import jax.numpy as jnp
from jax import lax

D = 512
V = 1024
T_SIZE = 512
NSEQ = 8
UC = 24


def shared_lengths(key):
    key = jax.random.fold_in(key, 11)
    first, second, third, fourth = jax.random.split(key, 4)
    short_lens = jax.random.randint(first, (NSEQ,), T_SIZE // 6, T_SIZE // 3 + 1)
    long_lens = jax.random.randint(second, (NSEQ,), T_SIZE // 2, T_SIZE + 1)
    pick_long = jax.random.randint(third, (NSEQ,), 0, 4)
    chosen = jnp.where(pick_long == 0, long_lens, short_lens)
    fullest = jax.random.randint(fourth, (), 0, NSEQ)
    frames_all = jnp.where(jnp.arange(NSEQ) == fullest, T_SIZE, chosen).astype(jnp.int32)
    return (frames_all, fullest)


def draw_frame_lens(key, part):
    frames_all, fullest = shared_lengths(key)
    return frames_all


def draw_token_lens(key, part):
    frames_all, fullest = shared_lengths(key)
    key = jax.random.fold_in(key, 23)
    jitter = jax.random.randint(key, (NSEQ,), -2, 3)
    chosen = jnp.clip(frames_all * (UC - 1) // T_SIZE + jitter, 1, UC - 1)
    return jnp.where(jnp.arange(NSEQ) == fullest, UC - 1, chosen).astype(jnp.int32)


def with_ends(array, stream_key, low, top_value):
    longest = array.shape.index(max(array.shape))
    spots = []
    for shift in (0, 1):
        where = [jax.random.randint(jax.random.fold_in(stream_key, axis), (), 0, length) for axis, length in enumerate(array.shape)]
        where[longest] = (where[longest] + shift) % array.shape[longest]
        spots.append(tuple(where))
    return array.at[spots[0]].set(low).at[spots[1]].set(top_value)


def steps_of(own_key, extent, cuts, low, largest):
    def one(position, shards_of):
        heights = jax.random.uniform(jax.random.fold_in(jax.random.fold_in(own_key, 6), position), (shards_of,), jnp.float32, low / len(cuts), largest / len(cuts))
        return jnp.repeat(jnp.exp(heights), extent[position] // shards_of).reshape((-1,) + (1,) * (len(extent) - position - 1))

    loudness = one(*cuts[0])
    for cut in cuts[1:]:
        loudness = loudness * one(*cut)
    return loudness


def centred(stream_key, shape, spread, most, shards=(), kind=jnp.bfloat16):
    level = steps_of(stream_key, shape, shards, -0.22, 0.18) if shards else 1.0
    array = jax.random.normal(stream_key, shape, jnp.float32) * spread * level
    return jnp.minimum(jnp.maximum(array, -most), most).astype(kind)


def setup_inputs(seed: int = 0) -> dict:
    seeds = jax.random.split(jax.random.key(seed), 13)
    encoder_out = centred(seeds[0], (NSEQ, T_SIZE, D), 1.0, 6.0, ((0, 4), (1, 8)))
    encoder_weight = centred(seeds[1], (D, D), (2 * D) ** -0.5, 0.1875)
    encoder_bias = centred(seeds[2], (D,), 0.3, 2.0, (), jnp.float32)
    predictor_out = centred(seeds[3], (NSEQ, UC, D), 1.0, 6.0, ((0, 8), (1, 4)))
    predictor_weight = centred(seeds[4], (D, D), (2 * D) ** -0.5, 0.1875)
    predictor_bias = centred(seeds[5], (D,), 0.3, 2.0, (), jnp.float32)
    output_weight = centred(seeds[6], (D, V), (D // 4) ** -0.5, 0.5)
    output_bias = centred(seeds[7], (V,), 0.5, 3.0, (), jnp.float32)
    labels = with_ends(jax.random.randint(seeds[8], (NSEQ, UC), 1, V), jax.random.fold_in(seeds[8], 1), 1, V - 1).astype(jnp.int32)
    frame_lens = draw_frame_lens(jax.random.fold_in(seeds[12], 71), 0)
    token_lens = draw_token_lens(jax.random.fold_in(seeds[12], 71), 0)
    loss_scale = jnp.clip(jax.random.uniform(seeds[11], (NSEQ,), jnp.float32, 0.5, 1.5), 0.5, 1.5)
    return dict(encoder_out=encoder_out, encoder_weight=encoder_weight, encoder_bias=encoder_bias, predictor_out=predictor_out, predictor_weight=predictor_weight, predictor_bias=predictor_bias, output_weight=output_weight, output_bias=output_bias, labels=labels, frame_lens=frame_lens, token_lens=token_lens, loss_scale=loss_scale)


@jax.custom_vjp
def low(v):
    return lax.optimization_barrier(v.astype(jnp.bfloat16)).astype(jnp.float32)

@jax.custom_vjp
def low_back(v):
    return v

def low_keep(v):
    return (low(v), None)

def low_pass(kept, grad):
    return (grad,)

def back_keep(v):
    return (v, None)

def back_low(kept, grad):
    return (low(grad),)
low.defvjp(low_keep, low_pass)
low_back.defvjp(back_keep, back_low)
VERY_NEGATIVE = -1e+30
HIGHEST_PRECISION = lax.Precision.HIGHEST

def frame_block(frame_count, column_count):
    frame_span = frame_count
    while frame_span * column_count > 4096 and frame_span % 2 == 0:
        frame_span = frame_span // 2
    return frame_span

def exclusive_sum(rows):
    return jnp.concatenate([jnp.zeros_like(rows[..., :1]), jnp.cumsum(rows[..., :-1], axis=-1)], axis=-1)

def one_sequence(weight_out, bias_out, item):
    frame_seq, token_seq, label_seq, frame_len, token_len = item
    frame_span = frame_block(T_SIZE, UC)

    def block(frame_part):
        hidden = low(jnp.tanh(frame_part[:, None, :] + token_seq[None, :, :]))
        logits = jnp.dot(hidden.reshape(-1, D), weight_out, precision=HIGHEST_PRECISION).reshape(frame_span, UC, V) + bias_out
        logits = low_back(logits)
        log_total = jax.nn.logsumexp(logits, axis=2)
        chosen = jnp.broadcast_to(label_seq[None, :, None], (frame_span, UC, 1)).astype(jnp.int32)
        picked = jnp.take_along_axis(logits, chosen, axis=2)[:, :, 0]
        return (logits[:, :, 0] - log_total, picked - log_total)
    blank_score, label_score = lax.map(jax.checkpoint(block), frame_seq.reshape(T_SIZE // frame_span, frame_span, D))
    blank_score = blank_score.reshape(T_SIZE, UC)
    label_score = label_score.reshape(T_SIZE, UC)

    def frame_step(state_row, frame_row):
        row_blank, row_label = frame_row
        running = exclusive_sum(row_label)
        forward_log = running + lax.cumlogsumexp(state_row - running, axis=0)
        return (forward_log + row_blank, forward_log + row_blank)
    anchor_row = jnp.where(jnp.arange(UC) == 0, 0.0, VERY_NEGATIVE).astype(jnp.float32)
    _, leaving = lax.scan(frame_step, anchor_row, (blank_score, label_score))
    return -leaving[frame_len - 1, token_len]

def forward(encoder_in, weight_enc, bias_enc, predictor_in, weight_pred, bias_pred, weight_out, bias_out, labels, frame_lens, token_lens):
    frame_proj = low_back(low(jnp.dot(encoder_in.reshape(-1, D), weight_enc, precision=HIGHEST_PRECISION) + bias_enc)).reshape(NSEQ, T_SIZE, D)
    token_proj = low_back(low(jnp.dot(predictor_in.reshape(-1, D), weight_pred, precision=HIGHEST_PRECISION) + bias_pred)).reshape(NSEQ, UC, D)
    return lax.map(partial(one_sequence, weight_out, bias_out), (frame_proj, token_proj, labels, frame_lens, token_lens))

def reference(encoder_out, encoder_weight, encoder_bias, predictor_out, predictor_weight, predictor_bias, output_weight, output_bias, labels, frame_lens, token_lens, loss_scale):
    primals = (encoder_out.astype(jnp.float32), encoder_weight.astype(jnp.float32), encoder_bias, predictor_out.astype(jnp.float32), predictor_weight.astype(jnp.float32), predictor_bias, output_weight.astype(jnp.float32), output_bias)

    def loss_of(encoder_in, weight_enc, bias_enc, predictor_in, weight_pred, bias_pred, weight_out, bias_out):
        return forward(encoder_in, weight_enc, bias_enc, predictor_in, weight_pred, bias_pred, weight_out, bias_out, labels, frame_lens, token_lens)
    losses, pullback = jax.vjp(loss_of, *primals)
    tangents = pullback(loss_scale)
    return (losses, tangents[0], tangents[3], tangents[1], tangents[2], tangents[4], tangents[5], tangents[6], tangents[7])
```

```python
import functools

import jax
import jax.numpy as jnp
from jax import lax
from jax.experimental import pallas as pl
from jax.experimental.pallas import tpu as pltpu
from jax.sharding import PartitionSpec as P

NEG = -1e30
LOG2E = 1.4426950408889634
LN2 = 0.6931471805599453
BF16 = jnp.bfloat16
F32 = jnp.float32
GROUP = 32
SUB_UNITS = 4
AXES = ("frames", "tokens")


def lane_ids(rows):
    return lax.broadcasted_iota(jnp.int32, (rows, 128), 1)


def log2_add(a, b):
    return jnp.maximum(a, b) + jnp.log2(1.0 + jnp.exp2(-jnp.abs(a - b)))


def both_ways(blank_ref, label_ref, units, steps, ahead, behind, keep=None):
    def one_step(i, state):
        ahead, behind = state
        back = steps - 1 - i
        here = pl.ds(pl.multiple_of(i * units, 8), units)
        there = pl.ds(pl.multiple_of(back * units, 8), units)
        if keep is not None:
            keep[0][here, :] = ahead
            keep[1][there, :] = behind
        from_left = pltpu.roll(ahead + label_ref[here, :], 1, 0)
        to_right = pltpu.roll(behind, units - 1, 0) + label_ref[there, :]
        ahead = log2_add(ahead + blank_ref[here, :], from_left)
        behind = log2_add(behind + blank_ref[there, :], to_right)
        return ahead, behind

    return lax.fori_loop(0, steps, one_step, (ahead, behind))


def packet_kernel(predictor_ref, labels_ref, packets_ref):
    seqs, units = labels_ref.shape
    width = packets_ref.shape[2]
    flat = jnp.zeros((1, width), F32)
    for s in range(seqs):
        row = labels_ref[s : s + 1, :].astype(F32)
        row = jnp.concatenate([row, jnp.zeros((1, width - units), F32)], axis=1)
        flat = flat + (pltpu.roll(row, s * units, 1) if s else row)
    high = jnp.floor(flat * (1.0 / 32.0))
    packet = jnp.concatenate(
        [predictor_ref[...].astype(F32), high, flat - high * 32.0], axis=0
    ).astype(BF16)
    for d in range(packets_ref.shape[0]):
        packets_ref[d] = packet


def block_counts(lens_ref, tokens_ref, first_seq, first_frame):
    counts = []
    for s in range(2):
        inside = first_frame < lens_ref[first_seq + s]
        counts.append(jnp.where(inside, tokens_ref[first_seq + s] // SUB_UNITS + 1, 0))
    return counts


def score_kernel(
    seqs_here,
    offset_ref,
    packets_ref,
    lens_hbm,
    tokens_hbm,
    encoder_hbm,
    encoder_weight_hbm,
    encoder_bias_hbm,
    predictor_weight_hbm,
    predictor_bias_hbm,
    weight_hbm,
    bias_hbm,
    softmax_ref,
    frame_ref,
    token_ref,
    label_table_ref,
    blank_ref,
    label_ref,
    encoder_ref,
    encoder_weight_ref,
    predictor_weight_ref,
    weight_ref,
    matrix_ref,
    label_rows_ref,
    encoder_bias_ref,
    predictor_bias_ref,
    bias_ref,
    lens_ref,
    tokens_ref,
    load_sems,
):
    loads = [
        pltpu.make_async_copy(source, target, load_sems.at[n])
        for n, (source, target) in enumerate(
            (
                (predictor_weight_hbm, predictor_weight_ref),
                (predictor_bias_hbm, predictor_bias_ref),
                (encoder_hbm, encoder_ref),
                (encoder_weight_hbm, encoder_weight_ref),
                (encoder_bias_hbm, encoder_bias_ref),
                (weight_hbm, weight_ref),
                (bias_hbm, bias_ref),
                (lens_hbm, lens_ref),
                (tokens_hbm, tokens_ref),
            )
        )
    ]
    for load in loads:
        load.start()
    seqs, frame_count, width = encoder_ref.shape
    units = token_ref.shape[0] // seqs
    shards = label_rows_ref.shape[0]
    shard_units = units // shards
    steps = frame_count + units - 1
    first_frame = lax.axis_index("frames") * frame_count
    first_seq = lax.axis_index("tokens") * seqs_here + offset_ref[0]
    vocab = weight_ref.shape[1]
    blank_ref[...] = jnp.zeros_like(blank_ref)
    label_ref[...] = jnp.full(label_ref.shape, NEG, F32)
    for s in range(seqs):
        for k in range(shards):
            rows = packets_ref[(first_seq + s) * shards + k]
            at = s * units + k * shard_units
            token_ref[at : at + shard_units, :] = rows[:shard_units].astype(F32)
    for k in range(shards):
        halves = packets_ref[k, shard_units:, :].astype(F32)
        label_rows_ref[k : k + 1, :] = halves[:1] * 32.0 + halves[1:2]
    loads[0].wait()
    loads[1].wait()
    token_ref[...] = (
        jnp.dot(token_ref[...].astype(BF16), predictor_weight_ref[...], preferred_element_type=F32)
        + predictor_bias_ref[...]
    ).astype(BF16).astype(F32)
    wide = lax.broadcasted_iota(jnp.int32, (1, width), 1)
    for s in range(seqs):
        for u in range(units):
            lane = (first_seq + s) * shard_units + u % shard_units
            row = label_rows_ref[u // shard_units : u // shard_units + 1, :]
            value = jnp.sum(jnp.where(wide == lane, row, 0.0), axis=1, keepdims=True)
            label_table_ref[s * units + u : s * units + u + 1, :] = jnp.broadcast_to(
                value, (1, 128)
            ).astype(jnp.int32)
    loads[2].wait()
    loads[3].wait()
    loads[4].wait()
    frame_ref[...] = (
        (
            jnp.dot(
                encoder_ref[...].reshape(seqs * frame_count, width),
                encoder_weight_ref[...],
                preferred_element_type=F32,
            )
            + encoder_bias_ref[...]
        )
        .astype(BF16)
        .astype(F32)
        .reshape(frame_ref.shape)
    )
    for load in loads[5:]:
        load.wait()

    counts = block_counts(lens_ref, tokens_ref, first_seq, first_frame)
    lanes = lane_ids(frame_count)
    vocab_ids = lax.broadcasted_iota(jnp.int32, (frame_count, vocab), 1)
    times = first_frame + lax.broadcasted_iota(jnp.int32, (frame_count, 1), 0)

    def one_block(i, _):
        seq = jnp.where(i >= counts[0], 1, 0)
        sub = i - seq * counts[0]
        first_unit = sub * SUB_UNITS
        seq_len = lens_ref[first_seq + seq]
        last_unit = tokens_ref[first_seq + seq]
        own_lanes = (lanes // GROUP) % 2 == seq
        frames = frame_ref[seq]
        hidden = jnp.concatenate(
            [
                jnp.tanh(frames + token_ref[pl.ds(seq * units + first_unit + j, 1), :])
                for j in range(SUB_UNITS)
            ],
            axis=0,
        ).astype(BF16)
        logits = jnp.dot(hidden, weight_ref[...], preferred_element_type=F32) + bias_ref[...]
        top = jnp.max(logits, axis=1, keepdims=True)
        weights = jnp.exp(logits - top)
        total = jnp.sum(weights, axis=1, keepdims=True)
        softmax_ref[seq * (units // SUB_UNITS) + sub] = weights * (1.0 / total)
        log_total = top + jnp.log(total)
        blanks = (logits[:, :1] - log_total) * LOG2E
        for j in range(SUB_UNITS):
            unit = first_unit + j
            rows = slice(j * frame_count, (j + 1) * frame_count)
            label = label_table_ref[pl.ds(seq * units + unit, 1), :]
            label = jnp.concatenate([label] * (vocab // 128), axis=1)
            picked = jnp.sum(
                jnp.where(vocab_ids == label, logits[rows], 0.0), axis=1, keepdims=True
            )
            blank = blanks[rows]
            blank = jnp.where((times == seq_len - 1) & (unit < last_unit), NEG, blank)
            blank = jnp.where((times >= seq_len) | (unit > last_unit), 0.0, blank)
            step = jnp.where(
                (times >= seq_len) | (unit >= last_unit),
                NEG,
                (picked - log_total[rows]) * LOG2E,
            )
            at = (pl.ds(unit * (units + 1), frame_count, stride=units), slice(None))
            blank_ref[at] = jnp.where(own_lanes, blank, blank_ref[at])
            label_ref[at] = jnp.where(own_lanes, step, label_ref[at])
        return 0

    lax.fori_loop(0, counts[0] + counts[1], one_block, 0)
    eye = jnp.where(
        lane_ids(units) % GROUP == lax.broadcasted_iota(jnp.int32, (units, 128), 0), 0.0, NEG
    ).astype(F32)
    ahead, behind = both_ways(blank_ref, label_ref, units, steps, eye, eye)
    matrix_ref[0, 0] = jnp.where(lane_ids(units) < 64, behind, ahead)


def tangent_kernel(
    layout,
    lens_ref,
    tokens_ref,
    offset_ref,
    scale_ref,
    softmax_ref,
    frame_ref,
    token_ref,
    label_table_ref,
    blank_ref,
    label_ref,
    encoder_ref,
    encoder_weight_ref,
    weight_ref,
    *refs,
):
    hops = layout["hops"]
    matrix_refs, refs = refs[: hops + 1], refs[hops + 1 :]
    (
        encoder_gradient_ref,
        kept_ref,
        sent_ref,
        sums_ref,
        matrices_ref,
        ahead_ref,
        behind_ref,
        blank_part_ref,
        label_part_ref,
        frame_sum_ref,
        token_sum_ref,
        output_bias_ref,
        kept_sem,
        sent_sem,
    ) = refs
    seqs, frame_count, width = frame_ref.shape
    units = token_ref.shape[0] // seqs
    steps = frame_count + units - 1
    here = lax.axis_index("frames")
    first_frame = here * frame_count
    first_seq = lax.axis_index("tokens") * layout["seqs_here"] + offset_ref[0]
    chunks = matrices_ref.shape[0]
    vocab = weight_ref.shape[1]
    sums_ref[...] = jnp.zeros_like(sums_ref)
    output_bias_ref[...] = jnp.zeros_like(output_bias_ref)
    token_sum_ref[...] = jnp.zeros_like(token_sum_ref)
    frame_sum_ref[...] = jnp.zeros_like(frame_sum_ref)
    at = 0
    for matrix_ref in matrix_refs:
        matrices_ref[at : at + matrix_ref.shape[0]] = matrix_ref[:, 0]
        at += matrix_ref.shape[0]
    starts = lax.broadcasted_iota(jnp.int32, (units, 128), 0)
    lanes = lane_ids(units)
    early = lanes < 64
    gather_ids = lanes // GROUP * GROUP + starts
    own_first = (lane_ids(1) // GROUP) % 2 == 0

    def one_chunk(i, carry):
        column, kept = carry
        other = chunks - 1 - i
        kept = jnp.where(jnp.where(early, i, other) == here, column, kept)
        joined = column + jnp.where(early, matrices_ref[here ^ i], matrices_ref[here ^ other])
        top = jnp.max(joined, axis=0, keepdims=True)
        row = top + jnp.log2(jnp.sum(jnp.exp2(joined - top), axis=0, keepdims=True))
        row = jnp.broadcast_to(row, (units, 128))
        return jnp.take_along_axis(row, gather_ids, axis=1, mode="promise_in_bounds"), kept

    start = jnp.where(early & (starts > 0), NEG, 0.0).astype(F32)
    last, kept = lax.fori_loop(0, chunks, one_chunk, (start, start))
    swapped_halves = pltpu.roll(kept, 64, 1)
    both_ways(
        blank_ref,
        label_ref,
        units,
        steps,
        jnp.where(early, kept, swapped_halves),
        jnp.where(early, swapped_halves, kept),
        (ahead_ref, behind_ref),
    )
    log_norm = jnp.max(jnp.where(early, last, pltpu.roll(last, 64, 1)), axis=0, keepdims=True)
    scale = jnp.where(own_first, scale_ref[first_seq], scale_ref[first_seq + 1])
    length = jnp.where(own_first, lens_ref[first_seq], lens_ref[first_seq + 1])
    bound = jnp.where(own_first, tokens_ref[first_seq], tokens_ref[first_seq + 1])
    time_limit = jnp.minimum(length - first_frame, frame_count)

    def one_diagonal(e, _):
        rows = pl.ds(pl.multiple_of(e * units, 8), units)
        time = e - starts
        behind = behind_ref[rows, :]
        base = ahead_ref[rows, :] - log_norm
        live = (starts <= bound) & (time >= 0) & (time < time_limit)
        blank_part_ref[rows, :] = jnp.where(
            live, -scale * jnp.exp2(base + blank_ref[rows, :] + behind), 0.0
        )
        label_part_ref[rows, :] = jnp.where(
            live & (starts < bound),
            -scale * jnp.exp2(base + label_ref[rows, :] + pltpu.roll(behind, units - 1, 0)),
            0.0,
        )
        return 0

    lax.fori_loop(0, steps, one_diagonal, 0, unroll=3)

    counts = block_counts(lens_ref, tokens_ref, first_seq, first_frame)
    block_lanes = lane_ids(frame_count)

    def one_block(i, _):
        seq = jnp.where(i >= counts[0], 1, 0)
        sub = i - seq * counts[0]
        first_unit = sub * SUB_UNITS
        own_lanes = (block_lanes // GROUP) % 2 == seq
        frames = frame_ref[seq]
        block = seq * (units // SUB_UNITS) + sub
        hiddens, tangents = [], []
        for j in range(SUB_UNITS):
            unit = first_unit + j
            rows = slice(j * frame_count, (j + 1) * frame_count)
            hiddens.append(jnp.tanh(frames + token_ref[pl.ds(seq * units + unit, 1), :]))
            at = (pl.ds(unit * (units + 1), frame_count, stride=units), slice(None))
            blank, step = blank_part_ref[at], label_part_ref[at]
            blank = jnp.where(own_lanes, blank, pltpu.roll(blank, GROUP, 1))
            step = jnp.where(own_lanes, step, pltpu.roll(step, GROUP, 1))
            label = label_table_ref[pl.ds(seq * units + unit, 1), :]
            both = -(blank + step)
            pieces = []
            for v in range(vocab // 128):
                piece = softmax_ref[block, rows, v * 128 : (v + 1) * 128] * both
                if v == 0:
                    piece = piece + jnp.where(block_lanes == 0, blank, 0.0)
                piece = piece + jnp.where(block_lanes + v * 128 == label, step, 0.0)
                pieces.append(piece.astype(BF16))
            tangents.append(jnp.concatenate(pieces, axis=1))
        hidden = jnp.concatenate(hiddens, axis=0)
        low = hidden.astype(BF16)
        tangent = jnp.concatenate(tangents, axis=0)
        product = lax.dot_general(
            low, tangent, (((0,), (0,)), ((), ())), preferred_element_type=F32
        )
        for v in range(vocab // 128):
            sums_ref[v * width : (v + 1) * width, :] += product[:, v * 128 : (v + 1) * 128]
        output_bias_ref[...] += jnp.sum(tangent.astype(F32), axis=0, keepdims=True)
        inner = lax.dot_general(
            tangent, weight_ref[...], (((1,), (1,)), ((), ())), preferred_element_type=F32
        ) * (1.0 - hidden * hidden)
        total = frame_sum_ref[seq]
        for j in range(SUB_UNITS):
            rows = slice(j * frame_count, (j + 1) * frame_count)
            total = total + inner[rows]
            token_sum_ref[pl.ds(seq * units + first_unit + j, 1), :] = jnp.sum(
                inner[rows], axis=0, keepdims=True
            )
        frame_sum_ref[seq] = total
        return 0

    lax.fori_loop(0, counts[0] + counts[1], one_block, 0)

    low = frame_sum_ref[...].reshape(seqs * frame_count, width).astype(BF16)
    encoder_gradient_ref[...] = lax.dot_general(
        low, encoder_weight_ref[...], (((1,), (1,)), ((), ())), preferred_element_type=F32
    ).reshape(encoder_gradient_ref.shape)
    product = lax.dot_general(
        encoder_ref[...].reshape(seqs * frame_count, width),
        low,
        (((0,), (0,)), ((), ())),
        preferred_element_type=F32,
    )
    encoder_bias = jnp.sum(low.astype(F32), axis=0, keepdims=True)
    for v in range(width // 128):
        cut = slice(v * 128, (v + 1) * 128)
        at = layout["encoder"] + v * width
        sums_ref[at : at + width, :] = product[:, cut]
        at = layout["token"] + v * layout["token_rows"] + first_seq * units
        sums_ref[pl.ds(pl.multiple_of(at, 8), seqs * units), :] = token_sum_ref[:, cut]
        at = layout["encoder_bias"] + v
        sums_ref[at : at + 1, :] = encoder_bias[:, cut]
    for v in range(vocab // 128):
        at = layout["output_bias"] + v
        sums_ref[at : at + 1, :] = output_bias_ref[:, v * 128 : (v + 1) * 128]
    wide = lane_ids(1)
    loss = jnp.where(here == 0, -log_norm * LN2, 0.0)
    spread = jnp.where(wide == first_seq, loss[:, :1], 0.0)
    spread = spread + jnp.where(wide == first_seq + 1, loss[:, GROUP : GROUP + 1], 0.0)
    for k in range(3):
        part = spread.astype(BF16).astype(F32)
        sums_ref[layout["loss"] + k : layout["loss"] + k + 1, :] = part
        spread = spread - part
    half = sums_ref.shape[0] // 2
    place = lax.axis_index("tokens") & 1
    keep = pltpu.make_async_copy(
        sums_ref.at[pl.ds(pl.multiple_of(place * half, 8), half), :], kept_ref, kept_sem
    )
    send = pltpu.make_async_copy(
        sums_ref.at[pl.ds(pl.multiple_of((1 - place) * half, 8), half), :], sent_ref, sent_sem
    )
    send.start()
    keep.start()
    send.wait()
    keep.wait()


def halve_kernel(stage, kept_ref, received_ref, next_ref, sent_ref):
    even, odd = stage
    f, k = lax.axis_index("frames"), lax.axis_index("tokens")
    upper = jnp.where((k & 1) == 0, (f & even[0]) | (k & even[1]), (f & odd[0]) | (k & odd[1]))
    half = next_ref.shape[0]
    own = pl.ds(pl.multiple_of(jnp.where(upper != 0, half, 0), 16), half)
    other = pl.ds(pl.multiple_of(jnp.where(upper != 0, 0, half), 16), half)
    sent_ref[...] = (kept_ref[other, :] + received_ref[other, :].astype(F32)).astype(sent_ref.dtype)
    next_ref[...] = kept_ref[own, :] + received_ref[own, :].astype(F32)


def finish_kernel(
    layout,
    own_ref,
    other_ref,
    packets_ref,
    predictor_weight_ref,
    output_weight_ref,
    output_bias_ref,
    encoder_weight_ref,
    encoder_bias_ref,
    weight_gradient_ref,
    bias_gradient_ref,
    predictor_gradient_ref,
    losses_ref,
    full_ref,
    tokens_ref,
    predictor_ref,
    own_sem,
    other_sem,
):
    half = own_ref.shape[0]
    width, vocab = output_weight_ref.shape
    place = lax.axis_index("tokens") & 1
    own = pltpu.make_async_copy(
        own_ref, full_ref.at[pl.ds(pl.multiple_of(place * half, 16), half), :], own_sem
    )
    other = pltpu.make_async_copy(
        other_ref, full_ref.at[pl.ds(pl.multiple_of((1 - place) * half, 16), half), :], other_sem
    )
    own.start()
    other.start()
    own.wait()
    other.wait()
    for v in range(vocab // 128):
        output_weight_ref[:, v * 128 : (v + 1) * 128] = full_ref[
            v * width : (v + 1) * width, :
        ].astype(F32)
    for v in range(width // 128):
        at = layout["encoder"] + v * width
        encoder_weight_ref[:, v * 128 : (v + 1) * 128] = full_ref[at : at + width, :].astype(F32)
    rest = full_ref[layout["misc"] :, :].astype(F32)

    def row(name, k):
        at = layout[name] - layout["misc"] + k
        return rest[at : at + 1, :]

    output_bias_ref[...] = jnp.concatenate(
        [row("output_bias", v) for v in range(vocab // 128)], axis=1
    )
    encoder_bias_ref[...] = jnp.concatenate(
        [row("encoder_bias", v) for v in range(width // 128)], axis=1
    )
    count = layout["token_rows"]
    tokens = jnp.concatenate(
        [
            full_ref[layout["token"] + v * count : layout["token"] + (v + 1) * count, :]
            for v in range(width // 128)
        ],
        axis=1,
    )
    held_rows = packets_ref.shape[1] - 2
    for d in range(packets_ref.shape[0]):
        predictor_ref[d * held_rows : (d + 1) * held_rows, :] = packets_ref[
            d, :held_rows, :
        ].astype(F32)
    weight_gradient_ref[...] = lax.dot_general(
        predictor_ref[...].astype(BF16), tokens, (((0,), (0,)), ((), ())), preferred_element_type=F32
    )
    wide = tokens.astype(F32)
    bias_gradient_ref[...] = jnp.sum(wide, axis=0, keepdims=True)
    tokens_ref[...] = wide
    device = lax.axis_index("frames") * lax.axis_size("tokens") + lax.axis_index("tokens")
    mine = jnp.concatenate(
        [tokens_ref[pl.ds(device * held_rows + r, 1), :] for r in range(held_rows)], axis=0
    )
    predictor_gradient_ref[...] = lax.dot_general(
        mine.astype(BF16),
        predictor_weight_ref[...],
        (((1,), (1,)), ((), ())),
        preferred_element_type=F32,
    )
    loss = row("loss", 0) + row("loss", 1) + row("loss", 2)
    losses_ref[...] = jnp.sum(
        jnp.where(lane_ids(1) == lax.axis_index("frames"), loss, 0.0), axis=1, keepdims=True
    )


def in_hbm(array):
    return pltpu.with_memory_space_constraint(array, pltpu.HBM)


def in_vmem(array):
    return pltpu.with_memory_space_constraint(array, pltpu.VMEM)


def permuted(array, partner):
    frames, tokens = lax.axis_size("frames"), lax.axis_size("tokens")
    pairs = []
    for f in range(frames):
        for k in range(tokens):
            g, h = partner(f, k)
            pairs.append((f * tokens + k, g * tokens + h))
    return lax.ppermute(array, AXES, pairs)


def doubled(array):
    blocks, bit = [array], 1
    while bit < lax.axis_size("frames"):
        joined = jnp.concatenate(blocks, axis=0) if len(blocks) > 1 else blocks[0]
        blocks.append(permuted(joined, lambda f, k: (f ^ bit, k)))
        bit *= 2
    return blocks


def stages():
    frame_bits = [(1 << i, 0) for i in range(lax.axis_size("frames").bit_length() - 1)]
    token_bits = [(0, 1 << i) for i in range(1, lax.axis_size("tokens").bit_length() - 1)]
    if len(frame_bits) < 2 or not token_bits:
        order = token_bits + frame_bits
        return list(zip(order, order))
    x, z, y = frame_bits[0], frame_bits[1], token_bits[0]
    rest = frame_bits[2:] + token_bits[1:]
    return list(zip([x, y, z] + rest, [z, x, y] + rest))


def is_upper(stage):
    f, k = lax.axis_index("frames"), lax.axis_index("tokens")
    even, odd = stage
    return jnp.where(
        (k & 1) == 0, (f & even[0]) | (k & even[1]), (f & odd[0]) | (k & odd[1])
    ) != 0


def across(stage):
    even, odd = stage
    return lambda f, k: (f ^ (odd if k & 1 else even)[0], k ^ (odd if k & 1 else even)[1])


def reduced_and_gathered(kept, sent):
    neighbour = lambda f, k: (f, k ^ 1)
    received = permuted(sent, neighbour)
    plan = stages()
    for number, stage in enumerate(plan):
        half = kept.shape[0] // 2
        kept, sent = pl.pallas_call(
            functools.partial(halve_kernel, stage),
            in_specs=[pl.BlockSpec(memory_space=pltpu.VMEM)] * 2,
            out_specs=[pl.BlockSpec(memory_space=pltpu.VMEM)] * 2,
            out_shape=[
                pltpu.VMEM((half, 128), F32),
                pltpu.VMEM((half, 128), BF16 if number < 2 else F32),
            ],
            compiler_params=pltpu.CompilerParams(vmem_limit_bytes=4 * 2**20),
        )(in_vmem(kept), in_vmem(received))
        received = permuted(sent, across(stage))
    array = (kept + received).astype(BF16)
    for stage in reversed(plan):
        upper = is_upper(stage)
        other = permuted(array, across(stage))
        array = jnp.where(
            upper, jnp.concatenate([other, array]), jnp.concatenate([array, other])
        )
    return array, permuted(array, neighbour)


def per_device(
    encoder_out,
    encoder_weight,
    encoder_bias,
    predictor_out,
    predictor_weight,
    predictor_bias,
    output_weight,
    output_bias,
    labels,
    frame_lens,
    token_lens,
    loss_scale,
):
    seq_count, frame_count, width = encoder_out.shape
    vocab = output_weight.shape[1]
    all_seqs = labels.shape[0]
    held_seqs, held_units = predictor_out.shape[:2]
    assert held_seqs == 1
    frame_axis, token_axis = lax.axis_size("frames"), lax.axis_size("tokens")
    device_count = frame_axis * token_axis
    units = held_units * token_axis
    calls = seq_count // 2
    steps = frame_count + units - 1
    diagonals = (steps + 1) * units
    smem = pl.BlockSpec(memory_space=pltpu.SMEM)
    vmem = pl.BlockSpec(memory_space=pltpu.VMEM)
    anywhere = pl.BlockSpec(memory_space=pl.ANY)
    params = pltpu.CompilerParams(vmem_limit_bytes=28 * 2**20)

    packets = pl.pallas_call(
        packet_kernel,
        in_specs=[vmem] * 2,
        out_specs=vmem,
        out_shape=jax.ShapeDtypeStruct((device_count, held_units + 2, width), BF16),
    )(predictor_out.reshape(held_units, width), labels)
    packets = lax.all_to_all(packets, AXES, 0, 0, tiled=True)

    score_shapes = [
        ((2 * units // SUB_UNITS, SUB_UNITS * frame_count, vocab), F32),
        ((2, frame_count, width), F32),
        ((2 * units, width), F32),
        ((2 * units, 128), jnp.int32),
        ((diagonals, 128), F32),
        ((diagonals, 128), F32),
        ((2, frame_count, width), BF16),
        ((width, width), BF16),
        ((width, width), BF16),
        ((width, vocab), BF16),
        ((1, 1, units, 128), F32),
    ]

    def scores(given):
        offset, encoder = given
        return pl.pallas_call(
            functools.partial(score_kernel, seq_count),
            in_specs=[smem, vmem] + [anywhere] * 9,
            out_specs=[vmem] * len(score_shapes),
            out_shape=[pltpu.VMEM(s, t) for s, t in score_shapes],
            scratch_shapes=[
                pltpu.VMEM((token_axis, width), F32),
                pltpu.VMEM((1, width), F32),
                pltpu.VMEM((1, width), F32),
                pltpu.VMEM((1, vocab), F32),
                pltpu.SMEM(frame_lens.shape, jnp.int32),
                pltpu.SMEM(token_lens.shape, jnp.int32),
                pltpu.SemaphoreType.DMA((9,)),
            ],
            compiler_params=params,
        )(
            offset,
            in_vmem(packets),
            *map(
                in_hbm,
                (
                    frame_lens,
                    token_lens,
                    encoder,
                    encoder_weight,
                    encoder_bias.reshape(1, width),
                    predictor_weight,
                    predictor_bias.reshape(1, width),
                    output_weight,
                    output_bias.reshape(1, vocab),
                ),
            ),
        )

    offsets = 2 * jnp.arange(calls, dtype=jnp.int32).reshape(calls, 1)
    encoders = encoder_out.reshape(calls, 2, frame_count, width)
    if calls == 1:
        scored = scores((offsets[0], encoder_out))
        matrix = scored[-1]
    else:
        scored = lax.map(scores, (offsets, encoders))
        matrix = scored[-1].reshape(1, calls, units, 128)

    for_tangents = lambda scored: [*scored[:8], scored[9]]
    matrices = doubled(matrix)
    layout = {"seqs_here": seq_count}
    at = vocab // 128 * width
    layout["encoder"] = at
    at += width // 128 * width
    layout["token"], layout["token_rows"] = at, all_seqs * units
    at += width // 128 * all_seqs * units
    layout["misc"] = layout["output_bias"] = at
    at += vocab // 128
    layout["encoder_bias"] = at
    at += width // 128
    layout["loss"] = at
    at += 3
    rows = at + (-at % (16 * device_count))

    def tangents(given):
        offset, scored, matrices = given
        return pl.pallas_call(
            functools.partial(tangent_kernel, dict(layout, hops=len(matrices) - 1)),
            in_specs=[smem] * 4 + [vmem] * (9 + len(matrices)),
            out_specs=[vmem] * 3,
            out_shape=[
                jax.ShapeDtypeStruct((2, frame_count, width), F32),
                pltpu.VMEM((rows // 2, 128), F32),
                pltpu.VMEM((rows // 2, 128), F32),
            ],
            scratch_shapes=[
                pltpu.VMEM((rows, 128), F32),
                pltpu.VMEM((frame_axis, units, 128), F32),
                pltpu.VMEM((diagonals, 128), F32),
                pltpu.VMEM((diagonals, 128), F32),
                pltpu.VMEM((diagonals, 128), F32),
                pltpu.VMEM((diagonals, 128), F32),
                pltpu.VMEM((2, frame_count, width), F32),
                pltpu.VMEM((2 * units, width), F32),
                pltpu.VMEM((1, vocab), F32),
                pltpu.SemaphoreType.DMA,
                pltpu.SemaphoreType.DMA,
            ],
            compiler_params=params,
        )(
            frame_lens,
            token_lens,
            offset,
            loss_scale,
            *map(in_vmem, (*scored, *matrices)),
        )

    if calls == 1:
        encoder_gradient, kept, sent = tangents((offsets[0], for_tangents(scored), matrices))
    else:

        def add_call(sums, given):
            offset, scored, call = given
            own = [lax.dynamic_slice_in_dim(m, call, 1, 1) for m in matrices]
            gradient, kept, sent = tangents((offset, scored, own))
            return (sums[0] + kept, sums[1] + sent), gradient

        nothing = jnp.zeros((rows // 2, 128), F32)
        (kept, sent), encoder_gradient = lax.scan(
            add_call, (nothing, nothing), (offsets, for_tangents(scored), jnp.arange(calls))
        )
        encoder_gradient = encoder_gradient.reshape(encoder_out.shape)

    own, other = reduced_and_gathered(kept, sent)
    finished = pl.pallas_call(
        functools.partial(finish_kernel, layout),
        in_specs=[anywhere, anywhere, vmem, vmem],
        out_specs=[vmem] * 8,
        out_shape=[
            jax.ShapeDtypeStruct((width, vocab), F32),
            jax.ShapeDtypeStruct((1, vocab), F32),
            jax.ShapeDtypeStruct((width, width), F32),
            jax.ShapeDtypeStruct((1, width), F32),
            jax.ShapeDtypeStruct((width, width), F32),
            jax.ShapeDtypeStruct((1, width), F32),
            jax.ShapeDtypeStruct((held_units, width), F32),
            jax.ShapeDtypeStruct((1, 1), F32),
        ],
        scratch_shapes=[
            pltpu.VMEM((rows, 128), BF16),
            pltpu.VMEM((all_seqs * units, width), F32),
            pltpu.VMEM((all_seqs * units, width), F32),
            pltpu.SemaphoreType.DMA,
            pltpu.SemaphoreType.DMA,
        ],
        compiler_params=params,
    )(own, other, packets, in_vmem(scored[8]) if calls == 1 else predictor_weight)
    return (
        finished[7].reshape(1),
        encoder_gradient,
        finished[6].reshape(1, held_units, width),
        finished[2],
        finished[3].reshape(width),
        finished[4],
        finished[5].reshape(width),
        finished[0],
        finished[1].reshape(vocab),
    )


def solution(mesh):
    placed = (
        P("tokens", "frames", None),
        P(),
        P(),
        P("frames", "tokens", None),
        P(),
        P(),
        P(),
        P(),
        P(None, "tokens"),
        P(),
        P(),
        P(),
    )
    return jax.shard_map(
        per_device,
        mesh=mesh,
        in_specs=placed,
        out_specs=(
            P("frames"),
            P("tokens", "frames", None),
            P("frames", "tokens", None),
            P(),
            P(),
            P(),
            P(),
            P(),
            P(),
        ),
        check_vma=False,
    )
```

```python
import functools

import jax
import jax.numpy as jnp
from jax import lax
from jax.experimental import pallas as pl
from jax.experimental.pallas import tpu as pltpu
from jax.sharding import PartitionSpec as P

NEG = -1e30
LOG2E = 1.4426950408889634
LN2 = 0.6931471805599453
BF16 = jnp.bfloat16
F32 = jnp.float32
GROUP = 32
SUB_UNITS = 4
AXES = ("frames", "tokens")


def lane_ids(rows):
    return lax.broadcasted_iota(jnp.int32, (rows, 128), 1)


def log2_add(a, b):
    return jnp.maximum(a, b) + jnp.log2(1.0 + jnp.exp2(-jnp.abs(a - b)))


def both_ways(blank_ref, label_ref, units, steps, ahead, behind, keep=None):
    def one_step(i, state):
        ahead, behind = state
        back = steps - 1 - i
        here = pl.ds(pl.multiple_of(i * units, 8), units)
        there = pl.ds(pl.multiple_of(back * units, 8), units)
        if keep is not None:
            keep[0][here, :] = ahead
            keep[1][there, :] = behind
        from_left = pltpu.roll(ahead + label_ref[here, :], 1, 0)
        to_right = pltpu.roll(behind, units - 1, 0) + label_ref[there, :]
        ahead = log2_add(ahead + blank_ref[here, :], from_left)
        behind = log2_add(behind + blank_ref[there, :], to_right)
        return ahead, behind

    return lax.fori_loop(0, steps, one_step, (ahead, behind))


def in_two_stages(count, first, second, even, odd, between=None):
    def two_blocks(n, _):
        first(2 * n + 1, odd)
        second(2 * n, even)
        first(jnp.minimum(2 * n + 2, count - 1), even)
        second(2 * n + 1, odd)
        return 0

    @pl.when(count > 0)
    def _():
        first(0, even)

    if between is not None:
        between()

    @pl.when(count > 0)
    def _():
        lax.fori_loop(0, count // 2, two_blocks, 0)

        @pl.when(count % 2 == 1)
        def _():
            second(count - 1, even)


def packet_kernel(predictor_hbm, labels_hbm, *refs):
    *refs, predictor_ref, labels_ref, sems = refs
    count = len(refs) // 2
    packets_ref = refs[count]
    targets = (predictor_ref, labels_ref, *refs[count + 1 :])
    loads = [
        pltpu.make_async_copy(source, target, sems.at[n])
        for n, (source, target) in enumerate(
            zip((predictor_hbm, labels_hbm, *refs[:count]), targets)
        )
    ]
    for load in loads:
        load.start()
    loads[0].wait()
    loads[1].wait()
    seqs, units = labels_ref.shape
    width = packets_ref.shape[2]
    flat = jnp.zeros((1, width), F32)
    for s in range(seqs):
        row = labels_ref[s : s + 1, :].astype(F32)
        row = jnp.concatenate([row, jnp.zeros((1, width - units), F32)], axis=1)
        flat = flat + (pltpu.roll(row, s * units, 1) if s else row)
    high = jnp.floor(flat * (1.0 / 32.0))
    packet = jnp.concatenate(
        [predictor_ref[...].astype(F32), high, flat - high * 32.0], axis=0
    ).astype(BF16)
    for d in range(packets_ref.shape[0]):
        packets_ref[d] = packet
    for load in loads[2:]:
        load.wait()


def block_counts(lens_ref, tokens_ref, first_seq, first_frame):
    counts = []
    for s in range(2):
        inside = first_frame < lens_ref[first_seq + s]
        counts.append(jnp.where(inside, tokens_ref[first_seq + s] // SUB_UNITS + 1, 0))
    return counts


def score_kernel(
    seqs_here,
    offset_ref,
    packets_ref,
    lens_hbm,
    tokens_hbm,
    encoder_ref,
    encoder_weight_ref,
    encoder_bias_ref,
    predictor_weight_ref,
    predictor_bias_ref,
    weight_ref,
    bias_ref,
    softmax_ref,
    frame_ref,
    token_ref,
    label_table_ref,
    blank_ref,
    label_ref,
    hidden_ref,
    turned_ref,
    inverse_ref,
    matrix_ref,
    even_ref,
    odd_ref,
    labels_smem,
    label_rows_ref,
    lens_ref,
    tokens_ref,
    load_sems,
    label_sem,
):
    loads = [
        pltpu.make_async_copy(lens_hbm, lens_ref, load_sems.at[0]),
        pltpu.make_async_copy(tokens_hbm, tokens_ref, load_sems.at[1]),
    ]
    for load in loads:
        load.start()
    seqs, frame_count, width = encoder_ref.shape
    units = token_ref.shape[0] // seqs
    shards = label_rows_ref.shape[0]
    shard_units = units // shards
    steps = frame_count + units - 1
    first_frame = lax.axis_index("frames") * frame_count
    first_seq = lax.axis_index("tokens") * seqs_here + offset_ref[0]
    vocab = weight_ref.shape[1]
    blank_ref[...] = jnp.zeros_like(blank_ref)
    label_ref[...] = jnp.full(label_ref.shape, NEG, F32)
    for s in range(seqs):
        for k in range(shards):
            rows = packets_ref[(first_seq + s) * shards + k]
            at = s * units + k * shard_units
            token_ref[at : at + shard_units, :] = rows[:shard_units].astype(F32)
    for k in range(shards):
        halves = packets_ref[k, shard_units:, :].astype(F32)
        label_rows_ref[k : k + 1, :] = halves[:1] * 32.0 + halves[1:2]
    wide = lane_ids(1)
    table = jnp.zeros((1, 128), F32)
    for s in range(seqs):
        for k in range(shards):
            target = s * units + k * shard_units
            shift = (target - (first_seq + s) * shard_units) % width
            row = pltpu.roll(label_rows_ref[k : k + 1, :], shift, 1)[:, :128]
            table = jnp.where((wide >= target) & (wide < target + shard_units), row, table)
    label_table_ref[...] = table.astype(jnp.int32)
    label_copy = pltpu.make_async_copy(label_table_ref, labels_smem, label_sem)
    label_copy.start()
    token_ref[...] = (
        jnp.dot(token_ref[...].astype(BF16), predictor_weight_ref[...], preferred_element_type=F32)
        + predictor_bias_ref[...]
    ).astype(BF16).astype(F32)
    frame_ref[...] = (
        (
            jnp.dot(
                encoder_ref[...].reshape(seqs * frame_count, width),
                encoder_weight_ref[...],
                preferred_element_type=F32,
            )
            + encoder_bias_ref[...]
        )
        .astype(BF16)
        .astype(F32)
        .reshape(frame_ref.shape)
    )
    for load in loads:
        load.wait()

    counts = block_counts(lens_ref, tokens_ref, first_seq, first_frame)
    blocks = counts[0] + counts[1]
    lanes = lane_ids(frame_count)
    times = first_frame + lax.broadcasted_iota(jnp.int32, (frame_count, 1), 0)

    def place_of(i):
        seq = jnp.where(i >= counts[0], 1, 0)
        sub = i - seq * counts[0]
        return seq, sub, seq * (units // SUB_UNITS) + sub

    def multiply(i, logits_ref):
        seq, sub, block = place_of(i)
        frames = frame_ref[seq]
        hidden = jnp.concatenate(
            [
                jnp.tanh(frames + token_ref[pl.ds(seq * units + sub * SUB_UNITS + j, 1), :])
                for j in range(SUB_UNITS)
            ],
            axis=0,
        )
        hidden_ref[block] = hidden
        low = hidden.astype(BF16)
        turned_ref[block, :width, :] = low.T
        turned_ref[block, width:, :] = jnp.ones(
            (turned_ref.shape[1] - width, turned_ref.shape[2]), BF16
        )
        logits_ref[...] = (
            jnp.dot(low, weight_ref[...], preferred_element_type=F32) + bias_ref[...]
        )

    def score(i, logits_ref):
        seq, sub, block = place_of(i)
        first_unit = sub * SUB_UNITS
        seq_len = lens_ref[first_seq + seq]
        last_unit = tokens_ref[first_seq + seq]
        own_lanes = (lanes // GROUP) % 2 == seq
        logits = logits_ref[...]
        top = jnp.max(logits, axis=1, keepdims=True)
        weights = jnp.exp(logits - top)
        total = jnp.sum(weights, axis=1, keepdims=True)
        softmax_ref[block] = weights
        inverse_ref[block] = jnp.broadcast_to(1.0 / total, (weights.shape[0], 128))
        log_total = top + jnp.log(total)
        blanks = (logits[:, :1] - log_total) * LOG2E
        for j in range(SUB_UNITS):
            unit = first_unit + j
            rows = slice(j * frame_count, (j + 1) * frame_count)
            label = labels_smem[0, seq * units + unit]
            tile = logits_ref[rows, pl.ds(pl.multiple_of(label // 128 * 128, 128), 128)]
            picked = jnp.sum(
                jnp.where(lanes == label % 128, tile, 0.0), axis=1, keepdims=True
            )
            blank = blanks[rows]
            blank = jnp.where((times == seq_len - 1) & (unit < last_unit), NEG, blank)
            blank = jnp.where((times >= seq_len) | (unit > last_unit), 0.0, blank)
            step = jnp.where(
                (times >= seq_len) | (unit >= last_unit),
                NEG,
                (picked - log_total[rows]) * LOG2E,
            )
            at = (pl.ds(unit * (units + 1), frame_count, stride=units), slice(None))
            blank_ref[at] = jnp.where(own_lanes, blank, blank_ref[at])
            label_ref[at] = jnp.where(own_lanes, step, label_ref[at])

    in_two_stages(blocks, multiply, score, even_ref, odd_ref, label_copy.wait)
    eye = jnp.where(
        lane_ids(units) % GROUP == lax.broadcasted_iota(jnp.int32, (units, 128), 0), 0.0, NEG
    ).astype(F32)
    ahead, behind = both_ways(blank_ref, label_ref, units, steps, eye, eye)
    matrix_ref[0, 0] = jnp.where(lane_ids(units) < 64, behind, ahead)


def tangent_kernel(
    layout,
    lens_ref,
    tokens_ref,
    offset_ref,
    scale_ref,
    softmax_ref,
    label_table_ref,
    blank_ref,
    label_ref,
    turned_ref,
    inverse_ref,
    *refs,
):
    hops = layout["hops"]
    matrix_refs, refs = refs[: hops + 1], refs[hops + 1 :]
    (
        tangents_ref,
        output_bias_ref,
        loss_ref,
        *kept_refs,
        sums_ref,
        matrices_ref,
        ahead_ref,
        behind_ref,
        blank_part_ref,
        label_part_ref,
        even_ref,
        odd_ref,
        labels_smem,
        label_sem,
        sems,
    ) = refs
    label_copy = pltpu.make_async_copy(label_table_ref, labels_smem, label_sem)
    label_copy.start()
    sums_ref[...] = jnp.zeros_like(sums_ref)
    output_bias_ref[...] = jnp.zeros_like(output_bias_ref)
    frame_count = layout["frame_count"]
    width = turned_ref.shape[1] - 16
    units = layout["units"]
    steps = frame_count + units - 1
    here = lax.axis_index("frames")
    first_frame = here * frame_count
    first_seq = lax.axis_index("tokens") * layout["seqs_here"] + offset_ref[0]
    chunks = matrices_ref.shape[0]
    vocab = softmax_ref.shape[2]
    at = 0
    for matrix_ref in matrix_refs:
        matrices_ref[at : at + matrix_ref.shape[0]] = matrix_ref[:, 0]
        at += matrix_ref.shape[0]
    starts = lax.broadcasted_iota(jnp.int32, (units, 128), 0)
    lanes = lane_ids(units)
    early = lanes < 64
    gather_ids = lanes // GROUP * GROUP + starts
    own_first = (lane_ids(1) // GROUP) % 2 == 0

    def one_chunk(i, carry):
        column, kept = carry
        other = chunks - 1 - i
        kept = jnp.where(jnp.where(early, i, other) == here, column, kept)
        joined = column + jnp.where(early, matrices_ref[here ^ i], matrices_ref[here ^ other])
        top = jnp.max(joined, axis=0, keepdims=True)
        row = top + jnp.log2(jnp.sum(jnp.exp2(joined - top), axis=0, keepdims=True))
        row = jnp.broadcast_to(row, (units, 128))
        return jnp.take_along_axis(row, gather_ids, axis=1, mode="promise_in_bounds"), kept

    start = jnp.where(early & (starts > 0), NEG, 0.0).astype(F32)
    last, kept = lax.fori_loop(0, chunks, one_chunk, (start, start))
    swapped_halves = pltpu.roll(kept, 64, 1)
    both_ways(
        blank_ref,
        label_ref,
        units,
        steps,
        jnp.where(early, kept, swapped_halves),
        jnp.where(early, swapped_halves, kept),
        (ahead_ref, behind_ref),
    )
    log_norm = jnp.max(jnp.where(early, last, pltpu.roll(last, 64, 1)), axis=0, keepdims=True)
    scale = jnp.where(own_first, scale_ref[first_seq], scale_ref[first_seq + 1])
    length = jnp.where(own_first, lens_ref[first_seq], lens_ref[first_seq + 1])
    bound = jnp.where(own_first, tokens_ref[first_seq], tokens_ref[first_seq + 1])
    time_limit = jnp.minimum(length - first_frame, frame_count)

    def one_diagonal(e, _):
        rows = pl.ds(pl.multiple_of(e * units, 8), units)
        time = e - starts
        behind = behind_ref[rows, :]
        base = ahead_ref[rows, :] - log_norm
        live = (starts <= bound) & (time >= 0) & (time < time_limit)
        blank_part_ref[rows, :] = jnp.where(
            live, -scale * jnp.exp2(base + blank_ref[rows, :] + behind), 0.0
        )
        label_part_ref[rows, :] = jnp.where(
            live & (starts < bound),
            -scale * jnp.exp2(base + label_ref[rows, :] + pltpu.roll(behind, units - 1, 0)),
            0.0,
        )
        return 0

    lax.fori_loop(0, steps, one_diagonal, 0, unroll=3)

    counts = block_counts(lens_ref, tokens_ref, first_seq, first_frame)
    block_lanes = lane_ids(frame_count)

    def place_of(i):
        seq = jnp.where(i >= counts[0], 1, 0)
        sub = i - seq * counts[0]
        return seq, sub, seq * (units // SUB_UNITS) + sub

    wide = lane_ids(1)
    loss = jnp.where(here == 0, -log_norm * LN2, 0.0)
    spread = jnp.where(wide == first_seq, loss[:, :1], 0.0)
    loss_ref[...] = spread + jnp.where(wide == first_seq + 1, loss[:, GROUP : GROUP + 1], 0.0)
    label_copy.wait()

    def prepare(i, tangent_ref):
        seq, sub, block = place_of(i)
        own_lanes = (block_lanes // GROUP) % 2 == seq
        for j in range(SUB_UNITS):
            unit = sub * SUB_UNITS + j
            rows = slice(j * frame_count, (j + 1) * frame_count)
            at = (pl.ds(unit * (units + 1), frame_count, stride=units), slice(None))
            blank, step = blank_part_ref[at], label_part_ref[at]
            blank = jnp.where(own_lanes, blank, pltpu.roll(blank, GROUP, 1))
            step = jnp.where(own_lanes, step, pltpu.roll(step, GROUP, 1))
            both = -(blank + step) * inverse_ref[block, rows, :]
            for v in range(vocab // 128):
                cut = slice(v * 128, (v + 1) * 128)
                piece = softmax_ref[block, rows, cut] * both
                if v == 0:
                    piece = piece + jnp.where(block_lanes == 0, blank, 0.0)
                piece = piece.astype(BF16)
                tangent_ref[rows, cut] = piece
                tangents_ref[block, rows, cut] = piece
            label = labels_smem[0, seq * units + unit]
            cut = pl.ds(pl.multiple_of(label // 128 * 128, 128), 128)
            piece = softmax_ref[block, rows, cut] * both
            piece = piece + jnp.where((block_lanes == 0) & (label < 128), blank, 0.0)
            piece = (piece + jnp.where(block_lanes == label % 128, step, 0.0)).astype(BF16)
            tangent_ref[rows, cut] = piece
            tangents_ref[block, rows, cut] = piece

    def multiply(i, tangent_ref):
        _, _, block = place_of(i)
        product = jnp.dot(turned_ref[block], tangent_ref[...], preferred_element_type=F32)
        for v in range(vocab // 128):
            sums_ref[v * width : (v + 1) * width, :] += product[:width, v * 128 : (v + 1) * 128]
        output_bias_ref[...] += product[width : width + 1, :]

    in_two_stages(counts[0] + counts[1], prepare, multiply, even_ref, odd_ref)
    part_halves(sums_ref, kept_refs, sems)


def part_halves(sums_ref, piece_refs, sems):
    place = lax.axis_index("tokens") & 1
    copies, start = [], 0
    for kept_ref, sent_ref in zip(piece_refs[::2], piece_refs[1::2]):
        half = kept_ref.shape[0]
        for part, target in ((1 - place, sent_ref), (place, kept_ref)):
            source = sums_ref.at[pl.ds(pl.multiple_of(start + part * half, 8), half), :]
            copies.append(pltpu.make_async_copy(source, target, sems.at[len(copies)]))
        start += 2 * half
    for copy in copies:
        copy.start()
    for copy in copies:
        copy.wait()


def inner_kernel(
    layout,
    lens_ref,
    tokens_ref,
    offset_ref,
    tangents_ref,
    hidden_ref,
    weight_ref,
    encoder_ref,
    output_bias_ref,
    loss_ref,
    frame_tangent_ref,
    kept_ref,
    sent_ref,
    sums_ref,
    frame_sum_ref,
    token_sum_ref,
    even_ref,
    odd_ref,
    sems,
):
    seqs, frame_count, width = encoder_ref.shape
    units = token_sum_ref.shape[0] // seqs
    vocab = weight_ref.shape[1]
    first_frame = lax.axis_index("frames") * frame_count
    first_seq = lax.axis_index("tokens") * layout["seqs_here"] + offset_ref[0]
    frame_sum_ref[...] = jnp.zeros_like(frame_sum_ref)
    token_sum_ref[...] = jnp.zeros_like(token_sum_ref)
    unset = slice(layout["token"], sums_ref.shape[0])
    sums_ref[unset, :] = jnp.zeros_like(sums_ref[unset, :])
    counts = block_counts(lens_ref, tokens_ref, first_seq, first_frame)

    def place_of(i):
        seq = jnp.where(i >= counts[0], 1, 0)
        sub = i - seq * counts[0]
        return seq, sub, seq * (units // SUB_UNITS) + sub

    def multiply(i, product_ref):
        _, _, block = place_of(i)
        product_ref[...] = lax.dot_general(
            tangents_ref[block],
            weight_ref[...],
            (((1,), (1,)), ((), ())),
            preferred_element_type=F32,
        )

    def add_up(i, product_ref):
        seq, sub, block = place_of(i)
        hidden = hidden_ref[block]
        inner = product_ref[...] * (1.0 - hidden * hidden)
        total = frame_sum_ref[seq]
        for j in range(SUB_UNITS):
            rows = slice(j * frame_count, (j + 1) * frame_count)
            total = total + inner[rows]
            token_sum_ref[pl.ds(seq * units + sub * SUB_UNITS + j, 1), :] = jnp.sum(
                inner[rows], axis=0, keepdims=True
            )
        frame_sum_ref[seq] = total

    in_two_stages(counts[0] + counts[1], multiply, add_up, even_ref, odd_ref)
    low = frame_sum_ref[...].reshape(seqs * frame_count, width).astype(BF16)
    frame_tangent_ref[...] = low
    product = lax.dot_general(
        encoder_ref[...].reshape(seqs * frame_count, width),
        low,
        (((0,), (0,)), ((), ())),
        preferred_element_type=F32,
    )
    encoder_bias = jnp.sum(low.astype(F32), axis=0, keepdims=True)
    for v in range(width // 128):
        cut = slice(v * 128, (v + 1) * 128)
        at = layout["encoder"] + v * width
        sums_ref[at : at + width, :] = product[:, cut]
        at = layout["token"] + v * layout["token_rows"] + first_seq * units
        sums_ref[pl.ds(pl.multiple_of(at, 8), seqs * units), :] = token_sum_ref[:, cut]
        at = layout["encoder_bias"] + v
        sums_ref[at : at + 1, :] = encoder_bias[:, cut]
    for v in range(vocab // 128):
        at = layout["output_bias"] + v
        sums_ref[at : at + 1, :] = output_bias_ref[:, v * 128 : (v + 1) * 128]
    spread = loss_ref[...]
    for k in range(3):
        part = spread.astype(BF16).astype(F32)
        sums_ref[layout["loss"] + k : layout["loss"] + k + 1, :] = part
        spread = spread - part
    part_halves(sums_ref, (kept_ref, sent_ref), sems)


def encoder_kernel(frame_tangent_ref, encoder_weight_ref, encoder_gradient_ref):
    encoder_gradient_ref[...] = lax.dot_general(
        frame_tangent_ref[...],
        encoder_weight_ref[...],
        (((1,), (1,)), ((), ())),
        preferred_element_type=F32,
    ).reshape(encoder_gradient_ref.shape)


def two_halves(stage, half):
    upper = upper_of(stage)
    own = pl.ds(pl.multiple_of(jnp.where(upper != 0, half, 0), 16), half)
    other = pl.ds(pl.multiple_of(jnp.where(upper != 0, 0, half), 16), half)
    return own, other


def halve_kernel(stages, merge, *refs):
    count, at = len(stages), 0
    for n, stage in enumerate(stages):
        kept_ref, received_ref = refs[2 * n : 2 * n + 2]
        half = kept_ref.shape[0] // 2
        own, other = two_halves(stage, half)
        if merge:
            next_ref, sent_ref = (ref.at[at : at + half, :] for ref in refs[2 * count :])
            at += half
        else:
            next_ref, sent_ref = refs[2 * count + 2 * n : 2 * count + 2 * n + 2]
        sent_ref[...] = (kept_ref[other, :] + received_ref[other, :].astype(F32)).astype(
            sent_ref.dtype
        )
        next_ref[...] = kept_ref[own, :] + received_ref[own, :].astype(F32)


def last_kernel(kept_ref, received_ref, sum_ref):
    sum_ref[...] = (kept_ref[...] + received_ref[...].astype(F32)).astype(BF16)


def join_kernel(stages, merged, *refs):
    count, at = len(stages), 0
    joined_refs = refs[2:] if merged else refs[2 * count :]
    for n, (stage, joined_ref) in enumerate(zip(stages, joined_refs)):
        half = joined_ref.shape[0] // 2
        own, other = two_halves(stage, half)
        if merged:
            own_ref, other_ref = (ref.at[at : at + half, :] for ref in refs[:2])
            at += half
        else:
            own_ref, other_ref = refs[2 * n : 2 * n + 2]
        joined_ref[own, :] = own_ref[...]
        joined_ref[other, :] = other_ref[...]


def put_together(halves, full_refs, sems):
    place = lax.axis_index("tokens") & 1
    copies = []
    for n, (full_ref, start) in enumerate(full_refs):
        own_ref, other_ref = halves[2 * n : 2 * n + 2]
        half = own_ref.shape[0]
        for part, source in ((place, own_ref), (1 - place, other_ref)):
            target = full_ref.at[pl.ds(pl.multiple_of(start + part * half, 16), half), :]
            copies.append(pltpu.make_async_copy(source, target, sems.at[len(copies)]))
    for copy in copies:
        copy.start()
    for copy in copies:
        copy.wait()


def finish_kernel(
    layout,
    *refs,
):
    halves, refs = refs[:4], refs[4:]
    (
        packets_ref,
        predictor_weight_ref,
        output_weight_ref,
        output_bias_ref,
        encoder_weight_ref,
        encoder_bias_ref,
        weight_gradient_ref,
        bias_gradient_ref,
        predictor_gradient_ref,
        losses_ref,
        output_ref,
        full_ref,
        tokens_ref,
        predictor_ref,
        sems,
    ) = refs
    put_together(halves, ((output_ref, 0), (full_ref, 0)), sems)
    width, vocab = output_weight_ref.shape
    for v in range(vocab // 128):
        output_weight_ref[:, v * 128 : (v + 1) * 128] = output_ref[
            v * width : (v + 1) * width, :
        ].astype(F32)
    for v in range(width // 128):
        at = layout["encoder"] + v * width
        encoder_weight_ref[:, v * 128 : (v + 1) * 128] = full_ref[at : at + width, :].astype(F32)
    rest = full_ref[layout["misc"] :, :].astype(F32)

    def row(name, k):
        at = layout[name] - layout["misc"] + k
        return rest[at : at + 1, :]

    output_bias_ref[...] = jnp.concatenate(
        [row("output_bias", v) for v in range(vocab // 128)], axis=1
    )
    encoder_bias_ref[...] = jnp.concatenate(
        [row("encoder_bias", v) for v in range(width // 128)], axis=1
    )
    count = layout["token_rows"]
    tokens = jnp.concatenate(
        [
            full_ref[layout["token"] + v * count : layout["token"] + (v + 1) * count, :]
            for v in range(width // 128)
        ],
        axis=1,
    )
    held_rows = packets_ref.shape[1] - 2
    for d in range(packets_ref.shape[0]):
        predictor_ref[d * held_rows : (d + 1) * held_rows, :] = packets_ref[
            d, :held_rows, :
        ].astype(F32)
    weight_gradient_ref[...] = lax.dot_general(
        predictor_ref[...].astype(BF16),
        tokens,
        (((0,), (0,)), ((), ())),
        preferred_element_type=F32,
    )
    wide = tokens.astype(F32)
    bias_gradient_ref[...] = jnp.sum(wide, axis=0, keepdims=True)
    tokens_ref[...] = wide
    device = lax.axis_index("frames") * lax.axis_size("tokens") + lax.axis_index("tokens")
    mine = jnp.concatenate(
        [tokens_ref[pl.ds(device * held_rows + r, 1), :] for r in range(held_rows)], axis=0
    )
    predictor_gradient_ref[:, 0, :] = lax.dot_general(
        mine.astype(BF16),
        predictor_weight_ref[...],
        (((1,), (1,)), ((), ())),
        preferred_element_type=F32,
    )
    loss = row("loss", 0) + row("loss", 1) + row("loss", 2)
    losses_ref[...] = jnp.sum(
        jnp.where(lane_ids(1) == lax.axis_index("frames"), loss, 0.0), axis=1, keepdims=True
    )


def in_hbm(array):
    return pltpu.with_memory_space_constraint(array, pltpu.HBM)


def in_vmem(array):
    return pltpu.with_memory_space_constraint(array, pltpu.VMEM)


def permuted(array, partner):
    frames, tokens = lax.axis_size("frames"), lax.axis_size("tokens")
    pairs = []
    for f in range(frames):
        for k in range(tokens):
            g, h = partner(f, k)
            pairs.append((f * tokens + k, g * tokens + h))
    return lax.ppermute(array, AXES, pairs)


def doubled(array):
    blocks, bit = [array], 1
    while bit < lax.axis_size("frames"):
        joined = jnp.concatenate(blocks, axis=0) if len(blocks) > 1 else blocks[0]
        blocks.append(permuted(joined, lambda f, k: (f ^ bit, k)))
        bit *= 2
    return blocks


def stages(shift):
    frame_bits = [(1 << i, 0) for i in range(lax.axis_size("frames").bit_length() - 1)]
    token_bits = [(0, 1 << i) for i in range(1, lax.axis_size("tokens").bit_length() - 1)]
    first = frame_bits[:1] + token_bits + frame_bits[1:2]
    return first[shift:] + first[:shift] + frame_bits[2:]


def upper_of(stage):
    return (lax.axis_index("frames") & stage[0]) | (lax.axis_index("tokens") & stage[1])


def across(stage):
    return lambda f, k: (f ^ stage[0], k ^ stage[1])


def neighbour(f, k):
    return f, k ^ 1


def call(body, ins, outs, smem=(), scratch=(), limit=4):
    vmem = pl.BlockSpec(memory_space=pltpu.VMEM)
    return pl.pallas_call(
        body,
        in_specs=[pl.BlockSpec(memory_space=pltpu.SMEM)] * len(smem) + [vmem] * len(ins),
        out_specs=[vmem] * len(outs),
        out_shape=[
            pltpu.VMEM(shape, kind) if inside else jax.ShapeDtypeStruct(shape, kind)
            for shape, kind, inside in outs
        ],
        scratch_shapes=list(scratch),
        compiler_params=pltpu.CompilerParams(vmem_limit_bytes=limit * 2**20),
    )(*smem, *map(in_vmem, ins))


def reduced_and_gathered(pieces):
    plans = list(zip(*(stages(n) for n in range(len(pieces)))))
    flat = [a for kept, sent in pieces for a in (kept, permuted(sent, neighbour))]
    way_back = []
    for number, plan in enumerate(plans):
        plan = plan[: len(flat) // 2]
        merge = len(plan) > 1 and len(set(plan)) == 1
        halves = [kept.shape[0] // 2 for kept in flat[::2]]
        way_back.append((plan, merge, [2 * half for half in halves]))
        if merge:
            halves = [sum(halves)]
        sent_type = BF16 if number < 2 else F32
        flat = call(
            functools.partial(halve_kernel, plan, merge),
            flat,
            [out for half in halves for out in (((half, 128), F32, True), ((half, 128), sent_type, True))],
        )
        flat = [
            permuted(a, across(plan[n // 2])) if n % 2 else a for n, a in enumerate(flat)
        ]
    arrays = [
        call(last_kernel, flat[n : n + 2], [(flat[n].shape, BF16, True)])[0]
        for n in range(0, len(flat), 2)
    ]
    for plan, merged, sizes in reversed(way_back):
        flat = [a for array, stage in zip(arrays, plan) for a in (array, permuted(array, across(stage)))]
        arrays = call(
            functools.partial(join_kernel, plan, merged),
            flat,
            [((size, 128), BF16, True) for size in sizes],
        )
    return [(array, permuted(array, neighbour)) for array in arrays]


def per_device(
    encoder_out,
    encoder_weight,
    encoder_bias,
    predictor_out,
    predictor_weight,
    predictor_bias,
    output_weight,
    output_bias,
    labels,
    frame_lens,
    token_lens,
    loss_scale,
):
    seq_count, frame_count, width = encoder_out.shape
    vocab = output_weight.shape[1]
    all_seqs = labels.shape[0]
    held_seqs, held_units = predictor_out.shape[:2]
    assert held_seqs == 1
    frame_axis, token_axis = lax.axis_size("frames"), lax.axis_size("tokens")
    device_count = frame_axis * token_axis
    units = held_units * token_axis
    calls = seq_count // 2
    steps = frame_count + units - 1
    diagonals = (steps + 1) * units
    smem = pl.BlockSpec(memory_space=pltpu.SMEM)
    vmem = pl.BlockSpec(memory_space=pltpu.VMEM)
    anywhere = pl.BlockSpec(memory_space=pl.ANY)

    weights = (
        encoder_out,
        encoder_weight,
        encoder_bias.reshape(1, width),
        predictor_weight,
        predictor_bias.reshape(1, width),
        output_weight,
        output_bias.reshape(1, vocab),
    )
    packets, *weights = pl.pallas_call(
        packet_kernel,
        in_specs=[anywhere] * (2 + len(weights)),
        out_specs=[vmem] * (1 + len(weights)),
        out_shape=[jax.ShapeDtypeStruct((device_count, held_units + 2, width), BF16)]
        + [pltpu.VMEM(w.shape, w.dtype) for w in weights],
        scratch_shapes=[
            pltpu.VMEM((held_units, width), BF16),
            pltpu.VMEM(labels.shape, jnp.int32),
            pltpu.SemaphoreType.DMA((2 + len(weights),)),
        ],
        compiler_params=pltpu.CompilerParams(vmem_limit_bytes=4 * 2**20),
    )(*map(in_hbm, (predictor_out.reshape(held_units, width), labels, *weights)))
    packets = lax.all_to_all(packets, AXES, 0, 0, tiled=True)

    score_shapes = [
        ((2 * units // SUB_UNITS, SUB_UNITS * frame_count, vocab), F32),
        ((2, frame_count, width), F32),
        ((2 * units, width), F32),
        ((1, 128), jnp.int32),
        ((diagonals, 128), F32),
        ((diagonals, 128), F32),
        ((2 * units // SUB_UNITS, SUB_UNITS * frame_count, width), F32),
        ((2 * units // SUB_UNITS, width + 16, SUB_UNITS * frame_count), BF16),
        ((2 * units // SUB_UNITS, SUB_UNITS * frame_count, 128), F32),
        ((1, 1, units, 128), F32),
    ]

    def scores(given):
        offset, encoder = given
        return pl.pallas_call(
            functools.partial(score_kernel, seq_count),
            in_specs=[smem, vmem] + [anywhere] * 2 + [vmem] * len(weights),
            out_specs=[vmem] * len(score_shapes),
            out_shape=[pltpu.VMEM(s, t) for s, t in score_shapes],
            scratch_shapes=[
                pltpu.VMEM((SUB_UNITS * frame_count, vocab), F32),
                pltpu.VMEM((SUB_UNITS * frame_count, vocab), F32),
                pltpu.SMEM((1, 128), jnp.int32),
                pltpu.VMEM((token_axis, width), F32),
                pltpu.SMEM(frame_lens.shape, jnp.int32),
                pltpu.SMEM(token_lens.shape, jnp.int32),
                pltpu.SemaphoreType.DMA((2,)),
                pltpu.SemaphoreType.DMA,
            ],
            compiler_params=pltpu.CompilerParams(vmem_limit_bytes=8 * 2**20),
        )(
            offset,
            in_vmem(packets),
            in_hbm(frame_lens),
            in_hbm(token_lens),
            *map(in_vmem, (encoder, *weights[1:])),
        )

    offsets = 2 * jnp.arange(calls, dtype=jnp.int32).reshape(calls, 1)
    encoders = weights[0].reshape(calls, 2, frame_count, width)
    if calls == 1:
        scored = scores((offsets[0], weights[0]))
        matrix = scored[-1]
    else:
        scored = lax.map(scores, (offsets, encoders))
        matrix = scored[-1].reshape(1, calls, units, 128)

    matrices = doubled(matrix)
    layout = {"seqs_here": seq_count, "frame_count": frame_count, "units": units}
    layout["encoder"] = 0
    at = width // 128 * width
    layout["token"], layout["token_rows"] = at, all_seqs * units
    at += width // 128 * all_seqs * units
    layout["misc"] = layout["output_bias"] = at
    at += vocab // 128
    layout["encoder_bias"] = at
    at += width // 128
    layout["loss"] = at
    at += 3
    align = 16 * device_count
    output_rows = vocab // 128 * width
    output_rows += -output_rows % align
    rest_rows = at + (-at % align)

    blocks = 2 * units // SUB_UNITS
    block_rows = SUB_UNITS * frame_count

    def tangents(offset, scored, matrices):
        softmax, _, _, table, blank, label, _, turned, inverse = scored
        given = (softmax, table, blank, label, turned, inverse, *matrices)
        return pl.pallas_call(
            functools.partial(tangent_kernel, dict(layout, hops=len(matrices) - 1)),
            in_specs=[smem] * 4 + [vmem] * len(given),
            out_specs=[vmem] * 5,
            out_shape=[
                pltpu.VMEM((blocks, block_rows, vocab), BF16),
                pltpu.VMEM((1, vocab), F32),
                pltpu.VMEM((1, 128), F32),
            ]
            + [pltpu.VMEM((output_rows // 2, 128), F32)] * 2,
            scratch_shapes=[
                pltpu.VMEM((output_rows, 128), F32),
                pltpu.VMEM((frame_axis, units, 128), F32),
                pltpu.VMEM((diagonals, 128), F32),
                pltpu.VMEM((diagonals, 128), F32),
                pltpu.VMEM((diagonals, 128), F32),
                pltpu.VMEM((diagonals, 128), F32),
                pltpu.VMEM((block_rows, vocab), BF16),
                pltpu.VMEM((block_rows, vocab), BF16),
                pltpu.SMEM((1, 128), jnp.int32),
                pltpu.SemaphoreType.DMA,
                pltpu.SemaphoreType.DMA((4,)),
            ],
            compiler_params=pltpu.CompilerParams(vmem_limit_bytes=12 * 2**20),
        )(frame_lens, token_lens, offset, loss_scale, *map(in_vmem, given))

    def inners(offset, encoder, scored, tangent, output_bias_sum, loss):
        given = (tangent, scored[6], weights[5], encoder, output_bias_sum, loss)
        return call(
            functools.partial(inner_kernel, layout),
            given,
            [
                ((2 * frame_count, width), BF16, True),
                ((rest_rows // 2, 128), F32, True),
                ((rest_rows // 2, 128), F32, True),
            ],
            smem=(frame_lens, token_lens, offset),
            scratch=[
                pltpu.VMEM((rest_rows, 128), F32),
                pltpu.VMEM((2, frame_count, width), F32),
                pltpu.VMEM((2 * units, width), F32),
                pltpu.VMEM((block_rows, width), F32),
                pltpu.VMEM((block_rows, width), F32),
                pltpu.SemaphoreType.DMA((2,)),
            ],
            limit=10,
        )

    def encoder_gradient_of(frame_tangent):
        return call(
            encoder_kernel,
            (frame_tangent, weights[1]),
            [((2, frame_count, width), F32, False)],
        )[0]

    if calls == 1:
        scored = scored[:-1]
        tangent, output_bias_sum, loss, *output_sums = tangents(offsets[0], scored, matrices)

        frame_tangent, *rest = inners(
            offsets[0], weights[0], scored, tangent, output_bias_sum, loss
        )
        sums = [*output_sums, *rest]
        encoder_gradient = encoder_gradient_of(frame_tangent)
    else:

        def add_call(sums, given):
            offset, encoder, scored, call = given
            own = [lax.dynamic_slice_in_dim(m, call, 1, 1) for m in matrices]
            tangent, output_bias_sum, loss, *more = tangents(offset, scored, own)
            frame_tangent, *rest = inners(
                offset, encoder, scored, tangent, output_bias_sum, loss
            )
            return [a + b for a, b in zip(sums, more + rest)], encoder_gradient_of(frame_tangent)

        nothing = [jnp.zeros((r, 128), F32) for r in (output_rows // 2, rest_rows // 2)]
        sums, encoder_gradient = lax.scan(
            add_call,
            [nothing[0]] * 2 + [nothing[1]] * 2,
            (offsets, encoders, scored[:-1], jnp.arange(calls)),
        )
        encoder_gradient = encoder_gradient.reshape(encoder_out.shape)

    halves = reduced_and_gathered(list(zip(sums[::2], sums[1::2])))
    finished = call(
        functools.partial(finish_kernel, layout),
        [*(a for pair in halves for a in pair), packets, weights[3]],
        [
            ((width, vocab), F32, False),
            ((1, vocab), F32, False),
            ((width, width), F32, False),
            ((1, width), F32, False),
            ((width, width), F32, False),
            ((1, width), F32, False),
            ((held_units, 1, width), F32, False),
            ((1, 1), F32, False),
        ],
        scratch=[
            pltpu.VMEM((output_rows, 128), BF16),
            pltpu.VMEM((rest_rows, 128), BF16),
            pltpu.VMEM((all_seqs * units, width), F32),
            pltpu.VMEM((all_seqs * units, width), F32),
            pltpu.SemaphoreType.DMA((6,)),
        ],
        limit=20,
    )
    return (
        finished[7].reshape(1),
        encoder_gradient,
        finished[6].transpose(1, 0, 2),
        finished[2],
        finished[3].reshape(width),
        finished[4],
        finished[5].reshape(width),
        finished[0],
        finished[1].reshape(vocab),
    )


def solution(mesh):
    placed = (
        P("tokens", "frames", None),
        P(),
        P(),
        P("frames", "tokens", None),
        P(),
        P(),
        P(),
        P(),
        P(None, "tokens"),
        P(),
        P(),
        P(),
    )
    return jax.shard_map(
        per_device,
        mesh=mesh,
        in_specs=placed,
        out_specs=(
            P("frames"),
            P("tokens", "frames", None),
            P("frames", "tokens", None),
            P(),
            P(),
            P(),
            P(),
            P(),
            P(),
        ),
        check_vma=False,
    )
```

```python
import functools

import jax
import jax.numpy as jnp
from jax import lax
from jax.experimental import pallas as pl
from jax.experimental.pallas import tpu as pltpu
from jax.sharding import PartitionSpec as P

NEG = -1e30
LOG2E = 1.4426950408889634
LN2 = 0.6931471805599453
BF16 = jnp.bfloat16
F32 = jnp.float32
GROUP = 32
SUB_UNITS = 4
ORDERS = ((0, 1), (2, 1))
AXES = ("frames", "tokens")


def lane_ids(rows):
    return lax.broadcasted_iota(jnp.int32, (rows, 128), 1)


def log2_add(a, b):
    return jnp.maximum(a, b) + jnp.log2(1.0 + jnp.exp2(-jnp.abs(a - b)))


def both_ways(blank_ref, label_ref, units, steps, ahead, behind, keep=None):
    def one_step(i, state):
        ahead, behind = state
        back = steps - 1 - i
        here = pl.ds(pl.multiple_of(i * units, 8), units)
        there = pl.ds(pl.multiple_of(back * units, 8), units)
        if keep is not None:
            keep[0][here, :] = ahead
            keep[1][there, :] = behind
        from_left = pltpu.roll(ahead + label_ref[here, :], 1, 0)
        to_right = pltpu.roll(behind, units - 1, 0) + label_ref[there, :]
        ahead = log2_add(ahead + blank_ref[here, :], from_left)
        behind = log2_add(behind + blank_ref[there, :], to_right)
        return ahead, behind

    return lax.fori_loop(0, steps, one_step, (ahead, behind))


def in_two_stages(count, first, second, even, odd, between=None):
    def two_blocks(n, _):
        first(2 * n + 1, odd)
        second(2 * n, even)
        first(jnp.minimum(2 * n + 2, count - 1), even)
        second(2 * n + 1, odd)
        return 0

    @pl.when(count > 0)
    def _():
        first(0, even)

    if between is not None:
        between()

    @pl.when(count > 0)
    def _():
        lax.fori_loop(0, count // 2, two_blocks, 0)

        @pl.when(count % 2 == 1)
        def _():
            second(count - 1, even)


def packet_kernel(predictor_hbm, labels_hbm, *refs):
    *refs, predictor_ref, labels_ref, sems = refs
    count = len(refs) // 2
    packets_ref = refs[count]
    targets = (predictor_ref, labels_ref, *refs[count + 1 :])
    loads = [
        pltpu.make_async_copy(source, target, sems.at[n])
        for n, (source, target) in enumerate(
            zip((predictor_hbm, labels_hbm, *refs[:count]), targets)
        )
    ]
    for load in loads:
        load.start()
    loads[0].wait()
    loads[1].wait()
    seqs, units = labels_ref.shape
    width = packets_ref.shape[2]
    flat = jnp.zeros((1, width), F32)
    for s in range(seqs):
        row = labels_ref[s : s + 1, :].astype(F32)
        row = jnp.concatenate([row, jnp.zeros((1, width - units), F32)], axis=1)
        flat = flat + (pltpu.roll(row, s * units, 1) if s else row)
    high = jnp.floor(flat * (1.0 / 32.0))
    packet = jnp.concatenate(
        [predictor_ref[...].astype(F32), high, flat - high * 32.0], axis=0
    ).astype(BF16)
    for d in range(packets_ref.shape[0]):
        packets_ref[d] = packet
    for load in loads[2:]:
        load.wait()


def entry(row_ref, place):
    row = row_ref[...].astype(F32)
    ids = lax.broadcasted_iota(jnp.int32, row.shape, 1)
    return jnp.sum(jnp.where(ids == place, row, 0.0), axis=1, keepdims=True)


def whole_number(row_ref, place):
    return entry(row_ref, place).astype(jnp.int32)[0, 0]


def first_of(seqs_here, offset_ref):
    first_seq = lax.axis_index("tokens") * seqs_here
    return first_seq if offset_ref is None else first_seq + whole_number(offset_ref, 0)


def block_counts(lens_ref, tokens_ref, first_seq, first_frame):
    counts = []
    for s in range(2):
        inside = first_frame < whole_number(lens_ref, first_seq + s)
        units = whole_number(tokens_ref, first_seq + s)
        counts.append(jnp.where(inside, units // SUB_UNITS + 1, 0))
    return counts


def score_kernel(
    seqs_here,
    offset_ref,
    packets_ref,
    lens_ref,
    tokens_ref,
    encoder_ref,
    encoder_weight_ref,
    encoder_bias_ref,
    predictor_weight_ref,
    predictor_bias_ref,
    weight_ref,
    bias_ref,
    softmax_ref,
    frame_ref,
    token_ref,
    label_table_ref,
    blank_ref,
    label_ref,
    hidden_ref,
    inverse_ref,
    parts_ref,
    matrix_ref,
    even_ref,
    odd_ref,
    labels_smem,
    label_rows_ref,
    label_sem,
):
    seqs, frame_count, width = encoder_ref.shape
    units = token_ref.shape[0] // seqs
    shards = label_rows_ref.shape[0]
    shard_units = units // shards
    part = frame_count // 2
    steps = part + units - 1
    first_frame = lax.axis_index("frames") * frame_count
    first_seq = first_of(seqs_here, offset_ref)
    vocab = weight_ref.shape[1]
    blank_ref[...] = jnp.zeros_like(blank_ref)
    label_ref[...] = jnp.full(label_ref.shape, NEG, F32)
    for s in range(seqs):
        for k in range(shards):
            rows = packets_ref[(first_seq + s) * shards + k]
            at = s * units + k * shard_units
            token_ref[at : at + shard_units, :] = rows[:shard_units].astype(F32)
    for k in range(shards):
        halves = packets_ref[k, shard_units:, :].astype(F32)
        label_rows_ref[k : k + 1, :] = halves[:1] * 32.0 + halves[1:2]
    wide = lane_ids(1)
    table = jnp.zeros((1, 128), F32)
    for s in range(seqs):
        for k in range(shards):
            target = s * units + k * shard_units
            shift = (target - (first_seq + s) * shard_units) % width
            row = pltpu.roll(label_rows_ref[k : k + 1, :], shift, 1)[:, :128]
            table = jnp.where((wide >= target) & (wide < target + shard_units), row, table)
    label_table_ref[...] = table.astype(jnp.int32)
    label_copy = pltpu.make_async_copy(label_table_ref, labels_smem, label_sem)
    label_copy.start()
    token_ref[...] = (
        jnp.dot(token_ref[...].astype(BF16), predictor_weight_ref[...], preferred_element_type=F32)
        + predictor_bias_ref[...]
    ).astype(BF16).astype(F32)
    frame_ref[...] = (
        (
            jnp.dot(
                encoder_ref[...].reshape(seqs * frame_count, width),
                encoder_weight_ref[...],
                preferred_element_type=F32,
            )
            + encoder_bias_ref[...]
        )
        .astype(BF16)
        .astype(F32)
        .reshape(frame_ref.shape)
    )

    counts = block_counts(lens_ref, tokens_ref, first_seq, first_frame)
    blocks = counts[0] + counts[1]
    lens = [whole_number(lens_ref, first_seq + s) for s in range(2)]
    last_units = [whole_number(tokens_ref, first_seq + s) for s in range(2)]
    lanes = lane_ids(frame_count)
    part_lanes = lane_ids(part)
    times = first_frame + lax.broadcasted_iota(jnp.int32, (frame_count, 1), 0)

    def place_of(i):
        seq = jnp.where(i >= counts[0], 1, 0)
        sub = i - seq * counts[0]
        return seq, sub, seq * (units // SUB_UNITS) + sub

    def multiply(i, logits_ref):
        seq, sub, block = place_of(i)
        frames = frame_ref[seq]
        hidden = jnp.concatenate(
            [
                jnp.tanh(frames + token_ref[pl.ds(seq * units + sub * SUB_UNITS + j, 1), :])
                for j in range(SUB_UNITS)
            ],
            axis=0,
        )
        hidden_ref[block] = hidden
        low = hidden.astype(BF16)
        logits_ref[...] = (
            jnp.dot(low, weight_ref[...], preferred_element_type=F32) + bias_ref[...]
        )

    def score(i, logits_ref):
        seq, sub, block = place_of(i)
        first_unit = sub * SUB_UNITS
        seq_len = jnp.where(seq == 0, lens[0], lens[1])
        last_unit = jnp.where(seq == 0, last_units[0], last_units[1])
        own_lanes = (part_lanes // GROUP) % 2 == seq
        logits = logits_ref[...]
        top = jnp.max(logits, axis=1, keepdims=True)
        weights = jnp.exp(logits - top)
        total = jnp.sum(weights, axis=1, keepdims=True)
        softmax_ref[block] = weights
        inverse_ref[block] = jnp.broadcast_to(1.0 / total, (weights.shape[0], 128))
        log_total = top + jnp.log(total)
        blanks = (logits[:, :1] - log_total) * LOG2E
        for j in range(SUB_UNITS):
            unit = first_unit + j
            rows = slice(j * frame_count, (j + 1) * frame_count)
            label = labels_smem[0, seq * units + unit]
            tile = logits_ref[rows, pl.ds(pl.multiple_of(label // 128 * 128, 128), 128)]
            picked = jnp.sum(
                jnp.where(lanes == label % 128, tile, 0.0), axis=1, keepdims=True
            )
            blank = blanks[rows]
            blank = jnp.where((times == seq_len - 1) & (unit < last_unit), NEG, blank)
            blank = jnp.where((times >= seq_len) | (unit > last_unit), 0.0, blank)
            step = jnp.where(
                (times >= seq_len) | (unit >= last_unit),
                NEG,
                (picked - log_total[rows]) * LOG2E,
            )
            at = (pl.ds(unit * (units + 1), part, stride=units), slice(None))
            blank = jnp.where(part_lanes < 64, blank[:part], blank[part:])
            step = jnp.where(part_lanes < 64, step[:part], step[part:])
            blank_ref[at] = jnp.where(own_lanes, blank, blank_ref[at])
            label_ref[at] = jnp.where(own_lanes, step, label_ref[at])

    in_two_stages(blocks, multiply, score, even_ref, odd_ref, label_copy.wait)
    eye = jnp.where(
        lane_ids(units) % GROUP == lax.broadcasted_iota(jnp.int32, (units, 128), 0), 0.0, NEG
    ).astype(F32)
    ahead, behind = both_ways(blank_ref, label_ref, units, steps, eye, eye)
    lanes = lane_ids(units)
    early = lanes < 64
    columns = jnp.where(early, behind, ahead)
    parts_ref[...] = columns
    others = pltpu.roll(jnp.where(early, ahead, behind), 64, 1)
    ways = [
        jnp.take_along_axis(
            columns, lanes // GROUP * GROUP + k, axis=1, mode="promise_in_bounds"
        )
        + others[k : k + 1, :]
        for k in range(units)
    ]
    top = functools.reduce(jnp.maximum, ways)
    total = functools.reduce(jnp.add, [jnp.exp2(way - top) for way in ways])
    matrix_ref[0, 0] = top + jnp.log2(total)


def turn_kernel(layout, offset_ref, lens_ref, tokens_ref, hidden_ref, turned_ref):
    width = hidden_ref.shape[2]
    first_frame = lax.axis_index("frames") * layout["frame_count"]
    first_seq = first_of(layout["seqs_here"], offset_ref)
    counts = block_counts(lens_ref, tokens_ref, first_seq, first_frame)

    def one_block(i, _):
        seq = jnp.where(i >= counts[0], 1, 0)
        block = i + seq * (layout["units"] // SUB_UNITS - counts[0])
        turned_ref[block, :width, :] = hidden_ref[block].astype(BF16).T
        turned_ref[block, width:, :] = jnp.ones((16, turned_ref.shape[2]), BF16)
        return 0

    lax.fori_loop(0, counts[0] + counts[1], one_block, 0)


def tangent_kernel(
    layout,
    offset_ref,
    lens_ref,
    tokens_ref,
    scale_ref,
    softmax_ref,
    label_table_ref,
    blank_ref,
    label_ref,
    turned_ref,
    inverse_ref,
    parts_ref,
    *refs,
):
    hops = layout["hops"]
    matrix_refs, refs = refs[: hops + 1], refs[hops + 1 :]
    (
        tangents_ref,
        output_bias_ref,
        loss_ref,
        *kept_refs,
        sums_ref,
        matrices_ref,
        ahead_ref,
        behind_ref,
        blank_part_ref,
        label_part_ref,
        even_ref,
        odd_ref,
        labels_smem,
        label_sem,
        sems,
    ) = refs
    label_copy = pltpu.make_async_copy(label_table_ref, labels_smem, label_sem)
    label_copy.start()
    frame_count = layout["frame_count"]
    width = turned_ref.shape[1] - 16
    units = layout["units"]
    part = frame_count // 2
    steps = part + units - 1
    here = lax.axis_index("frames")
    first_frame = here * frame_count
    first_seq = first_of(layout["seqs_here"], offset_ref)
    chunks = matrices_ref.shape[0]
    vocab = softmax_ref.shape[2]
    at = 0
    for matrix_ref in matrix_refs:
        matrices_ref[at : at + matrix_ref.shape[0]] = matrix_ref[:, 0]
        at += matrix_ref.shape[0]
    starts = lax.broadcasted_iota(jnp.int32, (units, 128), 0)
    lanes = lane_ids(units)
    early = lanes < 64
    gather_ids = lanes // GROUP * GROUP + starts
    own_first = (lane_ids(1) // GROUP) % 2 == 0

    def through(column, matrix):
        ways = column + matrix
        top = jnp.max(ways, axis=0, keepdims=True)
        row = top + jnp.log2(jnp.sum(jnp.exp2(ways - top), axis=0, keepdims=True))
        row = jnp.broadcast_to(row, (units, 128))
        return jnp.take_along_axis(row, gather_ids, axis=1, mode="promise_in_bounds")

    def one_chunk(i, carry):
        column, kept = carry
        other = chunks - 1 - i
        kept = jnp.where(jnp.where(early, i, other) == here, column, kept)
        matrix = jnp.where(early, matrices_ref[here ^ i], matrices_ref[here ^ other])
        return through(column, matrix), kept

    start = jnp.where(early & (starts > 0), NEG, 0.0).astype(F32)
    last, kept = lax.fori_loop(0, chunks, one_chunk, (start, start))
    middle = pltpu.roll(through(kept, parts_ref[...]), 64, 1)
    both_ways(
        blank_ref,
        label_ref,
        units,
        steps,
        jnp.where(early, kept, middle),
        jnp.where(early, middle, kept),
        (ahead_ref, behind_ref),
    )
    log_norm = jnp.max(jnp.where(early, last, pltpu.roll(last, 64, 1)), axis=0, keepdims=True)
    scale, length, bound = (
        jnp.where(own_first, entry(ref, first_seq), entry(ref, first_seq + 1))
        for ref in (scale_ref, lens_ref, tokens_ref)
    )
    length, bound = length.astype(jnp.int32), bound.astype(jnp.int32)
    part_start = first_frame + jnp.where(lane_ids(1) < 64, 0, part)
    last_diagonal = starts + jnp.minimum(length - part_start, part)
    first_blank = jnp.where(starts <= bound, starts, steps)
    first_label = jnp.where(starts < bound, starts, steps)
    norm = log_norm - jnp.log2(scale)

    def one_diagonal(e, _):
        rows = pl.ds(pl.multiple_of(e * units, 8), units)
        behind = behind_ref[rows, :]
        base = ahead_ref[rows, :] - norm
        before_end = last_diagonal > e
        blank_part_ref[rows, :] = jnp.where(
            before_end & (first_blank <= e), jnp.exp2(base + blank_ref[rows, :] + behind), 0.0
        )
        label_part_ref[rows, :] = jnp.where(
            before_end & (first_label <= e),
            jnp.exp2(base + label_ref[rows, :] + pltpu.roll(behind, units - 1, 0)),
            0.0,
        )
        return 0

    lax.fori_loop(0, steps, one_diagonal, 0, unroll=5)

    counts = block_counts(lens_ref, tokens_ref, first_seq, first_frame)
    block_lanes = lane_ids(frame_count)
    part_lanes = lane_ids(part)

    def place_of(i):
        seq = jnp.where(i >= counts[0], 1, 0)
        sub = i - seq * counts[0]
        return seq, sub, seq * (units // SUB_UNITS) + sub

    wide = lane_ids(1)
    loss = jnp.where(here == 0, -log_norm * LN2, 0.0)
    spread = jnp.where(wide == first_seq, loss[:, :1], 0.0)
    loss_ref[...] = spread + jnp.where(wide == first_seq + 1, loss[:, GROUP : GROUP + 1], 0.0)
    label_copy.wait()

    counts_all = counts[0] + counts[1]
    sums_ref[...] = jnp.zeros_like(sums_ref)
    output_bias_ref[...] = jnp.zeros_like(output_bias_ref)

    def prepare(i, tangent_ref):
        seq, sub, block = place_of(i)
        own_lanes = [part_lanes % GROUP + GROUP * (seq + 2 * half) for half in (0, 1)]
        for j in range(SUB_UNITS):
            unit = sub * SUB_UNITS + j
            rows = slice(j * frame_count, (j + 1) * frame_count)
            at = (pl.ds(unit * (units + 1), part, stride=units), slice(None))
            blank, step = (
                jnp.concatenate(
                    [
                        jnp.take_along_axis(ref[at], ids, axis=1, mode="promise_in_bounds")
                        for ids in own_lanes
                    ],
                    axis=0,
                )
                for ref in (blank_part_ref, label_part_ref)
            )
            both = (blank + step) * inverse_ref[block, rows, :]
            for v in range(vocab // 128):
                cut = slice(v * 128, (v + 1) * 128)
                piece = softmax_ref[block, rows, cut] * both
                if v == 0:
                    piece = piece - jnp.where(block_lanes == 0, blank, 0.0)
                piece = piece.astype(BF16)
                tangent_ref[rows, cut] = piece
                tangents_ref[block, rows, cut] = piece
            label = labels_smem[0, seq * units + unit]
            cut = pl.ds(pl.multiple_of(label // 128 * 128, 128), 128)
            piece = softmax_ref[block, rows, cut] * both
            piece = piece - jnp.where((block_lanes == 0) & (label < 128), blank, 0.0)
            piece = (piece - jnp.where(block_lanes == label % 128, step, 0.0)).astype(BF16)
            tangent_ref[rows, cut] = piece
            tangents_ref[block, rows, cut] = piece

    def multiply(i, tangent_ref):
        _, _, block = place_of(i)
        product = jnp.dot(turned_ref[block], tangent_ref[...], preferred_element_type=F32)
        for v in range(vocab // 128):
            sums_ref[v * width : (v + 1) * width, :] += product[:width, v * 128 : (v + 1) * 128]
        output_bias_ref[...] += product[width : width + 1, :]

    in_two_stages(counts_all, prepare, multiply, even_ref, odd_ref)
    part_halves(sums_ref, kept_refs, sems)


def part_halves(sums_ref, piece_refs, sems):
    place = lax.axis_index("tokens") & 1
    copies, start = [], 0
    for kept_ref, sent_ref in zip(piece_refs[::2], piece_refs[1::2]):
        half = kept_ref.shape[0]
        for part, target in ((1 - place, sent_ref), (place, kept_ref)):
            source = sums_ref.at[pl.ds(pl.multiple_of(start + part * half, 8), half), :]
            copies.append(pltpu.make_async_copy(source, target, sems.at[len(copies)]))
        start += 2 * half
    for copy in copies:
        copy.start()
    for copy in copies:
        copy.wait()


def inner_kernel(
    layout,
    offset_ref,
    lens_ref,
    tokens_ref,
    tangents_ref,
    hidden_ref,
    weight_ref,
    encoder_ref,
    output_bias_ref,
    loss_ref,
    frame_tangent_ref,
    kept_ref,
    sent_ref,
    sums_ref,
    frame_sum_ref,
    token_sum_ref,
    even_ref,
    odd_ref,
    sems,
):
    seqs, frame_count, width = encoder_ref.shape
    units = token_sum_ref.shape[0] // seqs
    vocab = weight_ref.shape[1]
    first_frame = lax.axis_index("frames") * frame_count
    first_seq = first_of(layout["seqs_here"], offset_ref)
    frame_sum_ref[...] = jnp.zeros_like(frame_sum_ref)
    token_sum_ref[...] = jnp.zeros_like(token_sum_ref)
    unset = slice(layout["token"], sums_ref.shape[0])
    sums_ref[unset, :] = jnp.zeros_like(sums_ref[unset, :])
    counts = block_counts(lens_ref, tokens_ref, first_seq, first_frame)

    def place_of(i):
        seq = jnp.where(i >= counts[0], 1, 0)
        sub = i - seq * counts[0]
        return seq, sub, seq * (units // SUB_UNITS) + sub

    def product_of(tangents):
        return lax.dot_general(
            tangents, weight_ref[...], (((1,), (1,)), ((), ())), preferred_element_type=F32
        )

    def add_up(i, product):
        seq, sub, block = place_of(i)
        hidden = hidden_ref[block]
        inner = product * (1.0 - hidden * hidden)
        total = frame_sum_ref[seq]
        for j in range(SUB_UNITS):
            rows = slice(j * frame_count, (j + 1) * frame_count)
            total = total + inner[rows]
            token_sum_ref[pl.ds(seq * units + sub * SUB_UNITS + j, 1), :] = jnp.sum(
                inner[rows], axis=0, keepdims=True
            )
        frame_sum_ref[seq] = total

    def multiply_two(n, product_ref):
        both = [tangents_ref[place_of(2 * n + m)[2]] for m in (0, 1)]
        product_ref[...] = product_of(jnp.concatenate(both, axis=0))

    def add_up_two(n, product_ref):
        half = product_ref.shape[0] // 2
        add_up(2 * n, product_ref[:half])
        add_up(2 * n + 1, product_ref[half:])

    blocks = counts[0] + counts[1]
    in_two_stages(blocks // 2, multiply_two, add_up_two, even_ref, odd_ref)

    @pl.when(blocks % 2 == 1)
    def _():
        add_up(blocks - 1, product_of(tangents_ref[place_of(blocks - 1)[2]]))

    low = frame_sum_ref[...].reshape(seqs * frame_count, width).astype(BF16)
    frame_tangent_ref[...] = low
    product = lax.dot_general(
        encoder_ref[...].reshape(seqs * frame_count, width),
        low,
        (((0,), (0,)), ((), ())),
        preferred_element_type=F32,
    )
    encoder_bias = jnp.sum(low.astype(F32), axis=0, keepdims=True)
    for v in range(width // 128):
        cut = slice(v * 128, (v + 1) * 128)
        at = layout["encoder"] + v * width
        sums_ref[at : at + width, :] = product[:, cut]
        at = layout["token"] + v * layout["token_rows"] + first_seq * units
        sums_ref[pl.ds(pl.multiple_of(at, 8), seqs * units), :] = token_sum_ref[:, cut]
        at = layout["encoder_bias"] + v
        sums_ref[at : at + 1, :] = encoder_bias[:, cut]
    for v in range(vocab // 128):
        at = layout["output_bias"] + v
        sums_ref[at : at + 1, :] = output_bias_ref[:, v * 128 : (v + 1) * 128]
    spread = loss_ref[...]
    for k in range(3):
        part = spread.astype(BF16).astype(F32)
        sums_ref[layout["loss"] + k : layout["loss"] + k + 1, :] = part
        spread = spread - part
    part_halves(sums_ref, (kept_ref, sent_ref), sems)


def encoder_kernel(frame_tangent_ref, encoder_weight_ref, encoder_gradient_ref):
    encoder_gradient_ref[...] = lax.dot_general(
        frame_tangent_ref[...],
        encoder_weight_ref[...],
        (((1,), (1,)), ((), ())),
        preferred_element_type=F32,
    ).reshape(encoder_gradient_ref.shape)


def two_halves(stage, half):
    upper = upper_of(stage)
    own = pl.ds(pl.multiple_of(jnp.where(upper != 0, half, 0), 16), half)
    other = pl.ds(pl.multiple_of(jnp.where(upper != 0, 0, half), 16), half)
    return own, other


def halve_kernel(stages, merge, *refs):
    count, at = len(stages), 0
    for n, stage in enumerate(stages):
        kept_ref, received_ref = refs[2 * n : 2 * n + 2]
        half = kept_ref.shape[0] // 2
        own, other = two_halves(stage, half)
        if merge:
            next_ref, sent_ref = (ref.at[at : at + half, :] for ref in refs[2 * count :])
            at += half
        else:
            next_ref, sent_ref = refs[2 * count + 2 * n : 2 * count + 2 * n + 2]
        sent_ref[...] = (kept_ref[other, :] + received_ref[other, :].astype(F32)).astype(
            sent_ref.dtype
        )
        next_ref[...] = kept_ref[own, :] + received_ref[own, :].astype(F32)


def last_kernel(kept_ref, received_ref, sum_ref):
    sum_ref[...] = (kept_ref[...] + received_ref[...].astype(F32)).astype(BF16)


def join_kernel(stages, merged, *refs):
    count, at = len(stages), 0
    joined_refs = refs[2:] if merged else refs[2 * count :]
    for n, (stage, joined_ref) in enumerate(zip(stages, joined_refs)):
        half = joined_ref.shape[0] // 2
        own, other = two_halves(stage, half)
        if merged:
            own_ref, other_ref = (ref.at[at : at + half, :] for ref in refs[:2])
            at += half
        else:
            own_ref, other_ref = refs[2 * n : 2 * n + 2]
        joined_ref[own, :] = own_ref[...]
        joined_ref[other, :] = other_ref[...]


def finish_kernel(
    layout,
    output_own_ref,
    output_other_ref,
    rest_own_ref,
    rest_other_ref,
    packets_ref,
    predictor_weight_ref,
    output_weight_hbm,
    encoder_weight_hbm,
    weight_gradient_hbm,
    output_bias_ref,
    encoder_bias_ref,
    bias_gradient_ref,
    predictor_gradient_ref,
    losses_ref,
    output_weight_ref,
    encoder_weight_ref,
    weight_gradient_ref,
    tail_ref,
    tokens_ref,
    predictor_ref,
    sems,
):
    width, vocab = output_weight_ref.shape
    place = lax.axis_index("tokens") & 1
    copies = []

    def send(source, target):
        copies.append(pltpu.make_async_copy(source, target, sems.at[len(copies)]))
        copies[-1].start()

    def in_order(own_ref, other_ref, body):
        def reader(low_ref, high_ref):
            def rows(start, stop):
                half = low_ref.shape[0]
                if stop <= half:
                    return low_ref[start:stop, :]
                if start >= half:
                    return high_ref[start - half : stop - half, :]
                return jnp.concatenate([low_ref[start:, :], high_ref[: stop - half, :]], axis=0)

            return rows

        @pl.when(place == 0)
        def _():
            body(reader(own_ref, other_ref))

        @pl.when(place == 1)
        def _():
            body(reader(other_ref, own_ref))

    chunk = width // 4

    def unpack(target, start):
        def body(rows):
            for v in range(target.shape[1] // 128):
                at = start + v * width
                for r in range(0, width, chunk):
                    target[r : r + chunk, v * 128 : (v + 1) * 128] = rows(
                        at + r, at + r + chunk
                    ).astype(F32)

        return body

    half = vocab // 2
    for n in (0, 1):
        columns = slice(n * half, (n + 1) * half)
        in_order(
            output_own_ref,
            output_other_ref,
            unpack(output_weight_ref.at[:, columns], n * half // 128 * width),
        )
        send(output_weight_ref.at[:, columns], output_weight_hbm.at[:, columns])
    in_order(rest_own_ref, rest_other_ref, unpack(encoder_weight_ref, layout["encoder"]))
    send(encoder_weight_ref, encoder_weight_hbm)
    tail_start = layout["token"]

    def keep_tail(rows):
        tail_ref[...] = rows(tail_start, tail_start + tail_ref.shape[0]).astype(F32)

    in_order(rest_own_ref, rest_other_ref, keep_tail)
    count = layout["token_rows"]
    for v in range(width // 128):
        tokens_ref[:, v * 128 : (v + 1) * 128] = tail_ref[v * count : (v + 1) * count, :]
    tokens = tokens_ref[...]
    held_rows = packets_ref.shape[1] - 2
    for d in range(packets_ref.shape[0]):
        predictor_ref[d * held_rows : (d + 1) * held_rows, :] = packets_ref[
            d, :held_rows, :
        ].astype(F32)
    weight_gradient_ref[...] = lax.dot_general(
        predictor_ref[...].astype(BF16),
        tokens.astype(BF16),
        (((0,), (0,)), ((), ())),
        preferred_element_type=F32,
    )
    send(weight_gradient_ref, weight_gradient_hbm)

    def row(name, k):
        at = layout[name] - tail_start + k
        return tail_ref[at : at + 1, :]

    output_bias_ref[...] = jnp.concatenate(
        [row("output_bias", v) for v in range(vocab // 128)], axis=1
    )
    encoder_bias_ref[...] = jnp.concatenate(
        [row("encoder_bias", v) for v in range(width // 128)], axis=1
    )
    bias_gradient_ref[...] = jnp.sum(tokens, axis=0, keepdims=True)
    device = lax.axis_index("frames") * lax.axis_size("tokens") + lax.axis_index("tokens")
    mine = jnp.concatenate(
        [tokens_ref[pl.ds(device * held_rows + r, 1), :] for r in range(held_rows)], axis=0
    )
    predictor_gradient_ref[:, 0, :] = lax.dot_general(
        mine.astype(BF16),
        predictor_weight_ref[...],
        (((1,), (1,)), ((), ())),
        preferred_element_type=F32,
    )
    loss = row("loss", 0) + row("loss", 1) + row("loss", 2)
    losses_ref[...] = jnp.sum(
        jnp.where(lane_ids(1) == lax.axis_index("frames"), loss, 0.0), axis=1, keepdims=True
    )
    for copy in copies:
        copy.wait()


def in_hbm(array):
    return pltpu.with_memory_space_constraint(array, pltpu.HBM)


def in_vmem(array):
    return pltpu.with_memory_space_constraint(array, pltpu.VMEM)


def permuted(array, partner):
    frames, tokens = lax.axis_size("frames"), lax.axis_size("tokens")
    pairs = []
    for f in range(frames):
        for k in range(tokens):
            g, h = partner(f, k)
            pairs.append((f * tokens + k, g * tokens + h))
    return lax.ppermute(array, AXES, pairs)


def doubled(array):
    blocks, bit = [array], 1
    while bit < lax.axis_size("frames"):
        joined = jnp.concatenate(blocks, axis=0) if len(blocks) > 1 else blocks[0]
        blocks.append(permuted(joined, lambda f, k: (f ^ bit, k)))
        bit *= 2
    return blocks


def stages(even, odd):
    frame_bits = [(1 << i, 0) for i in range(lax.axis_size("frames").bit_length() - 1)]
    token_bits = [(0, 1 << i) for i in range(1, lax.axis_size("tokens").bit_length() - 1)]
    first = frame_bits[:1] + token_bits + frame_bits[1:2]
    orders = [first[shift:] + first[:shift] + frame_bits[2:] for shift in (even, odd)]
    return list(zip(*orders))


def upper_of(stage):
    f, k = lax.axis_index("frames"), lax.axis_index("tokens")
    even, odd = ((f & frame_bit) | (k & token_bit) for frame_bit, token_bit in stage)
    return jnp.where((k & 1) == 0, even, odd)


def across(stage):
    return lambda f, k: (f ^ stage[k & 1][0], k ^ stage[k & 1][1])


def neighbour(f, k):
    return f, k ^ 1


def call(body, ins, outs, scratch=(), limit=4):
    vmem = pl.BlockSpec(memory_space=pltpu.VMEM)
    there = [array is not None for array in ins]

    def kernel(*refs):
        given = iter(refs)
        body(*(next(given) if here else None for here in there), *given)

    return pl.pallas_call(
        kernel,
        in_specs=[vmem] * sum(there),
        out_specs=[
            pl.BlockSpec(memory_space=pl.ANY) if inside is None else vmem for _, _, inside in outs
        ],
        out_shape=[
            pltpu.VMEM(shape, kind) if inside else jax.ShapeDtypeStruct(shape, kind)
            for shape, kind, inside in outs
        ],
        scratch_shapes=list(scratch),
        compiler_params=pltpu.CompilerParams(vmem_limit_bytes=limit * 2**20),
    )(*(in_vmem(array) for array in ins if array is not None))


def reduced_and_gathered(pieces):
    plans = list(zip(*(stages(*shifts) for shifts in ORDERS)))
    flat = [a for kept, sent in pieces for a in (kept, permuted(sent, neighbour))]
    way_back = []
    for number, plan in enumerate(plans):
        plan = plan[: len(flat) // 2]
        merge = len(plan) > 1 and len(set(plan)) == 1
        halves = [kept.shape[0] // 2 for kept in flat[::2]]
        way_back.append((plan, merge, [2 * half for half in halves]))
        if merge:
            halves = [sum(halves)]
        sent_type = BF16 if number < 2 else F32
        outs = [
            out
            for half in halves
            for out in (((half, 128), F32, True), ((half, 128), sent_type, True))
        ]
        if number in (0, 1):
            flat = [
                a
                for n, stage in enumerate(plan)
                for a in call(
                    functools.partial(halve_kernel, [stage], False),
                    flat[2 * n : 2 * n + 2],
                    outs[2 * n : 2 * n + 2],
                )
            ]
        else:
            flat = call(functools.partial(halve_kernel, plan, merge), flat, outs)
        flat = [
            permuted(a, across(plan[n // 2])) if n % 2 else a for n, a in enumerate(flat)
        ]
    arrays = [
        call(last_kernel, flat[n : n + 2], [(flat[n].shape, BF16, True)])[0]
        for n in range(0, len(flat), 2)
    ]
    for number, (plan, merged, sizes) in reversed(list(enumerate(way_back))):
        flat = [a for array, stage in zip(arrays, plan) for a in (array, permuted(array, across(stage)))]
        outs = [((size, 128), BF16, True) for size in sizes]
        if number in (0,):
            arrays = [
                call(
                    functools.partial(join_kernel, [stage], False),
                    flat[2 * n : 2 * n + 2],
                    outs[n : n + 1],
                )[0]
                for n, stage in enumerate(plan)
            ]
        else:
            arrays = call(functools.partial(join_kernel, plan, merged), flat, outs)
    return [(array, permuted(array, neighbour)) for array in arrays]


def per_device(
    encoder_out,
    encoder_weight,
    encoder_bias,
    predictor_out,
    predictor_weight,
    predictor_bias,
    output_weight,
    output_bias,
    labels,
    frame_lens,
    token_lens,
    loss_scale,
):
    seq_count, frame_count, width = encoder_out.shape
    vocab = output_weight.shape[1]
    all_seqs = labels.shape[0]
    held_seqs, held_units = predictor_out.shape[:2]
    assert held_seqs == 1
    frame_axis, token_axis = lax.axis_size("frames"), lax.axis_size("tokens")
    device_count = frame_axis * token_axis
    units = held_units * token_axis
    calls = seq_count // 2
    diagonals = (frame_count // 2 + units) * units
    vmem = pl.BlockSpec(memory_space=pltpu.VMEM)
    anywhere = pl.BlockSpec(memory_space=pl.ANY)

    weights = (
        encoder_out,
        encoder_weight,
        encoder_bias.reshape(1, width),
        predictor_weight,
        predictor_bias.reshape(1, width),
        output_weight,
        output_bias.reshape(1, vocab),
        frame_lens.reshape(1, all_seqs),
        token_lens.reshape(1, all_seqs),
        loss_scale.reshape(1, all_seqs),
    )
    packets, *weights = pl.pallas_call(
        packet_kernel,
        in_specs=[anywhere] * (2 + len(weights)),
        out_specs=[vmem] * (1 + len(weights)),
        out_shape=[jax.ShapeDtypeStruct((device_count, held_units + 2, width), BF16)]
        + [pltpu.VMEM(w.shape, w.dtype) for w in weights],
        scratch_shapes=[
            pltpu.VMEM((held_units, width), BF16),
            pltpu.VMEM(labels.shape, jnp.int32),
            pltpu.SemaphoreType.DMA((2 + len(weights),)),
        ],
        compiler_params=pltpu.CompilerParams(vmem_limit_bytes=4 * 2**20),
    )(*map(in_hbm, (predictor_out.reshape(held_units, width), labels, *weights)))
    *weights, frame_lens, token_lens, loss_scale = weights
    lens = frame_lens, token_lens
    packets = lax.all_to_all(packets, AXES, 0, 0, tiled=True)

    score_shapes = [
        ((2 * units // SUB_UNITS, SUB_UNITS * frame_count, vocab), F32),
        ((2, frame_count, width), F32),
        ((2 * units, width), F32),
        ((1, 128), jnp.int32),
        ((diagonals, 128), F32),
        ((diagonals, 128), F32),
        ((2 * units // SUB_UNITS, SUB_UNITS * frame_count, width), F32),
        ((2 * units // SUB_UNITS, SUB_UNITS * frame_count, 128), F32),
        ((units, 128), F32),
        ((1, 1, units, 128), F32),
    ]

    def scores(offset, encoder):
        return call(
            functools.partial(score_kernel, seq_count),
            (offset, packets, *lens, encoder, *weights[1:]),
            [(shape, kind, True) for shape, kind in score_shapes],
            scratch=[
                pltpu.VMEM((SUB_UNITS * frame_count, vocab), F32),
                pltpu.VMEM((SUB_UNITS * frame_count, vocab), F32),
                pltpu.SMEM((1, 128), jnp.int32),
                pltpu.VMEM((token_axis, width), F32),
                pltpu.SemaphoreType.DMA,
            ],
            limit=8,
        )

    offsets = 2 * jnp.arange(calls, dtype=jnp.int32).reshape(calls, 1, 1)
    encoders = weights[0].reshape(calls, 2, frame_count, width)
    if calls == 1:
        scored = scores(None, weights[0])
        matrix = scored[-1]
    else:
        scored = lax.map(lambda given: scores(*given), (offsets, encoders))
        matrix = scored[-1].reshape(1, calls, units, 128)

    matrices = doubled(matrix)
    layout = {"seqs_here": seq_count, "frame_count": frame_count, "units": units}
    layout["encoder"] = 0
    at = width // 128 * width
    layout["token"], layout["token_rows"] = at, all_seqs * units
    at += width // 128 * all_seqs * units
    layout["misc"] = layout["output_bias"] = at
    at += vocab // 128
    layout["encoder_bias"] = at
    at += width // 128
    layout["loss"] = at
    at += 3
    align = 16 * device_count
    output_rows = vocab // 128 * width
    output_rows += -output_rows % align
    rest_rows = at + (-at % align)

    blocks = 2 * units // SUB_UNITS
    block_rows = SUB_UNITS * frame_count

    def turns(offset, scored):
        hidden = scored[6]
        (turned,) = call(
            functools.partial(turn_kernel, layout),
            (offset, *lens, hidden),
            [((hidden.shape[0], width + 16, hidden.shape[1]), BF16, True)],
        )
        return turned

    def tangents(offset, scored, turned, matrices):
        softmax, _, _, table, blank, label, _, inverse, parts = scored
        return call(
            functools.partial(tangent_kernel, dict(layout, hops=len(matrices) - 1)),
            (
                *(offset, *lens, loss_scale, softmax, table, blank, label),
                *(turned, inverse, parts, *matrices),
            ),
            [
                ((blocks, block_rows, vocab), BF16, True),
                ((1, vocab), F32, True),
                ((1, 128), F32, True),
                ((output_rows // 2, 128), F32, True),
                ((output_rows // 2, 128), F32, True),
            ],
            scratch=[
                pltpu.VMEM((output_rows, 128), F32),
                pltpu.VMEM((frame_axis, units, 128), F32),
                pltpu.VMEM((diagonals, 128), F32),
                pltpu.VMEM((diagonals, 128), F32),
                pltpu.VMEM((diagonals, 128), F32),
                pltpu.VMEM((diagonals, 128), F32),
                pltpu.VMEM((block_rows, vocab), BF16),
                pltpu.VMEM((block_rows, vocab), BF16),
                pltpu.SMEM((1, 128), jnp.int32),
                pltpu.SemaphoreType.DMA,
                pltpu.SemaphoreType.DMA((4,)),
            ],
            limit=12,
        )

    def inners(offset, encoder, scored, tangent, output_bias_sum, loss):
        return call(
            functools.partial(inner_kernel, layout),
            (offset, *lens, tangent, scored[6], weights[5], encoder, output_bias_sum, loss),
            [
                ((2 * frame_count, width), BF16, True),
                ((rest_rows // 2, 128), F32, True),
                ((rest_rows // 2, 128), F32, True),
            ],
            scratch=[
                pltpu.VMEM((rest_rows, 128), F32),
                pltpu.VMEM((2, frame_count, width), F32),
                pltpu.VMEM((2 * units, width), F32),
                pltpu.VMEM((2 * block_rows, width), F32),
                pltpu.VMEM((2 * block_rows, width), F32),
                pltpu.SemaphoreType.DMA((2,)),
            ],
            limit=10,
        )

    def encoder_gradient_of(frame_tangent):
        return call(
            encoder_kernel,
            (frame_tangent, weights[1]),
            [((2, frame_count, width), F32, False)],
        )[0]

    if calls == 1:
        scored = scored[:-1]
        turned = turns(None, scored)
        tangent, output_bias_sum, loss, *output_sums = tangents(None, scored, turned, matrices)

        frame_tangent, *rest = inners(
            None, weights[0], scored, tangent, output_bias_sum, loss
        )
        sums = [*output_sums, *rest]
        encoder_gradient = encoder_gradient_of(frame_tangent)
    else:

        def add_call(sums, given):
            offset, encoder, scored, call = given
            own = [lax.dynamic_slice_in_dim(m, call, 1, 1) for m in matrices]
            turned = turns(offset, scored)
            tangent, output_bias_sum, loss, *more = tangents(offset, scored, turned, own)
            frame_tangent, *rest = inners(
                offset, encoder, scored, tangent, output_bias_sum, loss
            )
            return [a + b for a, b in zip(sums, more + rest)], encoder_gradient_of(frame_tangent)

        nothing = [jnp.zeros((r, 128), F32) for r in (output_rows // 2, rest_rows // 2)]
        sums, encoder_gradient = lax.scan(
            add_call,
            [nothing[0]] * 2 + [nothing[1]] * 2,
            (offsets, encoders, scored[:-1], jnp.arange(calls)),
        )
        encoder_gradient = encoder_gradient.reshape(encoder_out.shape)

    halves = reduced_and_gathered(list(zip(sums[::2], sums[1::2])))
    tail_rows = width // 128 * all_seqs * units + vocab // 128 + width // 128 + 3
    tail_rows += -tail_rows % 16
    finished = call(
        functools.partial(finish_kernel, layout),
        [*(a for pair in halves for a in pair), packets, weights[3]],
        [
            ((width, vocab), F32, None),
            ((width, width), F32, None),
            ((width, width), F32, None),
            ((1, vocab), F32, False),
            ((1, width), F32, False),
            ((1, width), F32, False),
            ((held_units, 1, width), F32, False),
            ((1, 1), F32, False),
        ],
        scratch=[
            pltpu.VMEM((width, vocab), F32),
            pltpu.VMEM((width, width), F32),
            pltpu.VMEM((width, width), F32),
            pltpu.VMEM((tail_rows, 128), F32),
            pltpu.VMEM((all_seqs * units, width), F32),
            pltpu.VMEM((all_seqs * units, width), F32),
            pltpu.SemaphoreType.DMA((4,)),
        ],
        limit=20,
    )
    return (
        finished[7].reshape(1),
        encoder_gradient,
        finished[6].transpose(1, 0, 2),
        finished[1],
        finished[4].reshape(width),
        finished[2],
        finished[5].reshape(width),
        finished[0],
        finished[3].reshape(vocab),
    )


def solution(mesh):
    placed = (
        P("tokens", "frames", None),
        P(),
        P(),
        P("frames", "tokens", None),
        P(),
        P(),
        P(),
        P(),
        P(None, "tokens"),
        P(),
        P(),
        P(),
    )
    return jax.shard_map(
        per_device,
        mesh=mesh,
        in_specs=placed,
        out_specs=(
            P("frames"),
            P("tokens", "frames", None),
            P("frames", "tokens", None),
            P(),
            P(),
            P(),
            P(),
            P(),
            P(),
        ),
        check_vma=False,
    )
```

```python
import functools

import jax
import jax.numpy as jnp
from jax import lax
from jax.experimental import pallas as pl
from jax.experimental.pallas import tpu as pltpu
from jax.sharding import PartitionSpec as P

NEG = -1e30
LOG2E = 1.4426950408889634
LN2 = 0.6931471805599453
BF16 = jnp.bfloat16
F32 = jnp.float32
GROUP = 32
SUB_UNITS = 4
ORDERS = ((0, 1), (2, 1))
AXES = ("frames", "tokens")


def lane_ids(rows):
    return lax.broadcasted_iota(jnp.int32, (rows, 128), 1)


def log2_add(a, b):
    return jnp.maximum(a, b) + jnp.log2(1.0 + jnp.exp2(-jnp.abs(a - b)))


def both_ways(blank_ref, label_ref, units, steps, ahead, behind, keep=None):
    def one_step(i, state):
        ahead, behind = state
        back = steps - 1 - i
        here = pl.ds(pl.multiple_of(i * units, 8), units)
        there = pl.ds(pl.multiple_of(back * units, 8), units)
        if keep is not None:
            keep[0][here, :] = ahead
            keep[1][there, :] = behind
        from_left = pltpu.roll(ahead + label_ref[here, :], 1, 0)
        to_right = pltpu.roll(behind, units - 1, 0) + label_ref[there, :]
        ahead = log2_add(ahead + blank_ref[here, :], from_left)
        behind = log2_add(behind + blank_ref[there, :], to_right)
        return ahead, behind

    return lax.fori_loop(0, steps, one_step, (ahead, behind))


def in_two_stages(count, first, second, even, odd, between=None):
    def two_blocks(n, _):
        first(2 * n + 1, odd)
        second(2 * n, even)
        first(2 * n + 2, even)
        second(2 * n + 1, odd)
        return 0

    @pl.when(count > 0)
    def _():
        first(0, even)

    if between is not None:
        between()

    @pl.when(count > 0)
    def _():
        lax.fori_loop(0, (count - 1) // 2, two_blocks, 0)

        @pl.when(count % 2 == 1)
        def _():
            second(count - 1, even)

        @pl.when(count % 2 == 0)
        def _():
            first(count - 1, odd)
            second(count - 2, even)
            second(count - 1, odd)


def packet_kernel(predictor_hbm, labels_hbm, packets_ref, predictor_ref, labels_ref, sems):
    loads = [
        pltpu.make_async_copy(predictor_hbm, predictor_ref, sems.at[0]),
        pltpu.make_async_copy(labels_hbm, labels_ref, sems.at[1]),
    ]
    for load in loads:
        load.start()
    for load in loads:
        load.wait()
    seqs, units = labels_ref.shape
    width = packets_ref.shape[2]
    flat = jnp.zeros((1, width), F32)
    for s in range(seqs):
        row = labels_ref[s : s + 1, :].astype(F32)
        row = jnp.concatenate([row, jnp.zeros((1, width - units), F32)], axis=1)
        flat = flat + (pltpu.roll(row, s * units, 1) if s else row)
    high = jnp.floor(flat * (1.0 / 32.0))
    packet = jnp.concatenate(
        [predictor_ref[...].astype(F32), high, flat - high * 32.0], axis=0
    ).astype(BF16)
    for d in range(packets_ref.shape[0]):
        packets_ref[d] = packet


def load_kernel(*refs):
    count = (len(refs) - 2) // 2
    *loaded_refs, frame_ref, sems = refs[count:]
    loads = [
        pltpu.make_async_copy(source, target, sems.at[n])
        for n, (source, target) in enumerate(zip(refs[:count], loaded_refs))
    ]
    for load in loads:
        load.start()
    for load in loads:
        load.wait()
    encoder_ref, weight_ref, bias_ref = loaded_refs[:3]
    frame_ref[...] = (
        (
            jnp.dot(
                encoder_ref[...].reshape(-1, encoder_ref.shape[-1]),
                weight_ref[...],
                preferred_element_type=F32,
            )
            + bias_ref[...]
        )
        .astype(BF16)
        .astype(F32)
        .reshape(frame_ref.shape)
    )


def entry(row_ref, place):
    row = row_ref[...].astype(F32)
    ids = lax.broadcasted_iota(jnp.int32, row.shape, 1)
    return jnp.sum(jnp.where(ids == place, row, 0.0), axis=1, keepdims=True)


def whole_number(row_ref, place):
    return entry(row_ref, place).astype(jnp.int32)[0, 0]


def first_of(seqs_here, offset_ref):
    first_seq = lax.axis_index("tokens") * seqs_here
    return first_seq if offset_ref is None else first_seq + whole_number(offset_ref, 0)


def block_counts(lens_ref, tokens_ref, first_seq, first_frame):
    counts = []
    for s in range(2):
        inside = first_frame < whole_number(lens_ref, first_seq + s)
        units = whole_number(tokens_ref, first_seq + s)
        counts.append(jnp.where(inside, units // SUB_UNITS + 1, 0))
    return counts


def score_kernel(
    seqs_here,
    offset_ref,
    packets_ref,
    lens_ref,
    tokens_ref,
    frame_ref,
    predictor_weight_ref,
    predictor_bias_ref,
    weight_ref,
    bias_ref,
    softmax_ref,
    token_ref,
    label_table_ref,
    blank_ref,
    label_ref,
    hidden_ref,
    inverse_ref,
    parts_ref,
    matrix_ref,
    even_ref,
    odd_ref,
    labels_smem,
    label_rows_ref,
    label_sem,
):
    seqs, frame_count, width = frame_ref.shape
    units = token_ref.shape[0] // seqs
    shards = label_rows_ref.shape[0]
    shard_units = units // shards
    part = frame_count // 2
    steps = part + units - 1
    first_frame = lax.axis_index("frames") * frame_count
    first_seq = first_of(seqs_here, offset_ref)
    vocab = weight_ref.shape[1]
    blank_ref[...] = jnp.zeros_like(blank_ref)
    label_ref[...] = jnp.full(label_ref.shape, NEG, F32)
    for s in range(seqs):
        for k in range(shards):
            rows = packets_ref[(first_seq + s) * shards + k]
            at = s * units + k * shard_units
            token_ref[at : at + shard_units, :] = rows[:shard_units].astype(F32)
    for k in range(shards):
        halves = packets_ref[k, shard_units:, :].astype(F32)
        label_rows_ref[k : k + 1, :] = halves[:1] * 32.0 + halves[1:2]
    wide = lane_ids(1)
    table = jnp.zeros((1, 128), F32)
    for s in range(seqs):
        for k in range(shards):
            target = s * units + k * shard_units
            shift = (target - (first_seq + s) * shard_units) % width
            row = pltpu.roll(label_rows_ref[k : k + 1, :], shift, 1)[:, :128]
            table = jnp.where((wide >= target) & (wide < target + shard_units), row, table)
    label_table_ref[...] = table.astype(jnp.int32)
    label_copy = pltpu.make_async_copy(label_table_ref, labels_smem, label_sem)
    label_copy.start()
    token_ref[...] = (
        jnp.dot(token_ref[...].astype(BF16), predictor_weight_ref[...], preferred_element_type=F32)
        + predictor_bias_ref[...]
    ).astype(BF16).astype(F32)

    counts = block_counts(lens_ref, tokens_ref, first_seq, first_frame)
    blocks = counts[0] + counts[1]
    lens = [whole_number(lens_ref, first_seq + s) for s in range(2)]
    last_units = [whole_number(tokens_ref, first_seq + s) for s in range(2)]
    lanes = lane_ids(frame_count)
    part_lanes = lane_ids(part)
    times = first_frame + lax.broadcasted_iota(jnp.int32, (frame_count, 1), 0)

    def place_of(i):
        seq = jnp.where(i >= counts[0], 1, 0)
        sub = i - seq * counts[0]
        return seq, sub, seq * (units // SUB_UNITS) + sub

    def multiply(i, logits_ref):
        seq, sub, block = place_of(i)
        frames = frame_ref[seq]
        hidden = jnp.concatenate(
            [
                jnp.tanh(frames + token_ref[pl.ds(seq * units + sub * SUB_UNITS + j, 1), :])
                for j in range(SUB_UNITS)
            ],
            axis=0,
        )
        hidden_ref[block] = hidden
        low = hidden.astype(BF16)
        logits_ref[...] = (
            jnp.dot(low, weight_ref[...], preferred_element_type=F32) + bias_ref[...]
        )

    def score(i, logits_ref):
        seq, sub, block = place_of(i)
        first_unit = sub * SUB_UNITS
        seq_len = jnp.where(seq == 0, lens[0], lens[1])
        last_unit = jnp.where(seq == 0, last_units[0], last_units[1])
        own_lanes = (part_lanes // GROUP) % 2 == seq
        logits = logits_ref[...]
        top = jnp.max(logits, axis=1, keepdims=True)
        weights = jnp.exp(logits - top)
        total = jnp.sum(weights, axis=1, keepdims=True)
        softmax_ref[block] = weights
        inverse_ref[block] = jnp.broadcast_to(1.0 / total, (weights.shape[0], 128))
        log_total = top + jnp.log(total)
        blanks = (logits[:, :1] - log_total) * LOG2E
        for j in range(SUB_UNITS):
            unit = first_unit + j
            rows = slice(j * frame_count, (j + 1) * frame_count)
            label = labels_smem[0, seq * units + unit]
            tile = logits_ref[rows, pl.ds(pl.multiple_of(label // 128 * 128, 128), 128)]
            picked = jnp.sum(
                jnp.where(lanes == label % 128, tile, 0.0), axis=1, keepdims=True
            )
            blank = blanks[rows]
            blank = jnp.where((times == seq_len - 1) & (unit < last_unit), NEG, blank)
            blank = jnp.where((times >= seq_len) | (unit > last_unit), 0.0, blank)
            step = jnp.where(
                (times >= seq_len) | (unit >= last_unit),
                NEG,
                (picked - log_total[rows]) * LOG2E,
            )
            at = (pl.ds(unit * (units + 1), part, stride=units), slice(None))
            blank = jnp.where(part_lanes < 64, blank[:part], blank[part:])
            step = jnp.where(part_lanes < 64, step[:part], step[part:])
            blank_ref[at] = jnp.where(own_lanes, blank, blank_ref[at])
            label_ref[at] = jnp.where(own_lanes, step, label_ref[at])

    in_two_stages(blocks, multiply, score, even_ref, odd_ref, label_copy.wait)
    eye = jnp.where(
        lane_ids(units) % GROUP == lax.broadcasted_iota(jnp.int32, (units, 128), 0), 0.0, NEG
    ).astype(F32)
    ahead, behind = both_ways(blank_ref, label_ref, units, steps, eye, eye)
    lanes = lane_ids(units)
    early = lanes < 64
    columns = jnp.where(early, behind, ahead)
    parts_ref[...] = columns
    others = pltpu.roll(jnp.where(early, ahead, behind), 64, 1)
    ways = [
        jnp.take_along_axis(
            columns, lanes // GROUP * GROUP + k, axis=1, mode="promise_in_bounds"
        )
        + others[k : k + 1, :]
        for k in range(units)
    ]
    top = functools.reduce(jnp.maximum, ways)
    total = functools.reduce(jnp.add, [jnp.exp2(way - top) for way in ways])
    matrix_ref[0, 0] = top + jnp.log2(total)


def turn_kernel(layout, offset_ref, lens_ref, tokens_ref, hidden_ref, turned_ref):
    width = hidden_ref.shape[2]
    first_frame = lax.axis_index("frames") * layout["frame_count"]
    first_seq = first_of(layout["seqs_here"], offset_ref)
    counts = block_counts(lens_ref, tokens_ref, first_seq, first_frame)

    def one_block(i, _):
        seq = jnp.where(i >= counts[0], 1, 0)
        block = i + seq * (layout["units"] // SUB_UNITS - counts[0])
        turned_ref[block, :width, :] = hidden_ref[block].astype(BF16).T
        turned_ref[block, width:, :] = jnp.ones((16, turned_ref.shape[2]), BF16)
        return 0

    lax.fori_loop(0, counts[0] + counts[1], one_block, 0)


def tangent_kernel(
    layout,
    offset_ref,
    lens_ref,
    tokens_ref,
    scale_ref,
    softmax_ref,
    label_table_ref,
    blank_ref,
    label_ref,
    turned_ref,
    inverse_ref,
    parts_ref,
    *refs,
):
    hops = layout["hops"]
    matrix_refs, refs = refs[: hops + 1], refs[hops + 1 :]
    (
        tangents_ref,
        output_bias_ref,
        loss_ref,
        *kept_refs,
        sums_ref,
        matrices_ref,
        ahead_ref,
        behind_ref,
        blank_part_ref,
        label_part_ref,
        even_ref,
        odd_ref,
        labels_smem,
        label_sem,
        sems,
    ) = refs
    label_copy = pltpu.make_async_copy(label_table_ref, labels_smem, label_sem)
    label_copy.start()
    frame_count = layout["frame_count"]
    width = turned_ref.shape[1] - 16
    units = layout["units"]
    part = frame_count // 2
    steps = part + units - 1
    here = lax.axis_index("frames")
    first_frame = here * frame_count
    first_seq = first_of(layout["seqs_here"], offset_ref)
    chunks = matrices_ref.shape[0]
    vocab = softmax_ref.shape[2]
    received = [(ref, n) for ref in matrix_refs for n in range(ref.shape[0])]
    for place, (matrix_ref, n) in zip(layout["matrix_places"], received):
        matrices_ref[place] = matrix_ref[n, 0]
    starts = lax.broadcasted_iota(jnp.int32, (units, 128), 0)
    lanes = lane_ids(units)
    early = lanes < 64
    gather_ids = lanes // GROUP * GROUP + starts
    own_first = (lane_ids(1) // GROUP) % 2 == 0

    def through(column, matrix):
        ways = column + matrix
        top = jnp.max(ways, axis=0, keepdims=True)
        row = top + jnp.log2(jnp.sum(jnp.exp2(ways - top), axis=0, keepdims=True))
        row = jnp.broadcast_to(row, (units, 128))
        return jnp.take_along_axis(row, gather_ids, axis=1, mode="promise_in_bounds")

    def one_chunk(i, carry):
        column, kept = carry
        other = chunks - 1 - i
        kept = jnp.where(jnp.where(early, i, other) == here, column, kept)
        matrix = jnp.where(early, matrices_ref[here ^ i], matrices_ref[here ^ other])
        return through(column, matrix), kept

    start = jnp.where(early & (starts > 0), NEG, 0.0).astype(F32)
    last, kept = lax.fori_loop(0, chunks, one_chunk, (start, start))
    middle = pltpu.roll(through(kept, parts_ref[...]), 64, 1)
    both_ways(
        blank_ref,
        label_ref,
        units,
        steps,
        jnp.where(early, kept, middle),
        jnp.where(early, middle, kept),
        (ahead_ref, behind_ref),
    )
    log_norm = jnp.max(jnp.where(early, last, pltpu.roll(last, 64, 1)), axis=0, keepdims=True)
    scale, length, bound = (
        jnp.where(own_first, entry(ref, first_seq), entry(ref, first_seq + 1))
        for ref in (scale_ref, lens_ref, tokens_ref)
    )
    length, bound = length.astype(jnp.int32), bound.astype(jnp.int32)
    part_start = first_frame + jnp.where(lane_ids(1) < 64, 0, part)
    last_diagonal = starts + jnp.minimum(length - part_start, part)
    first_blank = jnp.where(starts <= bound, starts, steps)
    first_label = jnp.where(starts < bound, starts, steps)
    norm = log_norm - jnp.log2(scale)

    def one_diagonal(e, _):
        rows = pl.ds(pl.multiple_of(e * units, 8), units)
        behind = behind_ref[rows, :]
        base = ahead_ref[rows, :] - norm
        before_end = last_diagonal > e
        blank_part_ref[rows, :] = jnp.where(
            before_end & (first_blank <= e), jnp.exp2(base + blank_ref[rows, :] + behind), 0.0
        )
        label_part_ref[rows, :] = jnp.where(
            before_end & (first_label <= e),
            jnp.exp2(base + label_ref[rows, :] + pltpu.roll(behind, units - 1, 0)),
            0.0,
        )
        return 0

    lax.fori_loop(0, steps, one_diagonal, 0, unroll=5)

    counts = block_counts(lens_ref, tokens_ref, first_seq, first_frame)
    block_lanes = lane_ids(frame_count)
    part_lanes = lane_ids(part)

    def place_of(i):
        seq = jnp.where(i >= counts[0], 1, 0)
        sub = i - seq * counts[0]
        return seq, sub, seq * (units // SUB_UNITS) + sub

    wide = lane_ids(1)
    loss = jnp.where(here == 0, -log_norm * LN2, 0.0)
    spread = jnp.where(wide == first_seq, loss[:, :1], 0.0)
    loss_ref[...] = spread + jnp.where(wide == first_seq + 1, loss[:, GROUP : GROUP + 1], 0.0)
    label_copy.wait()

    counts_all = counts[0] + counts[1]
    sums_ref[...] = jnp.zeros_like(sums_ref)
    output_bias_ref[...] = jnp.zeros_like(output_bias_ref)

    def prepare(i, tangent_ref):
        seq, sub, block = place_of(i)
        own_lanes = [part_lanes % GROUP + GROUP * (seq + 2 * half) for half in (0, 1)]
        for j in range(SUB_UNITS):
            unit = sub * SUB_UNITS + j
            rows = slice(j * frame_count, (j + 1) * frame_count)
            at = (pl.ds(unit * (units + 1), part, stride=units), slice(None))
            blank, step = (
                jnp.concatenate(
                    [
                        jnp.take_along_axis(ref[at], ids, axis=1, mode="promise_in_bounds")
                        for ids in own_lanes
                    ],
                    axis=0,
                )
                for ref in (blank_part_ref, label_part_ref)
            )
            both = (blank + step) * inverse_ref[block, rows, :]
            for v in range(vocab // 128):
                cut = slice(v * 128, (v + 1) * 128)
                piece = softmax_ref[block, rows, cut] * both
                if v == 0:
                    piece = piece - jnp.where(block_lanes == 0, blank, 0.0)
                piece = piece.astype(BF16)
                tangent_ref[rows, cut] = piece
                tangents_ref[block, rows, cut] = piece
            label = labels_smem[0, seq * units + unit]
            cut = pl.ds(pl.multiple_of(label // 128 * 128, 128), 128)
            piece = softmax_ref[block, rows, cut] * both
            piece = piece - jnp.where((block_lanes == 0) & (label < 128), blank, 0.0)
            piece = (piece - jnp.where(block_lanes == label % 128, step, 0.0)).astype(BF16)
            tangent_ref[rows, cut] = piece
            tangents_ref[block, rows, cut] = piece

    def multiply(i, tangent_ref):
        _, _, block = place_of(i)
        product = jnp.dot(turned_ref[block], tangent_ref[...], preferred_element_type=F32)
        for v in range(vocab // 128):
            sums_ref[v * width : (v + 1) * width, :] += product[:width, v * 128 : (v + 1) * 128]
        output_bias_ref[...] += product[width : width + 1, :]

    in_two_stages(counts_all, prepare, multiply, even_ref, odd_ref)
    part_halves(sums_ref, kept_refs, sems)


def part_halves(sums_ref, piece_refs, sems):
    place = lax.axis_index("tokens") & 1
    copies, start = [], 0
    for kept_ref, sent_ref in zip(piece_refs[::2], piece_refs[1::2]):
        half = kept_ref.shape[0]
        for part, target in ((1 - place, sent_ref), (place, kept_ref)):
            source = sums_ref.at[pl.ds(pl.multiple_of(start + part * half, 8), half), :]
            copies.append(pltpu.make_async_copy(source, target, sems.at[len(copies)]))
        start += 2 * half
    for copy in copies:
        copy.start()
    for copy in copies:
        copy.wait()


def inner_kernel(
    layout,
    offset_ref,
    lens_ref,
    tokens_ref,
    tangents_ref,
    hidden_ref,
    weight_ref,
    encoder_ref,
    output_bias_ref,
    loss_ref,
    frame_tangent_ref,
    kept_ref,
    sent_ref,
    sums_ref,
    frame_sum_ref,
    token_sum_ref,
    even_ref,
    odd_ref,
    sems,
):
    seqs, frame_count, width = encoder_ref.shape
    units = token_sum_ref.shape[0] // seqs
    vocab = weight_ref.shape[1]
    first_frame = lax.axis_index("frames") * frame_count
    first_seq = first_of(layout["seqs_here"], offset_ref)
    frame_sum_ref[...] = jnp.zeros_like(frame_sum_ref)
    token_sum_ref[...] = jnp.zeros_like(token_sum_ref)
    unset = slice(layout["token"], sums_ref.shape[0])
    sums_ref[unset, :] = jnp.zeros_like(sums_ref[unset, :])
    counts = block_counts(lens_ref, tokens_ref, first_seq, first_frame)

    def place_of(i):
        seq = jnp.where(i >= counts[0], 1, 0)
        sub = i - seq * counts[0]
        return seq, sub, seq * (units // SUB_UNITS) + sub

    def product_of(tangents):
        return lax.dot_general(
            tangents, weight_ref[...], (((1,), (1,)), ((), ())), preferred_element_type=F32
        )

    def add_up(i, product):
        seq, sub, block = place_of(i)
        hidden = hidden_ref[block]
        inner = product * (1.0 - hidden * hidden)
        total = frame_sum_ref[seq]
        for j in range(SUB_UNITS):
            rows = slice(j * frame_count, (j + 1) * frame_count)
            total = total + inner[rows]
            token_sum_ref[pl.ds(seq * units + sub * SUB_UNITS + j, 1), :] = jnp.sum(
                inner[rows], axis=0, keepdims=True
            )
        frame_sum_ref[seq] = total

    def multiply_two(n, product_ref):
        both = [tangents_ref[place_of(2 * n + m)[2]] for m in (0, 1)]
        product_ref[...] = product_of(jnp.concatenate(both, axis=0))

    def add_up_two(n, product_ref):
        half = product_ref.shape[0] // 2
        add_up(2 * n, product_ref[:half])
        add_up(2 * n + 1, product_ref[half:])

    blocks = counts[0] + counts[1]
    in_two_stages(blocks // 2, multiply_two, add_up_two, even_ref, odd_ref)

    @pl.when(blocks % 2 == 1)
    def _():
        add_up(blocks - 1, product_of(tangents_ref[place_of(blocks - 1)[2]]))

    low = frame_sum_ref[...].reshape(seqs * frame_count, width).astype(BF16)
    frame_tangent_ref[...] = low
    product = lax.dot_general(
        encoder_ref[...].reshape(seqs * frame_count, width),
        low,
        (((0,), (0,)), ((), ())),
        preferred_element_type=F32,
    )
    encoder_bias = jnp.sum(low.astype(F32), axis=0, keepdims=True)
    for v in range(width // 128):
        cut = slice(v * 128, (v + 1) * 128)
        at = layout["encoder"] + v * width
        sums_ref[at : at + width, :] = product[:, cut]
        at = layout["token"] + v * layout["token_rows"] + first_seq * units
        sums_ref[pl.ds(pl.multiple_of(at, 8), seqs * units), :] = token_sum_ref[:, cut]
        at = layout["encoder_bias"] + v
        sums_ref[at : at + 1, :] = encoder_bias[:, cut]
    for v in range(vocab // 128):
        at = layout["output_bias"] + v
        sums_ref[at : at + 1, :] = output_bias_ref[:, v * 128 : (v + 1) * 128]
    spread = loss_ref[...]
    for k in range(3):
        part = spread.astype(BF16).astype(F32)
        sums_ref[layout["loss"] + k : layout["loss"] + k + 1, :] = part
        spread = spread - part
    part_halves(sums_ref, (kept_ref, sent_ref), sems)


def encoder_kernel(frame_tangent_ref, encoder_weight_ref, encoder_gradient_ref):
    encoder_gradient_ref[...] = lax.dot_general(
        frame_tangent_ref[...],
        encoder_weight_ref[...],
        (((1,), (1,)), ((), ())),
        preferred_element_type=F32,
    ).reshape(encoder_gradient_ref.shape)


def two_halves(stage, half):
    upper = upper_of(stage)
    own = pl.ds(pl.multiple_of(jnp.where(upper != 0, half, 0), 16), half)
    other = pl.ds(pl.multiple_of(jnp.where(upper != 0, 0, half), 16), half)
    return own, other


def halve_kernel(stages, merge, *refs):
    count, at = len(stages), 0
    for n, stage in enumerate(stages):
        kept_ref, received_ref = refs[2 * n : 2 * n + 2]
        half = kept_ref.shape[0] // 2
        own, other = two_halves(stage, half)
        if merge:
            next_ref, sent_ref = (ref.at[at : at + half, :] for ref in refs[2 * count :])
            at += half
        else:
            next_ref, sent_ref = refs[2 * count + 2 * n : 2 * count + 2 * n + 2]
        sent_ref[...] = (kept_ref[other, :] + received_ref[other, :].astype(F32)).astype(
            sent_ref.dtype
        )
        next_ref[...] = kept_ref[own, :] + received_ref[own, :].astype(F32)


def add_kernel(count, *refs):
    at = 0
    for n in range(count):
        kept_ref, received_ref = refs[2 * n : 2 * n + 2]
        rows = kept_ref.shape[0]
        refs[-1][at : at + rows, :] = kept_ref[...] + received_ref[...].astype(F32)
        at += rows


def last_kernel(own_ref, other_ref, beside_ref, *sum_refs):
    at = 0
    for sum_ref in sum_refs:
        rows = slice(at, at + sum_ref.shape[0])
        sum_ref[...] = (own_ref[rows, :] + other_ref[rows, :]).astype(BF16)
        at += sum_ref.shape[0]


def join_kernel(stages, merged, *refs):
    count, at = len(stages), 0
    joined_refs = refs[2:] if merged else refs[2 * count :]
    for n, (stage, joined_ref) in enumerate(zip(stages, joined_refs)):
        half = joined_ref.shape[0] // 2
        own, other = two_halves(stage, half)
        if merged:
            own_ref, other_ref = (ref.at[at : at + half, :] for ref in refs[:2])
            at += half
        else:
            own_ref, other_ref = refs[2 * n : 2 * n + 2]
        joined_ref[own, :] = own_ref[...]
        joined_ref[other, :] = other_ref[...]


def half_columns(half_rows, width, upper):
    return [
        v
        for v in range(width // 128)
        if (v * width >= half_rows if upper else (v + 1) * width <= half_rows)
    ]


def copy_out(output_ref, rest_ref, upper, output_hbm, encoder_hbm, output_buffer, encoder_buffer, sems):
    width = encoder_buffer.shape[0]
    rows = output_ref.shape[0]
    count = rows // width
    for v in range(count):
        output_buffer[:, v * 128 : (v + 1) * 128] = output_ref[
            v * width : (v + 1) * width, :
        ].astype(F32)
    start = pl.multiple_of(upper * count * 128, 128)
    whole_copy = pltpu.make_async_copy(
        output_buffer, output_hbm.at[:, pl.ds(start, count * 128)], sems.at[0]
    )
    whole_copy.start()
    half = rest_ref.shape[0]
    copies = []
    for side in (0, 1):
        blocks = half_columns(half, width, side)
        if not blocks:
            continue
        columns = slice(blocks[0] * 128, (blocks[-1] + 1) * 128)
        copy = pltpu.make_async_copy(
            encoder_buffer.at[:, columns], encoder_hbm.at[:, columns], sems.at[1]
        )
        copies.append((side, copy))

        @pl.when(upper == side)
        def _():
            for v in blocks:
                at = v * width - side * half
                encoder_buffer[:, v * 128 : (v + 1) * 128] = rest_ref[at : at + width, :].astype(F32)
            copy.start()

    def wait():
        whole_copy.wait()
        for side, copy in copies:
            pl.when(upper == side)(copy.wait)

    return wait


def finish_own_kernel(output_ref, rest_ref, output_hbm, encoder_hbm, *scratch):
    place = lax.axis_index("tokens") & 1
    copy_out(output_ref, rest_ref, place, output_hbm, encoder_hbm, *scratch)()


def finish_kernel(
    layout,
    output_other_ref,
    rest_own_ref,
    rest_other_ref,
    packets_ref,
    predictor_weight_ref,
    output_weight_begun,
    encoder_weight_begun,
    output_weight_hbm,
    encoder_weight_hbm,
    weight_gradient_hbm,
    output_bias_ref,
    encoder_bias_ref,
    bias_gradient_ref,
    predictor_gradient_ref,
    losses_ref,
    output_buffer,
    encoder_buffer,
    weight_gradient_ref,
    tail_ref,
    tokens_ref,
    predictor_ref,
    sems,
    gradient_sem,
):
    width, vocab = encoder_buffer.shape[0], output_bias_ref.shape[1]
    place = lax.axis_index("tokens") & 1
    wait = copy_out(
        output_other_ref,
        rest_other_ref,
        1 - place,
        output_weight_hbm,
        encoder_weight_hbm,
        output_buffer,
        encoder_buffer,
        sems,
    )
    tail_start = layout["token"]

    def keep_tail(low_ref, high_ref):
        half = low_ref.shape[0]
        stop = tail_start + tail_ref.shape[0]
        cut = min(max(half, tail_start), stop)
        if cut > tail_start:
            tail_ref[: cut - tail_start, :] = low_ref[tail_start:cut, :].astype(F32)
        if stop > cut:
            tail_ref[cut - tail_start :, :] = high_ref[cut - half : stop - half, :].astype(F32)

    pl.when(place == 0)(lambda: keep_tail(rest_own_ref, rest_other_ref))
    pl.when(place == 1)(lambda: keep_tail(rest_other_ref, rest_own_ref))
    count = layout["token_rows"]
    for v in range(width // 128):
        tokens_ref[:, v * 128 : (v + 1) * 128] = tail_ref[v * count : (v + 1) * count, :]
    tokens = tokens_ref[...]
    held_rows = packets_ref.shape[1] - 2
    for d in range(packets_ref.shape[0]):
        predictor_ref[d * held_rows : (d + 1) * held_rows, :] = packets_ref[
            d, :held_rows, :
        ].astype(F32)
    weight_gradient_ref[...] = lax.dot_general(
        predictor_ref[...].astype(BF16),
        tokens.astype(BF16),
        (((0,), (0,)), ((), ())),
        preferred_element_type=F32,
    )
    gradient_copy = pltpu.make_async_copy(weight_gradient_ref, weight_gradient_hbm, gradient_sem)
    gradient_copy.start()

    def row(name, k):
        at = layout[name] - tail_start + k
        return tail_ref[at : at + 1, :]

    output_bias_ref[...] = jnp.concatenate(
        [row("output_bias", v) for v in range(vocab // 128)], axis=1
    )
    encoder_bias_ref[...] = jnp.concatenate(
        [row("encoder_bias", v) for v in range(width // 128)], axis=1
    )
    bias_gradient_ref[...] = jnp.sum(tokens, axis=0, keepdims=True)
    device = lax.axis_index("frames") * lax.axis_size("tokens") + lax.axis_index("tokens")
    mine = jnp.concatenate(
        [tokens_ref[pl.ds(device * held_rows + r, 1), :] for r in range(held_rows)], axis=0
    )
    predictor_gradient_ref[:, 0, :] = lax.dot_general(
        mine.astype(BF16),
        predictor_weight_ref[...],
        (((1,), (1,)), ((), ())),
        preferred_element_type=F32,
    )
    loss = row("loss", 0) + row("loss", 1) + row("loss", 2)
    losses_ref[...] = jnp.sum(
        jnp.where(lane_ids(1) == lax.axis_index("frames"), loss, 0.0), axis=1, keepdims=True
    )
    wait()
    gradient_copy.wait()


def in_hbm(array):
    return pltpu.with_memory_space_constraint(array, pltpu.HBM)


def in_vmem(array):
    return pltpu.with_memory_space_constraint(array, pltpu.VMEM)


def permuted(array, partner):
    frames, tokens = lax.axis_size("frames"), lax.axis_size("tokens")
    pairs = []
    for f in range(frames):
        for k in range(tokens):
            g, h = partner(f, k)
            pairs.append((f * tokens + k, g * tokens + h))
    return lax.ppermute(array, AXES, pairs)


def doubled(array):
    blocks, places = [array], [[0]]
    bit = lax.axis_size("frames") // 2
    while bit:
        joined = jnp.concatenate(blocks, axis=0) if len(blocks) > 1 else blocks[0]
        blocks.append(permuted(joined, lambda f, k: (f ^ bit, k)))
        places.append([place ^ bit for held in places for place in held])
        bit //= 2
    return blocks, [place for held in places for place in held]


def stages(even, odd):
    frame_bits = [(1 << i, 0) for i in range(lax.axis_size("frames").bit_length() - 1)]
    token_bits = [(0, 1 << i) for i in range(1, lax.axis_size("tokens").bit_length() - 1)]
    first = frame_bits[:1] + token_bits + frame_bits[1:2]
    orders = [first[shift:] + first[:shift] + frame_bits[2:] for shift in (even, odd)]
    return list(zip(*orders))


def upper_of(stage):
    f, k = lax.axis_index("frames"), lax.axis_index("tokens")
    even, odd = ((f & frame_bit) | (k & token_bit) for frame_bit, token_bit in stage)
    return jnp.where((k & 1) == 0, even, odd)


def across(stage):
    return lambda f, k: (f ^ stage[k & 1][0], k ^ stage[k & 1][1])


def neighbour(f, k):
    return f, k ^ 1


def call(body, ins, outs, scratch=(), limit=4):
    vmem = pl.BlockSpec(memory_space=pltpu.VMEM)
    there = [array is not None for array in ins]

    def kernel(*refs):
        given = iter(refs)
        body(*(next(given) if here else None for here in there), *given)

    return pl.pallas_call(
        kernel,
        in_specs=[vmem] * sum(there),
        out_specs=[
            pl.BlockSpec(memory_space=pl.ANY) if inside is None else vmem for _, _, inside in outs
        ],
        out_shape=[
            pltpu.VMEM(shape, kind) if inside else jax.ShapeDtypeStruct(shape, kind)
            for shape, kind, inside in outs
        ],
        scratch_shapes=list(scratch),
        compiler_params=pltpu.CompilerParams(vmem_limit_bytes=limit * 2**20),
    )(*(in_vmem(array) for array in ins if array is not None))


def reduced_and_gathered(pieces, beside):
    plans = list(zip(*(stages(*shifts) for shifts in ORDERS)))
    flat = [a for kept, sent in pieces for a in (kept, permuted(sent, neighbour))]
    way_back = []
    vmem = pl.BlockSpec(memory_space=pltpu.VMEM)
    *plans, last_plan = plans
    for number, plan in enumerate(plans):
        plan = plan[: len(flat) // 2]
        merge = len(plan) > 1 and len(set(plan)) == 1
        halves = [kept.shape[0] // 2 for kept in flat[::2]]
        way_back.append((plan, merge, [2 * half for half in halves]))
        if merge:
            halves = [sum(halves)]
        sent_type = BF16 if number < 2 else F32
        outs = [
            out
            for half in halves
            for out in (((half, 128), F32, True), ((half, 128), sent_type, True))
        ]
        if number in (0, 1):
            flat = [
                a
                for n, stage in enumerate(plan)
                for a in call(
                    functools.partial(halve_kernel, [stage], False),
                    flat[2 * n : 2 * n + 2],
                    outs[2 * n : 2 * n + 2],
                )
            ]
        else:
            flat = call(functools.partial(halve_kernel, plan, merge), flat, outs)
        flat = [
            permuted(a, across(plan[n // 2])) if n % 2 else a for n, a in enumerate(flat)
        ]
    vmem = pl.BlockSpec(memory_space=pltpu.VMEM)
    shapes = [kept.shape for kept in flat[::2]]
    rows = sum(shape[0] for shape in shapes)
    (own,) = call(functools.partial(add_kernel, len(shapes)), flat, [((rows, 128), F32, True)])
    other = permuted(own, across(last_plan[0]))
    arrays = pl.pallas_call(
        last_kernel,
        in_specs=[vmem, vmem, pl.BlockSpec(memory_space=pl.ANY)],
        out_specs=[vmem] * len(shapes),
        out_shape=[pltpu.VMEM(shape, BF16) for shape in shapes],
        compiler_params=pltpu.CompilerParams(vmem_limit_bytes=4 * 2**20),
    )(in_vmem(own), in_vmem(other), in_hbm(beside))
    for number, (plan, merged, sizes) in reversed(list(enumerate(way_back))):
        flat = [a for array, stage in zip(arrays, plan) for a in (array, permuted(array, across(stage)))]
        outs = [((size, 128), BF16, True) for size in sizes]
        if number in (0,):
            arrays = [
                call(
                    functools.partial(join_kernel, [stage], False),
                    flat[2 * n : 2 * n + 2],
                    outs[n : n + 1],
                )[0]
                for n, stage in enumerate(plan)
            ]
        else:
            arrays = call(functools.partial(join_kernel, plan, merged), flat, outs)
    return [(array, permuted(array, neighbour)) for array in arrays]


def per_device(
    encoder_out,
    encoder_weight,
    encoder_bias,
    predictor_out,
    predictor_weight,
    predictor_bias,
    output_weight,
    output_bias,
    labels,
    frame_lens,
    token_lens,
    loss_scale,
):
    seq_count, frame_count, width = encoder_out.shape
    vocab = output_weight.shape[1]
    all_seqs = labels.shape[0]
    held_seqs, held_units = predictor_out.shape[:2]
    assert held_seqs == 1
    frame_axis, token_axis = lax.axis_size("frames"), lax.axis_size("tokens")
    device_count = frame_axis * token_axis
    units = held_units * token_axis
    calls = seq_count // 2
    diagonals = (frame_count // 2 + units) * units
    vmem = pl.BlockSpec(memory_space=pltpu.VMEM)
    anywhere = pl.BlockSpec(memory_space=pl.ANY)

    weights = (
        encoder_out,
        encoder_weight,
        encoder_bias.reshape(1, width),
        predictor_weight,
        predictor_bias.reshape(1, width),
        output_weight,
        output_bias.reshape(1, vocab),
        frame_lens.reshape(1, all_seqs),
        token_lens.reshape(1, all_seqs),
        loss_scale.reshape(1, all_seqs),
    )
    packets = pl.pallas_call(
        packet_kernel,
        in_specs=[anywhere] * 2,
        out_specs=vmem,
        out_shape=jax.ShapeDtypeStruct((device_count, held_units + 2, width), BF16),
        scratch_shapes=[
            pltpu.VMEM((held_units, width), BF16),
            pltpu.VMEM(labels.shape, jnp.int32),
            pltpu.SemaphoreType.DMA((2,)),
        ],
        compiler_params=pltpu.CompilerParams(vmem_limit_bytes=4 * 2**20),
    )(in_hbm(predictor_out.reshape(held_units, width)), in_hbm(labels))
    *weights, frames = pl.pallas_call(
        load_kernel,
        in_specs=[anywhere] * len(weights),
        out_specs=[vmem] * (1 + len(weights)),
        out_shape=[pltpu.VMEM(w.shape, w.dtype) for w in weights]
        + [pltpu.VMEM(encoder_out.shape, F32)],
        scratch_shapes=[pltpu.SemaphoreType.DMA((len(weights),))],
        compiler_params=pltpu.CompilerParams(vmem_limit_bytes=4 * 2**20),
    )(*map(in_hbm, weights))
    *weights, frame_lens, token_lens, loss_scale = weights
    lens = frame_lens, token_lens
    packets = lax.all_to_all(packets, AXES, 0, 0, tiled=True)

    score_shapes = [
        ((2 * units // SUB_UNITS, SUB_UNITS * frame_count, vocab), F32),
        ((2 * units, width), F32),
        ((1, 128), jnp.int32),
        ((diagonals, 128), F32),
        ((diagonals, 128), F32),
        ((2 * units // SUB_UNITS, SUB_UNITS * frame_count, width), F32),
        ((2 * units // SUB_UNITS, SUB_UNITS * frame_count, 128), F32),
        ((units, 128), F32),
        ((1, 1, units, 128), F32),
    ]

    def scores(offset, frames):
        return call(
            functools.partial(score_kernel, seq_count),
            (offset, packets, *lens, frames, *weights[3:]),
            [(shape, kind, True) for shape, kind in score_shapes],
            scratch=[
                pltpu.VMEM((SUB_UNITS * frame_count, vocab), F32),
                pltpu.VMEM((SUB_UNITS * frame_count, vocab), F32),
                pltpu.SMEM((1, 128), jnp.int32),
                pltpu.VMEM((token_axis, width), F32),
                pltpu.SemaphoreType.DMA,
            ],
            limit=8,
        )

    offsets = 2 * jnp.arange(calls, dtype=jnp.int32).reshape(calls, 1, 1)
    encoders = weights[0].reshape(calls, 2, frame_count, width)
    if calls == 1:
        scored = scores(None, frames)
        matrix = scored[-1]
    else:
        scored = lax.map(
            lambda given: scores(*given),
            (offsets, frames.reshape(calls, 2, frame_count, width)),
        )
        matrix = scored[-1].reshape(1, calls, units, 128)

    matrices, matrix_places = doubled(matrix)
    layout = {"matrix_places": matrix_places, "seqs_here": seq_count, "frame_count": frame_count, "units": units}
    layout["encoder"] = 0
    at = width // 128 * width
    layout["token"], layout["token_rows"] = at, all_seqs * units
    at += width // 128 * all_seqs * units
    layout["misc"] = layout["output_bias"] = at
    at += vocab // 128
    layout["encoder_bias"] = at
    at += width // 128
    layout["loss"] = at
    at += 3
    align = 16 * device_count
    output_rows = vocab // 128 * width
    output_rows += -output_rows % align
    rest_rows = at + (-at % align)

    blocks = 2 * units // SUB_UNITS
    block_rows = SUB_UNITS * frame_count

    def turns(offset, scored):
        hidden = scored[5]
        (turned,) = call(
            functools.partial(turn_kernel, layout),
            (offset, *lens, hidden),
            [((hidden.shape[0], width + 16, hidden.shape[1]), BF16, True)],
        )
        return turned

    def tangents(offset, scored, turned, matrices):
        softmax, _, table, blank, label, _, inverse, parts = scored
        return call(
            functools.partial(tangent_kernel, dict(layout, hops=len(matrices) - 1)),
            (
                *(offset, *lens, loss_scale, softmax, table, blank, label),
                *(turned, inverse, parts, *matrices),
            ),
            [
                ((blocks, block_rows, vocab), BF16, True),
                ((1, vocab), F32, True),
                ((1, 128), F32, True),
                ((output_rows // 2, 128), F32, True),
                ((output_rows // 2, 128), F32, True),
            ],
            scratch=[
                pltpu.VMEM((output_rows, 128), F32),
                pltpu.VMEM((frame_axis, units, 128), F32),
                pltpu.VMEM((diagonals, 128), F32),
                pltpu.VMEM((diagonals, 128), F32),
                pltpu.VMEM((diagonals, 128), F32),
                pltpu.VMEM((diagonals, 128), F32),
                pltpu.VMEM((block_rows, vocab), BF16),
                pltpu.VMEM((block_rows, vocab), BF16),
                pltpu.SMEM((1, 128), jnp.int32),
                pltpu.SemaphoreType.DMA,
                pltpu.SemaphoreType.DMA((4,)),
            ],
            limit=12,
        )

    def inners(offset, encoder, scored, tangent, output_bias_sum, loss):
        return call(
            functools.partial(inner_kernel, layout),
            (offset, *lens, tangent, scored[5], weights[5], encoder, output_bias_sum, loss),
            [
                ((2 * frame_count, width), BF16, True),
                ((rest_rows // 2, 128), F32, True),
                ((rest_rows // 2, 128), F32, True),
            ],
            scratch=[
                pltpu.VMEM((rest_rows, 128), F32),
                pltpu.VMEM((2, frame_count, width), F32),
                pltpu.VMEM((2 * units, width), F32),
                pltpu.VMEM((2 * block_rows, width), F32),
                pltpu.VMEM((2 * block_rows, width), F32),
                pltpu.SemaphoreType.DMA((2,)),
            ],
            limit=10,
        )

    def encoder_gradient_of(frame_tangent):
        return call(
            encoder_kernel,
            (frame_tangent, weights[1]),
            [((2, frame_count, width), F32, False)],
        )[0]

    if calls == 1:
        scored = scored[:-1]
        turned = turns(None, scored)
        tangent, output_bias_sum, loss, *output_sums = tangents(None, scored, turned, matrices)

        frame_tangent, *rest = inners(
            None, weights[0], scored, tangent, output_bias_sum, loss
        )
        sums = [*output_sums, *rest]
        encoder_gradient = encoder_gradient_of(frame_tangent)
    else:

        def add_call(sums, given):
            offset, encoder, scored, call = given
            own = [lax.dynamic_slice_in_dim(m, call, 1, 1) for m in matrices]
            turned = turns(offset, scored)
            tangent, output_bias_sum, loss, *more = tangents(offset, scored, turned, own)
            frame_tangent, *rest = inners(
                offset, encoder, scored, tangent, output_bias_sum, loss
            )
            return [a + b for a, b in zip(sums, more + rest)], encoder_gradient_of(frame_tangent)

        nothing = [jnp.zeros((r, 128), F32) for r in (output_rows // 2, rest_rows // 2)]
        sums, encoder_gradient = lax.scan(
            add_call,
            [nothing[0]] * 2 + [nothing[1]] * 2,
            (offsets, encoders, scored[:-1], jnp.arange(calls)),
        )
        encoder_gradient = encoder_gradient.reshape(encoder_out.shape)

    halves = reduced_and_gathered(list(zip(sums[::2], sums[1::2])), encoder_gradient)
    tail_rows = width // 128 * all_seqs * units + vocab // 128 + width // 128 + 3
    tail_rows += -tail_rows % 16
    (output_own, output_other), (rest_own, rest_other) = halves
    buffers = [
        pltpu.VMEM((width, vocab // 2), F32),
        pltpu.VMEM((width, width), F32),
    ]
    begun = call(
        finish_own_kernel,
        (output_own, rest_own),
        [((width, vocab), F32, None), ((width, width), F32, None)],
        scratch=[*buffers, pltpu.SemaphoreType.DMA((2,))],
        limit=8,
    )
    finished = pl.pallas_call(
        functools.partial(finish_kernel, layout),
        in_specs=[vmem] * 5 + [anywhere] * 2,
        out_specs=[anywhere] * 3 + [vmem] * 5,
        out_shape=[
            jax.ShapeDtypeStruct((width, vocab), F32),
            jax.ShapeDtypeStruct((width, width), F32),
            jax.ShapeDtypeStruct((width, width), F32),
            jax.ShapeDtypeStruct((1, vocab), F32),
            jax.ShapeDtypeStruct((1, width), F32),
            jax.ShapeDtypeStruct((1, width), F32),
            jax.ShapeDtypeStruct((held_units, 1, width), F32),
            jax.ShapeDtypeStruct((1, 1), F32),
        ],
        input_output_aliases={5: 0, 6: 1},
        scratch_shapes=[
            *buffers,
            pltpu.VMEM((width, width), F32),
            pltpu.VMEM((tail_rows, 128), F32),
            pltpu.VMEM((all_seqs * units, width), F32),
            pltpu.VMEM((all_seqs * units, width), F32),
            pltpu.SemaphoreType.DMA((2,)),
            pltpu.SemaphoreType.DMA,
        ],
        compiler_params=pltpu.CompilerParams(vmem_limit_bytes=20 * 2**20),
    )(
        *map(in_vmem, (output_other, rest_own, rest_other, packets, weights[3])),
        *map(in_hbm, begun),
    )
    return (
        finished[7].reshape(1),
        encoder_gradient,
        finished[6].transpose(1, 0, 2),
        finished[1],
        finished[4].reshape(width),
        finished[2],
        finished[5].reshape(width),
        finished[0],
        finished[3].reshape(vocab),
    )


def solution(mesh):
    placed = (
        P("tokens", "frames", None),
        P(),
        P(),
        P("frames", "tokens", None),
        P(),
        P(),
        P(),
        P(),
        P(None, "tokens"),
        P(),
        P(),
        P(),
    )
    return jax.shard_map(
        per_device,
        mesh=mesh,
        in_specs=placed,
        out_specs=(
            P("frames"),
            P("tokens", "frames", None),
            P("frames", "tokens", None),
            P(),
            P(),
            P(),
            P(),
            P(),
            P(),
        ),
        check_vma=False,
    )
```

```python
import functools

import jax
import jax.numpy as jnp
from jax import lax
from jax.experimental import pallas as pl
from jax.experimental.pallas import tpu as pltpu
from jax.sharding import PartitionSpec as P

NEG = -1e30
LOG2E = 1.4426950408889634
LN2 = 0.6931471805599453
BF16 = jnp.bfloat16
F32 = jnp.float32
GROUP = 32
SUB_UNITS = 4
ORDERS = ((0, 1), (2, 1))
SENT_TYPES = (jnp.bfloat16, jnp.bfloat16, jnp.float32)
EXACT = 16
AXES = ("frames", "tokens")


def lane_ids(rows):
    return lax.broadcasted_iota(jnp.int32, (rows, 128), 1)


def log2_add(a, b):
    return jnp.maximum(a, b) + jnp.log2(1.0 + jnp.exp2(-jnp.abs(a - b)))


def both_ways(blank_ref, label_ref, units, steps, ahead, behind, keep=None):
    def one_step(i, state):
        ahead, behind = state
        back = steps - 1 - i
        here = pl.ds(pl.multiple_of(i * units, 8), units)
        there = pl.ds(pl.multiple_of(back * units, 8), units)
        if keep is not None:
            keep[0][here, :] = ahead
            keep[1][there, :] = behind
        from_left = pltpu.roll(ahead + label_ref[here, :], 1, 0)
        to_right = pltpu.roll(behind, units - 1, 0) + label_ref[there, :]
        ahead = log2_add(ahead + blank_ref[here, :], from_left)
        behind = log2_add(behind + blank_ref[there, :], to_right)
        return ahead, behind

    return lax.fori_loop(0, steps, one_step, (ahead, behind))


def in_two_stages(count, first, second, even, odd, between=None):
    def two_blocks(n, _):
        first(2 * n + 1, odd)
        second(2 * n, even)
        first(2 * n + 2, even)
        second(2 * n + 1, odd)
        return 0

    @pl.when(count > 0)
    def _():
        first(0, even)

    if between is not None:
        between()

    @pl.when(count > 0)
    def _():
        lax.fori_loop(0, (count - 1) // 2, two_blocks, 0)

        @pl.when(count % 2 == 1)
        def _():
            second(count - 1, even)

        @pl.when(count % 2 == 0)
        def _():
            first(count - 1, odd)
            second(count - 2, even)
            second(count - 1, odd)


def packet_kernel(predictor_hbm, packets_ref, predictor_ref, packet_ref, sem):
    load = pltpu.make_async_copy(predictor_hbm, predictor_ref, sem)
    load.start()
    load.wait()
    rows, width = predictor_ref.shape
    for v in range(width // 128):
        packet_ref[v * rows : (v + 1) * rows, :] = predictor_ref[
            :, v * 128 : (v + 1) * 128
        ].astype(F32)
    packet = packet_ref[...].astype(BF16)
    for d in range(packets_ref.shape[0]):
        packets_ref[d] = packet


def unpack_rows(packet, rows_ref, place):
    blocks = rows_ref.shape[1] // 128
    count = packet.shape[0] // blocks
    packet = packet.astype(F32)
    for v in range(blocks):
        rows_ref[place : place + count, v * 128 : (v + 1) * 128] = packet[
            v * count : (v + 1) * count
        ]


def table_kernel(places, seqs_here, offset_ref, *refs):
    *label_refs, table_ref = refs
    first_seq = first_of(seqs_here, offset_ref)
    shard_units = label_refs[0].shape[2]
    units = shard_units * len(places)
    lanes = lane_ids(1)
    table = jnp.zeros((1, 128), F32)
    received = [(ref, n) for ref in label_refs for n in range(ref.shape[0])]
    for place, (ref, n) in zip(places, received):
        shard = lax.axis_index("tokens") ^ place
        for s in range(2):
            row = ref[n, pl.ds(first_seq + s, 1), :].astype(F32)
            row = jnp.concatenate([row, jnp.zeros((1, 128 - shard_units), F32)], axis=1)
            start = s * units + shard * shard_units
            table = jnp.where(
                (lanes >= start) & (lanes < start + shard_units), pltpu.roll(row, start, 1), table
            )
    table_ref[...] = table.astype(jnp.int32)


def load_kernel(*refs):
    count = (len(refs) - 2) // 2
    *loaded_refs, frame_ref, sems = refs[count:]
    loads = [
        pltpu.make_async_copy(source, target, sems.at[n])
        for n, (source, target) in enumerate(zip(refs[:count], loaded_refs))
    ]
    for load in loads:
        load.start()
    for load in loads:
        load.wait()
    encoder_ref, weight_ref, bias_ref = loaded_refs[:3]
    frame_ref[...] = (
        (
            jnp.dot(
                encoder_ref[...].reshape(-1, encoder_ref.shape[-1]),
                weight_ref[...],
                preferred_element_type=F32,
            )
            + bias_ref[...]
        )
        .astype(BF16)
        .astype(F32)
        .reshape(frame_ref.shape)
    )


def entry(row_ref, place):
    row = row_ref[...].astype(F32)
    ids = lax.broadcasted_iota(jnp.int32, row.shape, 1)
    return jnp.sum(jnp.where(ids == place, row, 0.0), axis=1, keepdims=True)


def whole_number(row_ref, place):
    return entry(row_ref, place).astype(jnp.int32)[0, 0]


def first_of(seqs_here, offset_ref):
    first_seq = lax.axis_index("tokens") * seqs_here
    return first_seq if offset_ref is None else first_seq + whole_number(offset_ref, 0)


def block_counts(lens_ref, tokens_ref, first_seq, first_frame):
    counts = []
    for s in range(2):
        inside = first_frame < whole_number(lens_ref, first_seq + s)
        units = whole_number(tokens_ref, first_seq + s)
        counts.append(jnp.where(inside, units // SUB_UNITS + 1, 0))
    return counts


def score_kernel(
    seqs_here,
    offset_ref,
    packets_ref,
    lens_ref,
    tokens_ref,
    frame_ref,
    predictor_weight_ref,
    predictor_bias_ref,
    weight_ref,
    bias_ref,
    label_table_ref,
    softmax_ref,
    token_ref,
    blank_ref,
    label_ref,
    hidden_ref,
    inverse_ref,
    parts_ref,
    matrix_ref,
    even_ref,
    odd_ref,
    labels_smem,
    label_sem,
):
    label_copy = pltpu.make_async_copy(label_table_ref, labels_smem, label_sem)
    label_copy.start()
    seqs, frame_count, width = frame_ref.shape
    units = token_ref.shape[0] // seqs
    shards = lax.axis_size("tokens")
    shard_units = units // shards
    part = frame_count // 2
    steps = part + units - 1
    first_frame = lax.axis_index("frames") * frame_count
    first_seq = first_of(seqs_here, offset_ref)
    vocab = weight_ref.shape[1]
    blank_ref[...] = jnp.zeros_like(blank_ref)
    label_ref[...] = jnp.full(label_ref.shape, NEG, F32)
    for s in range(seqs):
        for k in range(shards):
            packet = packets_ref[(first_seq + s) * shards + k]
            unpack_rows(packet, token_ref, s * units + k * shard_units)
    token_ref[...] = (
        jnp.dot(token_ref[...].astype(BF16), predictor_weight_ref[...], preferred_element_type=F32)
        + predictor_bias_ref[...]
    ).astype(BF16).astype(F32)

    counts = block_counts(lens_ref, tokens_ref, first_seq, first_frame)
    blocks = counts[0] + counts[1]
    lens = [whole_number(lens_ref, first_seq + s) for s in range(2)]
    last_units = [whole_number(tokens_ref, first_seq + s) for s in range(2)]
    lanes = lane_ids(frame_count)
    part_lanes = lane_ids(part)
    times = first_frame + lax.broadcasted_iota(jnp.int32, (frame_count, 1), 0)

    def place_of(i):
        seq = jnp.where(i >= counts[0], 1, 0)
        sub = i - seq * counts[0]
        return seq, sub, seq * (units // SUB_UNITS) + sub

    def multiply(i, logits_ref):
        seq, sub, block = place_of(i)
        frames = frame_ref[seq]
        hidden = jnp.concatenate(
            [
                jnp.tanh(frames + token_ref[pl.ds(seq * units + sub * SUB_UNITS + j, 1), :])
                for j in range(SUB_UNITS)
            ],
            axis=0,
        )
        hidden_ref[block] = hidden
        low = hidden.astype(BF16)
        logits_ref[...] = (
            jnp.dot(low, weight_ref[...], preferred_element_type=F32) + bias_ref[...]
        )

    def score(i, logits_ref):
        seq, sub, block = place_of(i)
        first_unit = sub * SUB_UNITS
        seq_len = jnp.where(seq == 0, lens[0], lens[1])
        last_unit = jnp.where(seq == 0, last_units[0], last_units[1])
        own_lanes = (part_lanes // GROUP) % 2 == seq
        logits = logits_ref[...]
        top = jnp.max(logits, axis=1, keepdims=True)
        weights = jnp.exp(logits - top)
        total = jnp.sum(weights, axis=1, keepdims=True)
        softmax_ref[block] = weights
        inverse_ref[block] = jnp.broadcast_to(1.0 / total, (weights.shape[0], 128))
        log_total = top + jnp.log(total)
        blanks = (logits[:, :1] - log_total) * LOG2E
        for j in range(SUB_UNITS):
            unit = first_unit + j
            rows = slice(j * frame_count, (j + 1) * frame_count)
            label = labels_smem[0, seq * units + unit]
            tile = logits_ref[rows, pl.ds(pl.multiple_of(label // 128 * 128, 128), 128)]
            picked = jnp.sum(
                jnp.where(lanes == label % 128, tile, 0.0), axis=1, keepdims=True
            )
            blank = blanks[rows]
            blank = jnp.where((times == seq_len - 1) & (unit < last_unit), NEG, blank)
            blank = jnp.where((times >= seq_len) | (unit > last_unit), 0.0, blank)
            step = jnp.where(
                (times >= seq_len) | (unit >= last_unit),
                NEG,
                (picked - log_total[rows]) * LOG2E,
            )
            at = (pl.ds(unit * (units + 1), part, stride=units), slice(None))
            blank = jnp.where(part_lanes < 64, blank[:part], blank[part:])
            step = jnp.where(part_lanes < 64, step[:part], step[part:])
            blank_ref[at] = jnp.where(own_lanes, blank, blank_ref[at])
            label_ref[at] = jnp.where(own_lanes, step, label_ref[at])

    in_two_stages(blocks, multiply, score, even_ref, odd_ref, label_copy.wait)
    eye = jnp.where(
        lane_ids(units) % GROUP == lax.broadcasted_iota(jnp.int32, (units, 128), 0), 0.0, NEG
    ).astype(F32)
    ahead, behind = both_ways(blank_ref, label_ref, units, steps, eye, eye)
    lanes = lane_ids(units)
    early = lanes < 64
    columns = jnp.where(early, behind, ahead)
    parts_ref[...] = columns
    others = pltpu.roll(jnp.where(early, ahead, behind), 64, 1)
    ways = [
        jnp.take_along_axis(
            columns, lanes // GROUP * GROUP + k, axis=1, mode="promise_in_bounds"
        )
        + others[k : k + 1, :]
        for k in range(units)
    ]
    top = functools.reduce(jnp.maximum, ways)
    total = functools.reduce(jnp.add, [jnp.exp2(way - top) for way in ways])
    matrix_ref[0, 0] = top + jnp.log2(total)


def turn_kernel(layout, offset_ref, lens_ref, tokens_ref, hidden_ref, turned_ref):
    width = hidden_ref.shape[2]
    first_frame = lax.axis_index("frames") * layout["frame_count"]
    first_seq = first_of(layout["seqs_here"], offset_ref)
    counts = block_counts(lens_ref, tokens_ref, first_seq, first_frame)

    def one_block(i, _):
        seq = jnp.where(i >= counts[0], 1, 0)
        block = i + seq * (layout["units"] // SUB_UNITS - counts[0])
        turned_ref[block, :width, :] = hidden_ref[block].astype(BF16).T
        turned_ref[block, width:, :] = jnp.ones((16, turned_ref.shape[2]), BF16)
        return 0

    lax.fori_loop(0, counts[0] + counts[1], one_block, 0)


def tangent_kernel(
    layout,
    offset_ref,
    lens_ref,
    tokens_ref,
    scale_ref,
    softmax_ref,
    label_table_ref,
    blank_ref,
    label_ref,
    turned_ref,
    inverse_ref,
    parts_ref,
    *refs,
):
    hops = layout["hops"]
    matrix_refs, refs = refs[: hops + 1], refs[hops + 1 :]
    (
        tangents_ref,
        output_bias_ref,
        loss_ref,
        *kept_refs,
        sums_ref,
        matrices_ref,
        ahead_ref,
        behind_ref,
        blank_part_ref,
        label_part_ref,
        even_ref,
        odd_ref,
        labels_smem,
        label_sem,
        sems,
    ) = refs
    label_copy = pltpu.make_async_copy(label_table_ref, labels_smem, label_sem)
    label_copy.start()
    frame_count = layout["frame_count"]
    width = turned_ref.shape[1] - 16
    units = layout["units"]
    part = frame_count // 2
    steps = part + units - 1
    here = lax.axis_index("frames")
    first_frame = here * frame_count
    first_seq = first_of(layout["seqs_here"], offset_ref)
    chunks = matrices_ref.shape[0]
    vocab = softmax_ref.shape[2]
    received = [(ref, n) for ref in matrix_refs for n in range(ref.shape[0])]
    for place, (matrix_ref, n) in zip(layout["matrix_places"], received):
        matrices_ref[place] = matrix_ref[n, 0]
    starts = lax.broadcasted_iota(jnp.int32, (units, 128), 0)
    lanes = lane_ids(units)
    early = lanes < 64
    gather_ids = lanes // GROUP * GROUP + starts
    own_first = (lane_ids(1) // GROUP) % 2 == 0

    def through(column, matrix):
        ways = column + matrix
        top = jnp.max(ways, axis=0, keepdims=True)
        row = top + jnp.log2(jnp.sum(jnp.exp2(ways - top), axis=0, keepdims=True))
        row = jnp.broadcast_to(row, (units, 128))
        return jnp.take_along_axis(row, gather_ids, axis=1, mode="promise_in_bounds")

    def one_chunk(i, carry):
        column, kept = carry
        other = chunks - 1 - i
        kept = jnp.where(jnp.where(early, i, other) == here, column, kept)
        matrix = jnp.where(early, matrices_ref[here ^ i], matrices_ref[here ^ other])
        return through(column, matrix), kept

    start = jnp.where(early & (starts > 0), NEG, 0.0).astype(F32)
    last, kept = lax.fori_loop(0, chunks, one_chunk, (start, start))
    middle = pltpu.roll(through(kept, parts_ref[...]), 64, 1)
    both_ways(
        blank_ref,
        label_ref,
        units,
        steps,
        jnp.where(early, kept, middle),
        jnp.where(early, middle, kept),
        (ahead_ref, behind_ref),
    )
    log_norm = jnp.max(jnp.where(early, last, pltpu.roll(last, 64, 1)), axis=0, keepdims=True)
    scale, length, bound = (
        jnp.where(own_first, entry(ref, first_seq), entry(ref, first_seq + 1))
        for ref in (scale_ref, lens_ref, tokens_ref)
    )
    length, bound = length.astype(jnp.int32), bound.astype(jnp.int32)
    part_start = first_frame + jnp.where(lane_ids(1) < 64, 0, part)
    last_diagonal = starts + jnp.minimum(length - part_start, part)
    first_blank = jnp.where(starts <= bound, starts, steps)
    first_label = jnp.where(starts < bound, starts, steps)
    norm = log_norm - jnp.log2(scale)

    def one_diagonal(e, _):
        rows = pl.ds(pl.multiple_of(e * units, 8), units)
        behind = behind_ref[rows, :]
        base = ahead_ref[rows, :] - norm
        before_end = last_diagonal > e
        blank_part_ref[rows, :] = jnp.where(
            before_end & (first_blank <= e), jnp.exp2(base + blank_ref[rows, :] + behind), 0.0
        )
        label_part_ref[rows, :] = jnp.where(
            before_end & (first_label <= e),
            jnp.exp2(base + label_ref[rows, :] + pltpu.roll(behind, units - 1, 0)),
            0.0,
        )
        return 0

    lax.fori_loop(0, steps, one_diagonal, 0, unroll=5)

    counts = block_counts(lens_ref, tokens_ref, first_seq, first_frame)
    block_lanes = lane_ids(frame_count)
    part_lanes = lane_ids(part)

    def place_of(i):
        seq = jnp.where(i >= counts[0], 1, 0)
        sub = i - seq * counts[0]
        return seq, sub, seq * (units // SUB_UNITS) + sub

    wide = lane_ids(1)
    loss = jnp.where(here == 0, -log_norm * LN2, 0.0)
    spread = jnp.where(wide == first_seq, loss[:, :1], 0.0)
    loss_ref[...] = spread + jnp.where(wide == first_seq + 1, loss[:, GROUP : GROUP + 1], 0.0)
    label_copy.wait()

    counts_all = counts[0] + counts[1]
    sums_ref[...] = jnp.zeros_like(sums_ref)
    output_bias_ref[...] = jnp.zeros_like(output_bias_ref)

    def prepare(i, tangent_ref):
        seq, sub, block = place_of(i)
        own_lanes = [part_lanes % GROUP + GROUP * (seq + 2 * half) for half in (0, 1)]
        for j in range(SUB_UNITS):
            unit = sub * SUB_UNITS + j
            rows = slice(j * frame_count, (j + 1) * frame_count)
            at = (pl.ds(unit * (units + 1), part, stride=units), slice(None))
            blank, step = (
                jnp.concatenate(
                    [
                        jnp.take_along_axis(ref[at], ids, axis=1, mode="promise_in_bounds")
                        for ids in own_lanes
                    ],
                    axis=0,
                )
                for ref in (blank_part_ref, label_part_ref)
            )
            both = (blank + step) * inverse_ref[block, rows, :]
            for v in range(vocab // 128):
                cut = slice(v * 128, (v + 1) * 128)
                piece = softmax_ref[block, rows, cut] * both
                if v == 0:
                    piece = piece - jnp.where(block_lanes == 0, blank, 0.0)
                piece = piece.astype(BF16)
                tangent_ref[rows, cut] = piece
                tangents_ref[block, rows, cut] = piece
            label = labels_smem[0, seq * units + unit]
            cut = pl.ds(pl.multiple_of(label // 128 * 128, 128), 128)
            piece = softmax_ref[block, rows, cut] * both
            piece = piece - jnp.where((block_lanes == 0) & (label < 128), blank, 0.0)
            piece = (piece - jnp.where(block_lanes == label % 128, step, 0.0)).astype(BF16)
            tangent_ref[rows, cut] = piece
            tangents_ref[block, rows, cut] = piece

    def multiply(i, tangent_ref):
        _, _, block = place_of(i)
        product = jnp.dot(turned_ref[block], tangent_ref[...], preferred_element_type=F32)
        for v in range(vocab // 128):
            sums_ref[v * width : (v + 1) * width, :] += product[:width, v * 128 : (v + 1) * 128]
        output_bias_ref[...] += product[width : width + 1, :]

    in_two_stages(counts_all, prepare, multiply, even_ref, odd_ref)
    part_halves(sums_ref, kept_refs, sems)


def part_halves(sums_ref, piece_refs, sems):
    place = lax.axis_index("tokens") & 1
    copies, start = [], 0
    for kept_ref, sent_ref in zip(piece_refs[::2], piece_refs[1::2]):
        half = kept_ref.shape[0]
        for part, target in ((1 - place, sent_ref.at[:half, :]), (place, kept_ref)):
            source = sums_ref.at[pl.ds(pl.multiple_of(start + part * half, 8), half), :]
            copies.append(pltpu.make_async_copy(source, target, sems.at[len(copies)]))
        start += 2 * half
    for copy in copies:
        copy.start()
    for copy in copies:
        copy.wait()


def inner_kernel(
    layout,
    offset_ref,
    lens_ref,
    tokens_ref,
    tangents_ref,
    hidden_ref,
    weight_ref,
    encoder_ref,
    output_bias_ref,
    loss_ref,
    frame_tangent_ref,
    exact_ref,
    kept_ref,
    sent_ref,
    sums_ref,
    frame_sum_ref,
    token_sum_ref,
    even_ref,
    odd_ref,
    sems,
):
    seqs, frame_count, width = encoder_ref.shape
    units = token_sum_ref.shape[0] // seqs
    vocab = weight_ref.shape[1]
    first_frame = lax.axis_index("frames") * frame_count
    first_seq = first_of(layout["seqs_here"], offset_ref)
    frame_sum_ref[...] = jnp.zeros_like(frame_sum_ref)
    token_sum_ref[...] = jnp.zeros_like(token_sum_ref)
    half = layout["half"]
    for side in (0, 1):
        unset = slice(side * half + layout["token"], (side + 1) * half)
        sums_ref[unset, :] = jnp.zeros_like(sums_ref[unset, :])
    counts = block_counts(lens_ref, tokens_ref, first_seq, first_frame)

    def place_of(i):
        seq = jnp.where(i >= counts[0], 1, 0)
        sub = i - seq * counts[0]
        return seq, sub, seq * (units // SUB_UNITS) + sub

    def product_of(tangents):
        return lax.dot_general(
            tangents, weight_ref[...], (((1,), (1,)), ((), ())), preferred_element_type=F32
        )

    def add_up(i, product):
        seq, sub, block = place_of(i)
        hidden = hidden_ref[block]
        inner = product * (1.0 - hidden * hidden)
        total = frame_sum_ref[seq]
        for j in range(SUB_UNITS):
            rows = slice(j * frame_count, (j + 1) * frame_count)
            total = total + inner[rows]
            token_sum_ref[pl.ds(seq * units + sub * SUB_UNITS + j, 1), :] = jnp.sum(
                inner[rows], axis=0, keepdims=True
            )
        frame_sum_ref[seq] = total

    def multiply_two(n, product_ref):
        both = [tangents_ref[place_of(2 * n + m)[2]] for m in (0, 1)]
        product_ref[...] = product_of(jnp.concatenate(both, axis=0))

    def add_up_two(n, product_ref):
        half = product_ref.shape[0] // 2
        add_up(2 * n, product_ref[:half])
        add_up(2 * n + 1, product_ref[half:])

    blocks = counts[0] + counts[1]
    in_two_stages(blocks // 2, multiply_two, add_up_two, even_ref, odd_ref)

    @pl.when(blocks % 2 == 1)
    def _():
        add_up(blocks - 1, product_of(tangents_ref[place_of(blocks - 1)[2]]))

    low = frame_sum_ref[...].reshape(seqs * frame_count, width).astype(BF16)
    frame_tangent_ref[...] = low
    product = lax.dot_general(
        encoder_ref[...].reshape(seqs * frame_count, width),
        low,
        (((0,), (0,)), ((), ())),
        preferred_element_type=F32,
    )
    encoder_bias = jnp.sum(low.astype(F32), axis=0, keepdims=True)
    blocks_each = width // 128 // 2
    exact_ref[...] = jnp.zeros_like(exact_ref)
    for v in range(width // 128):
        cut = slice(v * 128, (v + 1) * 128)
        start, n = v // blocks_each * half, v % blocks_each
        sums_ref[start + n * width : start + (n + 1) * width, :] = product[:, cut]
        at = start + layout["token"] + n * layout["token_rows"] + first_seq * units
        sums_ref[pl.ds(pl.multiple_of(at, 8), seqs * units), :] = token_sum_ref[:, cut]
        at = vocab // 128 + v
        exact_ref[at : at + 1, :] = encoder_bias[:, cut]
    for v in range(vocab // 128):
        exact_ref[v : v + 1, :] = output_bias_ref[:, v * 128 : (v + 1) * 128]
    at = vocab // 128 + width // 128
    exact_ref[at : at + 1, :] = loss_ref[...]
    part_halves(sums_ref, (kept_ref, sent_ref), sems)
    write_exact(sent_ref, kept_ref.shape[0], exact_ref[...])


def encoder_kernel(frame_tangent_ref, encoder_weight_ref, encoder_gradient_ref):
    encoder_gradient_ref[...] = lax.dot_general(
        frame_tangent_ref[...],
        encoder_weight_ref[...],
        (((1,), (1,)), ((), ())),
        preferred_element_type=F32,
    ).reshape(encoder_gradient_ref.shape)


def two_halves(stage, half):
    upper = upper_of(stage)
    own = pl.ds(pl.multiple_of(jnp.where(upper != 0, half, 0), 16), half)
    other = pl.ds(pl.multiple_of(jnp.where(upper != 0, 0, half), 16), half)
    return own, other


def exact_rows(kind):
    return EXACT if kind == F32 else 3 * EXACT


def write_exact(sent_ref, at, values):
    if sent_ref.dtype == F32:
        sent_ref[at : at + EXACT, :] = values
        return
    for n in range(3):
        part = values.astype(BF16)
        sent_ref[at + n * EXACT : at + (n + 1) * EXACT, :] = part
        values = values - part.astype(F32)


def read_exact(received_ref, at):
    parts = [
        received_ref[at + n * EXACT : at + (n + 1) * EXACT, :].astype(F32)
        for n in range(exact_rows(received_ref.dtype) // EXACT)
    ]
    return sum(parts[1:], parts[0])


def halve_kernel(stages, merge, has_exact, *refs):
    count, at = len(stages), 0
    outs = refs[2 * count + has_exact :]
    for n, stage in enumerate(stages):
        kept_ref, received_ref = refs[2 * n : 2 * n + 2]
        half = kept_ref.shape[0] // 2
        own, other = two_halves(stage, half)
        if merge:
            next_ref, sent_ref = (ref.at[at : at + half, :] for ref in outs[:2])
            at += half
        else:
            next_ref, sent_ref = outs[2 * n : 2 * n + 2]
        sent = kept_ref[other, :] + received_ref[other, :].astype(F32)
        sent_ref[:half, :] = sent.astype(sent_ref.dtype)
        next_ref[...] = kept_ref[own, :] + received_ref[own, :].astype(F32)
    if has_exact:
        exact = refs[2 * count][...] + read_exact(received_ref, kept_ref.shape[0])
        outs[-1][...] = exact
        write_exact(outs[-2], outs[-3].shape[0], exact)


def add_kernel(count, *refs):
    sum_ref, exact_sum_ref = refs[2 * count + 1 :]
    at = 0
    for n in range(count):
        kept_ref, received_ref = refs[2 * n : 2 * n + 2]
        rows = kept_ref.shape[0]
        total = kept_ref[...] + received_ref[:rows, :].astype(F32)
        high = total.astype(BF16)
        sum_ref[at : at + rows, :] = high
        at += rows
    sum_ref[at : at + rows, :] = (total - high.astype(F32)).astype(BF16)
    exact = refs[2 * count][...] + read_exact(received_ref, rows)
    exact_sum_ref[...] = exact
    write_exact(sum_ref, at + rows, exact)


def last_kernel(own_ref, other_ref, exact_ref, beside_ref, *sum_refs):
    *sum_refs, exact_sum_ref = sum_refs
    at = 0
    for n, sum_ref in enumerate(sum_refs):
        rows = sum_ref.shape[0]
        totals = []
        for ref in (own_ref, other_ref):
            total = ref[at : at + rows, :].astype(F32)
            if n == len(sum_refs) - 1:
                total = total + ref[at + rows : at + 2 * rows, :].astype(F32)
            totals.append(total)
        sum_ref[...] = (totals[0] + totals[1]).astype(BF16)
        at += rows
    exact_sum_ref[...] = exact_ref[...] + read_exact(other_ref, at + rows)


def join_kernel(stages, merged, *refs):
    count, at = len(stages), 0
    joined_refs = refs[2:] if merged else refs[2 * count :]
    for n, (stage, joined_ref) in enumerate(zip(stages, joined_refs)):
        half = joined_ref.shape[0] // 2
        own, other = two_halves(stage, half)
        if merged:
            own_ref, other_ref = (ref.at[at : at + half, :] for ref in refs[:2])
            at += half
        else:
            own_ref, other_ref = refs[2 * n : 2 * n + 2]
        joined_ref[own, :] = own_ref[...]
        joined_ref[other, :] = other_ref[...]


def copy_out(output_ref, rest_ref, side, output_hbm, encoder_hbm, output_buffer, encoder_buffer, sems):
    copies = []
    for source, buffer, target in (
        (output_ref, output_buffer, output_hbm),
        (rest_ref, encoder_buffer, encoder_hbm),
    ):
        rows, columns = buffer.shape
        for v in range(columns // 128):
            buffer[:, v * 128 : (v + 1) * 128] = source[v * rows : (v + 1) * rows, :].astype(F32)
        start = pl.multiple_of(side * columns, 128)
        copy = pltpu.make_async_copy(
            buffer, target.at[:, pl.ds(start, columns)], sems.at[len(copies)]
        )
        copy.start()
        copies.append(copy)
    return copies


def finish_own_kernel(output_ref, rest_ref, output_hbm, encoder_hbm, *scratch):
    place = lax.axis_index("tokens") & 1
    for copy in copy_out(output_ref, rest_ref, place, output_hbm, encoder_hbm, *scratch):
        copy.wait()


def finish_kernel(
    layout,
    output_other_ref,
    rest_own_ref,
    rest_other_ref,
    packets_ref,
    predictor_weight_ref,
    exact_ref,
    output_weight_begun,
    encoder_weight_begun,
    output_weight_hbm,
    encoder_weight_hbm,
    weight_gradient_hbm,
    output_bias_ref,
    encoder_bias_ref,
    bias_gradient_ref,
    predictor_gradient_ref,
    losses_ref,
    output_buffer,
    encoder_buffer,
    weight_gradient_ref,
    tokens_ref,
    predictor_ref,
    sems,
    gradient_sem,
):
    width, vocab = encoder_buffer.shape[0], output_bias_ref.shape[1]
    place = lax.axis_index("tokens") & 1
    copies = copy_out(
        output_other_ref,
        rest_other_ref,
        1 - place,
        output_weight_hbm,
        encoder_weight_hbm,
        output_buffer,
        encoder_buffer,
        sems,
    )
    count = layout["token_rows"]
    blocks_each = width // 128 // 2

    def gather_tokens(*halves):
        for v in range(width // 128):
            at = layout["token"] + v % blocks_each * count
            tokens_ref[:, v * 128 : (v + 1) * 128] = halves[v // blocks_each][
                at : at + count, :
            ].astype(F32)

    pl.when(place == 0)(lambda: gather_tokens(rest_own_ref, rest_other_ref))
    pl.when(place == 1)(lambda: gather_tokens(rest_other_ref, rest_own_ref))
    tokens = tokens_ref[...]
    held_rows = packets_ref.shape[1] // (width // 128)
    for d in range(packets_ref.shape[0]):
        unpack_rows(packets_ref[d], predictor_ref, d * held_rows)
    weight_gradient_ref[...] = lax.dot_general(
        predictor_ref[...].astype(BF16),
        tokens.astype(BF16),
        (((0,), (0,)), ((), ())),
        preferred_element_type=F32,
    )
    gradient_copy = pltpu.make_async_copy(weight_gradient_ref, weight_gradient_hbm, gradient_sem)
    gradient_copy.start()

    def row(n):
        return exact_ref[n : n + 1, :]

    output_bias_ref[...] = jnp.concatenate([row(v) for v in range(vocab // 128)], axis=1)
    encoder_bias_ref[...] = jnp.concatenate(
        [row(vocab // 128 + v) for v in range(width // 128)], axis=1
    )
    bias_gradient_ref[...] = jnp.sum(tokens, axis=0, keepdims=True)
    device = lax.axis_index("frames") * lax.axis_size("tokens") + lax.axis_index("tokens")
    mine = jnp.concatenate(
        [tokens_ref[pl.ds(device * held_rows + r, 1), :] for r in range(held_rows)], axis=0
    )
    predictor_gradient_ref[:, 0, :] = lax.dot_general(
        mine.astype(BF16),
        predictor_weight_ref[...],
        (((1,), (1,)), ((), ())),
        preferred_element_type=F32,
    )
    loss = row(vocab // 128 + width // 128)
    losses_ref[...] = jnp.sum(
        jnp.where(lane_ids(1) == lax.axis_index("frames"), loss, 0.0), axis=1, keepdims=True
    )
    for copy in copies:
        copy.wait()
    gradient_copy.wait()


def in_hbm(array):
    return pltpu.with_memory_space_constraint(array, pltpu.HBM)


def in_vmem(array):
    return pltpu.with_memory_space_constraint(array, pltpu.VMEM)


def permuted(array, partner):
    frames, tokens = lax.axis_size("frames"), lax.axis_size("tokens")
    pairs = []
    for f in range(frames):
        for k in range(tokens):
            g, h = partner(f, k)
            pairs.append((f * tokens + k, g * tokens + h))
    return lax.ppermute(array, AXES, pairs)


def doubled(array, axis):
    blocks, places = [array], [[0]]
    bit = lax.axis_size(axis) // 2
    while bit:
        joined = jnp.concatenate(blocks, axis=0) if len(blocks) > 1 else blocks[0]
        flip = ((bit, 0), (bit, 0)) if axis == "frames" else ((0, bit), (0, bit))
        blocks.append(permuted(joined, across(flip)))
        places.append([place ^ bit for held in places for place in held])
        bit //= 2
    return blocks, [place for held in places for place in held]


def stages(even, odd):
    frame_bits = [(1 << i, 0) for i in range(lax.axis_size("frames").bit_length() - 1)]
    token_bits = [(0, 1 << i) for i in range(1, lax.axis_size("tokens").bit_length() - 1)]
    first = frame_bits[:1] + token_bits + frame_bits[1:2]
    orders = [first[shift:] + first[:shift] + frame_bits[2:] for shift in (even, odd)]
    return list(zip(*orders))


def upper_of(stage):
    f, k = lax.axis_index("frames"), lax.axis_index("tokens")
    even, odd = ((f & frame_bit) | (k & token_bit) for frame_bit, token_bit in stage)
    return jnp.where((k & 1) == 0, even, odd)


def across(stage):
    return lambda f, k: (f ^ stage[k & 1][0], k ^ stage[k & 1][1])


def neighbour(f, k):
    return f, k ^ 1


def call(body, ins, outs, scratch=(), limit=4):
    vmem = pl.BlockSpec(memory_space=pltpu.VMEM)
    there = [array is not None for array in ins]

    def kernel(*refs):
        given = iter(refs)
        body(*(next(given) if here else None for here in there), *given)

    return pl.pallas_call(
        kernel,
        in_specs=[vmem] * sum(there),
        out_specs=[
            pl.BlockSpec(memory_space=pl.ANY) if inside is None else vmem for _, _, inside in outs
        ],
        out_shape=[
            pltpu.VMEM(shape, kind) if inside else jax.ShapeDtypeStruct(shape, kind)
            for shape, kind, inside in outs
        ],
        scratch_shapes=list(scratch),
        compiler_params=pltpu.CompilerParams(vmem_limit_bytes=limit * 2**20),
    )(*(in_vmem(array) for array in ins if array is not None))


def reduced_and_gathered(pieces, exact, beside):
    plans = list(zip(*(stages(*shifts) for shifts in ORDERS)))
    flat = [a for kept, sent in pieces for a in (kept, permuted(sent, neighbour))]
    way_back = []
    *plans, last_plan = plans
    for number, plan in enumerate(plans):
        plan = plan[: len(flat) // 2]
        merge = len(plan) > 1 and len(set(plan)) == 1
        halves = [kept.shape[0] // 2 for kept in flat[::2]]
        way_back.append((plan, merge, [2 * half for half in halves]))
        if merge:
            halves = [sum(halves)]
        sent_type = SENT_TYPES[min(number, len(SENT_TYPES) - 1)]
        outs = []
        for n, half in enumerate(halves):
            sent_rows = half + (exact_rows(sent_type) if n == len(halves) - 1 else 0)
            outs += [((half, 128), F32, True), ((sent_rows, 128), sent_type, True)]
        exact_out = ((EXACT, 128), F32, True)
        if number < 2:
            given, flat = flat, []
            for n, stage in enumerate(plan):
                last = n == len(plan) - 1
                made = call(
                    functools.partial(halve_kernel, [stage], False, last),
                    given[2 * n : 2 * n + 2] + [exact] * last,
                    outs[2 * n : 2 * n + 2] + [exact_out] * last,
                )
                flat += made[:2]
                if last:
                    exact = made[2]
        else:
            *flat, exact = call(
                functools.partial(halve_kernel, plan, merge, True),
                [*flat, exact],
                [*outs, exact_out],
            )
        flat = [
            permuted(a, across(plan[n // 2])) if n % 2 else a for n, a in enumerate(flat)
        ]
    shapes = [kept.shape for kept in flat[::2]]
    rows = sum(shape[0] for shape in shapes) + shapes[-1][0] + exact_rows(BF16)
    own, exact = call(
        functools.partial(add_kernel, len(shapes)),
        [*flat, exact],
        [((rows, 128), BF16, True), ((EXACT, 128), F32, True)],
    )
    other = permuted(own, across(last_plan[0]))
    vmem = pl.BlockSpec(memory_space=pltpu.VMEM)
    *arrays, exact = pl.pallas_call(
        last_kernel,
        in_specs=[vmem, vmem, vmem, pl.BlockSpec(memory_space=pl.ANY)],
        out_specs=[vmem] * (len(shapes) + 1),
        out_shape=[pltpu.VMEM(shape, BF16) for shape in shapes] + [pltpu.VMEM((EXACT, 128), F32)],
        compiler_params=pltpu.CompilerParams(vmem_limit_bytes=4 * 2**20),
    )(in_vmem(own), in_vmem(other), in_vmem(exact), in_hbm(beside))
    for number, (plan, merged, sizes) in reversed(list(enumerate(way_back))):
        flat = [a for array, stage in zip(arrays, plan) for a in (array, permuted(array, across(stage)))]
        outs = [((size, 128), BF16, True) for size in sizes]
        if number in (0,):
            arrays = [
                call(
                    functools.partial(join_kernel, [stage], False),
                    flat[2 * n : 2 * n + 2],
                    outs[n : n + 1],
                )[0]
                for n, stage in enumerate(plan)
            ]
        else:
            arrays = call(functools.partial(join_kernel, plan, merged), flat, outs)
    return [(array, permuted(array, neighbour)) for array in arrays], exact


def per_device(
    encoder_out,
    encoder_weight,
    encoder_bias,
    predictor_out,
    predictor_weight,
    predictor_bias,
    output_weight,
    output_bias,
    labels,
    frame_lens,
    token_lens,
    loss_scale,
):
    seq_count, frame_count, width = encoder_out.shape
    vocab = output_weight.shape[1]
    all_seqs = labels.shape[0]
    held_seqs, held_units = predictor_out.shape[:2]
    assert held_seqs == 1
    frame_axis, token_axis = lax.axis_size("frames"), lax.axis_size("tokens")
    device_count = frame_axis * token_axis
    units = held_units * token_axis
    calls = seq_count // 2
    diagonals = (frame_count // 2 + units) * units
    vmem = pl.BlockSpec(memory_space=pltpu.VMEM)
    anywhere = pl.BlockSpec(memory_space=pl.ANY)

    weights = (
        encoder_out,
        encoder_weight,
        encoder_bias.reshape(1, width),
        predictor_weight,
        predictor_bias.reshape(1, width),
        output_weight,
        output_bias.reshape(1, vocab),
        frame_lens.reshape(1, all_seqs),
        token_lens.reshape(1, all_seqs),
        loss_scale.reshape(1, all_seqs),
    )
    packet_rows = held_units * width // 128
    packets = pl.pallas_call(
        packet_kernel,
        in_specs=[anywhere],
        out_specs=vmem,
        out_shape=jax.ShapeDtypeStruct((device_count, packet_rows, 128), BF16),
        scratch_shapes=[
            pltpu.VMEM((held_units, width), BF16),
            pltpu.VMEM((packet_rows, 128), F32),
            pltpu.SemaphoreType.DMA,
        ],
        compiler_params=pltpu.CompilerParams(vmem_limit_bytes=4 * 2**20),
    )(in_hbm(predictor_out.reshape(held_units, width)))
    label_blocks, label_places = doubled(labels[None], "tokens")
    *weights, frames = pl.pallas_call(
        load_kernel,
        in_specs=[anywhere] * len(weights),
        out_specs=[vmem] * (1 + len(weights)),
        out_shape=[pltpu.VMEM(w.shape, w.dtype) for w in weights]
        + [pltpu.VMEM(encoder_out.shape, F32)],
        scratch_shapes=[pltpu.SemaphoreType.DMA((len(weights),))],
        compiler_params=pltpu.CompilerParams(vmem_limit_bytes=4 * 2**20),
    )(*map(in_hbm, weights))
    *weights, frame_lens, token_lens, loss_scale = weights
    lens = frame_lens, token_lens
    packets = lax.all_to_all(packets, AXES, 0, 0, tiled=True)

    score_shapes = [
        ((2 * units // SUB_UNITS, SUB_UNITS * frame_count, vocab), F32),
        ((2 * units, width), F32),
        ((diagonals, 128), F32),
        ((diagonals, 128), F32),
        ((2 * units // SUB_UNITS, SUB_UNITS * frame_count, width), F32),
        ((2 * units // SUB_UNITS, SUB_UNITS * frame_count, 128), F32),
        ((units, 128), F32),
        ((1, 1, units, 128), F32),
    ]

    def scores(offset, frames):
        (table,) = call(
            functools.partial(table_kernel, label_places, seq_count),
            (offset, *label_blocks),
            [((1, 128), jnp.int32, True)],
        )
        scored = call(
            functools.partial(score_kernel, seq_count),
            (offset, packets, *lens, frames, *weights[3:], table),
            [(shape, kind, True) for shape, kind in score_shapes],
            scratch=[
                pltpu.VMEM((SUB_UNITS * frame_count, vocab), F32),
                pltpu.VMEM((SUB_UNITS * frame_count, vocab), F32),
                pltpu.SMEM((1, 128), jnp.int32),
                pltpu.SemaphoreType.DMA,
            ],
            limit=8,
        )
        return [table, *scored]

    offsets = 2 * jnp.arange(calls, dtype=jnp.int32).reshape(calls, 1, 1)
    encoders = weights[0].reshape(calls, 2, frame_count, width)
    if calls == 1:
        scored = scores(None, frames)
        matrix = scored[-1]
    else:
        scored = lax.map(
            lambda given: scores(*given),
            (offsets, frames.reshape(calls, 2, frame_count, width)),
        )
        matrix = scored[-1].reshape(1, calls, units, 128)

    matrices, matrix_places = doubled(matrix, "frames")
    layout = {"matrix_places": matrix_places, "seqs_here": seq_count, "frame_count": frame_count, "units": units}
    align = 16 * device_count // 4
    blocks_each = width // 128 // 2
    layout["token"], layout["token_rows"] = blocks_each * width, all_seqs * units
    half = layout["token"] + blocks_each * all_seqs * units
    layout["half"] = half + (-half % align)
    rest_rows = 2 * layout["half"]
    output_rows = vocab // 128 * width
    assert output_rows % (2 * align) == 0 and vocab // 128 + width // 128 < EXACT

    blocks = 2 * units // SUB_UNITS
    block_rows = SUB_UNITS * frame_count

    def turns(offset, scored):
        hidden = scored[5]
        (turned,) = call(
            functools.partial(turn_kernel, layout),
            (offset, *lens, hidden),
            [((hidden.shape[0], width + 16, hidden.shape[1]), BF16, True)],
        )
        return turned

    def tangents(offset, scored, turned, matrices):
        table, softmax, _, blank, label, _, inverse, parts = scored
        return call(
            functools.partial(tangent_kernel, dict(layout, hops=len(matrices) - 1)),
            (
                *(offset, *lens, loss_scale, softmax, table, blank, label),
                *(turned, inverse, parts, *matrices),
            ),
            [
                ((blocks, block_rows, vocab), BF16, True),
                ((1, vocab), F32, True),
                ((1, 128), F32, True),
                ((output_rows // 2, 128), F32, True),
                ((output_rows // 2, 128), F32, True),
            ],
            scratch=[
                pltpu.VMEM((output_rows, 128), F32),
                pltpu.VMEM((frame_axis, units, 128), F32),
                pltpu.VMEM((diagonals, 128), F32),
                pltpu.VMEM((diagonals, 128), F32),
                pltpu.VMEM((diagonals, 128), F32),
                pltpu.VMEM((diagonals, 128), F32),
                pltpu.VMEM((block_rows, vocab), BF16),
                pltpu.VMEM((block_rows, vocab), BF16),
                pltpu.SMEM((1, 128), jnp.int32),
                pltpu.SemaphoreType.DMA,
                pltpu.SemaphoreType.DMA((4,)),
            ],
            limit=12,
        )

    def inners(offset, encoder, scored, tangent, output_bias_sum, loss):
        return call(
            functools.partial(inner_kernel, layout),
            (offset, *lens, tangent, scored[5], weights[5], encoder, output_bias_sum, loss),
            [
                ((2 * frame_count, width), BF16, True),
                ((EXACT, 128), F32, True),
                ((rest_rows // 2, 128), F32, True),
                ((rest_rows // 2 + EXACT, 128), F32, True),
            ],
            scratch=[
                pltpu.VMEM((rest_rows, 128), F32),
                pltpu.VMEM((2, frame_count, width), F32),
                pltpu.VMEM((2 * units, width), F32),
                pltpu.VMEM((2 * block_rows, width), F32),
                pltpu.VMEM((2 * block_rows, width), F32),
                pltpu.SemaphoreType.DMA((2,)),
            ],
            limit=10,
        )

    def encoder_gradient_of(frame_tangent):
        return call(
            encoder_kernel,
            (frame_tangent, weights[1]),
            [((2, frame_count, width), F32, False)],
        )[0]

    if calls == 1:
        scored = scored[:-1]
        turned = turns(None, scored)
        tangent, output_bias_sum, loss, *output_sums = tangents(None, scored, turned, matrices)

        frame_tangent, exact, *rest = inners(
            None, weights[0], scored, tangent, output_bias_sum, loss
        )
        sums = [*output_sums, *rest, exact]
        encoder_gradient = encoder_gradient_of(frame_tangent)
    else:

        def add_call(sums, given):
            offset, encoder, scored, call = given
            own = [lax.dynamic_slice_in_dim(m, call, 1, 1) for m in matrices]
            turned = turns(offset, scored)
            tangent, output_bias_sum, loss, *more = tangents(offset, scored, turned, own)
            frame_tangent, exact, *rest = inners(
                offset, encoder, scored, tangent, output_bias_sum, loss
            )
            sums = [a + b for a, b in zip(sums, [*more, *rest, exact])]
            return sums, encoder_gradient_of(frame_tangent)

        sizes = (output_rows // 2,) * 2 + (rest_rows // 2, rest_rows // 2 + EXACT, EXACT)
        sums, encoder_gradient = lax.scan(
            add_call,
            [jnp.zeros((size, 128), F32) for size in sizes],
            (offsets, encoders, scored[:-1], jnp.arange(calls)),
        )
        encoder_gradient = encoder_gradient.reshape(encoder_out.shape)

    halves, exact = reduced_and_gathered(
        [sums[:2], sums[2:4]], sums[4], encoder_gradient
    )
    (output_own, output_other), (rest_own, rest_other) = halves
    buffers = [
        pltpu.VMEM((width, vocab // 2), F32),
        pltpu.VMEM((width, width // 2), F32),
    ]
    begun = call(
        finish_own_kernel,
        (output_own, rest_own),
        [((width, vocab), F32, None), ((width, width), F32, None)],
        scratch=[*buffers, pltpu.SemaphoreType.DMA((2,))],
        limit=8,
    )
    finished = pl.pallas_call(
        functools.partial(finish_kernel, layout),
        in_specs=[vmem] * 6 + [anywhere] * 2,
        out_specs=[anywhere] * 3 + [vmem] * 5,
        out_shape=[
            jax.ShapeDtypeStruct((width, vocab), F32),
            jax.ShapeDtypeStruct((width, width), F32),
            jax.ShapeDtypeStruct((width, width), F32),
            jax.ShapeDtypeStruct((1, vocab), F32),
            jax.ShapeDtypeStruct((1, width), F32),
            jax.ShapeDtypeStruct((1, width), F32),
            jax.ShapeDtypeStruct((held_units, 1, width), F32),
            jax.ShapeDtypeStruct((1, 1), F32),
        ],
        input_output_aliases={6: 0, 7: 1},
        scratch_shapes=[
            *buffers,
            pltpu.VMEM((width, width), F32),
            pltpu.VMEM((all_seqs * units, width), F32),
            pltpu.VMEM((all_seqs * units, width), F32),
            pltpu.SemaphoreType.DMA((2,)),
            pltpu.SemaphoreType.DMA,
        ],
        compiler_params=pltpu.CompilerParams(vmem_limit_bytes=20 * 2**20),
    )(
        *map(in_vmem, (output_other, rest_own, rest_other, packets, weights[3], exact)),
        *map(in_hbm, begun),
    )
    return (
        finished[7].reshape(1),
        encoder_gradient,
        finished[6].transpose(1, 0, 2),
        finished[1],
        finished[4].reshape(width),
        finished[2],
        finished[5].reshape(width),
        finished[0],
        finished[3].reshape(vocab),
    )


def solution(mesh):
    placed = (
        P("tokens", "frames", None),
        P(),
        P(),
        P("frames", "tokens", None),
        P(),
        P(),
        P(),
        P(),
        P(None, "tokens"),
        P(),
        P(),
        P(),
    )
    return jax.shard_map(
        per_device,
        mesh=mesh,
        in_specs=placed,
        out_specs=(
            P("frames"),
            P("tokens", "frames", None),
            P("frames", "tokens", None),
            P(),
            P(),
            P(),
            P(),
            P(),
            P(),
        ),
        check_vma=False,
    )
```

```python
import functools

import jax
import jax.numpy as jnp
from jax import lax
from jax.experimental import pallas as pl
from jax.experimental.pallas import tpu as pltpu
from jax.sharding import PartitionSpec as P

NEG = -1e30
LOG2E = 1.4426950408889634
LN2 = 0.6931471805599453
BF16 = jnp.bfloat16
F32 = jnp.float32
GROUP = 32
SUB_UNITS = 4
ORDERS = ((0, 1), (2, 1))
SENT_TYPES = (jnp.bfloat16, jnp.bfloat16, jnp.float32)
EXACT = 16
AXES = ("frames", "tokens")


def lane_ids(rows):
    return lax.broadcasted_iota(jnp.int32, (rows, 128), 1)


def log2_add(a, b):
    return jnp.maximum(a, b) + jnp.log2(1.0 + jnp.exp2(-jnp.abs(a - b)))


def both_ways(blank_ref, label_ref, units, steps, ahead, behind, keep):
    def one_step(i, state):
        ahead, behind = state
        back = steps - 1 - i
        here = pl.ds(pl.multiple_of(i * units, 8), units)
        there = pl.ds(pl.multiple_of(back * units, 8), units)
        keep[0][here, :] = ahead
        keep[1][there, :] = behind
        from_left = pltpu.roll(ahead + label_ref[here, :], 1, 0)
        to_right = pltpu.roll(behind, units - 1, 0) + label_ref[there, :]
        ahead = log2_add(ahead + blank_ref[here, :], from_left)
        behind = log2_add(behind + blank_ref[there, :], to_right)
        return ahead, behind

    return lax.fori_loop(0, steps, one_step, (ahead, behind))


def log2_add_three(a, b, c):
    top = jnp.maximum(jnp.maximum(a, b), c)
    return top + jnp.log2(jnp.exp2(a - top) + jnp.exp2(b - top) + jnp.exp2(c - top))


def both_ways_in_pairs(blank_ref, label_ref, units, steps, ahead, behind):
    pairs = -(-steps // 2)

    def rows_of(ref, diagonal):
        return ref[pl.ds(pl.multiple_of(diagonal * units, 8), units), :]

    def up(array, by=1):
        return pltpu.roll(array, by, 0)

    def down(array, by=1):
        return pltpu.roll(array, units - by, 0)

    def scores_of(first):
        return [rows_of(ref, first + n) for ref in (blank_ref, label_ref) for n in (0, 1)]

    def ways_ahead(i):
        blank, blank_next, label, label_next = scores_of(2 * i)
        one = log2_add(up(blank + label_next), up(label) + blank_next)
        return blank + blank_next, one, up(up(label) + label_next)

    def ways_behind(i):
        blank, blank_next, label, label_next = scores_of(2 * (pairs - 1 - i))
        one = log2_add(blank + label_next, label + down(blank_next))
        return blank + blank_next, one, label + down(label_next)

    def one_pair(i, state):
        ahead, behind, (none, one, two), (none_back, one_back, two_back) = state
        following = jnp.minimum(i + 1, pairs - 1)
        ahead = log2_add_three(ahead + none, up(ahead) + one, up(ahead, 2) + two)
        behind = log2_add_three(
            behind + none_back, down(behind) + one_back, down(behind, 2) + two_back
        )
        return ahead, behind, ways_ahead(following), ways_behind(following)

    start = ahead, behind, ways_ahead(0), ways_behind(0)
    return lax.fori_loop(0, pairs, one_pair, start)[:2]


def in_two_stages(count, first, second, even, odd, between=None):
    def two_blocks(n, _):
        first(2 * n + 1, odd)
        second(2 * n, even)
        first(2 * n + 2, even)
        second(2 * n + 1, odd)
        return 0

    @pl.when(count > 0)
    def _():
        first(0, even)

    if between is not None:
        between()

    @pl.when(count > 0)
    def _():
        lax.fori_loop(0, (count - 1) // 2, two_blocks, 0)

        @pl.when(count % 2 == 1)
        def _():
            second(count - 1, even)

        @pl.when(count % 2 == 0)
        def _():
            first(count - 1, odd)
            second(count - 2, even)
            second(count - 1, odd)


def packet_kernel(predictor_hbm, packets_ref, predictor_ref, packet_ref, sem):
    load = pltpu.make_async_copy(predictor_hbm, predictor_ref, sem)
    load.start()
    load.wait()
    rows, width = predictor_ref.shape
    for v in range(width // 128):
        packet_ref[v * rows : (v + 1) * rows, :] = predictor_ref[
            :, v * 128 : (v + 1) * 128
        ].astype(F32)
    packet = packet_ref[...].astype(BF16)
    for d in range(packets_ref.shape[0]):
        packets_ref[d] = packet


def unpack_rows(packet, rows_ref, place):
    blocks = rows_ref.shape[1] // 128
    count = packet.shape[0] // blocks
    packet = packet.astype(F32)
    for v in range(blocks):
        rows_ref[place : place + count, v * 128 : (v + 1) * 128] = packet[
            v * count : (v + 1) * count
        ]


def table_kernel(places, seqs_here, offset_ref, *refs):
    *label_refs, table_ref = refs
    first_seq = first_of(seqs_here, offset_ref)
    shard_units = label_refs[0].shape[2]
    units = shard_units * len(places)
    lanes = lane_ids(1)
    table = jnp.zeros((1, 128), F32)
    received = [(ref, n) for ref in label_refs for n in range(ref.shape[0])]
    for place, (ref, n) in zip(places, received):
        shard = lax.axis_index("tokens") ^ place
        for s in range(2):
            row = ref[n, pl.ds(first_seq + s, 1), :].astype(F32)
            row = jnp.concatenate([row, jnp.zeros((1, 128 - shard_units), F32)], axis=1)
            start = s * units + shard * shard_units
            table = jnp.where(
                (lanes >= start) & (lanes < start + shard_units), pltpu.roll(row, start, 1), table
            )
    table_ref[...] = table.astype(jnp.int32)


def load_kernel(*refs):
    count = (len(refs) - 2) // 2
    *loaded_refs, frame_ref, sems = refs[count:]
    loads = [
        pltpu.make_async_copy(source, target, sems.at[n])
        for n, (source, target) in enumerate(zip(refs[:count], loaded_refs))
    ]
    for load in loads:
        load.start()
    for load in loads:
        load.wait()
    encoder_ref, weight_ref, bias_ref = loaded_refs[:3]
    frame_ref[...] = (
        (
            jnp.dot(
                encoder_ref[...].reshape(-1, encoder_ref.shape[-1]),
                weight_ref[...],
                preferred_element_type=F32,
            )
            + bias_ref[...]
        )
        .astype(BF16)
        .astype(F32)
        .reshape(frame_ref.shape)
    )


def entry(row_ref, place):
    row = row_ref[...].astype(F32)
    ids = lax.broadcasted_iota(jnp.int32, row.shape, 1)
    return jnp.sum(jnp.where(ids == place, row, 0.0), axis=1, keepdims=True)


def whole_number(row_ref, place):
    return entry(row_ref, place).astype(jnp.int32)[0, 0]


def first_of(seqs_here, offset_ref):
    first_seq = lax.axis_index("tokens") * seqs_here
    return first_seq if offset_ref is None else first_seq + whole_number(offset_ref, 0)


def block_counts(lens_ref, tokens_ref, first_seq, first_frame):
    counts = []
    for s in range(2):
        inside = first_frame < whole_number(lens_ref, first_seq + s)
        units = whole_number(tokens_ref, first_seq + s)
        counts.append(jnp.where(inside, units // SUB_UNITS + 1, 0))
    return counts


def score_kernel(
    seqs_here,
    offset_ref,
    packets_ref,
    lens_ref,
    tokens_ref,
    frame_ref,
    predictor_weight_ref,
    predictor_bias_ref,
    weight_ref,
    bias_ref,
    label_table_ref,
    softmax_ref,
    token_ref,
    blank_ref,
    label_ref,
    hidden_ref,
    inverse_ref,
    parts_ref,
    matrix_ref,
    even_ref,
    odd_ref,
    labels_smem,
    label_sem,
):
    label_copy = pltpu.make_async_copy(label_table_ref, labels_smem, label_sem)
    label_copy.start()
    seqs, frame_count, width = frame_ref.shape
    units = token_ref.shape[0] // seqs
    shards = lax.axis_size("tokens")
    shard_units = units // shards
    part = frame_count // 2
    steps = part + units - 1
    first_frame = lax.axis_index("frames") * frame_count
    first_seq = first_of(seqs_here, offset_ref)
    vocab = weight_ref.shape[1]
    blank_ref[...] = jnp.zeros_like(blank_ref)
    label_ref[...] = jnp.full(label_ref.shape, NEG, F32)
    for s in range(seqs):
        for k in range(shards):
            packet = packets_ref[(first_seq + s) * shards + k]
            unpack_rows(packet, token_ref, s * units + k * shard_units)
    token_ref[...] = (
        jnp.dot(token_ref[...].astype(BF16), predictor_weight_ref[...], preferred_element_type=F32)
        + predictor_bias_ref[...]
    ).astype(BF16).astype(F32)

    counts = block_counts(lens_ref, tokens_ref, first_seq, first_frame)
    blocks = counts[0] + counts[1]
    lens = [whole_number(lens_ref, first_seq + s) for s in range(2)]
    last_units = [whole_number(tokens_ref, first_seq + s) for s in range(2)]
    lanes = lane_ids(frame_count)
    part_lanes = lane_ids(part)
    times = first_frame + lax.broadcasted_iota(jnp.int32, (frame_count, 1), 0)

    def place_of(i):
        seq = jnp.where(i >= counts[0], 1, 0)
        sub = i - seq * counts[0]
        return seq, sub, seq * (units // SUB_UNITS) + sub

    def multiply(i, logits_ref):
        seq, sub, block = place_of(i)
        frames = frame_ref[seq]
        hidden = jnp.concatenate(
            [
                jnp.tanh(frames + token_ref[pl.ds(seq * units + sub * SUB_UNITS + j, 1), :])
                for j in range(SUB_UNITS)
            ],
            axis=0,
        )
        hidden_ref[block] = hidden
        low = hidden.astype(BF16)
        logits_ref[...] = (
            jnp.dot(low, weight_ref[...], preferred_element_type=F32) + bias_ref[...]
        )

    def score(i, logits_ref):
        seq, sub, block = place_of(i)
        first_unit = sub * SUB_UNITS
        seq_len = jnp.where(seq == 0, lens[0], lens[1])
        last_unit = jnp.where(seq == 0, last_units[0], last_units[1])
        own_lanes = (part_lanes // GROUP) % 2 == seq
        logits = logits_ref[...]
        top = jnp.max(logits, axis=1, keepdims=True)
        weights = jnp.exp(logits - top)
        total = jnp.sum(weights, axis=1, keepdims=True)
        softmax_ref[block] = weights
        inverse_ref[block] = jnp.broadcast_to(1.0 / total, (weights.shape[0], 128))
        log_total = top + jnp.log(total)
        blanks = (logits[:, :1] - log_total) * LOG2E
        for j in range(SUB_UNITS):
            unit = first_unit + j
            rows = slice(j * frame_count, (j + 1) * frame_count)
            label = labels_smem[0, seq * units + unit]
            tile = logits_ref[rows, pl.ds(pl.multiple_of(label // 128 * 128, 128), 128)]
            picked = jnp.sum(
                jnp.where(lanes == label % 128, tile, 0.0), axis=1, keepdims=True
            )
            blank = blanks[rows]
            blank = jnp.where((times == seq_len - 1) & (unit < last_unit), NEG, blank)
            blank = jnp.where((times >= seq_len) | (unit > last_unit), 0.0, blank)
            step = jnp.where(
                (times >= seq_len) | (unit >= last_unit),
                NEG,
                (picked - log_total[rows]) * LOG2E,
            )
            at = (pl.ds(unit * (units + 1), part, stride=units), slice(None))
            blank = jnp.where(part_lanes < 64, blank[:part], blank[part:])
            step = jnp.where(part_lanes < 64, step[:part], step[part:])
            blank_ref[at] = jnp.where(own_lanes, blank, blank_ref[at])
            label_ref[at] = jnp.where(own_lanes, step, label_ref[at])

    in_two_stages(blocks, multiply, score, even_ref, odd_ref, label_copy.wait)
    eye = jnp.where(
        lane_ids(units) % GROUP == lax.broadcasted_iota(jnp.int32, (units, 128), 0), 0.0, NEG
    ).astype(F32)
    ahead, behind = both_ways_in_pairs(blank_ref, label_ref, units, steps, eye, eye)
    lanes = lane_ids(units)
    early = lanes < 64
    columns = jnp.where(early, behind, ahead)
    parts_ref[...] = columns
    others = pltpu.roll(jnp.where(early, ahead, behind), 64, 1)
    ways = [
        jnp.take_along_axis(
            columns, lanes // GROUP * GROUP + k, axis=1, mode="promise_in_bounds"
        )
        + others[k : k + 1, :]
        for k in range(units)
    ]
    top = functools.reduce(jnp.maximum, ways)
    total = functools.reduce(jnp.add, [jnp.exp2(way - top) for way in ways])
    matrix_ref[0, 0] = top + jnp.log2(total)


def turn_kernel(layout, offset_ref, lens_ref, tokens_ref, hidden_ref, turned_ref):
    width = hidden_ref.shape[2]
    first_frame = lax.axis_index("frames") * layout["frame_count"]
    first_seq = first_of(layout["seqs_here"], offset_ref)
    counts = block_counts(lens_ref, tokens_ref, first_seq, first_frame)

    def one_block(i, _):
        seq = jnp.where(i >= counts[0], 1, 0)
        block = i + seq * (layout["units"] // SUB_UNITS - counts[0])
        turned_ref[block, :width, :] = hidden_ref[block].astype(BF16).T
        turned_ref[block, width:, :] = jnp.ones((16, turned_ref.shape[2]), BF16)
        return 0

    lax.fori_loop(0, counts[0] + counts[1], one_block, 0)


def tangent_kernel(
    layout,
    offset_ref,
    lens_ref,
    tokens_ref,
    scale_ref,
    softmax_ref,
    label_table_ref,
    blank_ref,
    label_ref,
    turned_ref,
    inverse_ref,
    parts_ref,
    *refs,
):
    hops = layout["hops"]
    matrix_refs, refs = refs[: hops + 1], refs[hops + 1 :]
    (
        tangents_ref,
        output_bias_ref,
        loss_ref,
        kept_ref,
        sent_ref,
        sums_ref,
        matrices_ref,
        ahead_ref,
        behind_ref,
        blank_part_ref,
        label_part_ref,
        even_ref,
        odd_ref,
        labels_smem,
        label_sem,
    ) = refs
    label_copy = pltpu.make_async_copy(label_table_ref, labels_smem, label_sem)
    label_copy.start()
    frame_count = layout["frame_count"]
    width = turned_ref.shape[1] - 16
    units = layout["units"]
    part = frame_count // 2
    steps = part + units - 1
    here = lax.axis_index("frames")
    first_frame = here * frame_count
    first_seq = first_of(layout["seqs_here"], offset_ref)
    chunks = matrices_ref.shape[0]
    vocab = softmax_ref.shape[2]
    received = [(ref, n) for ref in matrix_refs for n in range(ref.shape[0])]
    for place, (matrix_ref, n) in zip(layout["matrix_places"], received):
        matrices_ref[place] = matrix_ref[n, 0]
    starts = lax.broadcasted_iota(jnp.int32, (units, 128), 0)
    lanes = lane_ids(units)
    early = lanes < 64
    gather_ids = lanes // GROUP * GROUP + starts
    own_first = (lane_ids(1) // GROUP) % 2 == 0

    def through(column, matrix):
        ways = column + matrix
        top = jnp.max(ways, axis=0, keepdims=True)
        row = top + jnp.log2(jnp.sum(jnp.exp2(ways - top), axis=0, keepdims=True))
        row = jnp.broadcast_to(row, (units, 128))
        return jnp.take_along_axis(row, gather_ids, axis=1, mode="promise_in_bounds")

    def one_chunk(i, carry):
        column, kept = carry
        other = chunks - 1 - i
        kept = jnp.where(jnp.where(early, i, other) == here, column, kept)
        matrix = jnp.where(early, matrices_ref[here ^ i], matrices_ref[here ^ other])
        return through(column, matrix), kept

    start = jnp.where(early & (starts > 0), NEG, 0.0).astype(F32)
    last, kept = lax.fori_loop(0, chunks, one_chunk, (start, start))
    middle = pltpu.roll(through(kept, parts_ref[...]), 64, 1)
    both_ways(
        blank_ref,
        label_ref,
        units,
        steps,
        jnp.where(early, kept, middle),
        jnp.where(early, middle, kept),
        (ahead_ref, behind_ref),
    )
    log_norm = jnp.max(jnp.where(early, last, pltpu.roll(last, 64, 1)), axis=0, keepdims=True)
    scale, length, bound = (
        jnp.where(own_first, entry(ref, first_seq), entry(ref, first_seq + 1))
        for ref in (scale_ref, lens_ref, tokens_ref)
    )
    length, bound = length.astype(jnp.int32), bound.astype(jnp.int32)
    part_start = first_frame + jnp.where(lane_ids(1) < 64, 0, part)
    last_diagonal = starts + jnp.minimum(length - part_start, part)
    first_blank = jnp.where(starts <= bound, starts, steps)
    first_label = jnp.where(starts < bound, starts, steps)
    norm = log_norm - jnp.log2(scale)

    def one_diagonal(e, _):
        rows = pl.ds(pl.multiple_of(e * units, 8), units)
        behind = behind_ref[rows, :]
        base = ahead_ref[rows, :] - norm
        before_end = last_diagonal > e
        blank_part_ref[rows, :] = jnp.where(
            before_end & (first_blank <= e), jnp.exp2(base + blank_ref[rows, :] + behind), 0.0
        )
        label_part_ref[rows, :] = jnp.where(
            before_end & (first_label <= e),
            jnp.exp2(base + label_ref[rows, :] + pltpu.roll(behind, units - 1, 0)),
            0.0,
        )
        return 0

    lax.fori_loop(0, steps, one_diagonal, 0, unroll=5)

    counts = block_counts(lens_ref, tokens_ref, first_seq, first_frame)
    block_lanes = lane_ids(frame_count)
    part_lanes = lane_ids(part)

    def place_of(i):
        seq = jnp.where(i >= counts[0], 1, 0)
        sub = i - seq * counts[0]
        return seq, sub, seq * (units // SUB_UNITS) + sub

    wide = lane_ids(1)
    loss = jnp.where(here == 0, -log_norm * LN2, 0.0)
    spread = jnp.where(wide == first_seq, loss[:, :1], 0.0)
    loss_ref[...] = spread + jnp.where(wide == first_seq + 1, loss[:, GROUP : GROUP + 1], 0.0)
    label_copy.wait()

    counts_all = counts[0] + counts[1]
    sums_ref[...] = jnp.zeros_like(sums_ref)
    output_bias_ref[...] = jnp.zeros_like(output_bias_ref)

    def prepare(i, tangent_ref):
        seq, sub, block = place_of(i)
        own_lanes = [part_lanes % GROUP + GROUP * (seq + 2 * half) for half in (0, 1)]
        for j in range(SUB_UNITS):
            unit = sub * SUB_UNITS + j
            rows = slice(j * frame_count, (j + 1) * frame_count)
            at = (pl.ds(unit * (units + 1), part, stride=units), slice(None))
            blank, step = (
                jnp.concatenate(
                    [
                        jnp.take_along_axis(ref[at], ids, axis=1, mode="promise_in_bounds")
                        for ids in own_lanes
                    ],
                    axis=0,
                )
                for ref in (blank_part_ref, label_part_ref)
            )
            both = (blank + step) * inverse_ref[block, rows, :]
            for v in range(vocab // 128):
                cut = slice(v * 128, (v + 1) * 128)
                piece = softmax_ref[block, rows, cut] * both
                if v == 0:
                    piece = piece - jnp.where(block_lanes == 0, blank, 0.0)
                piece = piece.astype(BF16)
                tangent_ref[rows, cut] = piece
                tangents_ref[block, rows, cut] = piece
            label = labels_smem[0, seq * units + unit]
            cut = pl.ds(pl.multiple_of(label // 128 * 128, 128), 128)
            piece = softmax_ref[block, rows, cut] * both
            piece = piece - jnp.where((block_lanes == 0) & (label < 128), blank, 0.0)
            piece = (piece - jnp.where(block_lanes == label % 128, step, 0.0)).astype(BF16)
            tangent_ref[rows, cut] = piece
            tangents_ref[block, rows, cut] = piece

    def multiply(i, tangent_ref):
        _, _, block = place_of(i)
        product = jnp.dot(turned_ref[block], tangent_ref[...], preferred_element_type=F32)
        for v in range(vocab // 128):
            sums_ref[v * width : (v + 1) * width, :] += product[:width, v * 128 : (v + 1) * 128]
        output_bias_ref[...] += product[width : width + 1, :]

    in_two_stages(counts_all, prepare, multiply, even_ref, odd_ref)
    part_halves(sums_ref, kept_ref, sent_ref)


def part_halves(sums_ref, kept_ref, sent_ref):
    half = kept_ref.shape[0]
    place = lax.axis_index("tokens") & 1
    sent_ref[:half, :] = sums_ref[pl.ds(pl.multiple_of((1 - place) * half, 8), half), :]
    kept_ref[...] = sums_ref[pl.ds(pl.multiple_of(place * half, 8), half), :]


def inner_kernel(
    layout,
    offset_ref,
    lens_ref,
    tokens_ref,
    tangents_ref,
    hidden_ref,
    weight_ref,
    encoder_ref,
    output_bias_ref,
    loss_ref,
    frame_tangent_ref,
    exact_ref,
    kept_ref,
    sent_ref,
    sums_ref,
    frame_sum_ref,
    token_sum_ref,
    even_ref,
    odd_ref,
):
    seqs, frame_count, width = encoder_ref.shape
    units = token_sum_ref.shape[0] // seqs
    vocab = weight_ref.shape[1]
    first_frame = lax.axis_index("frames") * frame_count
    first_seq = first_of(layout["seqs_here"], offset_ref)
    frame_sum_ref[...] = jnp.zeros_like(frame_sum_ref)
    token_sum_ref[...] = jnp.zeros_like(token_sum_ref)
    half = layout["half"]
    for side in (0, 1):
        unset = slice(side * half + layout["token"], (side + 1) * half)
        sums_ref[unset, :] = jnp.zeros_like(sums_ref[unset, :])
    counts = block_counts(lens_ref, tokens_ref, first_seq, first_frame)

    def place_of(i):
        seq = jnp.where(i >= counts[0], 1, 0)
        sub = i - seq * counts[0]
        return seq, sub, seq * (units // SUB_UNITS) + sub

    def product_of(tangents):
        return lax.dot_general(
            tangents, weight_ref[...], (((1,), (1,)), ((), ())), preferred_element_type=F32
        )

    def add_up(i, product):
        seq, sub, block = place_of(i)
        hidden = hidden_ref[block]
        inner = product * (1.0 - hidden * hidden)
        total = frame_sum_ref[seq]
        for j in range(SUB_UNITS):
            rows = slice(j * frame_count, (j + 1) * frame_count)
            total = total + inner[rows]
            token_sum_ref[pl.ds(seq * units + sub * SUB_UNITS + j, 1), :] = jnp.sum(
                inner[rows], axis=0, keepdims=True
            )
        frame_sum_ref[seq] = total

    def multiply_two(n, product_ref):
        both = [tangents_ref[place_of(2 * n + m)[2]] for m in (0, 1)]
        product_ref[...] = product_of(jnp.concatenate(both, axis=0))

    def add_up_two(n, product_ref):
        half = product_ref.shape[0] // 2
        add_up(2 * n, product_ref[:half])
        add_up(2 * n + 1, product_ref[half:])

    blocks = counts[0] + counts[1]
    in_two_stages(blocks // 2, multiply_two, add_up_two, even_ref, odd_ref)

    @pl.when(blocks % 2 == 1)
    def _():
        add_up(blocks - 1, product_of(tangents_ref[place_of(blocks - 1)[2]]))

    low = frame_sum_ref[...].reshape(seqs * frame_count, width).astype(BF16)
    frame_tangent_ref[...] = low
    product = lax.dot_general(
        encoder_ref[...].reshape(seqs * frame_count, width),
        low,
        (((0,), (0,)), ((), ())),
        preferred_element_type=F32,
    )
    encoder_bias = jnp.sum(low.astype(F32), axis=0, keepdims=True)
    blocks_each = width // 128 // 2
    exact_ref[...] = jnp.zeros_like(exact_ref)
    for v in range(width // 128):
        cut = slice(v * 128, (v + 1) * 128)
        start, n = v // blocks_each * half, v % blocks_each
        sums_ref[start + n * width : start + (n + 1) * width, :] = product[:, cut]
        at = start + layout["token"] + n * layout["token_rows"] + first_seq * units
        sums_ref[pl.ds(pl.multiple_of(at, 8), seqs * units), :] = token_sum_ref[:, cut]
        at = vocab // 128 + v
        exact_ref[at : at + 1, :] = encoder_bias[:, cut]
    for v in range(vocab // 128):
        exact_ref[v : v + 1, :] = output_bias_ref[:, v * 128 : (v + 1) * 128]
    at = vocab // 128 + width // 128
    exact_ref[at : at + 1, :] = loss_ref[...]
    part_halves(sums_ref, kept_ref, sent_ref)
    write_exact(sent_ref, kept_ref.shape[0], exact_ref[...])


def encoder_kernel(frame_tangent_ref, encoder_weight_ref, encoder_gradient_ref):
    encoder_gradient_ref[...] = lax.dot_general(
        frame_tangent_ref[...],
        encoder_weight_ref[...],
        (((1,), (1,)), ((), ())),
        preferred_element_type=F32,
    ).reshape(encoder_gradient_ref.shape)


def two_halves(stage, half):
    upper = upper_of(stage)
    own = pl.ds(pl.multiple_of(jnp.where(upper != 0, half, 0), 16), half)
    other = pl.ds(pl.multiple_of(jnp.where(upper != 0, 0, half), 16), half)
    return own, other


def exact_rows(kind):
    return EXACT if kind == F32 else 3 * EXACT


def write_exact(sent_ref, at, values):
    if sent_ref.dtype == F32:
        sent_ref[at : at + EXACT, :] = values
        return
    for n in range(3):
        part = values.astype(BF16)
        sent_ref[at + n * EXACT : at + (n + 1) * EXACT, :] = part
        values = values - part.astype(F32)


def read_exact(received_ref, at):
    parts = [
        received_ref[at + n * EXACT : at + (n + 1) * EXACT, :].astype(F32)
        for n in range(exact_rows(received_ref.dtype) // EXACT)
    ]
    return sum(parts[1:], parts[0])


def halve_kernel(stages, merge, has_exact, *refs):
    count, at = len(stages), 0
    outs = refs[2 * count + has_exact :]
    for n, stage in enumerate(stages):
        kept_ref, received_ref = refs[2 * n : 2 * n + 2]
        half = kept_ref.shape[0] // 2
        own, other = two_halves(stage, half)
        if merge:
            next_ref, sent_ref = (ref.at[at : at + half, :] for ref in outs[:2])
            at += half
        else:
            next_ref, sent_ref = outs[2 * n : 2 * n + 2]
        sent = kept_ref[other, :] + received_ref[other, :].astype(F32)
        sent_ref[:half, :] = sent.astype(sent_ref.dtype)
        next_ref[...] = kept_ref[own, :] + received_ref[own, :].astype(F32)
    if has_exact:
        exact = refs[2 * count][...] + read_exact(received_ref, kept_ref.shape[0])
        outs[-1][...] = exact
        write_exact(outs[-2], outs[-3].shape[0], exact)


def add_kernel(count, *refs):
    sum_ref, exact_sum_ref = refs[2 * count + 1 :]
    at = 0
    for n in range(count):
        kept_ref, received_ref = refs[2 * n : 2 * n + 2]
        rows = kept_ref.shape[0]
        total = kept_ref[...] + received_ref[:rows, :].astype(F32)
        high = total.astype(BF16)
        sum_ref[at : at + rows, :] = high
        at += rows
    sum_ref[at : at + rows, :] = (total - high.astype(F32)).astype(BF16)
    exact = refs[2 * count][...] + read_exact(received_ref, rows)
    exact_sum_ref[...] = exact
    write_exact(sum_ref, at + rows, exact)


def last_kernel(own_ref, other_ref, exact_ref, beside_ref, *sum_refs):
    *sum_refs, exact_sum_ref = sum_refs
    at = 0
    for n, sum_ref in enumerate(sum_refs):
        rows = sum_ref.shape[0]
        totals = []
        for ref in (own_ref, other_ref):
            total = ref[at : at + rows, :].astype(F32)
            if n == len(sum_refs) - 1:
                total = total + ref[at + rows : at + 2 * rows, :].astype(F32)
            totals.append(total)
        sum_ref[...] = (totals[0] + totals[1]).astype(BF16)
        at += rows
    exact_sum_ref[...] = exact_ref[...] + read_exact(other_ref, at + rows)


def join_kernel(stages, merged, *refs):
    count, at = len(stages), 0
    joined_refs = refs[2:] if merged else refs[2 * count :]
    for n, (stage, joined_ref) in enumerate(zip(stages, joined_refs)):
        half = joined_ref.shape[0] // 2
        own, other = two_halves(stage, half)
        if merged:
            own_ref, other_ref = (ref.at[at : at + half, :] for ref in refs[:2])
            at += half
        else:
            own_ref, other_ref = refs[2 * n : 2 * n + 2]
        joined_ref[own, :] = own_ref[...]
        joined_ref[other, :] = other_ref[...]


def copy_out(output_ref, rest_ref, side, output_hbm, encoder_hbm, output_buffer, encoder_buffer, sems):
    copies = []
    for source, buffer, target in (
        (output_ref, output_buffer, output_hbm),
        (rest_ref, encoder_buffer, encoder_hbm),
    ):
        rows, columns = buffer.shape
        for v in range(columns // 128):
            buffer[:, v * 128 : (v + 1) * 128] = source[v * rows : (v + 1) * rows, :].astype(F32)
        start = pl.multiple_of(side * columns, 128)
        copy = pltpu.make_async_copy(
            buffer, target.at[:, pl.ds(start, columns)], sems.at[len(copies)]
        )
        copy.start()
        copies.append(copy)
    return copies


def finish_own_kernel(
    output_ref,
    rest_ref,
    exact_ref,
    output_hbm,
    encoder_hbm,
    output_bias_hbm,
    encoder_bias_hbm,
    losses_hbm,
    output_buffer,
    encoder_buffer,
    output_bias_ref,
    encoder_bias_ref,
    losses_ref,
    sems,
):
    place = lax.axis_index("tokens") & 1
    copies = copy_out(
        output_ref,
        rest_ref,
        place,
        output_hbm,
        encoder_hbm,
        output_buffer,
        encoder_buffer,
        sems,
    )

    def rows(start, count):
        return jnp.concatenate([exact_ref[start + n : start + n + 1, :] for n in range(count)], axis=1)

    output_blocks, encoder_blocks = output_bias_ref.shape[1] // 128, encoder_bias_ref.shape[1] // 128
    output_bias_ref[...] = rows(0, output_blocks)
    encoder_bias_ref[...] = rows(output_blocks, encoder_blocks)
    loss = rows(output_blocks + encoder_blocks, 1)
    losses_ref[...] = jnp.sum(
        jnp.where(lane_ids(1) == lax.axis_index("frames"), loss, 0.0), axis=1, keepdims=True
    )
    for source, target in (
        (output_bias_ref, output_bias_hbm),
        (encoder_bias_ref, encoder_bias_hbm),
        (losses_ref, losses_hbm),
    ):
        copy = pltpu.make_async_copy(source, target, sems.at[len(copies)])
        copy.start()
        copies.append(copy)
    for copy in copies:
        copy.wait()


def finish_kernel(
    layout,
    output_other_ref,
    rest_own_ref,
    rest_other_ref,
    packets_ref,
    predictor_weight_ref,
    output_weight_begun,
    encoder_weight_begun,
    output_weight_hbm,
    encoder_weight_hbm,
    weight_gradient_hbm,
    bias_gradient_hbm,
    predictor_gradient_hbm,
    output_buffer,
    encoder_buffer,
    weight_gradient_ref,
    bias_gradient_ref,
    predictor_gradient_ref,
    tokens_ref,
    predictor_ref,
    sems,
):
    width = encoder_buffer.shape[0]
    place = lax.axis_index("tokens") & 1
    copies = copy_out(
        output_other_ref,
        rest_other_ref,
        1 - place,
        output_weight_hbm,
        encoder_weight_hbm,
        output_buffer,
        encoder_buffer,
        sems,
    )
    count = layout["token_rows"]
    blocks_each = width // 128 // 2

    def gather_tokens(*halves):
        for v in range(width // 128):
            at = layout["token"] + v % blocks_each * count
            tokens_ref[:, v * 128 : (v + 1) * 128] = halves[v // blocks_each][
                at : at + count, :
            ].astype(F32)

    pl.when(place == 0)(lambda: gather_tokens(rest_own_ref, rest_other_ref))
    pl.when(place == 1)(lambda: gather_tokens(rest_other_ref, rest_own_ref))
    tokens = tokens_ref[...]
    held_rows = packets_ref.shape[1] // (width // 128)
    for d in range(packets_ref.shape[0]):
        unpack_rows(packets_ref[d], predictor_ref, d * held_rows)
    def send(source, target):
        copy = pltpu.make_async_copy(source, target, sems.at[len(copies)])
        copy.start()
        copies.append(copy)

    weight_gradient_ref[...] = lax.dot_general(
        predictor_ref[...].astype(BF16),
        tokens.astype(BF16),
        (((0,), (0,)), ((), ())),
        preferred_element_type=F32,
    )
    send(weight_gradient_ref, weight_gradient_hbm)
    bias_gradient_ref[...] = jnp.sum(tokens, axis=0, keepdims=True)
    send(bias_gradient_ref, bias_gradient_hbm)
    device = lax.axis_index("frames") * lax.axis_size("tokens") + lax.axis_index("tokens")
    mine = jnp.concatenate(
        [tokens_ref[pl.ds(device * held_rows + r, 1), :] for r in range(held_rows)], axis=0
    )
    predictor_gradient_ref[:, 0, :] = lax.dot_general(
        mine.astype(BF16),
        predictor_weight_ref[...],
        (((1,), (1,)), ((), ())),
        preferred_element_type=F32,
    )
    send(predictor_gradient_ref, predictor_gradient_hbm)
    for copy in copies:
        copy.wait()


def in_hbm(array):
    return pltpu.with_memory_space_constraint(array, pltpu.HBM)


def in_vmem(array):
    return pltpu.with_memory_space_constraint(array, pltpu.VMEM)


def permuted(array, partner):
    frames, tokens = lax.axis_size("frames"), lax.axis_size("tokens")
    pairs = []
    for f in range(frames):
        for k in range(tokens):
            g, h = partner(f, k)
            pairs.append((f * tokens + k, g * tokens + h))
    return lax.ppermute(array, AXES, pairs)


def doubled(array, axis):
    blocks, places = [array], [[0]]
    bit = lax.axis_size(axis) // 2
    while bit:
        joined = jnp.concatenate(blocks, axis=0) if len(blocks) > 1 else blocks[0]
        flip = ((bit, 0), (bit, 0)) if axis == "frames" else ((0, bit), (0, bit))
        blocks.append(permuted(joined, across(flip)))
        places.append([place ^ bit for held in places for place in held])
        bit //= 2
    return blocks, [place for held in places for place in held]


def stages(even, odd):
    frame_bits = [(1 << i, 0) for i in range(lax.axis_size("frames").bit_length() - 1)]
    token_bits = [(0, 1 << i) for i in range(1, lax.axis_size("tokens").bit_length() - 1)]
    first = frame_bits[:1] + token_bits + frame_bits[1:2]
    orders = [first[shift:] + first[:shift] + frame_bits[2:] for shift in (even, odd)]
    return list(zip(*orders))


def upper_of(stage):
    f, k = lax.axis_index("frames"), lax.axis_index("tokens")
    even, odd = ((f & frame_bit) | (k & token_bit) for frame_bit, token_bit in stage)
    return jnp.where((k & 1) == 0, even, odd)


def across(stage):
    return lambda f, k: (f ^ stage[k & 1][0], k ^ stage[k & 1][1])


def neighbour(f, k):
    return f, k ^ 1


def call(body, ins, outs, scratch=(), limit=4):
    vmem = pl.BlockSpec(memory_space=pltpu.VMEM)
    there = [array is not None for array in ins]

    def kernel(*refs):
        given = iter(refs)
        body(*(next(given) if here else None for here in there), *given)

    return pl.pallas_call(
        kernel,
        in_specs=[vmem] * sum(there),
        out_specs=[
            pl.BlockSpec(memory_space=pl.ANY) if inside is None else vmem for _, _, inside in outs
        ],
        out_shape=[
            pltpu.VMEM(shape, kind) if inside else jax.ShapeDtypeStruct(shape, kind)
            for shape, kind, inside in outs
        ],
        scratch_shapes=list(scratch),
        compiler_params=pltpu.CompilerParams(vmem_limit_bytes=limit * 2**20),
    )(*(in_vmem(array) for array in ins if array is not None))


def reduced_and_gathered(pieces, exact, beside):
    plans = list(zip(*(stages(*shifts) for shifts in ORDERS)))
    flat = [a for kept, sent in pieces for a in (kept, permuted(sent, neighbour))]
    way_back = []
    *plans, last_plan = plans
    for number, plan in enumerate(plans):
        plan = plan[: len(flat) // 2]
        merge = len(plan) > 1 and len(set(plan)) == 1
        halves = [kept.shape[0] // 2 for kept in flat[::2]]
        way_back.append((plan, merge, [2 * half for half in halves]))
        if merge:
            halves = [sum(halves)]
        sent_type = SENT_TYPES[min(number, len(SENT_TYPES) - 1)]
        outs = []
        for n, half in enumerate(halves):
            sent_rows = half + (exact_rows(sent_type) if n == len(halves) - 1 else 0)
            outs += [((half, 128), F32, True), ((sent_rows, 128), sent_type, True)]
        exact_out = ((EXACT, 128), F32, True)
        if number < 2:
            given, flat = flat, []
            for n, stage in enumerate(plan):
                last = n == len(plan) - 1
                made = call(
                    functools.partial(halve_kernel, [stage], False, last),
                    given[2 * n : 2 * n + 2] + [exact] * last,
                    outs[2 * n : 2 * n + 2] + [exact_out] * last,
                )
                flat += made[:2]
                if last:
                    exact = made[2]
        else:
            *flat, exact = call(
                functools.partial(halve_kernel, plan, merge, True),
                [*flat, exact],
                [*outs, exact_out],
            )
        flat = [
            permuted(a, across(plan[n // 2])) if n % 2 else a for n, a in enumerate(flat)
        ]
    shapes = [kept.shape for kept in flat[::2]]
    rows = sum(shape[0] for shape in shapes) + shapes[-1][0] + exact_rows(BF16)
    own, exact = call(
        functools.partial(add_kernel, len(shapes)),
        [*flat, exact],
        [((rows, 128), BF16, True), ((EXACT, 128), F32, True)],
    )
    other = permuted(own, across(last_plan[0]))
    vmem = pl.BlockSpec(memory_space=pltpu.VMEM)
    *arrays, exact = pl.pallas_call(
        last_kernel,
        in_specs=[vmem, vmem, vmem, pl.BlockSpec(memory_space=pl.ANY)],
        out_specs=[vmem] * (len(shapes) + 1),
        out_shape=[pltpu.VMEM(shape, BF16) for shape in shapes] + [pltpu.VMEM((EXACT, 128), F32)],
        compiler_params=pltpu.CompilerParams(vmem_limit_bytes=4 * 2**20),
    )(in_vmem(own), in_vmem(other), in_vmem(exact), in_hbm(beside))
    for number, (plan, merged, sizes) in reversed(list(enumerate(way_back))):
        flat = [a for array, stage in zip(arrays, plan) for a in (array, permuted(array, across(stage)))]
        outs = [((size, 128), BF16, True) for size in sizes]
        if number in (0,):
            arrays = [
                call(
                    functools.partial(join_kernel, [stage], False),
                    flat[2 * n : 2 * n + 2],
                    outs[n : n + 1],
                )[0]
                for n, stage in enumerate(plan)
            ]
        else:
            arrays = call(functools.partial(join_kernel, plan, merged), flat, outs)
    return [(array, permuted(array, neighbour)) for array in arrays], exact


def per_device(
    encoder_out,
    encoder_weight,
    encoder_bias,
    predictor_out,
    predictor_weight,
    predictor_bias,
    output_weight,
    output_bias,
    labels,
    frame_lens,
    token_lens,
    loss_scale,
):
    seq_count, frame_count, width = encoder_out.shape
    vocab = output_weight.shape[1]
    all_seqs = labels.shape[0]
    held_seqs, held_units = predictor_out.shape[:2]
    assert held_seqs == 1
    frame_axis, token_axis = lax.axis_size("frames"), lax.axis_size("tokens")
    device_count = frame_axis * token_axis
    units = held_units * token_axis
    calls = seq_count // 2
    diagonals = (frame_count // 2 + units) * units
    vmem = pl.BlockSpec(memory_space=pltpu.VMEM)
    anywhere = pl.BlockSpec(memory_space=pl.ANY)

    weights = (
        encoder_out,
        encoder_weight,
        encoder_bias.reshape(1, width),
        predictor_weight,
        predictor_bias.reshape(1, width),
        output_weight,
        output_bias.reshape(1, vocab),
        frame_lens.reshape(1, all_seqs),
        token_lens.reshape(1, all_seqs),
        loss_scale.reshape(1, all_seqs),
    )
    packet_rows = held_units * width // 128
    packets = pl.pallas_call(
        packet_kernel,
        in_specs=[anywhere],
        out_specs=vmem,
        out_shape=jax.ShapeDtypeStruct((device_count, packet_rows, 128), BF16),
        scratch_shapes=[
            pltpu.VMEM((held_units, width), BF16),
            pltpu.VMEM((packet_rows, 128), F32),
            pltpu.SemaphoreType.DMA,
        ],
        compiler_params=pltpu.CompilerParams(vmem_limit_bytes=4 * 2**20),
    )(in_hbm(predictor_out.reshape(held_units, width)))
    label_blocks, label_places = doubled(labels[None], "tokens")
    *weights, frames = pl.pallas_call(
        load_kernel,
        in_specs=[anywhere] * len(weights),
        out_specs=[vmem] * (1 + len(weights)),
        out_shape=[pltpu.VMEM(w.shape, w.dtype) for w in weights]
        + [pltpu.VMEM(encoder_out.shape, F32)],
        scratch_shapes=[pltpu.SemaphoreType.DMA((len(weights),))],
        compiler_params=pltpu.CompilerParams(vmem_limit_bytes=4 * 2**20),
    )(*map(in_hbm, weights))
    *weights, frame_lens, token_lens, loss_scale = weights
    lens = frame_lens, token_lens
    packets = lax.all_to_all(packets, AXES, 0, 0, tiled=True)

    score_shapes = [
        ((2 * units // SUB_UNITS, SUB_UNITS * frame_count, vocab), F32),
        ((2 * units, width), F32),
        ((diagonals, 128), F32),
        ((diagonals, 128), F32),
        ((2 * units // SUB_UNITS, SUB_UNITS * frame_count, width), F32),
        ((2 * units // SUB_UNITS, SUB_UNITS * frame_count, 128), F32),
        ((units, 128), F32),
        ((1, 1, units, 128), F32),
    ]

    def scores(offset, frames):
        (table,) = call(
            functools.partial(table_kernel, label_places, seq_count),
            (offset, *label_blocks),
            [((1, 128), jnp.int32, True)],
        )
        scored = call(
            functools.partial(score_kernel, seq_count),
            (offset, packets, *lens, frames, *weights[3:], table),
            [(shape, kind, True) for shape, kind in score_shapes],
            scratch=[
                pltpu.VMEM((SUB_UNITS * frame_count, vocab), F32),
                pltpu.VMEM((SUB_UNITS * frame_count, vocab), F32),
                pltpu.SMEM((1, 128), jnp.int32),
                pltpu.SemaphoreType.DMA,
            ],
            limit=8,
        )
        return [table, *scored]

    offsets = 2 * jnp.arange(calls, dtype=jnp.int32).reshape(calls, 1, 1)
    encoders = weights[0].reshape(calls, 2, frame_count, width)
    if calls == 1:
        scored = scores(None, frames)
        matrix = scored[-1]
    else:
        scored = lax.map(
            lambda given: scores(*given),
            (offsets, frames.reshape(calls, 2, frame_count, width)),
        )
        matrix = scored[-1].reshape(1, calls, units, 128)

    matrices, matrix_places = doubled(matrix, "frames")
    layout = {"matrix_places": matrix_places, "seqs_here": seq_count, "frame_count": frame_count, "units": units}
    align = 16 * device_count // 4
    blocks_each = width // 128 // 2
    layout["token"], layout["token_rows"] = blocks_each * width, all_seqs * units
    half = layout["token"] + blocks_each * all_seqs * units
    layout["half"] = half + (-half % align)
    rest_rows = 2 * layout["half"]
    output_rows = vocab // 128 * width
    assert output_rows % (2 * align) == 0 and vocab // 128 + width // 128 < EXACT

    blocks = 2 * units // SUB_UNITS
    block_rows = SUB_UNITS * frame_count

    def turns(offset, scored):
        hidden = scored[5]
        (turned,) = call(
            functools.partial(turn_kernel, layout),
            (offset, *lens, hidden),
            [((hidden.shape[0], width + 16, hidden.shape[1]), BF16, True)],
        )
        return turned

    def tangents(offset, scored, turned, matrices):
        table, softmax, _, blank, label, _, inverse, parts = scored
        return call(
            functools.partial(tangent_kernel, dict(layout, hops=len(matrices) - 1)),
            (
                *(offset, *lens, loss_scale, softmax, table, blank, label),
                *(turned, inverse, parts, *matrices),
            ),
            [
                ((blocks, block_rows, vocab), BF16, True),
                ((1, vocab), F32, True),
                ((1, 128), F32, True),
                ((output_rows // 2, 128), F32, True),
                ((output_rows // 2, 128), F32, True),
            ],
            scratch=[
                pltpu.VMEM((output_rows, 128), F32),
                pltpu.VMEM((frame_axis, units, 128), F32),
                pltpu.VMEM((diagonals, 128), F32),
                pltpu.VMEM((diagonals, 128), F32),
                pltpu.VMEM((diagonals, 128), F32),
                pltpu.VMEM((diagonals, 128), F32),
                pltpu.VMEM((block_rows, vocab), BF16),
                pltpu.VMEM((block_rows, vocab), BF16),
                pltpu.SMEM((1, 128), jnp.int32),
                pltpu.SemaphoreType.DMA,
            ],
            limit=12,
        )

    def inners(offset, encoder, scored, tangent, output_bias_sum, loss):
        return call(
            functools.partial(inner_kernel, layout),
            (offset, *lens, tangent, scored[5], weights[5], encoder, output_bias_sum, loss),
            [
                ((2 * frame_count, width), BF16, True),
                ((EXACT, 128), F32, True),
                ((rest_rows // 2, 128), F32, True),
                ((rest_rows // 2 + EXACT, 128), F32, True),
            ],
            scratch=[
                pltpu.VMEM((rest_rows, 128), F32),
                pltpu.VMEM((2, frame_count, width), F32),
                pltpu.VMEM((2 * units, width), F32),
                pltpu.VMEM((2 * block_rows, width), F32),
                pltpu.VMEM((2 * block_rows, width), F32),
            ],
            limit=10,
        )

    def encoder_gradient_of(frame_tangent):
        return call(
            encoder_kernel,
            (frame_tangent, weights[1]),
            [((2, frame_count, width), F32, False)],
        )[0]

    if calls == 1:
        scored = scored[:-1]
        turned = turns(None, scored)
        tangent, output_bias_sum, loss, *output_sums = tangents(None, scored, turned, matrices)

        frame_tangent, exact, *rest = inners(
            None, weights[0], scored, tangent, output_bias_sum, loss
        )
        sums = [*output_sums, *rest, exact]
        encoder_gradient = encoder_gradient_of(frame_tangent)
    else:

        def add_call(sums, given):
            offset, encoder, scored, call = given
            own = [lax.dynamic_slice_in_dim(m, call, 1, 1) for m in matrices]
            turned = turns(offset, scored)
            tangent, output_bias_sum, loss, *more = tangents(offset, scored, turned, own)
            frame_tangent, exact, *rest = inners(
                offset, encoder, scored, tangent, output_bias_sum, loss
            )
            sums = [a + b for a, b in zip(sums, [*more, *rest, exact])]
            return sums, encoder_gradient_of(frame_tangent)

        sizes = (output_rows // 2,) * 2 + (rest_rows // 2, rest_rows // 2 + EXACT, EXACT)
        sums, encoder_gradient = lax.scan(
            add_call,
            [jnp.zeros((size, 128), F32) for size in sizes],
            (offsets, encoders, scored[:-1], jnp.arange(calls)),
        )
        encoder_gradient = encoder_gradient.reshape(encoder_out.shape)

    halves, exact = reduced_and_gathered(
        [sums[:2], sums[2:4]], sums[4], encoder_gradient
    )
    (output_own, output_other), (rest_own, rest_other) = halves
    buffers = [
        pltpu.VMEM((width, vocab // 2), F32),
        pltpu.VMEM((width, width // 2), F32),
    ]
    *begun, output_bias_gradient, encoder_bias_gradient, losses = call(
        finish_own_kernel,
        (output_own, rest_own, exact),
        [
            ((width, vocab), F32, None),
            ((width, width), F32, None),
            ((1, vocab), F32, None),
            ((1, width), F32, None),
            ((1, 1), F32, None),
        ],
        scratch=[
            *buffers,
            pltpu.VMEM((1, vocab), F32),
            pltpu.VMEM((1, width), F32),
            pltpu.VMEM((1, 1), F32),
            pltpu.SemaphoreType.DMA((5,)),
        ],
        limit=8,
    )
    shapes = [(width, vocab), (width, width), (width, width), (1, width), (held_units, 1, width)]
    finished = pl.pallas_call(
        functools.partial(finish_kernel, layout),
        in_specs=[vmem] * 5 + [anywhere] * 2,
        out_specs=[anywhere] * len(shapes),
        out_shape=[jax.ShapeDtypeStruct(shape, F32) for shape in shapes],
        input_output_aliases={5: 0, 6: 1},
        scratch_shapes=[
            *buffers,
            *(pltpu.VMEM(shape, F32) for shape in shapes[2:]),
            pltpu.VMEM((all_seqs * units, width), F32),
            pltpu.VMEM((all_seqs * units, width), F32),
            pltpu.SemaphoreType.DMA((5,)),
        ],
        compiler_params=pltpu.CompilerParams(vmem_limit_bytes=20 * 2**20),
    )(
        *map(in_vmem, (output_other, rest_own, rest_other, packets, weights[3])),
        *map(in_hbm, begun),
    )
    return (
        losses.reshape(1),
        encoder_gradient,
        finished[4].transpose(1, 0, 2),
        finished[1],
        encoder_bias_gradient.reshape(width),
        finished[2],
        finished[3].reshape(width),
        finished[0],
        output_bias_gradient.reshape(vocab),
    )


def solution(mesh):
    placed = (
        P("tokens", "frames", None),
        P(),
        P(),
        P("frames", "tokens", None),
        P(),
        P(),
        P(),
        P(),
        P(None, "tokens"),
        P(),
        P(),
        P(),
    )
    return jax.shard_map(
        per_device,
        mesh=mesh,
        in_specs=placed,
        out_specs=(
            P("frames"),
            P("tokens", "frames", None),
            P("frames", "tokens", None),
            P(),
            P(),
            P(),
            P(),
            P(),
            P(),
        ),
        check_vma=False,
    )
```

```python
import functools

import jax
import jax.numpy as jnp
from jax import lax
from jax.experimental import pallas as pl
from jax.experimental.pallas import tpu as pltpu
from jax.sharding import PartitionSpec as P

NEG = -1e30
LOG2E = 1.4426950408889634
LN2 = 0.6931471805599453
BF16 = jnp.bfloat16
F32 = jnp.float32
GROUP = 32
SUB_UNITS = 4
ORDERS = ((0, 1), (2, 1))
SENT_TYPES = (jnp.bfloat16, jnp.bfloat16, jnp.float32)
EXACT = 16
AXES = ("frames", "tokens")


def lane_ids(rows):
    return lax.broadcasted_iota(jnp.int32, (rows, 128), 1)


def log2_add(a, b):
    return jnp.maximum(a, b) + jnp.log2(1.0 + jnp.exp2(-jnp.abs(a - b)))


def both_ways(blank_ref, label_ref, units, steps, ahead, behind, keep):
    def one_step(i, state):
        ahead, behind = state
        back = steps - 1 - i
        here = pl.ds(pl.multiple_of(i * units, 8), units)
        there = pl.ds(pl.multiple_of(back * units, 8), units)
        keep[0][here, :] = ahead
        keep[1][there, :] = behind
        from_left = pltpu.roll(ahead + label_ref[here, :], 1, 0)
        to_right = pltpu.roll(behind, units - 1, 0) + label_ref[there, :]
        ahead = log2_add(ahead + blank_ref[here, :], from_left)
        behind = log2_add(behind + blank_ref[there, :], to_right)
        return ahead, behind

    return lax.fori_loop(0, steps, one_step, (ahead, behind))


def log2_add_three(a, b, c):
    top = jnp.maximum(jnp.maximum(a, b), c)
    return top + jnp.log2(jnp.exp2(a - top) + jnp.exp2(b - top) + jnp.exp2(c - top))


def both_ways_in_pairs(blank_ref, label_ref, units, steps, ahead, behind):
    pairs = -(-steps // 2)

    def rows_of(ref, diagonal):
        return ref[pl.ds(pl.multiple_of(diagonal * units, 8), units), :]

    def up(array, by=1):
        return pltpu.roll(array, by, 0)

    def down(array, by=1):
        return pltpu.roll(array, units - by, 0)

    def scores_of(first):
        return [rows_of(ref, first + n) for ref in (blank_ref, label_ref) for n in (0, 1)]

    def ways_ahead(i):
        blank, blank_next, label, label_next = scores_of(2 * i)
        one = log2_add(up(blank + label_next), up(label) + blank_next)
        return blank + blank_next, one, up(up(label) + label_next)

    def ways_behind(i):
        blank, blank_next, label, label_next = scores_of(2 * (pairs - 1 - i))
        one = log2_add(blank + label_next, label + down(blank_next))
        return blank + blank_next, one, label + down(label_next)

    def one_pair(i, state):
        ahead, behind, (none, one, two), (none_back, one_back, two_back) = state
        following = jnp.minimum(i + 1, pairs - 1)
        ahead = log2_add_three(ahead + none, up(ahead) + one, up(ahead, 2) + two)
        behind = log2_add_three(
            behind + none_back, down(behind) + one_back, down(behind, 2) + two_back
        )
        return ahead, behind, ways_ahead(following), ways_behind(following)

    start = ahead, behind, ways_ahead(0), ways_behind(0)
    return lax.fori_loop(0, pairs, one_pair, start)[:2]


def in_two_stages(count, first, second, even, odd, between=None):
    def two_blocks(n, _):
        first(2 * n + 1, odd)
        second(2 * n, even)
        first(2 * n + 2, even)
        second(2 * n + 1, odd)
        return 0

    @pl.when(count > 0)
    def _():
        first(0, even)

    if between is not None:
        between()

    @pl.when(count > 0)
    def _():
        lax.fori_loop(0, (count - 1) // 2, two_blocks, 0)

        @pl.when(count % 2 == 1)
        def _():
            second(count - 1, even)

        @pl.when(count % 2 == 0)
        def _():
            first(count - 1, odd)
            second(count - 2, even)
            second(count - 1, odd)


def packet_kernel(predictor_hbm, packets_ref, predictor_ref, packet_ref, sem):
    load = pltpu.make_async_copy(predictor_hbm, predictor_ref, sem)
    load.start()
    load.wait()
    rows, width = predictor_ref.shape
    for v in range(width // 128):
        packet_ref[v * rows : (v + 1) * rows, :] = predictor_ref[
            :, v * 128 : (v + 1) * 128
        ].astype(F32)
    packet = packet_ref[...].astype(BF16)
    for d in range(packets_ref.shape[0]):
        packets_ref[d] = packet


def label_packet_kernel(predictor_hbm, labels_hbm, packet_ref, predictor_ref, labels_ref, sems):
    loads = [
        pltpu.make_async_copy(predictor_hbm, predictor_ref, sems.at[0]),
        pltpu.make_async_copy(labels_hbm, labels_ref, sems.at[1]),
    ]
    for load in loads:
        load.start()
    for load in loads:
        load.wait()
    seqs, units = labels_ref.shape
    width = packet_ref.shape[2]
    flat = jnp.zeros((1, width), F32)
    for s in range(seqs):
        row = labels_ref[s : s + 1, :].astype(F32)
        row = jnp.concatenate([row, jnp.zeros((1, width - units), F32)], axis=1)
        flat = flat + (pltpu.roll(row, s * units, 1) if s else row)
    high = jnp.floor(flat * (1.0 / 32.0))
    packet_ref[0] = jnp.concatenate(
        [predictor_ref[...].astype(F32), high, flat - high * 32.0], axis=0
    ).astype(BF16)


def packet_table_kernel(places, *refs):
    *packet_refs, table_ref = refs
    first_seq = first_of(None, None)
    held_units, width = packet_refs[0].shape[1] - 2, packet_refs[0].shape[2]
    units = held_units * lax.axis_size("tokens")
    lanes = lane_ids(1)
    table = jnp.zeros((1, 128), F32)
    for ref, n, f, k in sources_of(places, packet_refs):
        halves = ref[n].astype(F32)[held_units:]
        row = halves[:1] * 32.0 + halves[1:2]
        for s in range(2):
            start = s * units + k * held_units
            shift = start - (first_seq + s) * held_units
            shifted = pltpu.roll(row, jnp.where(shift < 0, shift + width, shift), 1)[:, :128]
            table = jnp.where((lanes >= start) & (lanes < start + held_units), shifted, table)
    table_ref[...] = table.astype(jnp.int32)


def unpack_rows(packet, rows_ref, place):
    blocks = rows_ref.shape[1] // 128
    count = packet.shape[0] // blocks
    packet = packet.astype(F32)
    for v in range(blocks):
        rows_ref[place : place + count, v * 128 : (v + 1) * 128] = packet[
            v * count : (v + 1) * count
        ]


def table_kernel(places, seqs_here, offset_ref, *refs):
    *label_refs, table_ref = refs
    first_seq = first_of(seqs_here, offset_ref)
    shard_units = label_refs[0].shape[2]
    units = shard_units * len(places)
    lanes = lane_ids(1)
    table = jnp.zeros((1, 128), F32)
    received = [(ref, n) for ref in label_refs for n in range(ref.shape[0])]
    for place, (ref, n) in zip(places, received):
        shard = lax.axis_index("tokens") ^ place
        for s in range(2):
            row = ref[n, pl.ds(first_seq + s, 1), :].astype(F32)
            row = jnp.concatenate([row, jnp.zeros((1, 128 - shard_units), F32)], axis=1)
            start = s * units + shard * shard_units
            table = jnp.where(
                (lanes >= start) & (lanes < start + shard_units), pltpu.roll(row, start, 1), table
            )
    table_ref[...] = table.astype(jnp.int32)


def load_kernel(*refs):
    count = (len(refs) - 1) // 2
    loads = [
        pltpu.make_async_copy(source, target, refs[-1].at[n])
        for n, (source, target) in enumerate(zip(refs[:count], refs[count:-1]))
    ]
    for load in loads:
        load.start()
    for load in loads:
        load.wait()


def project_kernel(encoder_ref, weight_ref, bias_ref, frame_ref):
    frame_ref[...] = (
        (
            jnp.dot(
                encoder_ref[...].reshape(-1, encoder_ref.shape[-1]),
                weight_ref[...],
                preferred_element_type=F32,
            )
            + bias_ref[...]
        )
        .astype(BF16)
        .astype(F32)
        .reshape(frame_ref.shape)
    )


def stack_kernel(*refs):
    at = 0
    for ref in refs[:-1]:
        refs[-1][at : at + ref.shape[0]] = ref[...]
        at += ref.shape[0]


def sources_of(places, refs):
    f, k = lax.axis_index("frames"), lax.axis_index("tokens")
    entries = [(ref, n) for ref in refs for n in range(ref.shape[0])]
    return [(ref, n, f ^ (place >> 8), k ^ (place & 255)) for place, (ref, n) in zip(places, entries)]


def predictor_kernel(places, *refs):
    *packet_refs, predictor_ref, rows_ref = refs
    if places is None:
        held_rows = rows_ref.shape[0] // packet_refs[0].shape[0]
        for d in range(packet_refs[0].shape[0]):
            unpack_rows(packet_refs[0][d], rows_ref, d * held_rows)
    else:
        for ref, n, f, k in sources_of(places, packet_refs):
            rows = ref[n].astype(F32)
            count = rows.shape[0] - 2
            start = (f * lax.axis_size("tokens") + k) * count
            for r in range(count):
                rows_ref[pl.ds(start + r, 1), :] = rows[r : r + 1]
    predictor_ref[...] = rows_ref[...].astype(BF16)


def entry(row_ref, place):
    row = row_ref[...].astype(F32)
    ids = lax.broadcasted_iota(jnp.int32, row.shape, 1)
    return jnp.sum(jnp.where(ids == place, row, 0.0), axis=1, keepdims=True)


def whole_number(row_ref, place):
    return entry(row_ref, place).astype(jnp.int32)[0, 0]


def first_of(seqs_here, offset_ref):
    if seqs_here is None:
        return lax.axis_index("frames") // 2 * 2
    first_seq = lax.axis_index("tokens") * seqs_here
    return first_seq if offset_ref is None else first_seq + whole_number(offset_ref, 0)


def chunk_of(seqs_here):
    f, k = lax.axis_index("frames"), lax.axis_index("tokens")
    return f if seqs_here is not None else 2 * k + (f & 1)


def block_counts(lens_ref, tokens_ref, first_seq, first_frame):
    counts = []
    for s in range(2):
        inside = first_frame < whole_number(lens_ref, first_seq + s)
        units = whole_number(tokens_ref, first_seq + s)
        counts.append(jnp.where(inside, units // SUB_UNITS + 1, 0))
    return counts


def score_kernel(
    seqs_here,
    packet_places,
    offset_ref,
    lens_ref,
    tokens_ref,
    frame_ref,
    predictor_weight_ref,
    predictor_bias_ref,
    weight_ref,
    bias_ref,
    label_table_ref,
    *refs,
):
    *packet_refs, softmax_ref, token_ref, blank_ref, label_ref, hidden_ref, inverse_ref = refs[:-6]
    parts_ref, matrix_ref, even_ref, odd_ref, labels_smem, label_sem = refs[-6:]
    label_copy = pltpu.make_async_copy(label_table_ref, labels_smem, label_sem)
    label_copy.start()
    seqs, frame_count, width = frame_ref.shape
    units = token_ref.shape[0] // seqs
    shards = lax.axis_size("tokens")
    shard_units = units // shards
    part = frame_count // 2
    steps = part + units - 1
    first_frame = chunk_of(seqs_here) * frame_count
    first_seq = first_of(seqs_here, offset_ref)
    vocab = weight_ref.shape[1]
    blank_ref[...] = jnp.zeros_like(blank_ref)
    label_ref[...] = jnp.full(label_ref.shape, NEG, F32)
    if packet_places is None:
        for s in range(seqs):
            for k in range(shards):
                packet = packet_refs[0][(first_seq + s) * shards + k]
                unpack_rows(packet, token_ref, s * units + k * shard_units)
    else:
        for ref, n, f, k in sources_of(packet_places, packet_refs):
            rows = ref[n].astype(F32)
            start = (f & 1) * units + k * shard_units
            for r in range(shard_units):
                token_ref[pl.ds(start + r, 1), :] = rows[r : r + 1]
    token_ref[...] = (
        jnp.dot(token_ref[...].astype(BF16), predictor_weight_ref[...], preferred_element_type=F32)
        + predictor_bias_ref[...]
    ).astype(BF16).astype(F32)

    counts = block_counts(lens_ref, tokens_ref, first_seq, first_frame)
    blocks = counts[0] + counts[1]
    lens = [whole_number(lens_ref, first_seq + s) for s in range(2)]
    last_units = [whole_number(tokens_ref, first_seq + s) for s in range(2)]
    lanes = lane_ids(frame_count)
    part_lanes = lane_ids(part)
    times = first_frame + lax.broadcasted_iota(jnp.int32, (frame_count, 1), 0)

    def place_of(i):
        seq = jnp.where(i >= counts[0], 1, 0)
        sub = i - seq * counts[0]
        return seq, sub, seq * (units // SUB_UNITS) + sub

    def multiply(i, logits_ref):
        seq, sub, block = place_of(i)
        frames = frame_ref[seq]
        hidden = jnp.concatenate(
            [
                jnp.tanh(frames + token_ref[pl.ds(seq * units + sub * SUB_UNITS + j, 1), :])
                for j in range(SUB_UNITS)
            ],
            axis=0,
        )
        hidden_ref[block] = hidden
        low = hidden.astype(BF16)
        logits_ref[...] = (
            jnp.dot(low, weight_ref[...], preferred_element_type=F32) + bias_ref[...]
        )

    def score(i, logits_ref):
        seq, sub, block = place_of(i)
        first_unit = sub * SUB_UNITS
        seq_len = jnp.where(seq == 0, lens[0], lens[1])
        last_unit = jnp.where(seq == 0, last_units[0], last_units[1])
        own_lanes = (part_lanes // GROUP) % 2 == seq
        logits = logits_ref[...]
        top = jnp.max(logits, axis=1, keepdims=True)
        weights = jnp.exp(logits - top)
        total = jnp.sum(weights, axis=1, keepdims=True)
        softmax_ref[block] = weights
        inverse_ref[block] = jnp.broadcast_to(1.0 / total, (weights.shape[0], 128))
        log_total = top + jnp.log(total)
        blanks = (logits[:, :1] - log_total) * LOG2E
        for j in range(SUB_UNITS):
            unit = first_unit + j
            rows = slice(j * frame_count, (j + 1) * frame_count)
            label = labels_smem[0, seq * units + unit]
            tile = logits_ref[rows, pl.ds(pl.multiple_of(label // 128 * 128, 128), 128)]
            picked = jnp.sum(
                jnp.where(lanes == label % 128, tile, 0.0), axis=1, keepdims=True
            )
            blank = blanks[rows]
            blank = jnp.where((times == seq_len - 1) & (unit < last_unit), NEG, blank)
            blank = jnp.where((times >= seq_len) | (unit > last_unit), 0.0, blank)
            step = jnp.where(
                (times >= seq_len) | (unit >= last_unit),
                NEG,
                (picked - log_total[rows]) * LOG2E,
            )
            at = (pl.ds(unit * (units + 1), part, stride=units), slice(None))
            blank = jnp.where(part_lanes < 64, blank[:part], blank[part:])
            step = jnp.where(part_lanes < 64, step[:part], step[part:])
            blank_ref[at] = jnp.where(own_lanes, blank, blank_ref[at])
            label_ref[at] = jnp.where(own_lanes, step, label_ref[at])

    in_two_stages(blocks, multiply, score, even_ref, odd_ref, label_copy.wait)
    eye = jnp.where(
        lane_ids(units) % GROUP == lax.broadcasted_iota(jnp.int32, (units, 128), 0), 0.0, NEG
    ).astype(F32)
    ahead, behind = both_ways_in_pairs(blank_ref, label_ref, units, steps, eye, eye)
    lanes = lane_ids(units)
    early = lanes < 64
    columns = jnp.where(early, behind, ahead)
    parts_ref[...] = columns
    others = pltpu.roll(jnp.where(early, ahead, behind), 64, 1)
    ways = [
        jnp.take_along_axis(
            columns, lanes // GROUP * GROUP + k, axis=1, mode="promise_in_bounds"
        )
        + others[k : k + 1, :]
        for k in range(units)
    ]
    top = functools.reduce(jnp.maximum, ways)
    total = functools.reduce(jnp.add, [jnp.exp2(way - top) for way in ways])
    matrix_ref[0, 0] = top + jnp.log2(total)


def turn_kernel(layout, offset_ref, lens_ref, tokens_ref, hidden_ref, turned_ref):
    width = hidden_ref.shape[2]
    first_frame = chunk_of(layout["seqs_here"]) * layout["frame_count"]
    first_seq = first_of(layout["seqs_here"], offset_ref)
    counts = block_counts(lens_ref, tokens_ref, first_seq, first_frame)

    def one_block(i, _):
        seq = jnp.where(i >= counts[0], 1, 0)
        block = i + seq * (layout["units"] // SUB_UNITS - counts[0])
        turned_ref[block, :width, :] = hidden_ref[block].astype(BF16).T
        turned_ref[block, width:, :] = jnp.ones((16, turned_ref.shape[2]), BF16)
        return 0

    lax.fori_loop(0, counts[0] + counts[1], one_block, 0)


def tangent_kernel(
    layout,
    offset_ref,
    lens_ref,
    tokens_ref,
    scale_ref,
    softmax_ref,
    label_table_ref,
    blank_ref,
    label_ref,
    turned_ref,
    inverse_ref,
    parts_ref,
    *refs,
):
    hops = layout["hops"]
    matrix_refs, refs = refs[: hops + 1], refs[hops + 1 :]
    (
        tangents_ref,
        output_bias_ref,
        loss_ref,
        kept_ref,
        sent_ref,
        sums_ref,
        matrices_ref,
        ahead_ref,
        behind_ref,
        blank_part_ref,
        label_part_ref,
        even_ref,
        odd_ref,
        labels_smem,
        label_sem,
    ) = refs
    label_copy = pltpu.make_async_copy(label_table_ref, labels_smem, label_sem)
    label_copy.start()
    frame_count = layout["frame_count"]
    width = turned_ref.shape[1] - 16
    units = layout["units"]
    part = frame_count // 2
    steps = part + units - 1
    here = chunk_of(layout["seqs_here"])
    first_frame = here * frame_count
    first_seq = first_of(layout["seqs_here"], offset_ref)
    chunks = matrices_ref.shape[0]
    vocab = softmax_ref.shape[2]
    received = [(ref, n) for ref in matrix_refs for n in range(ref.shape[0])]
    for place, (matrix_ref, n) in zip(layout["matrix_places"], received):
        matrices_ref[place] = matrix_ref[n, 0]
    starts = lax.broadcasted_iota(jnp.int32, (units, 128), 0)
    lanes = lane_ids(units)
    early = lanes < 64
    gather_ids = lanes // GROUP * GROUP + starts
    own_first = (lane_ids(1) // GROUP) % 2 == 0

    def through(column, matrix):
        ways = column + matrix
        top = jnp.max(ways, axis=0, keepdims=True)
        row = top + jnp.log2(jnp.sum(jnp.exp2(ways - top), axis=0, keepdims=True))
        row = jnp.broadcast_to(row, (units, 128))
        return jnp.take_along_axis(row, gather_ids, axis=1, mode="promise_in_bounds")

    def one_chunk(i, carry):
        column, kept = carry
        other = chunks - 1 - i
        kept = jnp.where(jnp.where(early, i, other) == here, column, kept)
        matrix = jnp.where(early, matrices_ref[here ^ i], matrices_ref[here ^ other])
        return through(column, matrix), kept

    start = jnp.where(early & (starts > 0), NEG, 0.0).astype(F32)
    last, kept = lax.fori_loop(0, chunks, one_chunk, (start, start))
    middle = pltpu.roll(through(kept, parts_ref[...]), 64, 1)
    both_ways(
        blank_ref,
        label_ref,
        units,
        steps,
        jnp.where(early, kept, middle),
        jnp.where(early, middle, kept),
        (ahead_ref, behind_ref),
    )
    log_norm = jnp.max(jnp.where(early, last, pltpu.roll(last, 64, 1)), axis=0, keepdims=True)
    scale, length, bound = (
        jnp.where(own_first, entry(ref, first_seq), entry(ref, first_seq + 1))
        for ref in (scale_ref, lens_ref, tokens_ref)
    )
    length, bound = length.astype(jnp.int32), bound.astype(jnp.int32)
    part_start = first_frame + jnp.where(lane_ids(1) < 64, 0, part)
    last_diagonal = starts + jnp.minimum(length - part_start, part)
    first_blank = jnp.where(starts <= bound, starts, steps)
    first_label = jnp.where(starts < bound, starts, steps)
    norm = log_norm - jnp.log2(scale)

    def one_diagonal(e, _):
        rows = pl.ds(pl.multiple_of(e * units, 8), units)
        behind = behind_ref[rows, :]
        base = ahead_ref[rows, :] - norm
        before_end = last_diagonal > e
        blank_part_ref[rows, :] = jnp.where(
            before_end & (first_blank <= e), jnp.exp2(base + blank_ref[rows, :] + behind), 0.0
        )
        label_part_ref[rows, :] = jnp.where(
            before_end & (first_label <= e),
            jnp.exp2(base + label_ref[rows, :] + pltpu.roll(behind, units - 1, 0)),
            0.0,
        )
        return 0

    lax.fori_loop(0, steps, one_diagonal, 0, unroll=5)

    counts = block_counts(lens_ref, tokens_ref, first_seq, first_frame)
    block_lanes = lane_ids(frame_count)
    part_lanes = lane_ids(part)

    def place_of(i):
        seq = jnp.where(i >= counts[0], 1, 0)
        sub = i - seq * counts[0]
        return seq, sub, seq * (units // SUB_UNITS) + sub

    wide = lane_ids(1)
    loss = jnp.where(here == 0, -log_norm * LN2, 0.0)
    spread = jnp.where(wide == first_seq, loss[:, :1], 0.0)
    loss_ref[...] = spread + jnp.where(wide == first_seq + 1, loss[:, GROUP : GROUP + 1], 0.0)
    label_copy.wait()

    counts_all = counts[0] + counts[1]
    sums_ref[...] = jnp.zeros_like(sums_ref)
    output_bias_ref[...] = jnp.zeros_like(output_bias_ref)

    def prepare(i, tangent_ref):
        seq, sub, block = place_of(i)
        own_lanes = [part_lanes % GROUP + GROUP * (seq + 2 * half) for half in (0, 1)]
        for j in range(SUB_UNITS):
            unit = sub * SUB_UNITS + j
            rows = slice(j * frame_count, (j + 1) * frame_count)
            at = (pl.ds(unit * (units + 1), part, stride=units), slice(None))
            blank, step = (
                jnp.concatenate(
                    [
                        jnp.take_along_axis(ref[at], ids, axis=1, mode="promise_in_bounds")
                        for ids in own_lanes
                    ],
                    axis=0,
                )
                for ref in (blank_part_ref, label_part_ref)
            )
            both = (blank + step) * inverse_ref[block, rows, :]
            for v in range(vocab // 128):
                cut = slice(v * 128, (v + 1) * 128)
                piece = softmax_ref[block, rows, cut] * both
                if v == 0:
                    piece = piece - jnp.where(block_lanes == 0, blank, 0.0)
                piece = piece.astype(BF16)
                tangent_ref[rows, cut] = piece
                tangents_ref[block, rows, cut] = piece
            label = labels_smem[0, seq * units + unit]
            cut = pl.ds(pl.multiple_of(label // 128 * 128, 128), 128)
            piece = softmax_ref[block, rows, cut] * both
            piece = piece - jnp.where((block_lanes == 0) & (label < 128), blank, 0.0)
            piece = (piece - jnp.where(block_lanes == label % 128, step, 0.0)).astype(BF16)
            tangent_ref[rows, cut] = piece
            tangents_ref[block, rows, cut] = piece

    def multiply(i, tangent_ref):
        _, _, block = place_of(i)
        product = jnp.dot(turned_ref[block], tangent_ref[...], preferred_element_type=F32)
        for v in range(vocab // 128):
            sums_ref[v * width : (v + 1) * width, :] += product[:width, v * 128 : (v + 1) * 128]
        output_bias_ref[...] += product[width : width + 1, :]

    in_two_stages(counts_all, prepare, multiply, even_ref, odd_ref)
    part_halves(sums_ref, kept_ref, sent_ref)


def part_halves(sums_ref, kept_ref, sent_ref):
    half = kept_ref.shape[0]
    place = lax.axis_index("tokens") & 1
    sent_ref[:half, :] = sums_ref[pl.ds(pl.multiple_of((1 - place) * half, 8), half), :]
    kept_ref[...] = sums_ref[pl.ds(pl.multiple_of(place * half, 8), half), :]


def inner_kernel(
    layout,
    offset_ref,
    lens_ref,
    tokens_ref,
    tangents_ref,
    hidden_ref,
    weight_ref,
    encoder_ref,
    output_bias_ref,
    loss_ref,
    frame_tangent_ref,
    exact_ref,
    kept_ref,
    sent_ref,
    sums_ref,
    frame_sum_ref,
    token_sum_ref,
    even_ref,
    odd_ref,
):
    seqs, frame_count, width = encoder_ref.shape
    units = token_sum_ref.shape[0] // seqs
    vocab = weight_ref.shape[1]
    first_frame = chunk_of(layout["seqs_here"]) * frame_count
    first_seq = first_of(layout["seqs_here"], offset_ref)
    frame_sum_ref[...] = jnp.zeros_like(frame_sum_ref)
    token_sum_ref[...] = jnp.zeros_like(token_sum_ref)
    half = layout["half"]
    for side in (0, 1):
        unset = slice(side * half + layout["token"], (side + 1) * half)
        sums_ref[unset, :] = jnp.zeros_like(sums_ref[unset, :])
    counts = block_counts(lens_ref, tokens_ref, first_seq, first_frame)

    def place_of(i):
        seq = jnp.where(i >= counts[0], 1, 0)
        sub = i - seq * counts[0]
        return seq, sub, seq * (units // SUB_UNITS) + sub

    def product_of(tangents):
        return lax.dot_general(
            tangents, weight_ref[...], (((1,), (1,)), ((), ())), preferred_element_type=F32
        )

    def add_up(i, product):
        seq, sub, block = place_of(i)
        hidden = hidden_ref[block]
        inner = product * (1.0 - hidden * hidden)
        total = frame_sum_ref[seq]
        for j in range(SUB_UNITS):
            rows = slice(j * frame_count, (j + 1) * frame_count)
            total = total + inner[rows]
            token_sum_ref[pl.ds(seq * units + sub * SUB_UNITS + j, 1), :] = jnp.sum(
                inner[rows], axis=0, keepdims=True
            )
        frame_sum_ref[seq] = total

    def multiply_two(n, product_ref):
        both = [tangents_ref[place_of(2 * n + m)[2]] for m in (0, 1)]
        product_ref[...] = product_of(jnp.concatenate(both, axis=0))

    def add_up_two(n, product_ref):
        half = product_ref.shape[0] // 2
        add_up(2 * n, product_ref[:half])
        add_up(2 * n + 1, product_ref[half:])

    blocks = counts[0] + counts[1]
    in_two_stages(blocks // 2, multiply_two, add_up_two, even_ref, odd_ref)

    @pl.when(blocks % 2 == 1)
    def _():
        add_up(blocks - 1, product_of(tangents_ref[place_of(blocks - 1)[2]]))

    low = frame_sum_ref[...].reshape(seqs * frame_count, width).astype(BF16)
    frame_tangent_ref[...] = low
    product = lax.dot_general(
        encoder_ref[...].reshape(seqs * frame_count, width),
        low,
        (((0,), (0,)), ((), ())),
        preferred_element_type=F32,
    )
    encoder_bias = jnp.sum(low.astype(F32), axis=0, keepdims=True)
    blocks_each = width // 128 // 2
    exact_ref[...] = jnp.zeros_like(exact_ref)
    for v in range(width // 128):
        cut = slice(v * 128, (v + 1) * 128)
        start, n = v // blocks_each * half, v % blocks_each
        sums_ref[start + n * width : start + (n + 1) * width, :] = product[:, cut]
        at = start + layout["token"] + n * layout["token_rows"] + first_seq * units
        sums_ref[pl.ds(pl.multiple_of(at, 8), seqs * units), :] = token_sum_ref[:, cut]
        at = vocab // 128 + v
        exact_ref[at : at + 1, :] = encoder_bias[:, cut]
    for v in range(vocab // 128):
        exact_ref[v : v + 1, :] = output_bias_ref[:, v * 128 : (v + 1) * 128]
    at = vocab // 128 + width // 128
    exact_ref[at : at + 1, :] = loss_ref[...]
    part_halves(sums_ref, kept_ref, sent_ref)
    write_exact(sent_ref, kept_ref.shape[0], exact_ref[...])


def encoder_kernel(frame_tangent_ref, encoder_weight_ref, encoder_gradient_ref, mark_ref):
    mark_ref[...] = jnp.zeros_like(mark_ref)
    encoder_gradient_ref[...] = lax.dot_general(
        frame_tangent_ref[...],
        encoder_weight_ref[...],
        (((1,), (1,)), ((), ())),
        preferred_element_type=F32,
    ).reshape(encoder_gradient_ref.shape)


def two_halves(stage, half):
    upper = upper_of(stage)
    own = pl.ds(pl.multiple_of(jnp.where(upper != 0, half, 0), 16), half)
    other = pl.ds(pl.multiple_of(jnp.where(upper != 0, 0, half), 16), half)
    return own, other


def exact_rows(kind):
    return EXACT if kind == F32 else 3 * EXACT


def write_exact(sent_ref, at, values):
    if sent_ref.dtype == F32:
        sent_ref[at : at + EXACT, :] = values
        return
    for n in range(3):
        part = values.astype(BF16)
        sent_ref[at + n * EXACT : at + (n + 1) * EXACT, :] = part
        values = values - part.astype(F32)


def read_exact(received_ref, at):
    parts = [
        received_ref[at + n * EXACT : at + (n + 1) * EXACT, :].astype(F32)
        for n in range(exact_rows(received_ref.dtype) // EXACT)
    ]
    return sum(parts[1:], parts[0])


def halve_kernel(stages, merge, has_exact, *refs):
    count, at = len(stages), 0
    outs = refs[2 * count + has_exact :]
    for n, stage in enumerate(stages):
        kept_ref, received_ref = refs[2 * n : 2 * n + 2]
        half = kept_ref.shape[0] // 2
        own, other = two_halves(stage, half)
        if merge:
            next_ref, sent_ref = (ref.at[at : at + half, :] for ref in outs[:2])
            at += half
        else:
            next_ref, sent_ref = outs[2 * n : 2 * n + 2]
        sent = kept_ref[other, :] + received_ref[other, :].astype(F32)
        sent_ref[:half, :] = sent.astype(sent_ref.dtype)
        next_ref[...] = kept_ref[own, :] + received_ref[own, :].astype(F32)
    if has_exact:
        exact = refs[2 * count][...] + read_exact(received_ref, kept_ref.shape[0])
        outs[-1][...] = exact
        write_exact(outs[-2], outs[-3].shape[0], exact)


def add_kernel(count, *refs):
    sum_ref, exact_sum_ref = refs[-2:]
    at = 0
    for n in range(count):
        kept_ref, received_ref = refs[2 * n : 2 * n + 2]
        rows = kept_ref.shape[0]
        total = kept_ref[...] + received_ref[:rows, :].astype(F32)
        high = total.astype(BF16)
        sum_ref[at : at + rows, :] = high
        at += rows
    sum_ref[at : at + rows, :] = (total - high.astype(F32)).astype(BF16)
    exact = refs[2 * count][...] + read_exact(received_ref, rows)
    exact_sum_ref[...] = exact
    write_exact(sum_ref, at + rows, exact)


def last_kernel(own_ref, other_ref, exact_ref, *sum_refs):
    *sum_refs, exact_sum_ref = sum_refs
    at = 0
    for n, sum_ref in enumerate(sum_refs):
        rows = sum_ref.shape[0]
        totals = []
        for ref in (own_ref, other_ref):
            total = ref[at : at + rows, :].astype(F32)
            if n == len(sum_refs) - 1:
                total = total + ref[at + rows : at + 2 * rows, :].astype(F32)
            totals.append(total)
        sum_ref[...] = (totals[0] + totals[1]).astype(BF16)
        at += rows
    exact_sum_ref[...] = exact_ref[...] + read_exact(other_ref, at + rows)


def join_kernel(stages, merged, *refs):
    count, at = len(stages), 0
    joined_refs = refs[-count:]
    for n, (stage, joined_ref) in enumerate(zip(stages, joined_refs)):
        half = joined_ref.shape[0] // 2
        own, other = two_halves(stage, half)
        if merged:
            own_ref, other_ref = (ref.at[at : at + half, :] for ref in refs[:2])
            at += half
        else:
            own_ref, other_ref = refs[2 * n : 2 * n + 2]
        joined_ref[own, :] = own_ref[...]
        joined_ref[other, :] = other_ref[...]


def copy_out(output_ref, rest_ref, side, output_hbm, encoder_hbm, output_buffer, encoder_buffer, sems):
    copies = []
    for source, buffer, target in (
        (output_ref, output_buffer, output_hbm),
        (rest_ref, encoder_buffer, encoder_hbm),
    ):
        rows, columns = buffer.shape
        for v in range(columns // 128):
            buffer[:, v * 128 : (v + 1) * 128] = source[v * rows : (v + 1) * rows, :].astype(F32)
        start = pl.multiple_of(side * columns, 128)
        copy = pltpu.make_async_copy(
            buffer, target.at[:, pl.ds(start, columns)], sems.at[len(copies)]
        )
        copy.start()
        copies.append(copy)
    return copies


def finish_own_kernel(
    output_ref,
    rest_ref,
    exact_ref,
    output_hbm,
    encoder_hbm,
    output_bias_hbm,
    encoder_bias_hbm,
    losses_hbm,
    output_buffer,
    encoder_buffer,
    output_bias_ref,
    encoder_bias_ref,
    losses_ref,
    sems,
):
    place = lax.axis_index("tokens") & 1
    copies = copy_out(
        output_ref,
        rest_ref,
        place,
        output_hbm,
        encoder_hbm,
        output_buffer,
        encoder_buffer,
        sems,
    )

    def rows(start, count):
        return jnp.concatenate([exact_ref[start + n : start + n + 1, :] for n in range(count)], axis=1)

    output_blocks, encoder_blocks = output_bias_ref.shape[1] // 128, encoder_bias_ref.shape[1] // 128
    output_bias_ref[...] = rows(0, output_blocks)
    encoder_bias_ref[...] = rows(output_blocks, encoder_blocks)
    loss = rows(output_blocks + encoder_blocks, 1)
    losses_ref[...] = jnp.sum(
        jnp.where(lane_ids(1) == lax.axis_index("frames"), loss, 0.0), axis=1, keepdims=True
    )
    for source, target in (
        (output_bias_ref, output_bias_hbm),
        (encoder_bias_ref, encoder_bias_hbm),
        (losses_ref, losses_hbm),
    ):
        copy = pltpu.make_async_copy(source, target, sems.at[len(copies)])
        copy.start()
        copies.append(copy)
    for copy in copies:
        copy.wait()


def finish_kernel(
    layout,
    output_other_ref,
    rest_own_ref,
    rest_other_ref,
    predictor_ref,
    predictor_weight_ref,
    output_weight_begun,
    encoder_weight_begun,
    output_weight_hbm,
    encoder_weight_hbm,
    weight_gradient_hbm,
    bias_gradient_hbm,
    predictor_gradient_hbm,
    output_buffer,
    encoder_buffer,
    weight_gradient_ref,
    bias_gradient_ref,
    predictor_gradient_ref,
    tokens_ref,
    sems,
):
    width = encoder_buffer.shape[0]
    place = lax.axis_index("tokens") & 1
    copies = copy_out(
        output_other_ref,
        rest_other_ref,
        1 - place,
        output_weight_hbm,
        encoder_weight_hbm,
        output_buffer,
        encoder_buffer,
        sems,
    )
    count = layout["token_rows"]
    blocks_each = width // 128 // 2

    def gather_tokens(*halves):
        for v in range(width // 128):
            at = layout["token"] + v % blocks_each * count
            tokens_ref[:, v * 128 : (v + 1) * 128] = halves[v // blocks_each][
                at : at + count, :
            ].astype(F32)

    pl.when(place == 0)(lambda: gather_tokens(rest_own_ref, rest_other_ref))
    pl.when(place == 1)(lambda: gather_tokens(rest_other_ref, rest_own_ref))
    tokens = tokens_ref[...]
    held_rows = predictor_gradient_ref.shape[0]

    def send(source, target):
        copy = pltpu.make_async_copy(source, target, sems.at[len(copies)])
        copy.start()
        copies.append(copy)

    weight_gradient_ref[...] = lax.dot_general(
        predictor_ref[...],
        tokens.astype(BF16),
        (((0,), (0,)), ((), ())),
        preferred_element_type=F32,
    )
    send(weight_gradient_ref, weight_gradient_hbm)
    bias_gradient_ref[...] = jnp.sum(tokens, axis=0, keepdims=True)
    send(bias_gradient_ref, bias_gradient_hbm)
    device = lax.axis_index("frames") * lax.axis_size("tokens") + lax.axis_index("tokens")
    mine = jnp.concatenate(
        [tokens_ref[pl.ds(device * held_rows + r, 1), :] for r in range(held_rows)], axis=0
    )
    predictor_gradient_ref[:, 0, :] = lax.dot_general(
        mine.astype(BF16),
        predictor_weight_ref[...],
        (((1,), (1,)), ((), ())),
        preferred_element_type=F32,
    )
    send(predictor_gradient_ref, predictor_gradient_hbm)
    for copy in copies:
        copy.wait()


def in_hbm(array):
    return pltpu.with_memory_space_constraint(array, pltpu.HBM)


def in_vmem(array):
    return pltpu.with_memory_space_constraint(array, pltpu.VMEM)


def permuted(array, partner):
    frames, tokens = lax.axis_size("frames"), lax.axis_size("tokens")
    pairs = []
    for f in range(frames):
        for k in range(tokens):
            g, h = partner(f, k)
            pairs.append((f * tokens + k, g * tokens + h))
    return lax.ppermute(array, AXES, pairs)


def axis_flips(axis):
    flips, bit = [], lax.axis_size(axis) // 2
    while bit:
        flips.append(((bit, 0) if axis == "frames" else (0, bit), bit))
        bit //= 2
    return flips


def stacked(blocks):
    if len(blocks) == 1:
        return blocks[0]
    shape = (sum(block.shape[0] for block in blocks),) + blocks[0].shape[1:]
    return call(stack_kernel, blocks, [(shape, blocks[0].dtype, True)])[0]


def doubled(blocks, places, flips):
    blocks, places = list(blocks), list(places)
    for bits, mark in flips:
        blocks.append(permuted(stacked(blocks), across((bits, bits))))
        places += [place ^ mark for place in places]
    return blocks, places


def stages(even, odd):
    frame_bits = [(1 << i, 0) for i in range(lax.axis_size("frames").bit_length() - 1)]
    token_bits = [(0, 1 << i) for i in range(1, lax.axis_size("tokens").bit_length() - 1)]
    first = frame_bits[:1] + token_bits + frame_bits[1:2]
    orders = [first[shift:] + first[:shift] + frame_bits[2:] for shift in (even, odd)]
    return list(zip(*orders))


def upper_of(stage):
    f, k = lax.axis_index("frames"), lax.axis_index("tokens")
    even, odd = ((f & frame_bit) | (k & token_bit) for frame_bit, token_bit in stage)
    return jnp.where((k & 1) == 0, even, odd)


def across(stage):
    return lambda f, k: (f ^ stage[k & 1][0], k ^ stage[k & 1][1])


def neighbour(f, k):
    return f, k ^ 1


def call(body, ins, outs, scratch=(), limit=4):
    vmem = pl.BlockSpec(memory_space=pltpu.VMEM)
    there = [array is not None for array in ins]

    def kernel(*refs):
        given = iter(refs)
        body(*(next(given) if here else None for here in there), *given)

    return pl.pallas_call(
        kernel,
        in_specs=[vmem] * sum(there),
        out_specs=[
            pl.BlockSpec(memory_space=pl.ANY) if inside is None else vmem for _, _, inside in outs
        ],
        out_shape=[
            pltpu.VMEM(shape, kind) if inside else jax.ShapeDtypeStruct(shape, kind)
            for shape, kind, inside in outs
        ],
        scratch_shapes=list(scratch),
        compiler_params=pltpu.CompilerParams(vmem_limit_bytes=limit * 2**20),
    )(*(in_vmem(array) for array in ins if array is not None))


def reduced_and_gathered(pieces, exact, beside, held):
    plans = list(zip(*(stages(*shifts) for shifts in ORDERS)))
    flat = [a for kept, sent in pieces for a in (kept, permuted(sent, neighbour))]
    way_back = []
    *plans, last_plan = plans
    for number, plan in enumerate(plans):
        plan = plan[: len(flat) // 2]
        merge = len(plan) > 1 and len(set(plan)) == 1
        halves = [kept.shape[0] // 2 for kept in flat[::2]]
        way_back.append((plan, merge, [2 * half for half in halves]))
        if merge:
            halves = [sum(halves)]
        sent_type = SENT_TYPES[min(number, len(SENT_TYPES) - 1)]
        outs = []
        for n, half in enumerate(halves):
            sent_rows = half + (exact_rows(sent_type) if n == len(halves) - 1 else 0)
            outs += [((half, 128), F32, True), ((sent_rows, 128), sent_type, True)]
        exact_out = ((EXACT, 128), F32, True)
        if number < 2:
            given, flat = flat, []
            for n, stage in enumerate(plan):
                last = n == len(plan) - 1
                made = call(
                    functools.partial(halve_kernel, [stage], False, last),
                    given[2 * n : 2 * n + 2] + [exact] * last,
                    outs[2 * n : 2 * n + 2] + [exact_out] * last,
                )
                flat += made[:2]
                if last:
                    exact = made[2]
        else:
            *flat, exact = call(
                functools.partial(halve_kernel, plan, merge, True),
                [*flat, exact],
                [*outs, exact_out],
            )
        flat = [
            permuted(a, across(plan[n // 2])) if n % 2 else a for n, a in enumerate(flat)
        ]
    shapes = [kept.shape for kept in flat[::2]]
    rows = sum(shape[0] for shape in shapes) + shapes[-1][0] + exact_rows(BF16)
    own, exact = call(
        functools.partial(add_kernel, len(shapes)),
        [*flat, exact, *beside],
        [((rows, 128), BF16, True), ((EXACT, 128), F32, True)],
    )
    other = permuted(own, across(last_plan[0]))
    vmem = pl.BlockSpec(memory_space=pltpu.VMEM)
    *arrays, exact = pl.pallas_call(
        last_kernel,
        in_specs=[vmem, vmem, vmem],
        out_specs=[vmem] * (len(shapes) + 1),
        out_shape=[pltpu.VMEM(shape, BF16) for shape in shapes] + [pltpu.VMEM((EXACT, 128), F32)],
        compiler_params=pltpu.CompilerParams(vmem_limit_bytes=4 * 2**20),
    )(in_vmem(own), in_vmem(other), in_vmem(exact))
    for number, (plan, merged, sizes) in reversed(list(enumerate(way_back))):
        flat = [a for array, stage in zip(arrays, plan) for a in (array, permuted(array, across(stage)))]
        outs = [((size, 128), BF16, True) for size in sizes]
        if number in (0,):
            arrays = [
                call(
                    functools.partial(join_kernel, [stage], False),
                    flat[2 * n : 2 * n + 2],
                    outs[n : n + 1],
                )[0]
                for n, stage in enumerate(plan)
            ]
        else:
            given = [*flat, *held] if number == 1 else flat
            arrays = call(functools.partial(join_kernel, plan, merged), given, outs)
    return [(array, permuted(array, neighbour)) for array in arrays], exact


def per_device(
    encoder_out,
    encoder_weight,
    encoder_bias,
    predictor_out,
    predictor_weight,
    predictor_bias,
    output_weight,
    output_bias,
    labels,
    frame_lens,
    token_lens,
    loss_scale,
):
    seq_count, frame_count, width = encoder_out.shape
    vocab = output_weight.shape[1]
    all_seqs = labels.shape[0]
    held_seqs, held_units = predictor_out.shape[:2]
    assert held_seqs == 1
    frame_axis, token_axis = lax.axis_size("frames"), lax.axis_size("tokens")
    device_count = frame_axis * token_axis
    units = held_units * token_axis
    calls = seq_count // 2
    diagonals = (frame_count // 2 + units) * units
    vmem = pl.BlockSpec(memory_space=pltpu.VMEM)
    anywhere = pl.BlockSpec(memory_space=pl.ANY)

    in_plane = seq_count == 2 and token_axis == 4 and frame_axis == 8

    def turned_over(f, k):
        return 2 * k + (f & 1), f >> 1

    weights = (
        encoder_weight,
        encoder_bias.reshape(1, width),
        predictor_weight,
        predictor_bias.reshape(1, width),
        output_weight,
        output_bias.reshape(1, vocab),
        frame_lens.reshape(1, all_seqs),
        token_lens.reshape(1, all_seqs),
        loss_scale.reshape(1, all_seqs),
    )
    if in_plane:
        plane = [((0, 1), 1), ((1, 0), 256), ((0, 2), 2)]
        encoder = permuted(encoder_out, turned_over)
        packet = pl.pallas_call(
            label_packet_kernel,
            in_specs=[anywhere] * 2,
            out_specs=vmem,
            out_shape=pltpu.VMEM((1, held_units + 2, width), BF16),
            scratch_shapes=[
                pltpu.VMEM((held_units, width), BF16),
                pltpu.VMEM(labels.shape, jnp.int32),
                pltpu.SemaphoreType.DMA((2,)),
            ],
            compiler_params=pltpu.CompilerParams(vmem_limit_bytes=4 * 2**20),
        )(in_hbm(predictor_out.reshape(held_units, width)), in_hbm(labels))
        packets, packet_places = doubled([packet], [0], plane)
        own_seqs = None
    else:
        packet_rows = held_units * width // 128
        packets = pl.pallas_call(
            packet_kernel,
            in_specs=[anywhere],
            out_specs=vmem,
            out_shape=jax.ShapeDtypeStruct((device_count, packet_rows, 128), BF16),
            scratch_shapes=[
                pltpu.VMEM((held_units, width), BF16),
                pltpu.VMEM((packet_rows, 128), F32),
                pltpu.SemaphoreType.DMA,
            ],
            compiler_params=pltpu.CompilerParams(vmem_limit_bytes=4 * 2**20),
        )(in_hbm(predictor_out.reshape(held_units, width)))
        packets, packet_places = [lax.all_to_all(packets, AXES, 0, 0, tiled=True)], None
        encoder, own_seqs = encoder_out, seq_count
    if not in_plane:
        label_blocks, label_places = doubled([labels[None]], [0], axis_flips("tokens"))
    weights = pl.pallas_call(
        load_kernel,
        in_specs=[anywhere] * len(weights),
        out_specs=[vmem] * len(weights),
        out_shape=[pltpu.VMEM(w.shape, w.dtype) for w in weights],
        scratch_shapes=[pltpu.SemaphoreType.DMA((len(weights),))],
        compiler_params=pltpu.CompilerParams(vmem_limit_bytes=4 * 2**20),
    )(*map(in_hbm, weights))
    *weights, frame_lens, token_lens, loss_scale = weights
    lens = frame_lens, token_lens
    (frames,) = call(
        project_kernel, (encoder, weights[0], weights[1]), [(encoder_out.shape, F32, True)]
    )

    score_shapes = [
        ((2 * units // SUB_UNITS, SUB_UNITS * frame_count, vocab), F32),
        ((2 * units, width), F32),
        ((diagonals, 128), F32),
        ((diagonals, 128), F32),
        ((2 * units // SUB_UNITS, SUB_UNITS * frame_count, width), F32),
        ((2 * units // SUB_UNITS, SUB_UNITS * frame_count, 128), F32),
        ((units, 128), F32),
        ((1, 1, units, 128), F32),
    ]

    def scores(offset, frames):
        if in_plane:
            body, given = functools.partial(packet_table_kernel, packet_places), packets
        else:
            body = functools.partial(table_kernel, label_places, own_seqs)
            given = (offset, *label_blocks)
        (table,) = call(body, given, [((1, 128), jnp.int32, True)])
        scored = call(
            functools.partial(score_kernel, own_seqs, packet_places),
            (offset, *lens, frames, *weights[2:], table, *packets),
            [(shape, kind, True) for shape, kind in score_shapes],
            scratch=[
                pltpu.VMEM((SUB_UNITS * frame_count, vocab), F32),
                pltpu.VMEM((SUB_UNITS * frame_count, vocab), F32),
                pltpu.SMEM((1, 128), jnp.int32),
                pltpu.SemaphoreType.DMA,
            ],
            limit=8,
        )
        return [table, *scored]

    offsets = 2 * jnp.arange(calls, dtype=jnp.int32).reshape(calls, 1, 1)
    encoders = encoder.reshape(calls, 2, frame_count, width)
    if calls == 1:
        scored = scores(None, frames)
        matrix = scored[-1]
    else:
        scored = lax.map(
            lambda given: scores(*given),
            (offsets, frames.reshape(calls, 2, frame_count, width)),
        )
        matrix = scored[-1].reshape(1, calls, units, 128)

    chunk_flips = [((0, 2), 4), ((1, 0), 1), ((0, 1), 2)] if in_plane else axis_flips("frames")
    matrices, matrix_places = doubled([matrix], [0], chunk_flips)
    if in_plane:
        packets, packet_places = doubled(
            [stacked(packets)], packet_places, [((4, 0), 1024), ((2, 0), 512)]
        )
    (predictor_all,) = call(
        functools.partial(predictor_kernel, packet_places),
        packets,
        [((all_seqs * units, width), BF16, True)],
        scratch=[pltpu.VMEM((all_seqs * units, width), F32)],
        limit=8,
    )
    layout = {"matrix_places": matrix_places, "seqs_here": own_seqs, "frame_count": frame_count, "units": units}
    align = 16 * device_count // 4
    blocks_each = width // 128 // 2
    layout["token"], layout["token_rows"] = blocks_each * width, all_seqs * units
    half = layout["token"] + blocks_each * all_seqs * units
    layout["half"] = half + (-half % align)
    rest_rows = 2 * layout["half"]
    output_rows = vocab // 128 * width
    assert output_rows % (2 * align) == 0 and vocab // 128 + width // 128 < EXACT

    blocks = 2 * units // SUB_UNITS
    block_rows = SUB_UNITS * frame_count

    def turns(offset, scored):
        hidden = scored[5]
        (turned,) = call(
            functools.partial(turn_kernel, layout),
            (offset, *lens, hidden),
            [((hidden.shape[0], width + 16, hidden.shape[1]), BF16, True)],
        )
        return turned

    def tangents(offset, scored, turned, matrices):
        table, softmax, _, blank, label, _, inverse, parts = scored
        return call(
            functools.partial(tangent_kernel, dict(layout, hops=len(matrices) - 1)),
            (
                *(offset, *lens, loss_scale, softmax, table, blank, label),
                *(turned, inverse, parts, *matrices),
            ),
            [
                ((blocks, block_rows, vocab), BF16, True),
                ((1, vocab), F32, True),
                ((1, 128), F32, True),
                ((output_rows // 2, 128), F32, True),
                ((output_rows // 2, 128), F32, True),
            ],
            scratch=[
                pltpu.VMEM((output_rows, 128), F32),
                pltpu.VMEM((frame_axis, units, 128), F32),
                pltpu.VMEM((diagonals, 128), F32),
                pltpu.VMEM((diagonals, 128), F32),
                pltpu.VMEM((diagonals, 128), F32),
                pltpu.VMEM((diagonals, 128), F32),
                pltpu.VMEM((block_rows, vocab), BF16),
                pltpu.VMEM((block_rows, vocab), BF16),
                pltpu.SMEM((1, 128), jnp.int32),
                pltpu.SemaphoreType.DMA,
            ],
            limit=12,
        )

    def inners(offset, encoder, scored, tangent, output_bias_sum, loss):
        return call(
            functools.partial(inner_kernel, layout),
            (
                *(offset, *lens, tangent, scored[5], weights[4], encoder),
                *(output_bias_sum, loss),
            ),
            [
                ((2 * frame_count, width), BF16, True),
                ((EXACT, 128), F32, True),
                ((rest_rows // 2, 128), F32, True),
                ((rest_rows // 2 + EXACT, 128), F32, True),
            ],
            scratch=[
                pltpu.VMEM((rest_rows, 128), F32),
                pltpu.VMEM((2, frame_count, width), F32),
                pltpu.VMEM((2 * units, width), F32),
                pltpu.VMEM((2 * block_rows, width), F32),
                pltpu.VMEM((2 * block_rows, width), F32),
            ],
            limit=10,
        )

    def encoder_gradient_of(frame_tangent):
        return call(
            encoder_kernel,
            (frame_tangent, weights[0]),
            [((2, frame_count, width), F32, False), ((8, 128), F32, True)],
        )

    if calls == 1:
        scored = scored[:-1]
        turned = turns(None, scored)
        tangent, output_bias_sum, loss, *output_sums = tangents(None, scored, turned, matrices)

        frame_tangent, exact, *rest = inners(
            None, encoder, scored, tangent, output_bias_sum, loss
        )
        sums = [*output_sums, *rest, exact]
        if in_plane:
            frame_tangent = permuted(frame_tangent, turned_over)
        encoder_gradient, mark = encoder_gradient_of(frame_tangent)
        beside, held = [frame_tangent], [predictor_all, mark]
    else:

        def add_call(sums, given):
            offset, encoder, scored, call = given
            own = [lax.dynamic_slice_in_dim(m, call, 1, 1) for m in matrices]
            turned = turns(offset, scored)
            tangent, output_bias_sum, loss, *more = tangents(offset, scored, turned, own)
            frame_tangent, exact, *rest = inners(
                offset, encoder, scored, tangent, output_bias_sum, loss
            )
            sums = [a + b for a, b in zip(sums, [*more, *rest, exact])]
            return sums, encoder_gradient_of(frame_tangent)[0]

        sizes = (output_rows // 2,) * 2 + (rest_rows // 2, rest_rows // 2 + EXACT, EXACT)
        sums, encoder_gradient = lax.scan(
            add_call,
            [jnp.zeros((size, 128), F32) for size in sizes],
            (offsets, encoders, scored[:-1], jnp.arange(calls)),
        )
        encoder_gradient = encoder_gradient.reshape(encoder_out.shape)
        beside, held = [], [predictor_all]

    halves, exact = reduced_and_gathered(
        [sums[:2], sums[2:4]], sums[4], beside, held
    )
    (output_own, output_other), (rest_own, rest_other) = halves
    buffers = [
        pltpu.VMEM((width, vocab // 2), F32),
        pltpu.VMEM((width, width // 2), F32),
    ]
    *begun, output_bias_gradient, encoder_bias_gradient, losses = call(
        finish_own_kernel,
        (output_own, rest_own, exact),
        [
            ((width, vocab), F32, None),
            ((width, width), F32, None),
            ((1, vocab), F32, None),
            ((1, width), F32, None),
            ((1, 1), F32, None),
        ],
        scratch=[
            *buffers,
            pltpu.VMEM((1, vocab), F32),
            pltpu.VMEM((1, width), F32),
            pltpu.VMEM((1, 1), F32),
            pltpu.SemaphoreType.DMA((5,)),
        ],
        limit=8,
    )
    shapes = [(width, vocab), (width, width), (width, width), (1, width), (held_units, 1, width)]
    finished = pl.pallas_call(
        functools.partial(finish_kernel, layout),
        in_specs=[vmem] * 5 + [anywhere] * 2,
        out_specs=[anywhere] * len(shapes),
        out_shape=[jax.ShapeDtypeStruct(shape, F32) for shape in shapes],
        input_output_aliases={5: 0, 6: 1},
        scratch_shapes=[
            *buffers,
            *(pltpu.VMEM(shape, F32) for shape in shapes[2:]),
            pltpu.VMEM((all_seqs * units, width), F32),
            pltpu.SemaphoreType.DMA((5,)),
        ],
        compiler_params=pltpu.CompilerParams(vmem_limit_bytes=20 * 2**20),
    )(
        *map(in_vmem, (output_other, rest_own, rest_other, predictor_all, weights[2])),
        *map(in_hbm, begun),
    )
    return (
        losses.reshape(1),
        encoder_gradient,
        finished[4].transpose(1, 0, 2),
        finished[1],
        encoder_bias_gradient.reshape(width),
        finished[2],
        finished[3].reshape(width),
        finished[0],
        output_bias_gradient.reshape(vocab),
    )


def solution(mesh):
    placed = (
        P("tokens", "frames", None),
        P(),
        P(),
        P("frames", "tokens", None),
        P(),
        P(),
        P(),
        P(),
        P(None, "tokens"),
        P(),
        P(),
        P(),
    )
    return jax.shard_map(
        per_device,
        mesh=mesh,
        in_specs=placed,
        out_specs=(
            P("frames"),
            P("tokens", "frames", None),
            P("frames", "tokens", None),
            P(),
            P(),
            P(),
            P(),
            P(),
            P(),
        ),
        check_vma=False,
    )
```

```python
import functools

import jax
import jax.numpy as jnp
from jax import lax
from jax.experimental import pallas as pl
from jax.experimental.pallas import tpu as pltpu
from jax.sharding import PartitionSpec as P

NEG = -1e30
LOG2E = 1.4426950408889634
LN2 = 0.6931471805599453
BF16 = jnp.bfloat16
F32 = jnp.float32
GROUP = 32
SUB_UNITS = 4
ORDERS = ((0, 1), (2, 1))
SENT_TYPES = (jnp.bfloat16, jnp.bfloat16, jnp.float32)
EXACT = 16
AXES = ("frames", "tokens")


def lane_ids(rows):
    return lax.broadcasted_iota(jnp.int32, (rows, 128), 1)


def log2_add(a, b):
    return jnp.maximum(a, b) + jnp.log2(1.0 + jnp.exp2(-jnp.abs(a - b)))


def both_ways(blank_ref, label_ref, units, steps, ahead, behind, keep):
    def one_step(i, state):
        ahead, behind = state
        back = steps - 1 - i
        here = pl.ds(pl.multiple_of(i * units, 8), units)
        there = pl.ds(pl.multiple_of(back * units, 8), units)
        keep[0][here, :] = ahead
        keep[1][there, :] = behind
        from_left = pltpu.roll(ahead + label_ref[here, :], 1, 0)
        to_right = pltpu.roll(behind, units - 1, 0) + label_ref[there, :]
        ahead = log2_add(ahead + blank_ref[here, :], from_left)
        behind = log2_add(behind + blank_ref[there, :], to_right)
        return ahead, behind

    return lax.fori_loop(0, steps, one_step, (ahead, behind))


def log2_add_three(a, b, c):
    top = jnp.maximum(jnp.maximum(a, b), c)
    return top + jnp.log2(jnp.exp2(a - top) + jnp.exp2(b - top) + jnp.exp2(c - top))


def both_ways_in_pairs(blank_ref, label_ref, units, steps, ahead, behind):
    pairs = -(-steps // 2)

    def rows_of(ref, diagonal):
        return ref[pl.ds(pl.multiple_of(diagonal * units, 8), units), :]

    def up(array, by=1):
        return pltpu.roll(array, by, 0)

    def down(array, by=1):
        return pltpu.roll(array, units - by, 0)

    def scores_of(first):
        return [rows_of(ref, first + n) for ref in (blank_ref, label_ref) for n in (0, 1)]

    def ways_ahead(i):
        blank, blank_next, label, label_next = scores_of(2 * i)
        one = log2_add(up(blank + label_next), up(label) + blank_next)
        return blank + blank_next, one, up(up(label) + label_next)

    def ways_behind(i):
        blank, blank_next, label, label_next = scores_of(2 * (pairs - 1 - i))
        one = log2_add(blank + label_next, label + down(blank_next))
        return blank + blank_next, one, label + down(label_next)

    def one_pair(i, state):
        ahead, behind, (none, one, two), (none_back, one_back, two_back) = state
        following = jnp.minimum(i + 1, pairs - 1)
        ahead = log2_add_three(ahead + none, up(ahead) + one, up(ahead, 2) + two)
        behind = log2_add_three(
            behind + none_back, down(behind) + one_back, down(behind, 2) + two_back
        )
        return ahead, behind, ways_ahead(following), ways_behind(following)

    start = ahead, behind, ways_ahead(0), ways_behind(0)
    return lax.fori_loop(0, pairs, one_pair, start)[:2]


def in_two_stages(count, first, second, even, odd, between=None):
    def two_blocks(n, _):
        first(2 * n + 1, odd)
        second(2 * n, even)
        first(2 * n + 2, even)
        second(2 * n + 1, odd)
        return 0

    @pl.when(count > 0)
    def _():
        first(0, even)

    if between is not None:
        between()

    @pl.when(count > 0)
    def _():
        lax.fori_loop(0, (count - 1) // 2, two_blocks, 0)

        @pl.when(count % 2 == 1)
        def _():
            second(count - 1, even)

        @pl.when(count % 2 == 0)
        def _():
            first(count - 1, odd)
            second(count - 2, even)
            second(count - 1, odd)


def packet_kernel(predictor_hbm, packets_ref, predictor_ref, packet_ref, sem):
    load = pltpu.make_async_copy(predictor_hbm, predictor_ref, sem)
    load.start()
    load.wait()
    rows, width = predictor_ref.shape
    for v in range(width // 128):
        packet_ref[v * rows : (v + 1) * rows, :] = predictor_ref[
            :, v * 128 : (v + 1) * 128
        ].astype(F32)
    packet = packet_ref[...].astype(BF16)
    for d in range(packets_ref.shape[0]):
        packets_ref[d] = packet


def label_packet_kernel(predictor_hbm, labels_hbm, packet_ref, predictor_ref, labels_ref, sems):
    loads = [
        pltpu.make_async_copy(predictor_hbm, predictor_ref, sems.at[0]),
        pltpu.make_async_copy(labels_hbm, labels_ref, sems.at[1]),
    ]
    for load in loads:
        load.start()
    for load in loads:
        load.wait()
    seqs, units = labels_ref.shape
    width = packet_ref.shape[2]
    flat = jnp.zeros((1, width), F32)
    for s in range(seqs):
        row = labels_ref[s : s + 1, :].astype(F32)
        row = jnp.concatenate([row, jnp.zeros((1, width - units), F32)], axis=1)
        flat = flat + (pltpu.roll(row, s * units, 1) if s else row)
    high = jnp.floor(flat * (1.0 / 32.0))
    packet_ref[0] = jnp.concatenate(
        [predictor_ref[...].astype(F32), high, flat - high * 32.0], axis=0
    ).astype(BF16)


def packet_table_kernel(places, *refs):
    *packet_refs, table_ref = refs
    first_seq = first_of(None, None)
    held_units, width = packet_refs[0].shape[1] - 2, packet_refs[0].shape[2]
    units = held_units * lax.axis_size("tokens")
    lanes = lane_ids(1)
    table = jnp.zeros((1, 128), F32)
    for ref, n, f, k in sources_of(places, packet_refs):
        halves = ref[n].astype(F32)[held_units:]
        row = halves[:1] * 32.0 + halves[1:2]
        for s in range(2):
            start = s * units + k * held_units
            shift = start - (first_seq + s) * held_units
            shifted = pltpu.roll(row, jnp.where(shift < 0, shift + width, shift), 1)[:, :128]
            table = jnp.where((lanes >= start) & (lanes < start + held_units), shifted, table)
    table_ref[...] = table.astype(jnp.int32)


def unpack_rows(packet, rows_ref, place):
    blocks = rows_ref.shape[1] // 128
    count = packet.shape[0] // blocks
    packet = packet.astype(F32)
    for v in range(blocks):
        rows_ref[place : place + count, v * 128 : (v + 1) * 128] = packet[
            v * count : (v + 1) * count
        ]


def table_kernel(places, seqs_here, offset_ref, *refs):
    *label_refs, table_ref = refs
    first_seq = first_of(seqs_here, offset_ref)
    shard_units = label_refs[0].shape[2]
    units = shard_units * len(places)
    lanes = lane_ids(1)
    table = jnp.zeros((1, 128), F32)
    received = [(ref, n) for ref in label_refs for n in range(ref.shape[0])]
    for place, (ref, n) in zip(places, received):
        shard = lax.axis_index("tokens") ^ place
        for s in range(2):
            row = ref[n, pl.ds(first_seq + s, 1), :].astype(F32)
            row = jnp.concatenate([row, jnp.zeros((1, 128 - shard_units), F32)], axis=1)
            start = s * units + shard * shard_units
            table = jnp.where(
                (lanes >= start) & (lanes < start + shard_units), pltpu.roll(row, start, 1), table
            )
    table_ref[...] = table.astype(jnp.int32)


def load_kernel(*refs):
    count = (len(refs) - 1) // 2
    loads = [
        pltpu.make_async_copy(source, target, refs[-1].at[n])
        for n, (source, target) in enumerate(zip(refs[:count], refs[count:-1]))
    ]
    for load in loads:
        load.start()
    for load in loads:
        load.wait()


def project_kernel(encoder_ref, weight_ref, bias_ref, frame_ref):
    frame_ref[...] = (
        (
            jnp.dot(
                encoder_ref[...].reshape(-1, encoder_ref.shape[-1]),
                weight_ref[...],
                preferred_element_type=F32,
            )
            + bias_ref[...]
        )
        .astype(BF16)
        .astype(F32)
        .reshape(frame_ref.shape)
    )


def stack_kernel(*refs):
    at = 0
    for ref in refs[:-1]:
        refs[-1][at : at + ref.shape[0]] = ref[...]
        at += ref.shape[0]


def sources_of(places, refs):
    f, k = lax.axis_index("frames"), lax.axis_index("tokens")
    entries = [(ref, n) for ref in refs for n in range(ref.shape[0])]
    return [(ref, n, f ^ (place >> 8), k ^ (place & 255)) for place, (ref, n) in zip(places, entries)]


def predictor_kernel(places, *refs):
    *packet_refs, predictor_ref, rows_ref = refs
    if places is None:
        held_rows = rows_ref.shape[0] // packet_refs[0].shape[0]
        for d in range(packet_refs[0].shape[0]):
            unpack_rows(packet_refs[0][d], rows_ref, d * held_rows)
    else:
        for ref, n, f, k in sources_of(places, packet_refs):
            rows = ref[n].astype(F32)
            count = rows.shape[0] - 2
            start = (f * lax.axis_size("tokens") + k) * count
            for r in range(count):
                rows_ref[pl.ds(start + r, 1), :] = rows[r : r + 1]
    predictor_ref[...] = rows_ref[...].astype(BF16)


def entry(row_ref, place):
    row = row_ref[...].astype(F32)
    ids = lax.broadcasted_iota(jnp.int32, row.shape, 1)
    return jnp.sum(jnp.where(ids == place, row, 0.0), axis=1, keepdims=True)


def whole_number(row_ref, place):
    return entry(row_ref, place).astype(jnp.int32)[0, 0]


def first_of(seqs_here, offset_ref):
    if seqs_here is None:
        return lax.axis_index("frames") // 2 * 2
    first_seq = lax.axis_index("tokens") * seqs_here
    return first_seq if offset_ref is None else first_seq + whole_number(offset_ref, 0)


def chunk_of(seqs_here):
    f, k = lax.axis_index("frames"), lax.axis_index("tokens")
    return f if seqs_here is not None else 2 * k + (f & 1)


def block_counts(lens_ref, tokens_ref, first_seq, first_frame):
    counts = []
    for s in range(2):
        inside = first_frame < whole_number(lens_ref, first_seq + s)
        units = whole_number(tokens_ref, first_seq + s)
        counts.append(jnp.where(inside, units // SUB_UNITS + 1, 0))
    return counts


def score_kernel(
    seqs_here,
    packet_places,
    offset_ref,
    lens_ref,
    tokens_ref,
    frame_ref,
    predictor_weight_ref,
    predictor_bias_ref,
    weight_ref,
    bias_ref,
    label_table_ref,
    *refs,
):
    *packet_refs, softmax_ref, token_ref, blank_ref, label_ref, hidden_ref, inverse_ref = refs[:-6]
    parts_ref, matrix_ref, even_ref, odd_ref, labels_smem, label_sem = refs[-6:]
    label_copy = pltpu.make_async_copy(label_table_ref, labels_smem, label_sem)
    label_copy.start()
    seqs, frame_count, width = frame_ref.shape
    units = token_ref.shape[0] // seqs
    shards = lax.axis_size("tokens")
    shard_units = units // shards
    part = frame_count // 2
    steps = part + units - 1
    first_frame = chunk_of(seqs_here) * frame_count
    first_seq = first_of(seqs_here, offset_ref)
    vocab = weight_ref.shape[1]
    blank_ref[...] = jnp.zeros_like(blank_ref)
    label_ref[...] = jnp.full(label_ref.shape, NEG, F32)
    if packet_places is None:
        for s in range(seqs):
            for k in range(shards):
                packet = packet_refs[0][(first_seq + s) * shards + k]
                unpack_rows(packet, token_ref, s * units + k * shard_units)
    else:
        for ref, n, f, k in sources_of(packet_places, packet_refs):
            rows = ref[n].astype(F32)
            start = (f & 1) * units + k * shard_units
            for r in range(shard_units):
                token_ref[pl.ds(start + r, 1), :] = rows[r : r + 1]
    token_ref[...] = (
        jnp.dot(token_ref[...].astype(BF16), predictor_weight_ref[...], preferred_element_type=F32)
        + predictor_bias_ref[...]
    ).astype(BF16).astype(F32)

    counts = block_counts(lens_ref, tokens_ref, first_seq, first_frame)
    blocks = counts[0] + counts[1]
    lens = [whole_number(lens_ref, first_seq + s) for s in range(2)]
    last_units = [whole_number(tokens_ref, first_seq + s) for s in range(2)]
    lanes = lane_ids(frame_count)
    part_lanes = lane_ids(part)
    times = first_frame + lax.broadcasted_iota(jnp.int32, (frame_count, 1), 0)

    def place_of(i):
        seq = jnp.where(i >= counts[0], 1, 0)
        sub = i - seq * counts[0]
        return seq, sub, seq * (units // SUB_UNITS) + sub

    def multiply(i, logits_ref):
        seq, sub, block = place_of(i)
        frames = frame_ref[seq]
        hidden = jnp.concatenate(
            [
                jnp.tanh(frames + token_ref[pl.ds(seq * units + sub * SUB_UNITS + j, 1), :])
                for j in range(SUB_UNITS)
            ],
            axis=0,
        )
        hidden_ref[block] = hidden
        low = hidden.astype(BF16)
        logits_ref[...] = (
            jnp.dot(low, weight_ref[...], preferred_element_type=F32) + bias_ref[...]
        )

    def score(i, logits_ref):
        seq, sub, block = place_of(i)
        first_unit = sub * SUB_UNITS
        seq_len = jnp.where(seq == 0, lens[0], lens[1])
        last_unit = jnp.where(seq == 0, last_units[0], last_units[1])
        own_lanes = (part_lanes // GROUP) % 2 == seq
        logits = logits_ref[...]
        top = jnp.max(logits, axis=1, keepdims=True)
        weights = jnp.exp(logits - top)
        total = jnp.sum(weights, axis=1, keepdims=True)
        softmax_ref[block] = weights
        inverse_ref[block] = jnp.broadcast_to(1.0 / total, (weights.shape[0], 128))
        log_total = top + jnp.log(total)
        blanks = (logits[:, :1] - log_total) * LOG2E
        for j in range(SUB_UNITS):
            unit = first_unit + j
            rows = slice(j * frame_count, (j + 1) * frame_count)
            label = labels_smem[0, seq * units + unit]
            tile = logits_ref[rows, pl.ds(pl.multiple_of(label // 128 * 128, 128), 128)]
            picked = jnp.sum(
                jnp.where(lanes == label % 128, tile, 0.0), axis=1, keepdims=True
            )
            blank = blanks[rows]
            blank = jnp.where((times == seq_len - 1) & (unit < last_unit), NEG, blank)
            blank = jnp.where((times >= seq_len) | (unit > last_unit), 0.0, blank)
            step = jnp.where(
                (times >= seq_len) | (unit >= last_unit),
                NEG,
                (picked - log_total[rows]) * LOG2E,
            )
            at = (pl.ds(unit * (units + 1), part, stride=units), slice(None))
            blank = jnp.where(part_lanes < 64, blank[:part], blank[part:])
            step = jnp.where(part_lanes < 64, step[:part], step[part:])
            blank_ref[at] = jnp.where(own_lanes, blank, blank_ref[at])
            label_ref[at] = jnp.where(own_lanes, step, label_ref[at])

    in_two_stages(blocks, multiply, score, even_ref, odd_ref, label_copy.wait)
    eye = jnp.where(
        lane_ids(units) % GROUP == lax.broadcasted_iota(jnp.int32, (units, 128), 0), 0.0, NEG
    ).astype(F32)
    ahead, behind = both_ways_in_pairs(blank_ref, label_ref, units, steps, eye, eye)
    lanes = lane_ids(units)
    early = lanes < 64
    columns = jnp.where(early, behind, ahead)
    parts_ref[...] = columns
    others = pltpu.roll(jnp.where(early, ahead, behind), 64, 1)
    ways = [
        jnp.take_along_axis(
            columns, lanes // GROUP * GROUP + k, axis=1, mode="promise_in_bounds"
        )
        + others[k : k + 1, :]
        for k in range(units)
    ]
    top = functools.reduce(jnp.maximum, ways)
    total = functools.reduce(jnp.add, [jnp.exp2(way - top) for way in ways])
    matrix_ref[0, 0] = top + jnp.log2(total)


def turn_kernel(layout, offset_ref, lens_ref, tokens_ref, hidden_ref, turned_ref):
    width = hidden_ref.shape[2]
    first_frame = chunk_of(layout["seqs_here"]) * layout["frame_count"]
    first_seq = first_of(layout["seqs_here"], offset_ref)
    counts = block_counts(lens_ref, tokens_ref, first_seq, first_frame)

    def one_block(i, _):
        seq = jnp.where(i >= counts[0], 1, 0)
        block = i + seq * (layout["units"] // SUB_UNITS - counts[0])
        turned_ref[block, :width, :] = hidden_ref[block].astype(BF16).T
        turned_ref[block, width:, :] = jnp.ones((16, turned_ref.shape[2]), BF16)
        return 0

    lax.fori_loop(0, counts[0] + counts[1], one_block, 0)


def tangent_kernel(
    layout,
    offset_ref,
    lens_ref,
    tokens_ref,
    scale_ref,
    softmax_ref,
    label_table_ref,
    blank_ref,
    label_ref,
    turned_ref,
    inverse_ref,
    parts_ref,
    *refs,
):
    hops = layout["hops"]
    matrix_refs, refs = refs[: hops + 1], refs[hops + 1 :]
    (
        tangents_ref,
        output_bias_ref,
        loss_ref,
        kept_ref,
        sent_ref,
        sums_ref,
        matrices_ref,
        ahead_ref,
        behind_ref,
        blank_part_ref,
        label_part_ref,
        even_ref,
        odd_ref,
        labels_smem,
        label_sem,
    ) = refs
    label_copy = pltpu.make_async_copy(label_table_ref, labels_smem, label_sem)
    label_copy.start()
    frame_count = layout["frame_count"]
    width = turned_ref.shape[1] - 16
    units = layout["units"]
    part = frame_count // 2
    steps = part + units - 1
    here = chunk_of(layout["seqs_here"])
    first_frame = here * frame_count
    first_seq = first_of(layout["seqs_here"], offset_ref)
    chunks = matrices_ref.shape[0]
    vocab = softmax_ref.shape[2]
    received = [(ref, n) for ref in matrix_refs for n in range(ref.shape[0])]
    for place, (matrix_ref, n) in zip(layout["matrix_places"], received):
        matrices_ref[place] = matrix_ref[n, 0]
    starts = lax.broadcasted_iota(jnp.int32, (units, 128), 0)
    lanes = lane_ids(units)
    early = lanes < 64
    gather_ids = lanes // GROUP * GROUP + starts
    own_first = (lane_ids(1) // GROUP) % 2 == 0

    def through(column, matrix):
        ways = column + matrix
        top = jnp.max(ways, axis=0, keepdims=True)
        row = top + jnp.log2(jnp.sum(jnp.exp2(ways - top), axis=0, keepdims=True))
        row = jnp.broadcast_to(row, (units, 128))
        return jnp.take_along_axis(row, gather_ids, axis=1, mode="promise_in_bounds")

    def one_chunk(i, carry):
        column, kept = carry
        other = chunks - 1 - i
        kept = jnp.where(jnp.where(early, i, other) == here, column, kept)
        matrix = jnp.where(early, matrices_ref[here ^ i], matrices_ref[here ^ other])
        return through(column, matrix), kept

    start = jnp.where(early & (starts > 0), NEG, 0.0).astype(F32)
    last, kept = lax.fori_loop(0, chunks, one_chunk, (start, start))
    middle = pltpu.roll(through(kept, parts_ref[...]), 64, 1)
    both_ways(
        blank_ref,
        label_ref,
        units,
        steps,
        jnp.where(early, kept, middle),
        jnp.where(early, middle, kept),
        (ahead_ref, behind_ref),
    )
    log_norm = jnp.max(jnp.where(early, last, pltpu.roll(last, 64, 1)), axis=0, keepdims=True)
    scale, length, bound = (
        jnp.where(own_first, entry(ref, first_seq), entry(ref, first_seq + 1))
        for ref in (scale_ref, lens_ref, tokens_ref)
    )
    length, bound = length.astype(jnp.int32), bound.astype(jnp.int32)
    part_start = first_frame + jnp.where(lane_ids(1) < 64, 0, part)
    last_diagonal = starts + jnp.minimum(length - part_start, part)
    first_blank = jnp.where(starts <= bound, starts, steps)
    first_label = jnp.where(starts < bound, starts, steps)
    norm = log_norm - jnp.log2(scale)

    def one_diagonal(e, _):
        rows = pl.ds(pl.multiple_of(e * units, 8), units)
        behind = behind_ref[rows, :]
        base = ahead_ref[rows, :] - norm
        before_end = last_diagonal > e
        blank_part_ref[rows, :] = jnp.where(
            before_end & (first_blank <= e), jnp.exp2(base + blank_ref[rows, :] + behind), 0.0
        )
        label_part_ref[rows, :] = jnp.where(
            before_end & (first_label <= e),
            jnp.exp2(base + label_ref[rows, :] + pltpu.roll(behind, units - 1, 0)),
            0.0,
        )
        return 0

    lax.fori_loop(0, steps, one_diagonal, 0, unroll=5)

    counts = block_counts(lens_ref, tokens_ref, first_seq, first_frame)
    block_lanes = lane_ids(frame_count)
    part_lanes = lane_ids(part)

    def place_of(i):
        seq = jnp.where(i >= counts[0], 1, 0)
        sub = i - seq * counts[0]
        return seq, sub, seq * (units // SUB_UNITS) + sub

    wide = lane_ids(1)
    loss = jnp.where(here == 0, -log_norm * LN2, 0.0)
    spread = jnp.where(wide == first_seq, loss[:, :1], 0.0)
    loss_ref[...] = spread + jnp.where(wide == first_seq + 1, loss[:, GROUP : GROUP + 1], 0.0)
    label_copy.wait()

    counts_all = counts[0] + counts[1]
    sums_ref[...] = jnp.zeros_like(sums_ref)
    output_bias_ref[...] = jnp.zeros_like(output_bias_ref)

    def prepare(i, tangent_ref):
        seq, sub, block = place_of(i)
        own_lanes = [part_lanes % GROUP + GROUP * (seq + 2 * half) for half in (0, 1)]
        for j in range(SUB_UNITS):
            unit = sub * SUB_UNITS + j
            rows = slice(j * frame_count, (j + 1) * frame_count)
            at = (pl.ds(unit * (units + 1), part, stride=units), slice(None))
            blank, step = (
                jnp.concatenate(
                    [
                        jnp.take_along_axis(ref[at], ids, axis=1, mode="promise_in_bounds")
                        for ids in own_lanes
                    ],
                    axis=0,
                )
                for ref in (blank_part_ref, label_part_ref)
            )
            both = (blank + step) * inverse_ref[block, rows, :]
            for v in range(vocab // 128):
                cut = slice(v * 128, (v + 1) * 128)
                piece = softmax_ref[block, rows, cut] * both
                if v == 0:
                    piece = piece - jnp.where(block_lanes == 0, blank, 0.0)
                piece = piece.astype(BF16)
                tangent_ref[rows, cut] = piece
                tangents_ref[block, rows, cut] = piece
            label = labels_smem[0, seq * units + unit]
            cut = pl.ds(pl.multiple_of(label // 128 * 128, 128), 128)
            piece = softmax_ref[block, rows, cut] * both
            piece = piece - jnp.where((block_lanes == 0) & (label < 128), blank, 0.0)
            piece = (piece - jnp.where(block_lanes == label % 128, step, 0.0)).astype(BF16)
            tangent_ref[rows, cut] = piece
            tangents_ref[block, rows, cut] = piece

    def multiply(i, tangent_ref):
        _, _, block = place_of(i)
        product = jnp.dot(turned_ref[block], tangent_ref[...], preferred_element_type=F32)
        for v in range(vocab // 128):
            sums_ref[v * width : (v + 1) * width, :] += product[:width, v * 128 : (v + 1) * 128]
        output_bias_ref[...] += product[width : width + 1, :]

    in_two_stages(counts_all, prepare, multiply, even_ref, odd_ref)
    part_halves(sums_ref, kept_ref, sent_ref)


def part_halves(sums_ref, kept_ref, sent_ref):
    half = kept_ref.shape[0]
    place = lax.axis_index("tokens") & 1
    sent_ref[:half, :] = sums_ref[pl.ds(pl.multiple_of((1 - place) * half, 8), half), :]
    kept_ref[...] = sums_ref[pl.ds(pl.multiple_of(place * half, 8), half), :]


def inner_kernel(
    layout,
    offset_ref,
    lens_ref,
    tokens_ref,
    tangents_ref,
    hidden_ref,
    weight_ref,
    encoder_ref,
    output_bias_ref,
    loss_ref,
    frame_tangent_ref,
    exact_ref,
    kept_ref,
    sent_ref,
    sums_ref,
    frame_sum_ref,
    token_sum_ref,
    even_ref,
    odd_ref,
):
    seqs, frame_count, width = encoder_ref.shape
    units = token_sum_ref.shape[0] // seqs
    vocab = weight_ref.shape[1]
    first_frame = chunk_of(layout["seqs_here"]) * frame_count
    first_seq = first_of(layout["seqs_here"], offset_ref)
    frame_sum_ref[...] = jnp.zeros_like(frame_sum_ref)
    token_sum_ref[...] = jnp.zeros_like(token_sum_ref)
    half = layout["half"]
    for side in (0, 1):
        unset = slice(side * half + layout["token"], (side + 1) * half)
        sums_ref[unset, :] = jnp.zeros_like(sums_ref[unset, :])
    counts = block_counts(lens_ref, tokens_ref, first_seq, first_frame)

    def place_of(i):
        seq = jnp.where(i >= counts[0], 1, 0)
        sub = i - seq * counts[0]
        return seq, sub, seq * (units // SUB_UNITS) + sub

    def product_of(tangents):
        return lax.dot_general(
            tangents, weight_ref[...], (((1,), (1,)), ((), ())), preferred_element_type=F32
        )

    def add_up(i, product):
        seq, sub, block = place_of(i)
        hidden = hidden_ref[block]
        inner = product * (1.0 - hidden * hidden)
        total = frame_sum_ref[seq]
        for j in range(SUB_UNITS):
            rows = slice(j * frame_count, (j + 1) * frame_count)
            total = total + inner[rows]
            token_sum_ref[pl.ds(seq * units + sub * SUB_UNITS + j, 1), :] = jnp.sum(
                inner[rows], axis=0, keepdims=True
            )
        frame_sum_ref[seq] = total

    def multiply_two(n, product_ref):
        both = [tangents_ref[place_of(2 * n + m)[2]] for m in (0, 1)]
        product_ref[...] = product_of(jnp.concatenate(both, axis=0))

    def add_up_two(n, product_ref):
        half = product_ref.shape[0] // 2
        add_up(2 * n, product_ref[:half])
        add_up(2 * n + 1, product_ref[half:])

    blocks = counts[0] + counts[1]
    in_two_stages(blocks // 2, multiply_two, add_up_two, even_ref, odd_ref)

    @pl.when(blocks % 2 == 1)
    def _():
        add_up(blocks - 1, product_of(tangents_ref[place_of(blocks - 1)[2]]))

    low = frame_sum_ref[...].reshape(seqs * frame_count, width).astype(BF16)
    frame_tangent_ref[...] = low
    product = lax.dot_general(
        encoder_ref[...].reshape(seqs * frame_count, width),
        low,
        (((0,), (0,)), ((), ())),
        preferred_element_type=F32,
    )
    encoder_bias = jnp.sum(low.astype(F32), axis=0, keepdims=True)
    blocks_each = width // 128 // 2
    exact_ref[...] = jnp.zeros_like(exact_ref)
    for v in range(width // 128):
        cut = slice(v * 128, (v + 1) * 128)
        start, n = v // blocks_each * half, v % blocks_each
        sums_ref[start + n * width : start + (n + 1) * width, :] = product[:, cut]
        at = start + layout["token"] + n * layout["token_rows"] + first_seq * units
        sums_ref[pl.ds(pl.multiple_of(at, 8), seqs * units), :] = token_sum_ref[:, cut]
        at = vocab // 128 + v
        exact_ref[at : at + 1, :] = encoder_bias[:, cut]
    for v in range(vocab // 128):
        exact_ref[v : v + 1, :] = output_bias_ref[:, v * 128 : (v + 1) * 128]
    at = vocab // 128 + width // 128
    exact_ref[at : at + 1, :] = loss_ref[...]
    part_halves(sums_ref, kept_ref, sent_ref)
    write_exact(sent_ref, kept_ref.shape[0], exact_ref[...])


def encoder_kernel(frame_tangent_ref, encoder_weight_ref, encoder_gradient_ref, mark_ref):
    mark_ref[...] = jnp.zeros_like(mark_ref)
    encoder_gradient_ref[...] = lax.dot_general(
        frame_tangent_ref[...],
        encoder_weight_ref[...],
        (((1,), (1,)), ((), ())),
        preferred_element_type=F32,
    ).reshape(encoder_gradient_ref.shape)


def two_halves(stage, half):
    upper = upper_of(stage)
    own = pl.ds(pl.multiple_of(jnp.where(upper != 0, half, 0), 16), half)
    other = pl.ds(pl.multiple_of(jnp.where(upper != 0, 0, half), 16), half)
    return own, other


def exact_rows(kind):
    return EXACT if kind == F32 else 3 * EXACT


def write_exact(sent_ref, at, values):
    if sent_ref.dtype == F32:
        sent_ref[at : at + EXACT, :] = values
        return
    for n in range(3):
        part = values.astype(BF16)
        sent_ref[at + n * EXACT : at + (n + 1) * EXACT, :] = part
        values = values - part.astype(F32)


def read_exact(received_ref, at):
    parts = [
        received_ref[at + n * EXACT : at + (n + 1) * EXACT, :].astype(F32)
        for n in range(exact_rows(received_ref.dtype) // EXACT)
    ]
    return sum(parts[1:], parts[0])


def halve_kernel(stages, merge, has_exact, *refs):
    count, at = len(stages), 0
    outs = refs[2 * count + has_exact :]
    for n, stage in enumerate(stages):
        kept_ref, received_ref = refs[2 * n : 2 * n + 2]
        half = kept_ref.shape[0] // 2
        own, other = two_halves(stage, half)
        if merge:
            next_ref, sent_ref = (ref.at[at : at + half, :] for ref in outs[:2])
            at += half
        else:
            next_ref, sent_ref = outs[2 * n : 2 * n + 2]
        sent = kept_ref[other, :] + received_ref[other, :].astype(F32)
        sent_ref[:half, :] = sent.astype(sent_ref.dtype)
        next_ref[...] = kept_ref[own, :] + received_ref[own, :].astype(F32)
    if has_exact:
        exact = refs[2 * count][...] + read_exact(received_ref, kept_ref.shape[0])
        outs[-1][...] = exact
        write_exact(outs[-2], outs[-3].shape[0], exact)


def add_kernel(count, *refs):
    sum_ref, exact_sum_ref = refs[-2:]
    at = 0
    for n in range(count):
        kept_ref, received_ref = refs[2 * n : 2 * n + 2]
        rows = kept_ref.shape[0]
        total = kept_ref[...] + received_ref[:rows, :].astype(F32)
        high = total.astype(BF16)
        sum_ref[at : at + rows, :] = high
        at += rows
    sum_ref[at : at + rows, :] = (total - high.astype(F32)).astype(BF16)
    exact = refs[2 * count][...] + read_exact(received_ref, rows)
    exact_sum_ref[...] = exact
    write_exact(sum_ref, at + rows, exact)


def last_kernel(own_ref, other_ref, exact_ref, *sum_refs):
    *sum_refs, exact_sum_ref = sum_refs
    at = 0
    for n, sum_ref in enumerate(sum_refs):
        rows = sum_ref.shape[0]
        totals = []
        for ref in (own_ref, other_ref):
            total = ref[at : at + rows, :].astype(F32)
            if n == len(sum_refs) - 1:
                total = total + ref[at + rows : at + 2 * rows, :].astype(F32)
            totals.append(total)
        sum_ref[...] = (totals[0] + totals[1]).astype(BF16)
        at += rows
    exact_sum_ref[...] = exact_ref[...] + read_exact(other_ref, at + rows)


def join_kernel(stages, merged, *refs):
    count, at = len(stages), 0
    joined_refs = refs[-count:]
    for n, (stage, joined_ref) in enumerate(zip(stages, joined_refs)):
        half = joined_ref.shape[0] // 2
        own, other = two_halves(stage, half)
        if merged:
            own_ref, other_ref = (ref.at[at : at + half, :] for ref in refs[:2])
            at += half
        else:
            own_ref, other_ref = refs[2 * n : 2 * n + 2]
        joined_ref[own, :] = own_ref[...]
        joined_ref[other, :] = other_ref[...]


def copy_out(output_ref, rest_ref, side, output_hbm, encoder_hbm, output_buffer, encoder_buffer, sems):
    copies = []
    for source, buffer, target in (
        (output_ref, output_buffer, output_hbm),
        (rest_ref, encoder_buffer, encoder_hbm),
    ):
        rows, columns = buffer.shape
        for v in range(columns // 128):
            buffer[:, v * 128 : (v + 1) * 128] = source[v * rows : (v + 1) * rows, :].astype(F32)
        start = pl.multiple_of(side * columns, 128)
        copy = pltpu.make_async_copy(
            buffer, target.at[:, pl.ds(start, columns)], sems.at[len(copies)]
        )
        copy.start()
        copies.append(copy)
    return copies


def finish_own_kernel(
    output_ref,
    rest_ref,
    exact_ref,
    output_hbm,
    encoder_hbm,
    output_bias_hbm,
    encoder_bias_hbm,
    losses_hbm,
    output_buffer,
    encoder_buffer,
    output_bias_ref,
    encoder_bias_ref,
    losses_ref,
    sems,
):
    place = lax.axis_index("tokens") & 1
    copies = copy_out(
        output_ref,
        rest_ref,
        place,
        output_hbm,
        encoder_hbm,
        output_buffer,
        encoder_buffer,
        sems,
    )

    def rows(start, count):
        return jnp.concatenate([exact_ref[start + n : start + n + 1, :] for n in range(count)], axis=1)

    output_blocks, encoder_blocks = output_bias_ref.shape[1] // 128, encoder_bias_ref.shape[1] // 128
    output_bias_ref[...] = rows(0, output_blocks)
    encoder_bias_ref[...] = rows(output_blocks, encoder_blocks)
    loss = rows(output_blocks + encoder_blocks, 1)
    losses_ref[...] = jnp.sum(
        jnp.where(lane_ids(1) == lax.axis_index("frames"), loss, 0.0), axis=1, keepdims=True
    )
    for source, target in (
        (output_bias_ref, output_bias_hbm),
        (encoder_bias_ref, encoder_bias_hbm),
        (losses_ref, losses_hbm),
    ):
        copy = pltpu.make_async_copy(source, target, sems.at[len(copies)])
        copy.start()
        copies.append(copy)
    for copy in copies:
        copy.wait()


def finish_kernel(
    layout,
    output_other_ref,
    rest_own_ref,
    rest_other_ref,
    predictor_ref,
    predictor_weight_ref,
    output_weight_begun,
    encoder_weight_begun,
    output_weight_hbm,
    encoder_weight_hbm,
    weight_gradient_hbm,
    bias_gradient_hbm,
    predictor_gradient_hbm,
    output_buffer,
    encoder_buffer,
    weight_gradient_ref,
    bias_gradient_ref,
    predictor_gradient_ref,
    tokens_ref,
    sems,
):
    width = encoder_buffer.shape[0]
    place = lax.axis_index("tokens") & 1
    copies = copy_out(
        output_other_ref,
        rest_other_ref,
        1 - place,
        output_weight_hbm,
        encoder_weight_hbm,
        output_buffer,
        encoder_buffer,
        sems,
    )
    count = layout["token_rows"]
    blocks_each = width // 128 // 2

    def gather_tokens(*halves):
        for v in range(width // 128):
            at = layout["token"] + v % blocks_each * count
            tokens_ref[:, v * 128 : (v + 1) * 128] = halves[v // blocks_each][
                at : at + count, :
            ].astype(F32)

    pl.when(place == 0)(lambda: gather_tokens(rest_own_ref, rest_other_ref))
    pl.when(place == 1)(lambda: gather_tokens(rest_other_ref, rest_own_ref))
    tokens = tokens_ref[...]
    held_rows = predictor_gradient_ref.shape[0]

    def send(source, target):
        copy = pltpu.make_async_copy(source, target, sems.at[len(copies)])
        copy.start()
        copies.append(copy)

    weight_gradient_ref[...] = lax.dot_general(
        predictor_ref[...],
        tokens.astype(BF16),
        (((0,), (0,)), ((), ())),
        preferred_element_type=F32,
    )
    send(weight_gradient_ref, weight_gradient_hbm)
    bias_gradient_ref[...] = jnp.sum(tokens, axis=0, keepdims=True)
    send(bias_gradient_ref, bias_gradient_hbm)
    device = lax.axis_index("frames") * lax.axis_size("tokens") + lax.axis_index("tokens")
    mine = jnp.concatenate(
        [tokens_ref[pl.ds(device * held_rows + r, 1), :] for r in range(held_rows)], axis=0
    )
    predictor_gradient_ref[:, 0, :] = lax.dot_general(
        mine.astype(BF16),
        predictor_weight_ref[...],
        (((1,), (1,)), ((), ())),
        preferred_element_type=F32,
    )
    send(predictor_gradient_ref, predictor_gradient_hbm)
    for copy in copies:
        copy.wait()


def in_hbm(array):
    return pltpu.with_memory_space_constraint(array, pltpu.HBM)


def in_vmem(array):
    return pltpu.with_memory_space_constraint(array, pltpu.VMEM)


def permuted(array, partner):
    frames, tokens = lax.axis_size("frames"), lax.axis_size("tokens")
    pairs = []
    for f in range(frames):
        for k in range(tokens):
            g, h = partner(f, k)
            pairs.append((f * tokens + k, g * tokens + h))
    return lax.ppermute(array, AXES, pairs)


def axis_flips(axis):
    flips, bit = [], lax.axis_size(axis) // 2
    while bit:
        flips.append(((bit, 0) if axis == "frames" else (0, bit), bit))
        bit //= 2
    return flips


def stacked(blocks):
    if len(blocks) == 1:
        return blocks[0]
    shape = (sum(block.shape[0] for block in blocks),) + blocks[0].shape[1:]
    return call(stack_kernel, blocks, [(shape, blocks[0].dtype, True)])[0]


def doubled(blocks, places, flips):
    blocks, places = list(blocks), list(places)
    for bits, mark in flips:
        blocks.append(permuted(stacked(blocks), across((bits, bits))))
        places += [place ^ mark for place in places]
    return blocks, places


def stages(even, odd):
    frame_bits = [(1 << i, 0) for i in range(lax.axis_size("frames").bit_length() - 1)]
    token_bits = [(0, 1 << i) for i in range(1, lax.axis_size("tokens").bit_length() - 1)]
    first = frame_bits[:1] + token_bits + frame_bits[1:2]
    orders = [first[shift:] + first[:shift] + frame_bits[2:] for shift in (even, odd)]
    return list(zip(*orders))


def upper_of(stage):
    f, k = lax.axis_index("frames"), lax.axis_index("tokens")
    even, odd = ((f & frame_bit) | (k & token_bit) for frame_bit, token_bit in stage)
    return jnp.where((k & 1) == 0, even, odd)


def across(stage):
    return lambda f, k: (f ^ stage[k & 1][0], k ^ stage[k & 1][1])


def neighbour(f, k):
    return f, k ^ 1


def call(body, ins, outs, scratch=(), limit=4):
    vmem = pl.BlockSpec(memory_space=pltpu.VMEM)
    there = [array is not None for array in ins]

    def kernel(*refs):
        given = iter(refs)
        body(*(next(given) if here else None for here in there), *given)

    return pl.pallas_call(
        kernel,
        in_specs=[vmem] * sum(there),
        out_specs=[
            pl.BlockSpec(memory_space=pl.ANY) if inside is None else vmem for _, _, inside in outs
        ],
        out_shape=[
            pltpu.VMEM(shape, kind) if inside else jax.ShapeDtypeStruct(shape, kind)
            for shape, kind, inside in outs
        ],
        scratch_shapes=list(scratch),
        compiler_params=pltpu.CompilerParams(vmem_limit_bytes=limit * 2**20),
    )(*(in_vmem(array) for array in ins if array is not None))


def reduced_and_gathered(pieces, exact, beside, held):
    plans = list(zip(*(stages(*shifts) for shifts in ORDERS)))
    flat = [a for kept, sent in pieces for a in (kept, permuted(sent, neighbour))]
    way_back = []
    *plans, last_plan = plans
    for number, plan in enumerate(plans):
        plan = plan[: len(flat) // 2]
        merge = len(plan) > 1 and len(set(plan)) == 1
        halves = [kept.shape[0] // 2 for kept in flat[::2]]
        way_back.append((plan, merge, [2 * half for half in halves]))
        if merge:
            halves = [sum(halves)]
        sent_type = SENT_TYPES[min(number, len(SENT_TYPES) - 1)]
        outs = []
        for n, half in enumerate(halves):
            sent_rows = half + (exact_rows(sent_type) if n == len(halves) - 1 else 0)
            outs += [((half, 128), F32, True), ((sent_rows, 128), sent_type, True)]
        exact_out = ((EXACT, 128), F32, True)
        if number < 2:
            given, flat = flat, []
            for n, stage in enumerate(plan):
                last = n == len(plan) - 1
                made = call(
                    functools.partial(halve_kernel, [stage], False, last),
                    given[2 * n : 2 * n + 2] + [exact] * last,
                    outs[2 * n : 2 * n + 2] + [exact_out] * last,
                )
                flat += made[:2]
                if last:
                    exact = made[2]
        else:
            *flat, exact = call(
                functools.partial(halve_kernel, plan, merge, True),
                [*flat, exact],
                [*outs, exact_out],
            )
        flat = [
            permuted(a, across(plan[n // 2])) if n % 2 else a for n, a in enumerate(flat)
        ]
    shapes = [kept.shape for kept in flat[::2]]
    rows = sum(shape[0] for shape in shapes) + shapes[-1][0] + exact_rows(BF16)
    own, exact = call(
        functools.partial(add_kernel, len(shapes)),
        [*flat, exact, *beside],
        [((rows, 128), BF16, True), ((EXACT, 128), F32, True)],
    )
    other = permuted(own, across(last_plan[0]))
    vmem = pl.BlockSpec(memory_space=pltpu.VMEM)
    *arrays, exact = pl.pallas_call(
        last_kernel,
        in_specs=[vmem, vmem, vmem],
        out_specs=[vmem] * (len(shapes) + 1),
        out_shape=[pltpu.VMEM(shape, BF16) for shape in shapes] + [pltpu.VMEM((EXACT, 128), F32)],
        compiler_params=pltpu.CompilerParams(vmem_limit_bytes=4 * 2**20),
    )(in_vmem(own), in_vmem(other), in_vmem(exact))
    for number, (plan, merged, sizes) in reversed(list(enumerate(way_back))):
        flat = [a for array, stage in zip(arrays, plan) for a in (array, permuted(array, across(stage)))]
        outs = [((size, 128), BF16, True) for size in sizes]
        if number in (0,):
            arrays = [
                call(
                    functools.partial(join_kernel, [stage], False),
                    flat[2 * n : 2 * n + 2],
                    outs[n : n + 1],
                )[0]
                for n, stage in enumerate(plan)
            ]
        else:
            given = [*flat, *held] if number == 1 else flat
            arrays = call(functools.partial(join_kernel, plan, merged), given, outs)
    return [(array, permuted(array, neighbour)) for array in arrays], exact


def per_device(
    encoder_out,
    encoder_weight,
    encoder_bias,
    predictor_out,
    predictor_weight,
    predictor_bias,
    output_weight,
    output_bias,
    labels,
    frame_lens,
    token_lens,
    loss_scale,
):
    seq_count, frame_count, width = encoder_out.shape
    vocab = output_weight.shape[1]
    all_seqs = labels.shape[0]
    held_seqs, held_units = predictor_out.shape[:2]
    assert held_seqs == 1
    frame_axis, token_axis = lax.axis_size("frames"), lax.axis_size("tokens")
    device_count = frame_axis * token_axis
    units = held_units * token_axis
    calls = seq_count // 2
    diagonals = (frame_count // 2 + units) * units
    vmem = pl.BlockSpec(memory_space=pltpu.VMEM)
    anywhere = pl.BlockSpec(memory_space=pl.ANY)

    in_plane = seq_count == 2 and token_axis == 4 and frame_axis == 8

    def turned_over(f, k):
        return 2 * k + (f & 1), f >> 1

    weights = (
        encoder_weight,
        encoder_bias.reshape(1, width),
        predictor_weight,
        predictor_bias.reshape(1, width),
        output_weight,
        output_bias.reshape(1, vocab),
        frame_lens.reshape(1, all_seqs),
        token_lens.reshape(1, all_seqs),
        loss_scale.reshape(1, all_seqs),
    )
    if in_plane:
        plane = [((0, 2), 2), ((0, 1), 1), ((1, 0), 256)]
        encoder = permuted(encoder_out, turned_over)
        packet = pl.pallas_call(
            label_packet_kernel,
            in_specs=[anywhere] * 2,
            out_specs=vmem,
            out_shape=pltpu.VMEM((1, held_units + 2, width), BF16),
            scratch_shapes=[
                pltpu.VMEM((held_units, width), BF16),
                pltpu.VMEM(labels.shape, jnp.int32),
                pltpu.SemaphoreType.DMA((2,)),
            ],
            compiler_params=pltpu.CompilerParams(vmem_limit_bytes=4 * 2**20),
        )(in_hbm(predictor_out.reshape(held_units, width)), in_hbm(labels))
        packets, packet_places = doubled([packet], [0], plane)
        own_seqs = None
    else:
        packet_rows = held_units * width // 128
        packets = pl.pallas_call(
            packet_kernel,
            in_specs=[anywhere],
            out_specs=vmem,
            out_shape=jax.ShapeDtypeStruct((device_count, packet_rows, 128), BF16),
            scratch_shapes=[
                pltpu.VMEM((held_units, width), BF16),
                pltpu.VMEM((packet_rows, 128), F32),
                pltpu.SemaphoreType.DMA,
            ],
            compiler_params=pltpu.CompilerParams(vmem_limit_bytes=4 * 2**20),
        )(in_hbm(predictor_out.reshape(held_units, width)))
        packets, packet_places = [lax.all_to_all(packets, AXES, 0, 0, tiled=True)], None
        encoder, own_seqs = encoder_out, seq_count
    if not in_plane:
        label_blocks, label_places = doubled([labels[None]], [0], axis_flips("tokens"))
    weights = pl.pallas_call(
        load_kernel,
        in_specs=[anywhere] * len(weights),
        out_specs=[vmem] * len(weights),
        out_shape=[pltpu.VMEM(w.shape, w.dtype) for w in weights],
        scratch_shapes=[pltpu.SemaphoreType.DMA((len(weights),))],
        compiler_params=pltpu.CompilerParams(vmem_limit_bytes=4 * 2**20),
    )(*map(in_hbm, weights))
    *weights, frame_lens, token_lens, loss_scale = weights
    lens = frame_lens, token_lens
    (frames,) = call(
        project_kernel, (encoder, weights[0], weights[1]), [(encoder_out.shape, F32, True)]
    )

    score_shapes = [
        ((2 * units // SUB_UNITS, SUB_UNITS * frame_count, vocab), F32),
        ((2 * units, width), F32),
        ((diagonals, 128), F32),
        ((diagonals, 128), F32),
        ((2 * units // SUB_UNITS, SUB_UNITS * frame_count, width), F32),
        ((2 * units // SUB_UNITS, SUB_UNITS * frame_count, 128), F32),
        ((units, 128), F32),
        ((1, 1, units, 128), F32),
    ]

    def scores(offset, frames):
        if in_plane:
            body, given = functools.partial(packet_table_kernel, packet_places), packets
        else:
            body = functools.partial(table_kernel, label_places, own_seqs)
            given = (offset, *label_blocks)
        (table,) = call(body, given, [((1, 128), jnp.int32, True)])
        scored = call(
            functools.partial(score_kernel, own_seqs, packet_places),
            (offset, *lens, frames, *weights[2:], table, *packets),
            [(shape, kind, True) for shape, kind in score_shapes],
            scratch=[
                pltpu.VMEM((SUB_UNITS * frame_count, vocab), F32),
                pltpu.VMEM((SUB_UNITS * frame_count, vocab), F32),
                pltpu.SMEM((1, 128), jnp.int32),
                pltpu.SemaphoreType.DMA,
            ],
            limit=8,
        )
        return [table, *scored]

    offsets = 2 * jnp.arange(calls, dtype=jnp.int32).reshape(calls, 1, 1)
    encoders = encoder.reshape(calls, 2, frame_count, width)
    if calls == 1:
        scored = scores(None, frames)
        matrix = scored[-1]
    else:
        scored = lax.map(
            lambda given: scores(*given),
            (offsets, frames.reshape(calls, 2, frame_count, width)),
        )
        matrix = scored[-1].reshape(1, calls, units, 128)

    chunk_flips = [((0, 2), 4), ((1, 0), 1), ((0, 1), 2)] if in_plane else axis_flips("frames")
    matrices, matrix_places = doubled([matrix], [0], chunk_flips)
    if in_plane:
        packets, packet_places = doubled(
            [stacked(packets)], packet_places, [((4, 0), 1024), ((2, 0), 512)]
        )
    (predictor_all,) = call(
        functools.partial(predictor_kernel, packet_places),
        packets,
        [((all_seqs * units, width), BF16, True)],
        scratch=[pltpu.VMEM((all_seqs * units, width), F32)],
        limit=8,
    )
    layout = {"matrix_places": matrix_places, "seqs_here": own_seqs, "frame_count": frame_count, "units": units}
    align = 16 * device_count // 4
    blocks_each = width // 128 // 2
    layout["token"], layout["token_rows"] = blocks_each * width, all_seqs * units
    half = layout["token"] + blocks_each * all_seqs * units
    layout["half"] = half + (-half % align)
    rest_rows = 2 * layout["half"]
    output_rows = vocab // 128 * width
    assert output_rows % (2 * align) == 0 and vocab // 128 + width // 128 < EXACT

    blocks = 2 * units // SUB_UNITS
    block_rows = SUB_UNITS * frame_count

    def turns(offset, scored):
        hidden = scored[5]
        (turned,) = call(
            functools.partial(turn_kernel, layout),
            (offset, *lens, hidden),
            [((hidden.shape[0], width + 16, hidden.shape[1]), BF16, True)],
        )
        return turned

    def tangents(offset, scored, turned, matrices):
        table, softmax, _, blank, label, _, inverse, parts = scored
        return call(
            functools.partial(tangent_kernel, dict(layout, hops=len(matrices) - 1)),
            (
                *(offset, *lens, loss_scale, softmax, table, blank, label),
                *(turned, inverse, parts, *matrices),
            ),
            [
                ((blocks, block_rows, vocab), BF16, True),
                ((1, vocab), F32, True),
                ((1, 128), F32, True),
                ((output_rows // 2, 128), F32, True),
                ((output_rows // 2, 128), F32, True),
            ],
            scratch=[
                pltpu.VMEM((output_rows, 128), F32),
                pltpu.VMEM((frame_axis, units, 128), F32),
                pltpu.VMEM((diagonals, 128), F32),
                pltpu.VMEM((diagonals, 128), F32),
                pltpu.VMEM((diagonals, 128), F32),
                pltpu.VMEM((diagonals, 128), F32),
                pltpu.VMEM((block_rows, vocab), BF16),
                pltpu.VMEM((block_rows, vocab), BF16),
                pltpu.SMEM((1, 128), jnp.int32),
                pltpu.SemaphoreType.DMA,
            ],
            limit=12,
        )

    def inners(offset, encoder, scored, tangent, output_bias_sum, loss):
        return call(
            functools.partial(inner_kernel, layout),
            (
                *(offset, *lens, tangent, scored[5], weights[4], encoder),
                *(output_bias_sum, loss),
            ),
            [
                ((2 * frame_count, width), BF16, True),
                ((EXACT, 128), F32, True),
                ((rest_rows // 2, 128), F32, True),
                ((rest_rows // 2 + EXACT, 128), F32, True),
            ],
            scratch=[
                pltpu.VMEM((rest_rows, 128), F32),
                pltpu.VMEM((2, frame_count, width), F32),
                pltpu.VMEM((2 * units, width), F32),
                pltpu.VMEM((2 * block_rows, width), F32),
                pltpu.VMEM((2 * block_rows, width), F32),
            ],
            limit=10,
        )

    def encoder_gradient_of(frame_tangent):
        return call(
            encoder_kernel,
            (frame_tangent, weights[0]),
            [((2, frame_count, width), F32, False), ((8, 128), F32, True)],
        )

    if calls == 1:
        scored = scored[:-1]
        turned = turns(None, scored)
        tangent, output_bias_sum, loss, *output_sums = tangents(None, scored, turned, matrices)

        frame_tangent, exact, *rest = inners(
            None, encoder, scored, tangent, output_bias_sum, loss
        )
        sums = [*output_sums, *rest, exact]
        if in_plane:
            frame_tangent = permuted(frame_tangent, turned_over)
        encoder_gradient, mark = encoder_gradient_of(frame_tangent)
        beside, held = [frame_tangent], [predictor_all, mark]
    else:

        def add_call(sums, given):
            offset, encoder, scored, call = given
            own = [lax.dynamic_slice_in_dim(m, call, 1, 1) for m in matrices]
            turned = turns(offset, scored)
            tangent, output_bias_sum, loss, *more = tangents(offset, scored, turned, own)
            frame_tangent, exact, *rest = inners(
                offset, encoder, scored, tangent, output_bias_sum, loss
            )
            sums = [a + b for a, b in zip(sums, [*more, *rest, exact])]
            return sums, encoder_gradient_of(frame_tangent)[0]

        sizes = (output_rows // 2,) * 2 + (rest_rows // 2, rest_rows // 2 + EXACT, EXACT)
        sums, encoder_gradient = lax.scan(
            add_call,
            [jnp.zeros((size, 128), F32) for size in sizes],
            (offsets, encoders, scored[:-1], jnp.arange(calls)),
        )
        encoder_gradient = encoder_gradient.reshape(encoder_out.shape)
        beside, held = [], [predictor_all]

    halves, exact = reduced_and_gathered(
        [sums[:2], sums[2:4]], sums[4], beside, held
    )
    (output_own, output_other), (rest_own, rest_other) = halves
    buffers = [
        pltpu.VMEM((width, vocab // 2), F32),
        pltpu.VMEM((width, width // 2), F32),
    ]
    *begun, output_bias_gradient, encoder_bias_gradient, losses = call(
        finish_own_kernel,
        (output_own, rest_own, exact),
        [
            ((width, vocab), F32, None),
            ((width, width), F32, None),
            ((1, vocab), F32, None),
            ((1, width), F32, None),
            ((1, 1), F32, None),
        ],
        scratch=[
            *buffers,
            pltpu.VMEM((1, vocab), F32),
            pltpu.VMEM((1, width), F32),
            pltpu.VMEM((1, 1), F32),
            pltpu.SemaphoreType.DMA((5,)),
        ],
        limit=8,
    )
    shapes = [(width, vocab), (width, width), (width, width), (1, width), (held_units, 1, width)]
    finished = pl.pallas_call(
        functools.partial(finish_kernel, layout),
        in_specs=[vmem] * 5 + [anywhere] * 2,
        out_specs=[anywhere] * len(shapes),
        out_shape=[jax.ShapeDtypeStruct(shape, F32) for shape in shapes],
        input_output_aliases={5: 0, 6: 1},
        scratch_shapes=[
            *buffers,
            *(pltpu.VMEM(shape, F32) for shape in shapes[2:]),
            pltpu.VMEM((all_seqs * units, width), F32),
            pltpu.SemaphoreType.DMA((5,)),
        ],
        compiler_params=pltpu.CompilerParams(vmem_limit_bytes=20 * 2**20),
    )(
        *map(in_vmem, (output_other, rest_own, rest_other, predictor_all, weights[2])),
        *map(in_hbm, begun),
    )
    return (
        losses.reshape(1),
        encoder_gradient,
        finished[4].transpose(1, 0, 2),
        finished[1],
        encoder_bias_gradient.reshape(width),
        finished[2],
        finished[3].reshape(width),
        finished[0],
        output_bias_gradient.reshape(vocab),
    )


def solution(mesh):
    placed = (
        P("tokens", "frames", None),
        P(),
        P(),
        P("frames", "tokens", None),
        P(),
        P(),
        P(),
        P(),
        P(None, "tokens"),
        P(),
        P(),
        P(),
    )
    return jax.shard_map(
        per_device,
        mesh=mesh,
        in_specs=placed,
        out_specs=(
            P("frames"),
            P("tokens", "frames", None),
            P("frames", "tokens", None),
            P(),
            P(),
            P(),
            P(),
            P(),
            P(),
        ),
        check_vma=False,
    )
```

```python
import functools

import jax
import jax.numpy as jnp
from jax import lax
from jax.experimental import pallas as pl
from jax.experimental.pallas import tpu as pltpu
from jax.sharding import PartitionSpec as P

NEG = -1e30
LOG2E = 1.4426950408889634
LN2 = 0.6931471805599453
BF16 = jnp.bfloat16
F32 = jnp.float32
GROUP = 32
SUB_UNITS = 4
ORDERS = ((0, 1), (2, 1))
SENT_TYPES = (jnp.bfloat16, jnp.bfloat16, jnp.float32)
EXACT = 16
AXES = ("frames", "tokens")


def lane_ids(rows):
    return lax.broadcasted_iota(jnp.int32, (rows, 128), 1)


def log2_add(a, b):
    return jnp.maximum(a, b) + jnp.log2(1.0 + jnp.exp2(-jnp.abs(a - b)))


def both_ways(blank_ref, label_ref, units, steps, ahead, behind, keep):
    def one_step(i, state):
        ahead, behind = state
        back = steps - 1 - i
        here = pl.ds(pl.multiple_of(i * units, 8), units)
        there = pl.ds(pl.multiple_of(back * units, 8), units)
        keep[0][here, :] = ahead
        keep[1][there, :] = behind
        from_left = pltpu.roll(ahead + label_ref[here, :], 1, 0)
        to_right = pltpu.roll(behind, units - 1, 0) + label_ref[there, :]
        ahead = log2_add(ahead + blank_ref[here, :], from_left)
        behind = log2_add(behind + blank_ref[there, :], to_right)
        return ahead, behind

    return lax.fori_loop(0, steps, one_step, (ahead, behind))


def log2_add_three(a, b, c):
    top = jnp.maximum(jnp.maximum(a, b), c)
    return top + jnp.log2(jnp.exp2(a - top) + jnp.exp2(b - top) + jnp.exp2(c - top))


def both_ways_in_pairs(blank_ref, label_ref, units, steps, ahead, behind):
    pairs = -(-steps // 2)

    def rows_of(ref, diagonal):
        return ref[pl.ds(pl.multiple_of(diagonal * units, 8), units), :]

    def up(array, by=1):
        return pltpu.roll(array, by, 0)

    def down(array, by=1):
        return pltpu.roll(array, units - by, 0)

    def scores_of(first):
        return [rows_of(ref, first + n) for ref in (blank_ref, label_ref) for n in (0, 1)]

    def ways_ahead(i):
        blank, blank_next, label, label_next = scores_of(2 * i)
        one = log2_add(up(blank + label_next), up(label) + blank_next)
        return blank + blank_next, one, up(up(label) + label_next)

    def ways_behind(i):
        blank, blank_next, label, label_next = scores_of(2 * (pairs - 1 - i))
        one = log2_add(blank + label_next, label + down(blank_next))
        return blank + blank_next, one, label + down(label_next)

    def one_pair(i, state):
        ahead, behind, (none, one, two), (none_back, one_back, two_back) = state
        following = jnp.minimum(i + 1, pairs - 1)
        ahead = log2_add_three(ahead + none, up(ahead) + one, up(ahead, 2) + two)
        behind = log2_add_three(
            behind + none_back, down(behind) + one_back, down(behind, 2) + two_back
        )
        return ahead, behind, ways_ahead(following), ways_behind(following)

    start = ahead, behind, ways_ahead(0), ways_behind(0)
    return lax.fori_loop(0, pairs, one_pair, start)[:2]


def in_two_stages(count, first, second, even, odd, between=None):
    def two_blocks(n, _):
        first(2 * n + 1, odd)
        second(2 * n, even)
        first(2 * n + 2, even)
        second(2 * n + 1, odd)
        return 0

    @pl.when(count > 0)
    def _():
        first(0, even)

    if between is not None:
        between()

    @pl.when(count > 0)
    def _():
        lax.fori_loop(0, (count - 1) // 2, two_blocks, 0)

        @pl.when(count % 2 == 1)
        def _():
            second(count - 1, even)

        @pl.when(count % 2 == 0)
        def _():
            first(count - 1, odd)
            second(count - 2, even)
            second(count - 1, odd)


def packet_kernel(predictor_hbm, packets_ref, predictor_ref, packet_ref, sem):
    load = pltpu.make_async_copy(predictor_hbm, predictor_ref, sem)
    load.start()
    load.wait()
    rows, width = predictor_ref.shape
    for v in range(width // 128):
        packet_ref[v * rows : (v + 1) * rows, :] = predictor_ref[
            :, v * 128 : (v + 1) * 128
        ].astype(F32)
    packet = packet_ref[...].astype(BF16)
    for d in range(packets_ref.shape[0]):
        packets_ref[d] = packet


def label_packet_kernel(predictor_hbm, labels_hbm, packet_ref, predictor_ref, labels_ref, sems):
    loads = [
        pltpu.make_async_copy(predictor_hbm, predictor_ref, sems.at[0]),
        pltpu.make_async_copy(labels_hbm, labels_ref, sems.at[1]),
    ]
    for load in loads:
        load.start()
    for load in loads:
        load.wait()
    seqs, units = labels_ref.shape
    width = packet_ref.shape[2]
    flat = jnp.zeros((1, width), F32)
    for s in range(seqs):
        row = labels_ref[s : s + 1, :].astype(F32)
        row = jnp.concatenate([row, jnp.zeros((1, width - units), F32)], axis=1)
        flat = flat + (pltpu.roll(row, s * units, 1) if s else row)
    high = jnp.floor(flat * (1.0 / 32.0))
    packet_ref[0] = jnp.concatenate(
        [predictor_ref[...].astype(F32), high, flat - high * 32.0], axis=0
    ).astype(BF16)


def packet_table_kernel(places, *refs):
    *packet_refs, table_ref = refs
    first_seq = first_of(None, None)
    held_units, width = packet_refs[0].shape[1] - 2, packet_refs[0].shape[2]
    units = held_units * lax.axis_size("tokens")
    lanes = lane_ids(1)
    table = jnp.zeros((1, 128), F32)
    for ref, n, f, k in sources_of(places, packet_refs):
        halves = ref[n].astype(F32)[held_units:]
        row = halves[:1] * 32.0 + halves[1:2]
        for s in range(2):
            start = s * units + k * held_units
            shift = start - (first_seq + s) * held_units
            shifted = pltpu.roll(row, jnp.where(shift < 0, shift + width, shift), 1)[:, :128]
            table = jnp.where((lanes >= start) & (lanes < start + held_units), shifted, table)
    table_ref[...] = table.astype(jnp.int32)


def unpack_rows(packet, rows_ref, place):
    blocks = rows_ref.shape[1] // 128
    count = packet.shape[0] // blocks
    packet = packet.astype(F32)
    for v in range(blocks):
        rows_ref[place : place + count, v * 128 : (v + 1) * 128] = packet[
            v * count : (v + 1) * count
        ]


def table_kernel(places, seqs_here, offset_ref, *refs):
    *label_refs, table_ref = refs
    first_seq = first_of(seqs_here, offset_ref)
    shard_units = label_refs[0].shape[2]
    units = shard_units * len(places)
    lanes = lane_ids(1)
    table = jnp.zeros((1, 128), F32)
    received = [(ref, n) for ref in label_refs for n in range(ref.shape[0])]
    for place, (ref, n) in zip(places, received):
        shard = lax.axis_index("tokens") ^ place
        for s in range(2):
            row = ref[n, pl.ds(first_seq + s, 1), :].astype(F32)
            row = jnp.concatenate([row, jnp.zeros((1, 128 - shard_units), F32)], axis=1)
            start = s * units + shard * shard_units
            table = jnp.where(
                (lanes >= start) & (lanes < start + shard_units), pltpu.roll(row, start, 1), table
            )
    table_ref[...] = table.astype(jnp.int32)


def load_kernel(*refs):
    count = (len(refs) - 1) // 2
    loads = [
        pltpu.make_async_copy(source, target, refs[-1].at[n])
        for n, (source, target) in enumerate(zip(refs[:count], refs[count:-1]))
    ]
    for load in loads:
        load.start()
    for load in loads:
        load.wait()


def project_kernel(encoder_ref, weight_ref, bias_ref, frame_ref):
    frame_ref[...] = (
        (
            jnp.dot(
                encoder_ref[...].reshape(-1, encoder_ref.shape[-1]),
                weight_ref[...],
                preferred_element_type=F32,
            )
            + bias_ref[...]
        )
        .astype(BF16)
        .astype(F32)
        .reshape(frame_ref.shape)
    )


def stack_kernel(*refs):
    at = 0
    for ref in refs[:-1]:
        refs[-1][at : at + ref.shape[0]] = ref[...]
        at += ref.shape[0]


def sources_of(places, refs):
    f, k = lax.axis_index("frames"), lax.axis_index("tokens")
    entries = [(ref, n) for ref in refs for n in range(ref.shape[0])]
    return [(ref, n, f ^ (place >> 8), k ^ (place & 255)) for place, (ref, n) in zip(places, entries)]


def predictor_kernel(places, *refs):
    *packet_refs, predictor_ref, rows_ref = refs
    if places is None:
        held_rows = rows_ref.shape[0] // packet_refs[0].shape[0]
        for d in range(packet_refs[0].shape[0]):
            unpack_rows(packet_refs[0][d], rows_ref, d * held_rows)
    else:
        for ref, n, f, k in sources_of(places, packet_refs):
            rows = ref[n].astype(F32)
            count = rows.shape[0] - 2
            start = (f * lax.axis_size("tokens") + k) * count
            for r in range(count):
                rows_ref[pl.ds(start + r, 1), :] = rows[r : r + 1]
    predictor_ref[...] = rows_ref[...].astype(BF16)


def entry(row_ref, place):
    row = row_ref[...].astype(F32)
    ids = lax.broadcasted_iota(jnp.int32, row.shape, 1)
    return jnp.sum(jnp.where(ids == place, row, 0.0), axis=1, keepdims=True)


def whole_number(row_ref, place):
    return entry(row_ref, place).astype(jnp.int32)[0, 0]


def first_of(seqs_here, offset_ref):
    if seqs_here is None:
        return lax.axis_index("frames") // 2 * 2
    first_seq = lax.axis_index("tokens") * seqs_here
    return first_seq if offset_ref is None else first_seq + whole_number(offset_ref, 0)


def chunk_of(seqs_here):
    f, k = lax.axis_index("frames"), lax.axis_index("tokens")
    return f if seqs_here is not None else 2 * k + (f & 1)


def block_counts(lens_ref, tokens_ref, first_seq, first_frame):
    counts = []
    for s in range(2):
        inside = first_frame < whole_number(lens_ref, first_seq + s)
        units = whole_number(tokens_ref, first_seq + s)
        counts.append(jnp.where(inside, units // SUB_UNITS + 1, 0))
    return counts


def score_kernel(
    seqs_here,
    packet_places,
    offset_ref,
    lens_ref,
    tokens_ref,
    frame_ref,
    predictor_weight_ref,
    predictor_bias_ref,
    weight_ref,
    bias_ref,
    label_table_ref,
    *refs,
):
    *packet_refs, softmax_ref, token_ref, blank_ref, label_ref, hidden_ref, inverse_ref = refs[:-6]
    parts_ref, matrix_ref, even_ref, odd_ref, labels_smem, label_sem = refs[-6:]
    label_copy = pltpu.make_async_copy(label_table_ref, labels_smem, label_sem)
    label_copy.start()
    seqs, frame_count, width = frame_ref.shape
    units = token_ref.shape[0] // seqs
    shards = lax.axis_size("tokens")
    shard_units = units // shards
    part = frame_count // 2
    steps = part + units - 1
    first_frame = chunk_of(seqs_here) * frame_count
    first_seq = first_of(seqs_here, offset_ref)
    vocab = weight_ref.shape[1]
    blank_ref[...] = jnp.zeros_like(blank_ref)
    label_ref[...] = jnp.full(label_ref.shape, NEG, F32)
    if packet_places is None:
        for s in range(seqs):
            for k in range(shards):
                packet = packet_refs[0][(first_seq + s) * shards + k]
                unpack_rows(packet, token_ref, s * units + k * shard_units)
    else:
        for ref, n, f, k in sources_of(packet_places, packet_refs):
            rows = ref[n].astype(F32)
            start = (f & 1) * units + k * shard_units
            for r in range(shard_units):
                token_ref[pl.ds(start + r, 1), :] = rows[r : r + 1]
    token_ref[...] = (
        jnp.dot(token_ref[...].astype(BF16), predictor_weight_ref[...], preferred_element_type=F32)
        + predictor_bias_ref[...]
    ).astype(BF16).astype(F32)

    counts = block_counts(lens_ref, tokens_ref, first_seq, first_frame)
    blocks = counts[0] + counts[1]
    lens = [whole_number(lens_ref, first_seq + s) for s in range(2)]
    last_units = [whole_number(tokens_ref, first_seq + s) for s in range(2)]
    lanes = lane_ids(frame_count)
    part_lanes = lane_ids(part)
    times = first_frame + lax.broadcasted_iota(jnp.int32, (frame_count, 1), 0)

    def place_of(i):
        seq = jnp.where(i >= counts[0], 1, 0)
        sub = i - seq * counts[0]
        return seq, sub, seq * (units // SUB_UNITS) + sub

    def multiply(i, logits_ref):
        seq, sub, block = place_of(i)
        frames = frame_ref[seq]
        hidden = jnp.concatenate(
            [
                jnp.tanh(frames + token_ref[pl.ds(seq * units + sub * SUB_UNITS + j, 1), :])
                for j in range(SUB_UNITS)
            ],
            axis=0,
        )
        hidden_ref[block] = hidden
        low = hidden.astype(BF16)
        logits_ref[...] = (
            jnp.dot(low, weight_ref[...], preferred_element_type=F32) + bias_ref[...]
        )

    def score(i, logits_ref):
        seq, sub, block = place_of(i)
        first_unit = sub * SUB_UNITS
        seq_len = jnp.where(seq == 0, lens[0], lens[1])
        last_unit = jnp.where(seq == 0, last_units[0], last_units[1])
        own_lanes = (part_lanes // GROUP) % 2 == seq
        logits = logits_ref[...]
        top = jnp.max(logits, axis=1, keepdims=True)
        weights = jnp.exp(logits - top)
        total = jnp.sum(weights, axis=1, keepdims=True)
        softmax_ref[block] = weights
        inverse_ref[block] = jnp.broadcast_to(1.0 / total, (weights.shape[0], 128))
        log_total = top + jnp.log(total)
        blanks = (logits[:, :1] - log_total) * LOG2E
        for j in range(SUB_UNITS):
            unit = first_unit + j
            rows = slice(j * frame_count, (j + 1) * frame_count)
            label = labels_smem[0, seq * units + unit]
            tile = logits_ref[rows, pl.ds(pl.multiple_of(label // 128 * 128, 128), 128)]
            picked = jnp.sum(
                jnp.where(lanes == label % 128, tile, 0.0), axis=1, keepdims=True
            )
            blank = blanks[rows]
            blank = jnp.where((times == seq_len - 1) & (unit < last_unit), NEG, blank)
            blank = jnp.where((times >= seq_len) | (unit > last_unit), 0.0, blank)
            step = jnp.where(
                (times >= seq_len) | (unit >= last_unit),
                NEG,
                (picked - log_total[rows]) * LOG2E,
            )
            at = (pl.ds(unit * (units + 1), part, stride=units), slice(None))
            blank = jnp.where(part_lanes < 64, blank[:part], blank[part:])
            step = jnp.where(part_lanes < 64, step[:part], step[part:])
            blank_ref[at] = jnp.where(own_lanes, blank, blank_ref[at])
            label_ref[at] = jnp.where(own_lanes, step, label_ref[at])

    in_two_stages(blocks, multiply, score, even_ref, odd_ref, label_copy.wait)
    eye = jnp.where(
        lane_ids(units) % GROUP == lax.broadcasted_iota(jnp.int32, (units, 128), 0), 0.0, NEG
    ).astype(F32)
    ahead, behind = both_ways_in_pairs(blank_ref, label_ref, units, steps, eye, eye)
    lanes = lane_ids(units)
    early = lanes < 64
    columns = jnp.where(early, behind, ahead)
    parts_ref[...] = columns
    others = pltpu.roll(jnp.where(early, ahead, behind), 64, 1)
    ways = [
        jnp.take_along_axis(
            columns, lanes // GROUP * GROUP + k, axis=1, mode="promise_in_bounds"
        )
        + others[k : k + 1, :]
        for k in range(units)
    ]
    top = functools.reduce(jnp.maximum, ways)
    total = functools.reduce(jnp.add, [jnp.exp2(way - top) for way in ways])
    matrix_ref[0, 0] = top + jnp.log2(total)


def turn_kernel(layout, offset_ref, lens_ref, tokens_ref, hidden_ref, turned_ref):
    width = hidden_ref.shape[2]
    first_frame = chunk_of(layout["seqs_here"]) * layout["frame_count"]
    first_seq = first_of(layout["seqs_here"], offset_ref)
    counts = block_counts(lens_ref, tokens_ref, first_seq, first_frame)

    def one_block(i, _):
        seq = jnp.where(i >= counts[0], 1, 0)
        block = i + seq * (layout["units"] // SUB_UNITS - counts[0])
        turned_ref[block, :width, :] = hidden_ref[block].astype(BF16).T
        turned_ref[block, width:, :] = jnp.ones((16, turned_ref.shape[2]), BF16)
        return 0

    lax.fori_loop(0, counts[0] + counts[1], one_block, 0)


def tangent_kernel(
    layout,
    offset_ref,
    lens_ref,
    tokens_ref,
    scale_ref,
    softmax_ref,
    label_table_ref,
    blank_ref,
    label_ref,
    turned_ref,
    inverse_ref,
    parts_ref,
    *refs,
):
    hops = layout["hops"]
    matrix_refs, refs = refs[: hops + 1], refs[hops + 1 :]
    (
        tangents_ref,
        output_bias_ref,
        loss_ref,
        kept_ref,
        sent_ref,
        sums_ref,
        matrices_ref,
        ahead_ref,
        behind_ref,
        blank_part_ref,
        label_part_ref,
        even_ref,
        odd_ref,
        labels_smem,
        label_sem,
    ) = refs
    label_copy = pltpu.make_async_copy(label_table_ref, labels_smem, label_sem)
    label_copy.start()
    frame_count = layout["frame_count"]
    width = turned_ref.shape[1] - 16
    units = layout["units"]
    part = frame_count // 2
    steps = part + units - 1
    here = chunk_of(layout["seqs_here"])
    first_frame = here * frame_count
    first_seq = first_of(layout["seqs_here"], offset_ref)
    chunks = matrices_ref.shape[0]
    vocab = softmax_ref.shape[2]
    received = [(ref, n) for ref in matrix_refs for n in range(ref.shape[0])]
    for place, (matrix_ref, n) in zip(layout["matrix_places"], received):
        matrices_ref[place] = matrix_ref[n, 0]
    starts = lax.broadcasted_iota(jnp.int32, (units, 128), 0)
    lanes = lane_ids(units)
    early = lanes < 64
    gather_ids = lanes // GROUP * GROUP + starts
    own_first = (lane_ids(1) // GROUP) % 2 == 0

    def through(column, matrix):
        ways = column + matrix
        top = jnp.max(ways, axis=0, keepdims=True)
        row = top + jnp.log2(jnp.sum(jnp.exp2(ways - top), axis=0, keepdims=True))
        row = jnp.broadcast_to(row, (units, 128))
        return jnp.take_along_axis(row, gather_ids, axis=1, mode="promise_in_bounds")

    def one_chunk(i, carry):
        column, kept = carry
        other = chunks - 1 - i
        kept = jnp.where(jnp.where(early, i, other) == here, column, kept)
        matrix = jnp.where(early, matrices_ref[here ^ i], matrices_ref[here ^ other])
        return through(column, matrix), kept

    start = jnp.where(early & (starts > 0), NEG, 0.0).astype(F32)
    last, kept = lax.fori_loop(0, chunks, one_chunk, (start, start))
    middle = pltpu.roll(through(kept, parts_ref[...]), 64, 1)
    both_ways(
        blank_ref,
        label_ref,
        units,
        steps,
        jnp.where(early, kept, middle),
        jnp.where(early, middle, kept),
        (ahead_ref, behind_ref),
    )
    log_norm = jnp.max(jnp.where(early, last, pltpu.roll(last, 64, 1)), axis=0, keepdims=True)
    scale, length, bound = (
        jnp.where(own_first, entry(ref, first_seq), entry(ref, first_seq + 1))
        for ref in (scale_ref, lens_ref, tokens_ref)
    )
    length, bound = length.astype(jnp.int32), bound.astype(jnp.int32)
    part_start = first_frame + jnp.where(lane_ids(1) < 64, 0, part)
    last_diagonal = starts + jnp.minimum(length - part_start, part)
    first_blank = jnp.where(starts <= bound, starts, steps)
    first_label = jnp.where(starts < bound, starts, steps)
    norm = log_norm - jnp.log2(scale)

    def one_diagonal(e, _):
        rows = pl.ds(pl.multiple_of(e * units, 8), units)
        behind = behind_ref[rows, :]
        base = ahead_ref[rows, :] - norm
        before_end = last_diagonal > e
        blank_part_ref[rows, :] = jnp.where(
            before_end & (first_blank <= e), jnp.exp2(base + blank_ref[rows, :] + behind), 0.0
        )
        label_part_ref[rows, :] = jnp.where(
            before_end & (first_label <= e),
            jnp.exp2(base + label_ref[rows, :] + pltpu.roll(behind, units - 1, 0)),
            0.0,
        )
        return 0

    lax.fori_loop(0, steps, one_diagonal, 0, unroll=5)

    counts = block_counts(lens_ref, tokens_ref, first_seq, first_frame)
    block_lanes = lane_ids(frame_count)
    part_lanes = lane_ids(part)

    def place_of(i):
        seq = jnp.where(i >= counts[0], 1, 0)
        sub = i - seq * counts[0]
        return seq, sub, seq * (units // SUB_UNITS) + sub

    wide = lane_ids(1)
    loss = jnp.where(here == 0, -log_norm * LN2, 0.0)
    spread = jnp.where(wide == first_seq, loss[:, :1], 0.0)
    loss_ref[...] = spread + jnp.where(wide == first_seq + 1, loss[:, GROUP : GROUP + 1], 0.0)
    label_copy.wait()

    counts_all = counts[0] + counts[1]
    sums_ref[...] = jnp.zeros_like(sums_ref)
    output_bias_ref[...] = jnp.zeros_like(output_bias_ref)

    def prepare(i, tangent_ref):
        seq, sub, block = place_of(i)
        own_lanes = [part_lanes % GROUP + GROUP * (seq + 2 * half) for half in (0, 1)]
        for j in range(SUB_UNITS):
            unit = sub * SUB_UNITS + j
            rows = slice(j * frame_count, (j + 1) * frame_count)
            at = (pl.ds(unit * (units + 1), part, stride=units), slice(None))
            blank, step = (
                jnp.concatenate(
                    [
                        jnp.take_along_axis(ref[at], ids, axis=1, mode="promise_in_bounds")
                        for ids in own_lanes
                    ],
                    axis=0,
                )
                for ref in (blank_part_ref, label_part_ref)
            )
            both = (blank + step) * inverse_ref[block, rows, :]
            for v in range(vocab // 128):
                cut = slice(v * 128, (v + 1) * 128)
                piece = softmax_ref[block, rows, cut] * both
                if v == 0:
                    piece = piece - jnp.where(block_lanes == 0, blank, 0.0)
                piece = piece.astype(BF16)
                tangent_ref[rows, cut] = piece
                tangents_ref[block, rows, cut] = piece
            label = labels_smem[0, seq * units + unit]
            cut = pl.ds(pl.multiple_of(label // 128 * 128, 128), 128)
            piece = softmax_ref[block, rows, cut] * both
            piece = piece - jnp.where((block_lanes == 0) & (label < 128), blank, 0.0)
            piece = (piece - jnp.where(block_lanes == label % 128, step, 0.0)).astype(BF16)
            tangent_ref[rows, cut] = piece
            tangents_ref[block, rows, cut] = piece

    def multiply(i, tangent_ref):
        _, _, block = place_of(i)
        product = jnp.dot(turned_ref[block], tangent_ref[...], preferred_element_type=F32)
        for v in range(vocab // 128):
            sums_ref[v * width : (v + 1) * width, :] += product[:width, v * 128 : (v + 1) * 128]
        output_bias_ref[...] += product[width : width + 1, :]

    in_two_stages(counts_all, prepare, multiply, even_ref, odd_ref)
    part_halves(sums_ref, kept_ref, sent_ref)


def part_halves(sums_ref, kept_ref, sent_ref):
    half = kept_ref.shape[0]
    place = lax.axis_index("tokens") & 1
    sent_ref[:half, :] = sums_ref[pl.ds(pl.multiple_of((1 - place) * half, 8), half), :]
    kept_ref[...] = sums_ref[pl.ds(pl.multiple_of(place * half, 8), half), :]


def inner_kernel(
    layout,
    offset_ref,
    lens_ref,
    tokens_ref,
    tangents_ref,
    hidden_ref,
    weight_ref,
    encoder_ref,
    output_bias_ref,
    loss_ref,
    frame_tangent_ref,
    exact_ref,
    kept_ref,
    sent_ref,
    sums_ref,
    frame_sum_ref,
    token_sum_ref,
    even_ref,
    odd_ref,
):
    seqs, frame_count, width = encoder_ref.shape
    units = token_sum_ref.shape[0] // seqs
    vocab = weight_ref.shape[1]
    first_frame = chunk_of(layout["seqs_here"]) * frame_count
    first_seq = first_of(layout["seqs_here"], offset_ref)
    frame_sum_ref[...] = jnp.zeros_like(frame_sum_ref)
    token_sum_ref[...] = jnp.zeros_like(token_sum_ref)
    half = layout["half"]
    for side in (0, 1):
        unset = slice(side * half + layout["token"], (side + 1) * half)
        sums_ref[unset, :] = jnp.zeros_like(sums_ref[unset, :])
    counts = block_counts(lens_ref, tokens_ref, first_seq, first_frame)

    def place_of(i):
        seq = jnp.where(i >= counts[0], 1, 0)
        sub = i - seq * counts[0]
        return seq, sub, seq * (units // SUB_UNITS) + sub

    def product_of(tangents):
        return lax.dot_general(
            tangents, weight_ref[...], (((1,), (1,)), ((), ())), preferred_element_type=F32
        )

    def add_up(i, product):
        seq, sub, block = place_of(i)
        hidden = hidden_ref[block]
        inner = product * (1.0 - hidden * hidden)
        total = frame_sum_ref[seq]
        for j in range(SUB_UNITS):
            rows = slice(j * frame_count, (j + 1) * frame_count)
            total = total + inner[rows]
            token_sum_ref[pl.ds(seq * units + sub * SUB_UNITS + j, 1), :] = jnp.sum(
                inner[rows], axis=0, keepdims=True
            )
        frame_sum_ref[seq] = total

    def multiply_two(n, product_ref):
        both = [tangents_ref[place_of(2 * n + m)[2]] for m in (0, 1)]
        product_ref[...] = product_of(jnp.concatenate(both, axis=0))

    def add_up_two(n, product_ref):
        half = product_ref.shape[0] // 2
        add_up(2 * n, product_ref[:half])
        add_up(2 * n + 1, product_ref[half:])

    blocks = counts[0] + counts[1]
    in_two_stages(blocks // 2, multiply_two, add_up_two, even_ref, odd_ref)

    @pl.when(blocks % 2 == 1)
    def _():
        add_up(blocks - 1, product_of(tangents_ref[place_of(blocks - 1)[2]]))

    low = frame_sum_ref[...].reshape(seqs * frame_count, width).astype(BF16)
    frame_tangent_ref[...] = low
    product = lax.dot_general(
        encoder_ref[...].reshape(seqs * frame_count, width),
        low,
        (((0,), (0,)), ((), ())),
        preferred_element_type=F32,
    )
    encoder_bias = jnp.sum(low.astype(F32), axis=0, keepdims=True)
    blocks_each = width // 128 // 2
    exact_ref[...] = jnp.zeros_like(exact_ref)
    for v in range(width // 128):
        cut = slice(v * 128, (v + 1) * 128)
        start, n = v // blocks_each * half, v % blocks_each
        sums_ref[start + n * width : start + (n + 1) * width, :] = product[:, cut]
        at = start + layout["token"] + n * layout["token_rows"] + first_seq * units
        sums_ref[pl.ds(pl.multiple_of(at, 8), seqs * units), :] = token_sum_ref[:, cut]
        at = vocab // 128 + v
        exact_ref[at : at + 1, :] = encoder_bias[:, cut]
    for v in range(vocab // 128):
        exact_ref[v : v + 1, :] = output_bias_ref[:, v * 128 : (v + 1) * 128]
    at = vocab // 128 + width // 128
    exact_ref[at : at + 1, :] = loss_ref[...]
    part_halves(sums_ref, kept_ref, sent_ref)
    write_exact(sent_ref, kept_ref.shape[0], exact_ref[...])


def encoder_kernel(frame_tangent_ref, encoder_weight_ref, encoder_gradient_ref, mark_ref):
    mark_ref[...] = jnp.zeros_like(mark_ref)
    encoder_gradient_ref[...] = lax.dot_general(
        frame_tangent_ref[...],
        encoder_weight_ref[...],
        (((1,), (1,)), ((), ())),
        preferred_element_type=F32,
    ).reshape(encoder_gradient_ref.shape)


def two_halves(stage, half):
    upper = upper_of(stage)
    own = pl.ds(pl.multiple_of(jnp.where(upper != 0, half, 0), 16), half)
    other = pl.ds(pl.multiple_of(jnp.where(upper != 0, 0, half), 16), half)
    return own, other


def exact_rows(kind):
    return EXACT if kind == F32 else 3 * EXACT


def write_exact(sent_ref, at, values):
    if sent_ref.dtype == F32:
        sent_ref[at : at + EXACT, :] = values
        return
    for n in range(3):
        part = values.astype(BF16)
        sent_ref[at + n * EXACT : at + (n + 1) * EXACT, :] = part
        values = values - part.astype(F32)


def read_exact(received_ref, at):
    parts = [
        received_ref[at + n * EXACT : at + (n + 1) * EXACT, :].astype(F32)
        for n in range(exact_rows(received_ref.dtype) // EXACT)
    ]
    return sum(parts[1:], parts[0])


def halve_kernel(stages, merge, has_exact, *refs):
    count, at = len(stages), 0
    outs = refs[2 * count + has_exact :]
    for n, stage in enumerate(stages):
        kept_ref, received_ref = refs[2 * n : 2 * n + 2]
        half = kept_ref.shape[0] // 2
        own, other = two_halves(stage, half)
        if merge:
            next_ref, sent_ref = (ref.at[at : at + half, :] for ref in outs[:2])
            at += half
        else:
            next_ref, sent_ref = outs[2 * n : 2 * n + 2]
        sent = kept_ref[other, :] + received_ref[other, :].astype(F32)
        sent_ref[:half, :] = sent.astype(sent_ref.dtype)
        next_ref[...] = kept_ref[own, :] + received_ref[own, :].astype(F32)
    if has_exact:
        exact = refs[2 * count][...] + read_exact(received_ref, kept_ref.shape[0])
        outs[-1][...] = exact
        write_exact(outs[-2], outs[-3].shape[0], exact)


def add_kernel(count, *refs):
    sum_ref, exact_sum_ref = refs[-2:]
    at = 0
    for n in range(count):
        kept_ref, received_ref = refs[2 * n : 2 * n + 2]
        rows = kept_ref.shape[0]
        total = kept_ref[...] + received_ref[:rows, :].astype(F32)
        high = total.astype(BF16)
        sum_ref[at : at + rows, :] = high
        at += rows
    sum_ref[at : at + rows, :] = (total - high.astype(F32)).astype(BF16)
    exact = refs[2 * count][...] + read_exact(received_ref, rows)
    exact_sum_ref[...] = exact
    write_exact(sum_ref, at + rows, exact)


def last_kernel(own_ref, other_ref, exact_ref, *sum_refs):
    *sum_refs, exact_sum_ref = sum_refs
    at = 0
    for n, sum_ref in enumerate(sum_refs):
        rows = sum_ref.shape[0]
        totals = []
        for ref in (own_ref, other_ref):
            total = ref[at : at + rows, :].astype(F32)
            if n == len(sum_refs) - 1:
                total = total + ref[at + rows : at + 2 * rows, :].astype(F32)
            totals.append(total)
        sum_ref[...] = (totals[0] + totals[1]).astype(BF16)
        at += rows
    exact_sum_ref[...] = exact_ref[...] + read_exact(other_ref, at + rows)


def join_kernel(stages, merged, *refs):
    count, at = len(stages), 0
    joined_refs = refs[-count:]
    for n, (stage, joined_ref) in enumerate(zip(stages, joined_refs)):
        half = joined_ref.shape[0] // 2
        own, other = two_halves(stage, half)
        if merged:
            own_ref, other_ref = (ref.at[at : at + half, :] for ref in refs[:2])
            at += half
        else:
            own_ref, other_ref = refs[2 * n : 2 * n + 2]
        joined_ref[own, :] = own_ref[...]
        joined_ref[other, :] = other_ref[...]


def copy_out(output_ref, rest_ref, side, output_hbm, encoder_hbm, output_buffer, encoder_buffer, sems):
    copies = []
    for source, buffer, target in (
        (output_ref, output_buffer, output_hbm),
        (rest_ref, encoder_buffer, encoder_hbm),
    ):
        rows, columns = buffer.shape
        for v in range(columns // 128):
            buffer[:, v * 128 : (v + 1) * 128] = source[v * rows : (v + 1) * rows, :].astype(F32)
        start = pl.multiple_of(side * columns, 128)
        copy = pltpu.make_async_copy(
            buffer, target.at[:, pl.ds(start, columns)], sems.at[len(copies)]
        )
        copy.start()
        copies.append(copy)
    return copies


def finish_own_kernel(
    output_ref,
    rest_ref,
    exact_ref,
    output_hbm,
    encoder_hbm,
    output_bias_hbm,
    encoder_bias_hbm,
    losses_hbm,
    output_buffer,
    encoder_buffer,
    output_bias_ref,
    encoder_bias_ref,
    losses_ref,
    sems,
):
    place = lax.axis_index("tokens") & 1
    copies = copy_out(
        output_ref,
        rest_ref,
        place,
        output_hbm,
        encoder_hbm,
        output_buffer,
        encoder_buffer,
        sems,
    )

    def rows(start, count):
        return jnp.concatenate([exact_ref[start + n : start + n + 1, :] for n in range(count)], axis=1)

    output_blocks, encoder_blocks = output_bias_ref.shape[1] // 128, encoder_bias_ref.shape[1] // 128
    output_bias_ref[...] = rows(0, output_blocks)
    encoder_bias_ref[...] = rows(output_blocks, encoder_blocks)
    loss = rows(output_blocks + encoder_blocks, 1)
    losses_ref[...] = jnp.sum(
        jnp.where(lane_ids(1) == lax.axis_index("frames"), loss, 0.0), axis=1, keepdims=True
    )
    for source, target in (
        (output_bias_ref, output_bias_hbm),
        (encoder_bias_ref, encoder_bias_hbm),
        (losses_ref, losses_hbm),
    ):
        copy = pltpu.make_async_copy(source, target, sems.at[len(copies)])
        copy.start()
        copies.append(copy)
    for copy in copies:
        copy.wait()


def finish_kernel(
    layout,
    output_other_ref,
    rest_own_ref,
    rest_other_ref,
    predictor_ref,
    predictor_weight_ref,
    output_weight_begun,
    encoder_weight_begun,
    output_weight_hbm,
    encoder_weight_hbm,
    weight_gradient_hbm,
    bias_gradient_hbm,
    predictor_gradient_hbm,
    output_buffer,
    encoder_buffer,
    weight_gradient_ref,
    bias_gradient_ref,
    predictor_gradient_ref,
    tokens_ref,
    sems,
):
    width = encoder_buffer.shape[0]
    place = lax.axis_index("tokens") & 1
    copies = copy_out(
        output_other_ref,
        rest_other_ref,
        1 - place,
        output_weight_hbm,
        encoder_weight_hbm,
        output_buffer,
        encoder_buffer,
        sems,
    )
    count = layout["token_rows"]
    blocks_each = width // 128 // 2

    def gather_tokens(*halves):
        for v in range(width // 128):
            at = layout["token"] + v % blocks_each * count
            tokens_ref[:, v * 128 : (v + 1) * 128] = halves[v // blocks_each][
                at : at + count, :
            ].astype(F32)

    pl.when(place == 0)(lambda: gather_tokens(rest_own_ref, rest_other_ref))
    pl.when(place == 1)(lambda: gather_tokens(rest_other_ref, rest_own_ref))
    tokens = tokens_ref[...]
    held_rows = predictor_gradient_ref.shape[0]

    def send(source, target):
        copy = pltpu.make_async_copy(source, target, sems.at[len(copies)])
        copy.start()
        copies.append(copy)

    weight_gradient_ref[...] = lax.dot_general(
        predictor_ref[...],
        tokens.astype(BF16),
        (((0,), (0,)), ((), ())),
        preferred_element_type=F32,
    )
    send(weight_gradient_ref, weight_gradient_hbm)
    bias_gradient_ref[...] = jnp.sum(tokens, axis=0, keepdims=True)
    send(bias_gradient_ref, bias_gradient_hbm)
    device = lax.axis_index("frames") * lax.axis_size("tokens") + lax.axis_index("tokens")
    mine = jnp.concatenate(
        [tokens_ref[pl.ds(device * held_rows + r, 1), :] for r in range(held_rows)], axis=0
    )
    predictor_gradient_ref[:, 0, :] = lax.dot_general(
        mine.astype(BF16),
        predictor_weight_ref[...],
        (((1,), (1,)), ((), ())),
        preferred_element_type=F32,
    )
    send(predictor_gradient_ref, predictor_gradient_hbm)
    for copy in copies:
        copy.wait()


def in_hbm(array):
    return pltpu.with_memory_space_constraint(array, pltpu.HBM)


def in_vmem(array):
    return pltpu.with_memory_space_constraint(array, pltpu.VMEM)


def permuted(array, partner):
    frames, tokens = lax.axis_size("frames"), lax.axis_size("tokens")
    pairs = []
    for f in range(frames):
        for k in range(tokens):
            g, h = partner(f, k)
            pairs.append((f * tokens + k, g * tokens + h))
    return lax.ppermute(array, AXES, pairs)


def axis_flips(axis):
    flips, bit = [], lax.axis_size(axis) // 2
    while bit:
        flips.append(((bit, 0) if axis == "frames" else (0, bit), bit))
        bit //= 2
    return flips


def stacked(blocks):
    if len(blocks) == 1:
        return blocks[0]
    shape = (sum(block.shape[0] for block in blocks),) + blocks[0].shape[1:]
    return call(stack_kernel, blocks, [(shape, blocks[0].dtype, True)])[0]


def doubled(blocks, places, flips):
    blocks, places = list(blocks), list(places)
    for bits, mark in flips:
        blocks.append(permuted(stacked(blocks), across((bits, bits))))
        places += [place ^ mark for place in places]
    return blocks, places


def stages(even, odd):
    frame_bits = [(1 << i, 0) for i in range(lax.axis_size("frames").bit_length() - 1)]
    token_bits = [(0, 1 << i) for i in range(1, lax.axis_size("tokens").bit_length() - 1)]
    first = frame_bits[:1] + token_bits + frame_bits[1:2]
    orders = [first[shift:] + first[:shift] + frame_bits[2:] for shift in (even, odd)]
    return list(zip(*orders))


def upper_of(stage):
    f, k = lax.axis_index("frames"), lax.axis_index("tokens")
    even, odd = ((f & frame_bit) | (k & token_bit) for frame_bit, token_bit in stage)
    return jnp.where((k & 1) == 0, even, odd)


def across(stage):
    return lambda f, k: (f ^ stage[k & 1][0], k ^ stage[k & 1][1])


def neighbour(f, k):
    return f, k ^ 1


def call(body, ins, outs, scratch=(), limit=4):
    vmem = pl.BlockSpec(memory_space=pltpu.VMEM)
    there = [array is not None for array in ins]

    def kernel(*refs):
        given = iter(refs)
        body(*(next(given) if here else None for here in there), *given)

    return pl.pallas_call(
        kernel,
        in_specs=[vmem] * sum(there),
        out_specs=[
            pl.BlockSpec(memory_space=pl.ANY) if inside is None else vmem for _, _, inside in outs
        ],
        out_shape=[
            pltpu.VMEM(shape, kind) if inside else jax.ShapeDtypeStruct(shape, kind)
            for shape, kind, inside in outs
        ],
        scratch_shapes=list(scratch),
        compiler_params=pltpu.CompilerParams(vmem_limit_bytes=limit * 2**20),
    )(*(in_vmem(array) for array in ins if array is not None))


def reduced_and_gathered(pieces, exact, beside, held):
    plans = list(zip(*(stages(*shifts) for shifts in ORDERS)))
    flat = [a for kept, sent in pieces for a in (kept, permuted(sent, neighbour))]
    way_back = []
    *plans, last_plan = plans
    for number, plan in enumerate(plans):
        plan = plan[: len(flat) // 2]
        merge = len(plan) > 1 and len(set(plan)) == 1
        halves = [kept.shape[0] // 2 for kept in flat[::2]]
        way_back.append((plan, merge, [2 * half for half in halves]))
        if merge:
            halves = [sum(halves)]
        sent_type = SENT_TYPES[min(number, len(SENT_TYPES) - 1)]
        outs = []
        for n, half in enumerate(halves):
            last = n == len(halves) - 1
            sent_rows = half + (exact_rows(sent_type) if last else 0)
            kind = sent_type if last else BF16
            outs += [((half, 128), F32, True), ((sent_rows, 128), kind, True)]
        exact_out = ((EXACT, 128), F32, True)
        if number < 2:
            given, flat = flat, []
            for n, stage in enumerate(plan):
                last = n == len(plan) - 1
                made = call(
                    functools.partial(halve_kernel, [stage], False, last),
                    given[2 * n : 2 * n + 2] + [exact] * last,
                    outs[2 * n : 2 * n + 2] + [exact_out] * last,
                )
                flat += made[:2]
                if last:
                    exact = made[2]
        else:
            *flat, exact = call(
                functools.partial(halve_kernel, plan, merge, True),
                [*flat, exact],
                [*outs, exact_out],
            )
        flat = [
            permuted(a, across(plan[n // 2])) if n % 2 else a for n, a in enumerate(flat)
        ]
    shapes = [kept.shape for kept in flat[::2]]
    rows = sum(shape[0] for shape in shapes) + shapes[-1][0] + exact_rows(BF16)
    own, exact = call(
        functools.partial(add_kernel, len(shapes)),
        [*flat, exact, *beside],
        [((rows, 128), BF16, True), ((EXACT, 128), F32, True)],
    )
    other = permuted(own, across(last_plan[0]))
    vmem = pl.BlockSpec(memory_space=pltpu.VMEM)
    *arrays, exact = pl.pallas_call(
        last_kernel,
        in_specs=[vmem, vmem, vmem],
        out_specs=[vmem] * (len(shapes) + 1),
        out_shape=[pltpu.VMEM(shape, BF16) for shape in shapes] + [pltpu.VMEM((EXACT, 128), F32)],
        compiler_params=pltpu.CompilerParams(vmem_limit_bytes=4 * 2**20),
    )(in_vmem(own), in_vmem(other), in_vmem(exact))
    for number, (plan, merged, sizes) in reversed(list(enumerate(way_back))):
        flat = [a for array, stage in zip(arrays, plan) for a in (array, permuted(array, across(stage)))]
        outs = [((size, 128), BF16, True) for size in sizes]
        if number in (0,):
            arrays = [
                call(
                    functools.partial(join_kernel, [stage], False),
                    flat[2 * n : 2 * n + 2],
                    outs[n : n + 1],
                )[0]
                for n, stage in enumerate(plan)
            ]
        else:
            given = [*flat, *held] if number == 1 else flat
            arrays = call(functools.partial(join_kernel, plan, merged), given, outs)
    return [(array, permuted(array, neighbour)) for array in arrays], exact


def per_device(
    encoder_out,
    encoder_weight,
    encoder_bias,
    predictor_out,
    predictor_weight,
    predictor_bias,
    output_weight,
    output_bias,
    labels,
    frame_lens,
    token_lens,
    loss_scale,
):
    seq_count, frame_count, width = encoder_out.shape
    vocab = output_weight.shape[1]
    all_seqs = labels.shape[0]
    held_seqs, held_units = predictor_out.shape[:2]
    assert held_seqs == 1
    frame_axis, token_axis = lax.axis_size("frames"), lax.axis_size("tokens")
    device_count = frame_axis * token_axis
    units = held_units * token_axis
    calls = seq_count // 2
    diagonals = (frame_count // 2 + units) * units
    vmem = pl.BlockSpec(memory_space=pltpu.VMEM)
    anywhere = pl.BlockSpec(memory_space=pl.ANY)

    in_plane = seq_count == 2 and token_axis == 4 and frame_axis == 8

    def turned_over(f, k):
        return 2 * k + (f & 1), f >> 1

    weights = (
        encoder_weight,
        encoder_bias.reshape(1, width),
        predictor_weight,
        predictor_bias.reshape(1, width),
        output_weight,
        output_bias.reshape(1, vocab),
        frame_lens.reshape(1, all_seqs),
        token_lens.reshape(1, all_seqs),
        loss_scale.reshape(1, all_seqs),
    )
    if in_plane:
        plane = [((0, 2), 2), ((0, 1), 1), ((1, 0), 256)]
        encoder = permuted(encoder_out, turned_over)
        packet = pl.pallas_call(
            label_packet_kernel,
            in_specs=[anywhere] * 2,
            out_specs=vmem,
            out_shape=pltpu.VMEM((1, held_units + 2, width), BF16),
            scratch_shapes=[
                pltpu.VMEM((held_units, width), BF16),
                pltpu.VMEM(labels.shape, jnp.int32),
                pltpu.SemaphoreType.DMA((2,)),
            ],
            compiler_params=pltpu.CompilerParams(vmem_limit_bytes=4 * 2**20),
        )(in_hbm(predictor_out.reshape(held_units, width)), in_hbm(labels))
        packets, packet_places = doubled([packet], [0], plane)
        own_seqs = None
    else:
        packet_rows = held_units * width // 128
        packets = pl.pallas_call(
            packet_kernel,
            in_specs=[anywhere],
            out_specs=vmem,
            out_shape=jax.ShapeDtypeStruct((device_count, packet_rows, 128), BF16),
            scratch_shapes=[
                pltpu.VMEM((held_units, width), BF16),
                pltpu.VMEM((packet_rows, 128), F32),
                pltpu.SemaphoreType.DMA,
            ],
            compiler_params=pltpu.CompilerParams(vmem_limit_bytes=4 * 2**20),
        )(in_hbm(predictor_out.reshape(held_units, width)))
        packets, packet_places = [lax.all_to_all(packets, AXES, 0, 0, tiled=True)], None
        encoder, own_seqs = encoder_out, seq_count
    if not in_plane:
        label_blocks, label_places = doubled([labels[None]], [0], axis_flips("tokens"))
    weights = pl.pallas_call(
        load_kernel,
        in_specs=[anywhere] * len(weights),
        out_specs=[vmem] * len(weights),
        out_shape=[pltpu.VMEM(w.shape, w.dtype) for w in weights],
        scratch_shapes=[pltpu.SemaphoreType.DMA((len(weights),))],
        compiler_params=pltpu.CompilerParams(vmem_limit_bytes=4 * 2**20),
    )(*map(in_hbm, weights))
    *weights, frame_lens, token_lens, loss_scale = weights
    lens = frame_lens, token_lens
    (frames,) = call(
        project_kernel, (encoder, weights[0], weights[1]), [(encoder_out.shape, F32, True)]
    )

    score_shapes = [
        ((2 * units // SUB_UNITS, SUB_UNITS * frame_count, vocab), F32),
        ((2 * units, width), F32),
        ((diagonals, 128), F32),
        ((diagonals, 128), F32),
        ((2 * units // SUB_UNITS, SUB_UNITS * frame_count, width), F32),
        ((2 * units // SUB_UNITS, SUB_UNITS * frame_count, 128), F32),
        ((units, 128), F32),
        ((1, 1, units, 128), F32),
    ]

    def scores(offset, frames):
        if in_plane:
            body, given = functools.partial(packet_table_kernel, packet_places), packets
        else:
            body = functools.partial(table_kernel, label_places, own_seqs)
            given = (offset, *label_blocks)
        (table,) = call(body, given, [((1, 128), jnp.int32, True)])
        scored = call(
            functools.partial(score_kernel, own_seqs, packet_places),
            (offset, *lens, frames, *weights[2:], table, *packets),
            [(shape, kind, True) for shape, kind in score_shapes],
            scratch=[
                pltpu.VMEM((SUB_UNITS * frame_count, vocab), F32),
                pltpu.VMEM((SUB_UNITS * frame_count, vocab), F32),
                pltpu.SMEM((1, 128), jnp.int32),
                pltpu.SemaphoreType.DMA,
            ],
            limit=8,
        )
        return [table, *scored]

    offsets = 2 * jnp.arange(calls, dtype=jnp.int32).reshape(calls, 1, 1)
    encoders = encoder.reshape(calls, 2, frame_count, width)
    if calls == 1:
        scored = scores(None, frames)
        matrix = scored[-1]
    else:
        scored = lax.map(
            lambda given: scores(*given),
            (offsets, frames.reshape(calls, 2, frame_count, width)),
        )
        matrix = scored[-1].reshape(1, calls, units, 128)

    chunk_flips = [((0, 2), 4), ((1, 0), 1), ((0, 1), 2)] if in_plane else axis_flips("frames")
    matrices, matrix_places = doubled([matrix], [0], chunk_flips)
    if in_plane:
        packets, packet_places = doubled(
            [stacked(packets)], packet_places, [((4, 0), 1024), ((2, 0), 512)]
        )
    (predictor_all,) = call(
        functools.partial(predictor_kernel, packet_places),
        packets,
        [((all_seqs * units, width), BF16, True)],
        scratch=[pltpu.VMEM((all_seqs * units, width), F32)],
        limit=8,
    )
    layout = {"matrix_places": matrix_places, "seqs_here": own_seqs, "frame_count": frame_count, "units": units}
    align = 16 * device_count // 4
    blocks_each = width // 128 // 2
    layout["token"], layout["token_rows"] = blocks_each * width, all_seqs * units
    half = layout["token"] + blocks_each * all_seqs * units
    layout["half"] = half + (-half % align)
    rest_rows = 2 * layout["half"]
    output_rows = vocab // 128 * width
    assert output_rows % (2 * align) == 0 and vocab // 128 + width // 128 < EXACT

    blocks = 2 * units // SUB_UNITS
    block_rows = SUB_UNITS * frame_count

    def turns(offset, scored):
        hidden = scored[5]
        (turned,) = call(
            functools.partial(turn_kernel, layout),
            (offset, *lens, hidden),
            [((hidden.shape[0], width + 16, hidden.shape[1]), BF16, True)],
        )
        return turned

    def tangents(offset, scored, turned, matrices):
        table, softmax, _, blank, label, _, inverse, parts = scored
        return call(
            functools.partial(tangent_kernel, dict(layout, hops=len(matrices) - 1)),
            (
                *(offset, *lens, loss_scale, softmax, table, blank, label),
                *(turned, inverse, parts, *matrices),
            ),
            [
                ((blocks, block_rows, vocab), BF16, True),
                ((1, vocab), F32, True),
                ((1, 128), F32, True),
                ((output_rows // 2, 128), F32, True),
                ((output_rows // 2, 128), F32, True),
            ],
            scratch=[
                pltpu.VMEM((output_rows, 128), F32),
                pltpu.VMEM((frame_axis, units, 128), F32),
                pltpu.VMEM((diagonals, 128), F32),
                pltpu.VMEM((diagonals, 128), F32),
                pltpu.VMEM((diagonals, 128), F32),
                pltpu.VMEM((diagonals, 128), F32),
                pltpu.VMEM((block_rows, vocab), BF16),
                pltpu.VMEM((block_rows, vocab), BF16),
                pltpu.SMEM((1, 128), jnp.int32),
                pltpu.SemaphoreType.DMA,
            ],
            limit=12,
        )

    def inners(offset, encoder, scored, tangent, output_bias_sum, loss):
        return call(
            functools.partial(inner_kernel, layout),
            (
                *(offset, *lens, tangent, scored[5], weights[4], encoder),
                *(output_bias_sum, loss),
            ),
            [
                ((2 * frame_count, width), BF16, True),
                ((EXACT, 128), F32, True),
                ((rest_rows // 2, 128), F32, True),
                ((rest_rows // 2 + EXACT, 128), F32, True),
            ],
            scratch=[
                pltpu.VMEM((rest_rows, 128), F32),
                pltpu.VMEM((2, frame_count, width), F32),
                pltpu.VMEM((2 * units, width), F32),
                pltpu.VMEM((2 * block_rows, width), F32),
                pltpu.VMEM((2 * block_rows, width), F32),
            ],
            limit=10,
        )

    def encoder_gradient_of(frame_tangent):
        return call(
            encoder_kernel,
            (frame_tangent, weights[0]),
            [((2, frame_count, width), F32, False), ((8, 128), F32, True)],
        )

    if calls == 1:
        scored = scored[:-1]
        turned = turns(None, scored)
        tangent, output_bias_sum, loss, *output_sums = tangents(None, scored, turned, matrices)

        frame_tangent, exact, *rest = inners(
            None, encoder, scored, tangent, output_bias_sum, loss
        )
        sums = [*output_sums, *rest, exact]
        if in_plane:
            frame_tangent = permuted(frame_tangent, turned_over)
        encoder_gradient, mark = encoder_gradient_of(frame_tangent)
        beside, held = [frame_tangent], [predictor_all, mark]
    else:

        def add_call(sums, given):
            offset, encoder, scored, call = given
            own = [lax.dynamic_slice_in_dim(m, call, 1, 1) for m in matrices]
            turned = turns(offset, scored)
            tangent, output_bias_sum, loss, *more = tangents(offset, scored, turned, own)
            frame_tangent, exact, *rest = inners(
                offset, encoder, scored, tangent, output_bias_sum, loss
            )
            sums = [a + b for a, b in zip(sums, [*more, *rest, exact])]
            return sums, encoder_gradient_of(frame_tangent)[0]

        sizes = (output_rows // 2,) * 2 + (rest_rows // 2, rest_rows // 2 + EXACT, EXACT)
        sums, encoder_gradient = lax.scan(
            add_call,
            [jnp.zeros((size, 128), F32) for size in sizes],
            (offsets, encoders, scored[:-1], jnp.arange(calls)),
        )
        encoder_gradient = encoder_gradient.reshape(encoder_out.shape)
        beside, held = [], [predictor_all]

    halves, exact = reduced_and_gathered(
        [sums[:2], sums[2:4]], sums[4], beside, held
    )
    (output_own, output_other), (rest_own, rest_other) = halves
    buffers = [
        pltpu.VMEM((width, vocab // 2), F32),
        pltpu.VMEM((width, width // 2), F32),
    ]
    *begun, output_bias_gradient, encoder_bias_gradient, losses = call(
        finish_own_kernel,
        (output_own, rest_own, exact),
        [
            ((width, vocab), F32, None),
            ((width, width), F32, None),
            ((1, vocab), F32, None),
            ((1, width), F32, None),
            ((1, 1), F32, None),
        ],
        scratch=[
            *buffers,
            pltpu.VMEM((1, vocab), F32),
            pltpu.VMEM((1, width), F32),
            pltpu.VMEM((1, 1), F32),
            pltpu.SemaphoreType.DMA((5,)),
        ],
        limit=8,
    )
    shapes = [(width, vocab), (width, width), (width, width), (1, width), (held_units, 1, width)]
    finished = pl.pallas_call(
        functools.partial(finish_kernel, layout),
        in_specs=[vmem] * 5 + [anywhere] * 2,
        out_specs=[anywhere] * len(shapes),
        out_shape=[jax.ShapeDtypeStruct(shape, F32) for shape in shapes],
        input_output_aliases={5: 0, 6: 1},
        scratch_shapes=[
            *buffers,
            *(pltpu.VMEM(shape, F32) for shape in shapes[2:]),
            pltpu.VMEM((all_seqs * units, width), F32),
            pltpu.SemaphoreType.DMA((5,)),
        ],
        compiler_params=pltpu.CompilerParams(vmem_limit_bytes=20 * 2**20),
    )(
        *map(in_vmem, (output_other, rest_own, rest_other, predictor_all, weights[2])),
        *map(in_hbm, begun),
    )
    return (
        losses.reshape(1),
        encoder_gradient,
        finished[4].transpose(1, 0, 2),
        finished[1],
        encoder_bias_gradient.reshape(width),
        finished[2],
        finished[3].reshape(width),
        finished[0],
        output_bias_gradient.reshape(vocab),
    )


def solution(mesh):
    placed = (
        P("tokens", "frames", None),
        P(),
        P(),
        P("frames", "tokens", None),
        P(),
        P(),
        P(),
        P(),
        P(None, "tokens"),
        P(),
        P(),
        P(),
    )
    return jax.shard_map(
        per_device,
        mesh=mesh,
        in_specs=placed,
        out_specs=(
            P("frames"),
            P("tokens", "frames", None),
            P("frames", "tokens", None),
            P(),
            P(),
            P(),
            P(),
            P(),
            P(),
        ),
        check_vma=False,
    )
```
